32 devices in a mesh: point: 4 (over z), dom: 8 (over y, x, core).
Axes of the slice: x: 2, y: 2, z: 4, core: 2. Of those that a mesh axis runs over, the one named last changes fastest.
Arguments:
- sources: float32 [16, 16, 1024], P(None, 'dom'), may hold values from -17 to 17
- potential: float32 [16, 1024], P('dom'), may hold values from 0 to 2
- iter_counts: int32 [4], P('point'), may hold values from 1 to 6, as said below
Outputs:
- gram_b: float32 [2, 64, 64], replicated
- gram_a: float32 [2, 64, 64], replicated
The draws below stay inside these ranges and needn't reach their ends.
Inputs may be any that keep to these rules, and one draw needn't show every extreme that they name: `iter_counts`: iterations of each quadrature point; some point takes 6 in every draw.
All inputs are finite; a program needn't handle non-finite values.
Results may differ from the reference program's by a relative error of at most 0.00018.
Values sent between devices are 32-bit elements; how exact they have to be, the bound alone decides.
No kernel may reach another device: no remote copies, remote signals or barrier semaphores. Data moves between devices by JAX's collectives and lax.ppermute only.
A program may use at most 64 MiB of HBM per device.

```python
import math
import jax
import jax.numpy as jnp
from jax import lax

L = 16
MOMENTS = 4
ITERS = 6
GX = 32
POINTS = 4
NZ = 16


def plane_blocks(count):
    return jnp.arange(NZ) * count // NZ


def draw_iter_counts(key, part):
    key = jax.random.fold_in(key, 7)
    base_key, heavy_key = jax.random.split(key)
    base = jax.random.randint(base_key, (POINTS,), 1, 3)
    heavy = jax.random.randint(heavy_key, (), 0, POINTS)
    return jnp.where(jnp.arange(POINTS) == heavy, ITERS, base).astype(jnp.int32)


def draw_potential(key, part):
    key = jax.random.fold_in(key, 11)
    level_key, rough_key = jax.random.split(key)
    levels = jnp.exp(jax.random.uniform(level_key, (8,), jnp.float32, -3.0, 0.69))
    rough = jax.random.uniform(rough_key, (NZ, GX * GX), jnp.float32, 0.5, 1.0)
    blocks = plane_blocks(8)
    return (levels[blocks][:, None] * rough).astype(jnp.float32)


def draw_sources(key, part):
    key = jax.random.fold_in(key, 13)
    block_key, half_key, core_key = jax.random.split(key, 3)
    block_amp = jnp.exp(jax.random.uniform(block_key, (L, 8), jnp.float32, -2.5, 0.5))
    core = jnp.clip(jax.random.normal(core_key, (L, NZ, GX * GX), jnp.float32), -6.0, 6.0)
    half_amp = jnp.exp(jax.random.uniform(half_key, (L, 2), jnp.float32, -0.5, 0.5))
    amplitude = block_amp[:, plane_blocks(8)] * half_amp[:, plane_blocks(2)]
    return (core * amplitude[:, :, None]).astype(jnp.float32)


def setup_inputs(seed: int = 0) -> dict:
    key_of = jax.random.split(jax.random.key(seed), 4)
    return {
        "sources": draw_sources(jax.random.fold_in(key_of[3], 71), 0),
        "potential": draw_potential(jax.random.fold_in(key_of[3], 71), 0),
        "iter_counts": draw_iter_counts(jax.random.fold_in(key_of[3], 71), 0),
    }


COEF_NEAR = 4.0 / 3.0
COEF_FAR = -1.0 / 12.0
GAMMA = 2.0
RADIUS = 1.5


def plane_terms(values, side):
    lead = values.shape[:-1]
    planes = values.reshape(lead + (side, side))
    summed = COEF_NEAR * (jnp.roll(planes, 1, -2) + jnp.roll(planes, -1, -2) + jnp.roll(planes, 1, -1) + jnp.roll(planes, -1, -1))
    summed = summed + COEF_FAR * (jnp.roll(planes, 2, -2) + jnp.roll(planes, -2, -2) + jnp.roll(planes, 2, -1) + jnp.roll(planes, -2, -1))
    return summed.reshape(values.shape)


def hamiltonian(values, potential):
    lap = -7.5 * values + plane_terms(values, GX)
    lap = lap + COEF_NEAR * (jnp.roll(values, 1, 2) + jnp.roll(values, -1, 2))
    lap = lap + COEF_FAR * (jnp.roll(values, 2, 2) + jnp.roll(values, -2, 2))
    return -0.5 * lap + potential * values


def complex_mul(first, second):
    return jnp.stack([first[0] * second[0] - first[1] * second[1], first[0] * second[1] + first[1] * second[0]])


def complex_div(first, second):
    denom = second[0] * second[0] + second[1] * second[1]
    return jnp.stack([(first[0] * second[0] + first[1] * second[1]) / denom, (first[1] * second[0] - first[0] * second[1]) / denom])


def bilinear(first, second):
    real_part = jnp.sum(first[0] * second[0] - first[1] * second[1], axis=(1, 2))
    imag_part = jnp.sum(first[0] * second[1] + first[1] * second[0], axis=(1, 2))
    return jnp.stack([real_part, imag_part])


def scaled(coeffs, values):
    return complex_mul(coeffs[:, :, None, None], values)


def shifted(values, potential, shift_re, shift_im):
    applied = hamiltonian(values, potential)
    return jnp.stack([shift_re * values[0] - shift_im * values[1] - applied[0], shift_re * values[1] + shift_im * values[0] - applied[1]])


def moment_terms(solution, residual, sources, angle_now, shift_re, shift_im):
    applied = jnp.stack([shift_re * solution[0] - shift_im * solution[1] - sources[0] + residual[0], shift_re * solution[1] + shift_im * solution[0] - sources[1] + residual[1]])
    angles = (jnp.arange(MOMENTS).astype(jnp.float32) + 1.0) * angle_now
    coeffs = 0.25 * jnp.stack([jnp.cos(angles), jnp.sin(angles)])
    s_terms = complex_mul(coeffs[:, :, None, None, None], solution[:, None])
    h_terms = complex_mul(coeffs[:, :, None, None, None], applied[:, None])
    width = MOMENTS * solution.shape[1]
    return s_terms.reshape(2, width, -1), h_terms.reshape(2, width, -1)


def gram_of(left, right):
    width = left.shape[1]
    joined = lax.dot_general(left.reshape(2 * width, -1), right.reshape(2 * width, -1), (((1,), (1,)), ((), ())), precision=lax.Precision.HIGHEST, preferred_element_type=jnp.float32)
    blocks = joined.reshape(2, width, 2, width)
    return jnp.stack([blocks[0, :, 0] + blocks[1, :, 1], blocks[0, :, 1] - blocks[1, :, 0]])


def reference(sources, potential, iter_counts):
    cells = NZ * GX * GX
    complex_src = jnp.stack([sources, jnp.zeros_like(sources)])
    s_total = jnp.zeros((2, MOMENTS * L, cells), jnp.float32)
    h_total = jnp.zeros((2, MOMENTS * L, cells), jnp.float32)
    for point_idx in range(POINTS):
        angle_now = 2.0 * math.pi * (point_idx + 0.5) / POINTS
        shift_re = GAMMA + RADIUS * math.cos(angle_now)
        shift_im = RADIUS * math.sin(angle_now)
        limit = iter_counts[point_idx]
        solution = jnp.zeros_like(complex_src)
        residual = complex_src
        search = complex_src
        norm_now = bilinear(residual, residual)
        for turn_idx in range(ITERS):
            product = shifted(search, potential, shift_re, shift_im)
            step_size = complex_div(norm_now, bilinear(search, product))
            new_solution = solution + scaled(step_size, search)
            new_residual = residual - scaled(step_size, product)
            norm_next = bilinear(new_residual, new_residual)
            new_search = new_residual + scaled(complex_div(norm_next, norm_now), search)
            keep_mask = turn_idx < limit
            solution = jnp.where(keep_mask, new_solution, solution)
            residual = jnp.where(keep_mask, new_residual, residual)
            search = jnp.where(keep_mask, new_search, search)
            norm_now = jnp.where(keep_mask, norm_next, norm_now)
        s_terms, h_terms = moment_terms(solution, residual, complex_src, angle_now, shift_re, shift_im)
        s_total = s_total + s_terms
        h_total = h_total + h_terms
    gram_b = gram_of(s_total, s_total) / cells
    gram_a = gram_of(s_total, h_total) / cells
    return gram_b, gram_a
```

```python
import functools
import math

import jax
import jax.numpy as jnp
import numpy as np
from jax import lax
from jax.experimental import pallas as pl
from jax.experimental.pallas import tpu as pltpu
from jax.sharding import PartitionSpec as P

MOMENTS = 4
ITERS = 6
GX = 32


COEF_NEAR = 4.0 / 3.0
COEF_FAR = -1.0 / 12.0
GAMMA = 2.0
RADIUS = 1.5


def padded_2(block, sides, width):
    for axis, dim in sides:
        count = lax.axis_size(axis)
        forward = [(i, i + 1) for i in range(count - 1)]
        forward.append((count - 1, 0))
        backward = [(target, source) for source, target in forward]
        low = lax.ppermute(
            lax.slice_in_dim(block, block.shape[dim] - width, None, axis=dim), axis, forward
        )
        high = lax.ppermute(lax.slice_in_dim(block, 0, width, axis=dim), axis, backward)
        block = jnp.concatenate([low, block, high], axis=dim)
    return block


def plane_terms(values, side):
    lead = values.shape[:-1]
    planes = values.reshape(lead + (side, side))
    summed = COEF_NEAR * (
        jnp.roll(planes, 1, -2)
        + jnp.roll(planes, -1, -2)
        + jnp.roll(planes, 1, -1)
        + jnp.roll(planes, -1, -1)
    )
    summed = summed + COEF_FAR * (
        jnp.roll(planes, 2, -2)
        + jnp.roll(planes, -2, -2)
        + jnp.roll(planes, 2, -1)
        + jnp.roll(planes, -2, -1)
    )
    return summed.reshape(values.shape)


def complex_mul(first, second):
    return jnp.stack(
        [first[0] * second[0] - first[1] * second[1], first[0] * second[1] + first[1] * second[0]]
    )


def complex_div(first, second):
    denom = second[0] * second[0] + second[1] * second[1]
    return jnp.stack(
        [
            (first[0] * second[0] + first[1] * second[1]) / denom,
            (first[1] * second[0] - first[0] * second[1]) / denom,
        ]
    )


def bilinear(first, second):
    real_part = jnp.sum(first[0] * second[0] - first[1] * second[1], axis=(1, 2))
    imag_part = jnp.sum(first[0] * second[1] + first[1] * second[0], axis=(1, 2))
    return jnp.stack([real_part, imag_part])


def scaled(coeffs, values):
    return complex_mul(coeffs[:, :, None, None], values)


def shifted(values, potential, shift_re, shift_im):
    padded = padded_2(values, (("dom", 2),), 2)
    depth = values.shape[2]
    lap = -7.5 * values + plane_terms(values, GX)
    lap = lap + COEF_NEAR * (padded[:, :, 3 : 3 + depth] + padded[:, :, 1 : 1 + depth])
    lap = lap + COEF_FAR * (padded[:, :, 4 : 4 + depth] + padded[:, :, 0:depth])
    applied = -0.5 * lap + potential * values
    return jnp.stack(
        [
            shift_re * values[0] - shift_im * values[1] - applied[0],
            shift_re * values[1] + shift_im * values[0] - applied[1],
        ]
    )


def residual_sum(values):
    return lax.psum(bilinear(values, values), "dom")


def moment_terms(solution, residual, sources, angle_now, shift_re, shift_im):
    applied = jnp.stack(
        [
            shift_re * solution[0] - shift_im * solution[1] - sources[0] + residual[0],
            shift_re * solution[1] + shift_im * solution[0] - sources[1] + residual[1],
        ]
    )
    angles = (jnp.arange(MOMENTS).astype(jnp.float32) + 1.0) * angle_now
    coeffs = 0.25 * jnp.stack([jnp.cos(angles), jnp.sin(angles)])
    s_terms = complex_mul(coeffs[:, :, None, None, None], solution[:, None])
    h_terms = complex_mul(coeffs[:, :, None, None, None], applied[:, None])
    width = MOMENTS * solution.shape[1]
    return (s_terms.reshape(2, width, -1), h_terms.reshape(2, width, -1))


def gram_of(left, right):
    width = left.shape[1]
    joined = lax.dot_general(
        left.reshape(2 * width, -1),
        right.reshape(2 * width, -1),
        (((1,), (1,)), ((), ())),
        precision=lax.Precision.HIGHEST,
        preferred_element_type=jnp.float32,
    )
    blocks = joined.reshape(2, width, 2, width)
    return jnp.stack([blocks[0, :, 0] + blocks[1, :, 1], blocks[0, :, 1] - blocks[1, :, 0]])


def split_grid(sources, potential, iter_counts):
    complex_src = jnp.stack([sources, jnp.zeros_like(sources)])
    angle_now = (
        2.0 * math.pi * (lax.axis_index("point").astype(jnp.float32) + 0.5) / lax.axis_size("point")
    )
    shift_re = GAMMA + RADIUS * jnp.cos(angle_now)
    shift_im = RADIUS * jnp.sin(angle_now)
    limit = iter_counts[0]
    solution = jnp.zeros_like(complex_src)

    def one_turn(turn_idx, state):
        solution, residual, search, norm_now = state
        product = shifted(search, potential, shift_re, shift_im)
        curve = lax.psum(bilinear(search, product), "dom")
        step_size = complex_div(norm_now, curve)
        new_residual = residual - scaled(step_size, product)
        norm_next = residual_sum(new_residual)
        fresh = (
            solution + scaled(step_size, search),
            new_residual,
            new_residual + scaled(complex_div(norm_next, norm_now), search),
            norm_next,
        )
        keep_mask = turn_idx < limit
        return jax.tree.map(lambda newer, older: jnp.where(keep_mask, newer, older), fresh, state)

    start = (solution, complex_src, complex_src, residual_sum(complex_src))
    solution, residual, search, norm_now = lax.fori_loop(0, ITERS, one_turn, start)
    s_terms, h_terms = moment_terms(solution, residual, complex_src, angle_now, shift_re, shift_im)
    cells = sources.shape[1] * sources.shape[2] * lax.axis_size("dom")
    s_total, h_total = lax.psum((s_terms, h_terms), "point")
    gram_b, gram_a = lax.psum((gram_of(s_total, s_total), gram_of(s_total, h_total)), "dom")
    return (gram_b / cells, gram_a / cells)


Y_IN, X_IN = 2, 4
Y_OUT, X_OUT = GX // Y_IN, GX // X_IN
ROWS = Y_IN * X_IN
LANES = Y_OUT * X_OUT
SUB = 8
BASIS = ITERS + 1


def to_blocked(values):
    split = values.reshape(values.shape[:-1] + (Y_OUT, Y_IN, X_OUT, X_IN))
    lead = values.ndim - 1
    order = tuple(range(lead)) + (lead + 1, lead + 3, lead, lead + 2)
    return split.transpose(order).reshape(values.shape[:-1] + (ROWS, LANES))


def packed_block(sources, potential):
    count = sources.shape[0]
    rows = to_blocked(sources).transpose(1, 2, 0, 3).reshape(-1, LANES)
    levels = to_blocked(potential).reshape(-1, LANES)
    return jnp.concatenate([rows, levels], axis=0)


def lane_sum(values):
    return jnp.broadcast_to(jnp.sum(values, axis=1, keepdims=True), values.shape)


def ratio(top, bottom):
    return jnp.where(bottom > 0.0, top / jnp.where(bottom > 0.0, bottom, 1.0), 0.0)


def x_next(values, wrap_mask):
    return jnp.where(wrap_mask, pltpu.roll(values, X_OUT - 1, 1), pltpu.roll(values, LANES - 1, 1))


def x_prev(values, wrap_mask):
    return jnp.where(wrap_mask, pltpu.roll(values, LANES - X_OUT + 1, 1), pltpu.roll(values, 1, 1))


def plane_of(basis, plane, row):
    return [basis[plane, pl.ds(row, SUB), pl.ds(m * LANES, LANES)] for m in range(ROWS)]


def apply_plane(basis, diagonal, plane, planes, row, last_x, first_x):
    here = plane_of(basis, plane, row)
    above = plane_of(basis, lax.rem(plane + 1, planes), row)
    below = plane_of(basis, lax.rem(plane + planes - 1, planes), row)
    above_2 = plane_of(basis, lax.rem(plane + 2, planes), row)
    below_2 = plane_of(basis, lax.rem(plane + planes - 2, planes), row)
    y_up = [pltpu.roll(value, LANES - X_OUT, 1) for value in here]
    y_down = [pltpu.roll(value, X_OUT, 1) for value in here]
    out = []
    for yi in range(Y_IN):
        line = here[yi * X_IN : (yi + 1) * X_IN]
        before = [x_prev(line[X_IN - 2], first_x), x_prev(line[X_IN - 1], first_x)]
        after = [x_next(line[0], last_x), x_next(line[1], last_x)]
        wide = before + line + after
        for xi in range(X_IN):
            m = yi * X_IN + xi
            other = (1 - yi) * X_IN + xi
            y_next = here[other] if yi == 0 else y_up[other]
            y_prev = here[other] if yi == 1 else y_down[other]
            near = (wide[xi + 1] + wide[xi + 3]) + (y_next + y_prev) + (above[m] + below[m])
            far = (wide[xi] + wide[xi + 4]) + (y_up[m] + y_down[m]) + (above_2[m] + below_2[m])
            level = diagonal[plane, pl.ds(m, 1), :]
            out.append(level * here[m] - (0.5 * COEF_NEAR) * near - (0.5 * COEF_FAR) * far)
    return here, out


def cmul(first, second):
    return (
        first[0] * second[0] - first[1] * second[1],
        first[0] * second[1] + first[1] * second[0],
    )


def weights_of(alphas, norms, limits, coeffs, shape):
    points = len(limits)
    count = shape[0]
    half = MOMENTS * count
    lane = lax.broadcasted_iota(jnp.int32, shape, 1)
    source = lax.broadcasted_iota(jnp.int32, shape, 0)
    own = lax.rem(lane, count) == source
    left_half = lane < half
    betas = [ratio(norms[i + 1], norms[i]) for i in range(ITERS - 1)]
    sums = [[jnp.zeros(shape, jnp.float32)] * 2 for _ in range(BASIS)]
    zero = jnp.zeros(shape, jnp.float32)
    one = jnp.ones(shape, jnp.float32)
    for point in range(points):
        angle = 2.0 * math.pi * (point + 0.5) / points
        shift = (GAMMA + RADIUS * math.cos(angle), RADIUS * math.sin(angle))
        limit = limits[point]
        product = (one, zero)
        products = [product]
        links = []
        pivot = (shift[0] - alphas[0], zero + shift[1])
        for i in range(ITERS):
            size = pivot[0] * pivot[0] + pivot[1] * pivot[1]
            inverse = (pivot[0] / size, -pivot[1] / size)
            product = cmul(product, inverse)
            products.append(product)
            if i < ITERS - 1:
                link = (betas[i] * inverse[0], betas[i] * inverse[1])
                links.append(link)
                pivot = (shift[0] - alphas[i + 1] - link[0], shift[1] - link[1])
        solved = [None] * ITERS
        for i in reversed(range(ITERS)):
            value = products[i + 1]
            if i < ITERS - 1:
                step = cmul(links[i], solved[i + 1])
                value = (value[0] + step[0], value[1] + step[1])
            used = i < limit
            solved[i] = (jnp.where(used, value[0], 0.0), jnp.where(used, value[1], 0.0))
        applied = []
        for i in range(BASIS):
            left = limit == i
            rest = (
                jnp.where(left, products[i][0], 0.0),
                jnp.where(left, products[i][1], 0.0),
            )
            if i < ITERS:
                turned = (
                    shift[0] * solved[i][0] - shift[1] * solved[i][1],
                    shift[0] * solved[i][1] + shift[1] * solved[i][0],
                )
                rest = (rest[0] + turned[0], rest[1] + turned[1])
            if i == 0:
                rest = (rest[0] - 1.0, rest[1])
            applied.append(rest)
        tail = applied[ITERS]
        for back, factor in ((1, alphas[ITERS - 1]), (2, betas[ITERS - 2])):
            part = applied[ITERS - back]
            applied[ITERS - back] = (part[0] - factor * tail[0], part[1] - factor * tail[1])
        moment = (coeffs[2 * point : 2 * point + 1, :], coeffs[2 * point + 1 : 2 * point + 2, :])
        for i in range(BASIS):
            left = solved[i] if i < ITERS else (zero, zero)
            both = (
                jnp.where(left_half, left[0], applied[i][0]),
                jnp.where(left_half, left[1], applied[i][1]),
            )
            term = cmul(moment, both)
            sums[i] = [sums[i][0] + term[0], sums[i][1] + term[1]]
    return [[jnp.where(own, part, 0.0) for part in pair] for pair in sums]


def exact_dot(first, second, dims):
    return lax.dot_general(
        first,
        second,
        (dims, ((), ())),
        precision=lax.Precision.HIGHEST,
        preferred_element_type=jnp.float32,
    )


def solve_kernel(parts, count, planes, points, meta, coeffs, *refs):
    blocks = refs[:parts]
    out_b, out_a, basis, diagonal, gram = refs[parts:]
    depth = planes // parts
    groups = count // SUB
    lane = lax.broadcasted_iota(jnp.int32, (SUB, LANES), 1)
    last_x = lax.rem(lane, X_OUT) == X_OUT - 1
    first_x = lax.rem(lane, X_OUT) == 0

    for turn in range(parts):
        slab = jnp.bitwise_xor(meta[0], turn) * depth
        for deep in range(depth):
            for m in range(ROWS):
                start = (deep * ROWS + m) * count
                basis[slab + deep, 0:count, m * LANES : (m + 1) * LANES] = blocks[turn][
                    start : start + count, :
                ]
            start = depth * ROWS * count + deep * ROWS
            diagonal[slab + deep] = blocks[turn][start : start + ROWS, :] + 3.75

    blank = jnp.zeros((SUB, LANES), jnp.float32)
    alphas, norms = [], []
    for i in range(ITERS):

        def apply_turn(plane, sums, i=i):
            new_sums = []
            for group in range(groups):
                row = i * count + group * SUB
                here, out = apply_plane(basis, diagonal, plane, planes, row, last_x, first_x)
                curve, norm = sums[group]
                for m in range(ROWS):
                    basis[plane, pl.ds(row + count, SUB), pl.ds(m * LANES, LANES)] = out[m]
                    curve = curve + here[m] * out[m]
                    if i == 0:
                        norm = norm + here[m] * here[m]
                new_sums.append((curve, norm))
            return tuple(new_sums)

        sums = lax.fori_loop(0, planes, apply_turn, ((blank, blank),) * groups)
        if i == 0:
            norms.append([lane_sum(norm) for _, norm in sums])
        alphas.append([ratio(lane_sum(sums[g][0]), norms[i][g]) for g in range(groups)])
        if i == ITERS - 1:
            break
        betas = [ratio(norms[i][g], norms[i - 1][g]) for g in range(groups)] if i else None

        def step_turn(plane, sums, i=i, betas=betas):
            new_sums = []
            for group in range(groups):
                row = i * count + group * SUB
                norm = sums[group]
                for m in range(ROWS):
                    lanes = pl.ds(m * LANES, LANES)
                    value = basis[plane, pl.ds(row + count, SUB), lanes]
                    value = value - alphas[i][group] * basis[plane, pl.ds(row, SUB), lanes]
                    if i:
                        value = value - betas[group] * basis[plane, pl.ds(row - count, SUB), lanes]
                    basis[plane, pl.ds(row + count, SUB), lanes] = value
                    norm = norm + value * value
                new_sums.append(norm)
            return tuple(new_sums)

        sums = lax.fori_loop(0, planes, step_turn, (blank,) * groups)
        norms.append([lane_sum(norm) for norm in sums])

    size = BASIS * count
    gram[...] = jnp.zeros_like(gram)

    def gram_turn(plane, carry):
        values = basis[plane]
        high = values.astype(jnp.bfloat16)
        low = (values - high.astype(jnp.float32)).astype(jnp.bfloat16)
        gram[...] += lax.dot_general(
            high,
            jnp.concatenate([high, low], axis=0),
            (((1,), (1,)), ((), ())),
            preferred_element_type=jnp.float32,
        )
        return carry

    lax.fori_loop(0, planes, gram_turn, 0)
    cross = gram[:, size:]
    pairs = gram[:, :size] + cross + cross.T

    shape = (count, LANES)
    limits = [meta[2 + jnp.bitwise_xor(meta[1], point)] for point in range(points)]
    alphas = [jnp.concatenate(value, axis=0) for value in alphas]
    norms = [jnp.concatenate(value, axis=0) for value in norms]
    weights = weights_of(alphas, norms, limits, coeffs, shape)
    real = jnp.concatenate([pair[0] for pair in weights], axis=0)
    imag = jnp.concatenate([pair[1] for pair in weights], axis=0)
    right = exact_dot(pairs, jnp.concatenate([real, imag], axis=1), ((1,), (0,)))
    half = MOMENTS * count
    left = jnp.concatenate([real[:, :half], imag[:, :half]], axis=1)
    joined = exact_dot(left.T, right, ((1,), (0,)))
    scale = 1.0 / (planes * ROWS * LANES)
    width = 2 * half
    real = (joined[:half, :width] + joined[half:, width:]) * scale
    imag = (joined[:half, width:] - joined[half:, :width]) * scale
    out_b[0] = real[:, :half]
    out_b[1] = imag[:, :half]
    out_a[0] = real[:, half:]
    out_a[1] = imag[:, half:]


def swapped(values, axis, size, mask):
    return lax.ppermute(values, axis, [(i ^ mask, i) for i in range(size)])


def whole_grid(sources, potential, iter_counts, *, parts, points):
    count, depth, _ = sources.shape
    planes = parts * depth
    block = packed_block(sources, potential)
    even = [block] + [swapped(block, "dom", parts, mask) for mask in range(2, parts, 2)]
    odd = [swapped(value, "dom", parts, 1) for value in even]
    blocks = [value for pair in zip(even, odd) for value in pair]
    limits = [iter_counts] + [
        swapped(iter_counts, "point", points, mask) for mask in range(1, points)
    ]
    place = jnp.stack([lax.axis_index("dom"), lax.axis_index("point")]).astype(jnp.int32)
    meta = jnp.concatenate([place] + limits)
    angles = 2.0 * math.pi * (np.arange(points)[:, None] + 0.5) / points
    turns = np.tile(np.repeat(np.arange(MOMENTS) + 1.0, count), 2)[None, :] * angles
    coeffs = 0.25 * np.stack([np.cos(turns), np.sin(turns)], axis=1).reshape(2 * points, -1)
    vmem = pl.BlockSpec(memory_space=pltpu.VMEM)
    smem = pl.BlockSpec(memory_space=pltpu.SMEM)
    size = BASIS * count
    width = MOMENTS * count
    out = jax.ShapeDtypeStruct((2, width, width), jnp.float32)
    return pl.pallas_call(
        functools.partial(solve_kernel, parts, count, planes, points),
        out_shape=(out, out),
        in_specs=[smem, vmem] + [vmem] * parts,
        out_specs=(vmem, vmem),
        scratch_shapes=[
            pltpu.VMEM((planes, size, ROWS * LANES), jnp.float32),
            pltpu.VMEM((planes, ROWS, LANES), jnp.float32),
            pltpu.VMEM((size, 2 * size), jnp.float32),
        ],
        compiler_params=pltpu.CompilerParams(vmem_limit_bytes=40 * 2**20),
    )(meta, jnp.asarray(coeffs, jnp.float32), *blocks)


def power_of_two(value):
    return value > 0 and value & (value - 1) == 0


def on_device(sources, potential, iter_counts):
    parts, points = lax.axis_size("dom"), lax.axis_size("point")
    count, depth, cells = sources.shape
    held = BASIS * count * parts * depth * cells * 4
    fits = (
        held <= 16 * 2**20
        and power_of_two(parts)
        and power_of_two(points)
        and 2 * MOMENTS * count == LANES
        and cells == GX * GX == ROWS * LANES
    )
    if not fits:
        return split_grid(sources, potential, iter_counts)
    return whole_grid(sources, potential, iter_counts, parts=parts, points=points)


def solution(mesh):
    placed = (P(None, "dom", None), P("dom", None), P("point"))
    return jax.shard_map(
        on_device, mesh=mesh, in_specs=placed, out_specs=(P(), P()), check_vma=False
    )
```

```python
import functools
import math

import jax
import jax.numpy as jnp
import numpy as np
from jax import lax
from jax.experimental import pallas as pl
from jax.experimental.pallas import tpu as pltpu
from jax.sharding import PartitionSpec as P

MOMENTS = 4
ITERS = 6
GX = 32


COEF_NEAR = 4.0 / 3.0
COEF_FAR = -1.0 / 12.0
GAMMA = 2.0
RADIUS = 1.5


def padded_2(block, sides, width):
    for axis, dim in sides:
        count = lax.axis_size(axis)
        forward = [(i, i + 1) for i in range(count - 1)]
        forward.append((count - 1, 0))
        backward = [(target, source) for source, target in forward]
        low = lax.ppermute(
            lax.slice_in_dim(block, block.shape[dim] - width, None, axis=dim), axis, forward
        )
        high = lax.ppermute(lax.slice_in_dim(block, 0, width, axis=dim), axis, backward)
        block = jnp.concatenate([low, block, high], axis=dim)
    return block


def plane_terms(values, side):
    lead = values.shape[:-1]
    planes = values.reshape(lead + (side, side))
    summed = COEF_NEAR * (
        jnp.roll(planes, 1, -2)
        + jnp.roll(planes, -1, -2)
        + jnp.roll(planes, 1, -1)
        + jnp.roll(planes, -1, -1)
    )
    summed = summed + COEF_FAR * (
        jnp.roll(planes, 2, -2)
        + jnp.roll(planes, -2, -2)
        + jnp.roll(planes, 2, -1)
        + jnp.roll(planes, -2, -1)
    )
    return summed.reshape(values.shape)


def complex_mul(first, second):
    return jnp.stack(
        [first[0] * second[0] - first[1] * second[1], first[0] * second[1] + first[1] * second[0]]
    )


def complex_div(first, second):
    denom = second[0] * second[0] + second[1] * second[1]
    return jnp.stack(
        [
            (first[0] * second[0] + first[1] * second[1]) / denom,
            (first[1] * second[0] - first[0] * second[1]) / denom,
        ]
    )


def bilinear(first, second):
    real_part = jnp.sum(first[0] * second[0] - first[1] * second[1], axis=(1, 2))
    imag_part = jnp.sum(first[0] * second[1] + first[1] * second[0], axis=(1, 2))
    return jnp.stack([real_part, imag_part])


def scaled(coeffs, values):
    return complex_mul(coeffs[:, :, None, None], values)


def shifted(values, potential, shift_re, shift_im):
    padded = padded_2(values, (("dom", 2),), 2)
    depth = values.shape[2]
    lap = -7.5 * values + plane_terms(values, GX)
    lap = lap + COEF_NEAR * (padded[:, :, 3 : 3 + depth] + padded[:, :, 1 : 1 + depth])
    lap = lap + COEF_FAR * (padded[:, :, 4 : 4 + depth] + padded[:, :, 0:depth])
    applied = -0.5 * lap + potential * values
    return jnp.stack(
        [
            shift_re * values[0] - shift_im * values[1] - applied[0],
            shift_re * values[1] + shift_im * values[0] - applied[1],
        ]
    )


def residual_sum(values):
    return lax.psum(bilinear(values, values), "dom")


def moment_terms(solution, residual, sources, angle_now, shift_re, shift_im):
    applied = jnp.stack(
        [
            shift_re * solution[0] - shift_im * solution[1] - sources[0] + residual[0],
            shift_re * solution[1] + shift_im * solution[0] - sources[1] + residual[1],
        ]
    )
    angles = (jnp.arange(MOMENTS).astype(jnp.float32) + 1.0) * angle_now
    coeffs = 0.25 * jnp.stack([jnp.cos(angles), jnp.sin(angles)])
    s_terms = complex_mul(coeffs[:, :, None, None, None], solution[:, None])
    h_terms = complex_mul(coeffs[:, :, None, None, None], applied[:, None])
    width = MOMENTS * solution.shape[1]
    return (s_terms.reshape(2, width, -1), h_terms.reshape(2, width, -1))


def gram_of(left, right):
    width = left.shape[1]
    joined = lax.dot_general(
        left.reshape(2 * width, -1),
        right.reshape(2 * width, -1),
        (((1,), (1,)), ((), ())),
        precision=lax.Precision.HIGHEST,
        preferred_element_type=jnp.float32,
    )
    blocks = joined.reshape(2, width, 2, width)
    return jnp.stack([blocks[0, :, 0] + blocks[1, :, 1], blocks[0, :, 1] - blocks[1, :, 0]])


def split_grid(sources, potential, iter_counts):
    complex_src = jnp.stack([sources, jnp.zeros_like(sources)])
    angle_now = (
        2.0 * math.pi * (lax.axis_index("point").astype(jnp.float32) + 0.5) / lax.axis_size("point")
    )
    shift_re = GAMMA + RADIUS * jnp.cos(angle_now)
    shift_im = RADIUS * jnp.sin(angle_now)
    limit = iter_counts[0]
    solution = jnp.zeros_like(complex_src)

    def one_turn(turn_idx, state):
        solution, residual, search, norm_now = state
        product = shifted(search, potential, shift_re, shift_im)
        curve = lax.psum(bilinear(search, product), "dom")
        step_size = complex_div(norm_now, curve)
        new_residual = residual - scaled(step_size, product)
        norm_next = residual_sum(new_residual)
        fresh = (
            solution + scaled(step_size, search),
            new_residual,
            new_residual + scaled(complex_div(norm_next, norm_now), search),
            norm_next,
        )
        keep_mask = turn_idx < limit
        return jax.tree.map(lambda newer, older: jnp.where(keep_mask, newer, older), fresh, state)

    start = (solution, complex_src, complex_src, residual_sum(complex_src))
    solution, residual, search, norm_now = lax.fori_loop(0, ITERS, one_turn, start)
    s_terms, h_terms = moment_terms(solution, residual, complex_src, angle_now, shift_re, shift_im)
    cells = sources.shape[1] * sources.shape[2] * lax.axis_size("dom")
    s_total, h_total = lax.psum((s_terms, h_terms), "point")
    gram_b, gram_a = lax.psum((gram_of(s_total, s_total), gram_of(s_total, h_total)), "dom")
    return (gram_b / cells, gram_a / cells)


Y_IN, X_IN = 2, 4
Y_OUT, X_OUT = GX // Y_IN, GX // X_IN
ROWS = Y_IN * X_IN
LANES = Y_OUT * X_OUT
SUB = 8
BASIS = ITERS + 1


def pack_kernel(depth, groups, counts, rows, levels, *refs):
    outs = refs
    columns = rows.shape[0] // (SUB * groups * depth)
    source = lax.broadcasted_iota(jnp.int32, (LANES, LANES), 0)
    target = lax.broadcasted_iota(jnp.int32, (LANES, LANES), 1)
    inner = target // (LANES // ROWS)
    outer = target % (LANES // ROWS)
    cell = (outer // X_OUT * Y_IN + inner // X_IN) * GX + outer % X_OUT * X_IN + inner % X_IN
    swap = jnp.where(source == cell, 1.0, 0.0).astype(jnp.float32)
    parts = []
    for deep in range(depth):
        for group in range(groups):
            for column in range(columns):
                start = (group * SUB * columns + column) * depth + deep
                parts.append(rows[pl.ds(start, SUB, stride=columns * depth), :])
        parts.append(levels[pl.ds(deep, columns, stride=depth), :])
    mixed = exact_dot(jnp.concatenate(parts, axis=0), swap, ((1,), (0,)))
    block = LANES // ROWS
    lane_block = lax.broadcasted_iota(jnp.int32, (SUB, LANES), 1) // block
    row = lax.broadcasted_iota(jnp.int32, (SUB, LANES), 0)
    for deep in range(depth):
        base = deep * (groups + 1) * columns * SUB - deep * (columns - 1) * SUB
        for group in range(groups):
            pieces = [
                mixed[base + (group * columns + column) * SUB :][:SUB] for column in range(columns)
            ]
            for m in range(ROWS):
                value = pieces[m]
                for column in range(columns):
                    if column != m:
                        moved = pltpu.roll(pieces[column], (column - m) * block % LANES, 1)
                        value = jnp.where(lane_block == column, moved, value)
                start = (deep * ROWS + m) * SUB
                outs[group][start : start + SUB, :] = value
        piece = mixed[base + groups * columns * SUB :][:SUB]
        value = piece
        for far in range(1, columns):
            moved = pltpu.roll(pltpu.roll(piece, far * block, 1), columns - far, 0)
            value = jnp.where(lane_block == (row + far) % columns, moved, value)
        start = depth * ROWS * SUB + deep * ROWS
        outs[0][start : start + ROWS, :] = value
    count = jnp.full((SUB, LANES), counts[0].astype(jnp.float32))
    for out in outs:
        out[out.shape[0] - SUB :, :] = count


def packed_blocks(sources, potential, iter_counts):
    count, depth, cells = sources.shape
    columns = cells // LANES
    rows = sources.reshape(count, depth, columns, LANES).transpose(0, 2, 1, 3)
    levels = potential.reshape(depth, columns, LANES).transpose(1, 0, 2)
    vmem = pl.BlockSpec(memory_space=pltpu.VMEM)
    smem = pl.BlockSpec(memory_space=pltpu.SMEM)
    groups = count // SUB
    size = depth * ROWS * SUB + SUB
    sizes = [size + depth * ROWS] + [size] * (groups - 1)
    return pl.pallas_call(
        functools.partial(pack_kernel, depth, groups),
        out_shape=[jax.ShapeDtypeStruct((rows_out, LANES), jnp.float32) for rows_out in sizes],
        in_specs=[smem, vmem, vmem],
        out_specs=[vmem] * groups,
        name="pack",
    )(iter_counts, rows.reshape(-1, LANES), levels.reshape(-1, LANES))


def lane_sum(values):
    return jnp.broadcast_to(jnp.sum(values, axis=1, keepdims=True), values.shape)


def ratio(top, bottom):
    return jnp.where(bottom > 0.0, top / jnp.where(bottom > 0.0, bottom, 1.0), 0.0)


def x_next(values, wrap_mask):
    return jnp.where(wrap_mask, pltpu.roll(values, X_OUT - 1, 1), pltpu.roll(values, LANES - 1, 1))


def x_prev(values, wrap_mask):
    return jnp.where(wrap_mask, pltpu.roll(values, LANES - X_OUT + 1, 1), pltpu.roll(values, 1, 1))


def plane_of(basis, plane, row):
    return [basis[plane, pl.ds(row, SUB), pl.ds(m * LANES, LANES)] for m in range(ROWS)]


def apply_plane(basis, diagonal, plane, planes, row, last_x, first_x):
    here = plane_of(basis, plane, row)
    above = plane_of(basis, lax.rem(plane + 1, planes), row)
    below = plane_of(basis, lax.rem(plane + planes - 1, planes), row)
    above_2 = plane_of(basis, lax.rem(plane + 2, planes), row)
    below_2 = plane_of(basis, lax.rem(plane + planes - 2, planes), row)
    y_up = [pltpu.roll(value, LANES - X_OUT, 1) for value in here]
    y_down = [pltpu.roll(value, X_OUT, 1) for value in here]
    out = []
    for yi in range(Y_IN):
        line = here[yi * X_IN : (yi + 1) * X_IN]
        before = [x_prev(line[X_IN - 2], first_x), x_prev(line[X_IN - 1], first_x)]
        after = [x_next(line[0], last_x), x_next(line[1], last_x)]
        wide = before + line + after
        for xi in range(X_IN):
            m = yi * X_IN + xi
            other = (1 - yi) * X_IN + xi
            y_next = here[other] if yi == 0 else y_up[other]
            y_prev = here[other] if yi == 1 else y_down[other]
            near = (wide[xi + 1] + wide[xi + 3]) + (y_next + y_prev) + (above[m] + below[m])
            far = (wide[xi] + wide[xi + 4]) + (y_up[m] + y_down[m]) + (above_2[m] + below_2[m])
            level = diagonal[plane, pl.ds(m, 1), :]
            out.append(level * here[m] - (0.5 * COEF_NEAR) * near - (0.5 * COEF_FAR) * far)
    return here, out


def cmul(first, second):
    return (
        first[0] * second[0] - first[1] * second[1],
        first[0] * second[1] + first[1] * second[0],
    )


def weights_of(alphas, norms, limits, coeffs, group, groups):
    points = len(limits)
    shape = (SUB, LANES)
    count = groups * SUB
    half = MOMENTS * count
    lane = lax.broadcasted_iota(jnp.int32, shape, 1)
    source = lax.broadcasted_iota(jnp.int32, shape, 0)
    own = lax.rem(lane, count) == source + group * SUB
    left_half = lane < half
    betas = [ratio(norms[i + 1], norms[i]) for i in range(ITERS - 1)]
    sums = [[jnp.zeros(shape, jnp.float32)] * 2 for _ in range(BASIS)]
    zero = jnp.zeros(shape, jnp.float32)
    one = jnp.ones(shape, jnp.float32)
    for point in range(points):
        angle = 2.0 * math.pi * (point + 0.5) / points
        shift = (GAMMA + RADIUS * math.cos(angle), RADIUS * math.sin(angle))
        limit = limits[point]
        product = (one, zero)
        products = [product]
        links = []
        pivot = (shift[0] - alphas[0], zero + shift[1])
        for i in range(ITERS):
            size = pivot[0] * pivot[0] + pivot[1] * pivot[1]
            inverse = (pivot[0] / size, -pivot[1] / size)
            product = cmul(product, inverse)
            products.append(product)
            if i < ITERS - 1:
                link = (betas[i] * inverse[0], betas[i] * inverse[1])
                links.append(link)
                pivot = (shift[0] - alphas[i + 1] - link[0], shift[1] - link[1])
        solved = [None] * ITERS
        for i in reversed(range(ITERS)):
            value = products[i + 1]
            if i < ITERS - 1:
                step = cmul(links[i], solved[i + 1])
                value = (value[0] + step[0], value[1] + step[1])
            used = limit > i
            solved[i] = (jnp.where(used, value[0], 0.0), jnp.where(used, value[1], 0.0))
        applied = []
        for i in range(BASIS):
            left = limit == i
            rest = (
                jnp.where(left, products[i][0], 0.0),
                jnp.where(left, products[i][1], 0.0),
            )
            if i < ITERS:
                turned = (
                    shift[0] * solved[i][0] - shift[1] * solved[i][1],
                    shift[0] * solved[i][1] + shift[1] * solved[i][0],
                )
                rest = (rest[0] + turned[0], rest[1] + turned[1])
            if i == 0:
                rest = (rest[0] - 1.0, rest[1])
            applied.append(rest)
        tail = applied[ITERS]
        for back, factor in ((1, alphas[ITERS - 1]), (2, betas[ITERS - 2])):
            part = applied[ITERS - back]
            applied[ITERS - back] = (part[0] - factor * tail[0], part[1] - factor * tail[1])
        moment = (coeffs[2 * point : 2 * point + 1, :], coeffs[2 * point + 1 : 2 * point + 2, :])
        for i in range(BASIS):
            left = solved[i] if i < ITERS else (zero, zero)
            both = (
                jnp.where(left_half, left[0], applied[i][0]),
                jnp.where(left_half, left[1], applied[i][1]),
            )
            term = cmul(moment, both)
            sums[i] = [sums[i][0] + term[0], sums[i][1] + term[1]]
    return [[jnp.where(own, part, 0.0) for part in pair] for pair in sums]


def exact_dot(first, second, dims):
    return lax.dot_general(
        first,
        second,
        (dims, ((), ())),
        precision=lax.Precision.HIGHEST,
        preferred_element_type=jnp.float32,
    )


def krylov(blocks, basis, diagonal, fill_diagonal):
    parts, planes = len(blocks), basis.shape[0]
    depth = planes // parts
    lane = lax.broadcasted_iota(jnp.int32, (SUB, LANES), 1)
    last_x = lax.rem(lane, X_OUT) == X_OUT - 1
    first_x = lax.rem(lane, X_OUT) == 0
    here = lax.axis_index("dom")
    for turn in range(parts):
        slab = jnp.bitwise_xor(here, turn) * depth
        for deep in range(depth):
            for m in range(ROWS):
                start = (deep * ROWS + m) * SUB
                basis[slab + deep, 0:SUB, m * LANES : (m + 1) * LANES] = blocks[turn][
                    start : start + SUB, :
                ]
            if fill_diagonal:
                start = depth * ROWS * SUB + deep * ROWS
                diagonal[slab + deep] = blocks[turn][start : start + ROWS, :] + 3.75

    blank = jnp.zeros((SUB, LANES), jnp.float32)
    alphas, norms = [], []
    for i in range(ITERS):
        row = i * SUB

        def apply_turn(plane, sums, i=i, row=row):
            curve, norm = sums
            here, out = apply_plane(basis, diagonal, plane, planes, row, last_x, first_x)
            for m in range(ROWS):
                basis[plane, pl.ds(row + SUB, SUB), pl.ds(m * LANES, LANES)] = out[m]
                curve = curve + here[m] * out[m]
                if i == 0:
                    norm = norm + here[m] * here[m]
            return curve, norm

        curve, norm = lax.fori_loop(0, planes, apply_turn, (blank, blank), unroll=2)
        if i == 0:
            norms.append(lane_sum(norm))
        alphas.append(ratio(lane_sum(curve), norms[i]))
        if i == ITERS - 1:
            break
        beta = ratio(norms[i], norms[i - 1]) if i else None

        def step_turn(plane, norm, i=i, row=row, alpha=alphas[i], beta=beta):
            for m in range(ROWS):
                lanes = pl.ds(m * LANES, LANES)
                value = basis[plane, pl.ds(row + SUB, SUB), lanes]
                value = value - alpha * basis[plane, pl.ds(row, SUB), lanes]
                if i:
                    value = value - beta * basis[plane, pl.ds(row - SUB, SUB), lanes]
                basis[plane, pl.ds(row + SUB, SUB), lanes] = value
                norm = norm + value * value
            return norm

        norms.append(lane_sum(lax.fori_loop(0, planes, step_turn, blank, unroll=4)))
    return alphas, norms


def first_kernel(*refs):
    blocks, (basis, diagonal, scalars) = refs[:-3], refs[-3:]
    alphas, norms = krylov(blocks, basis, diagonal, True)
    for i, value in enumerate(alphas + norms):
        scalars[i] = value


def second_kernel(groups, points, masks, counts, coeffs, *refs):
    first = refs[: 3 * (groups - 1)]
    out_b, out_a, basis, gram, limits = refs[-5:]
    tails, blocks = refs[len(first) : len(first) + points - 1], refs[len(first) + points - 1 : -5]
    planes = basis.shape[0]
    alphas, norms = krylov(blocks, basis, first[1], False)
    bases = [first[3 * g] for g in range(groups - 1)] + [basis]
    size = BASIS * SUB * groups
    gram[...] = jnp.zeros_like(gram)

    def gram_turn(plane, carry):
        values = jnp.concatenate([part[plane] for part in bases], axis=0)
        high = values.astype(jnp.bfloat16)
        low = (values - high.astype(jnp.float32)).astype(jnp.bfloat16)
        gram[...] += lax.dot_general(
            high,
            jnp.concatenate([high, low], axis=0),
            (((1,), (1,)), ((), ())),
            preferred_element_type=jnp.float32,
        )
        return carry

    lax.fori_loop(0, planes, gram_turn, 0)
    cross = gram[:, size:]
    pairs = gram[:, :size] + cross + cross.T

    here = lax.axis_index("point")
    limits[here] = jnp.full((SUB, LANES), counts[0].astype(jnp.float32))
    for mask, tail in zip(masks, tails):
        limits[jnp.bitwise_xor(here, mask)] = tail[tail.shape[0] - SUB :, :]
    reals, imags = [], []
    for group in range(groups):
        if group < groups - 1:
            scalars = first[3 * group + 2]
            alpha = [scalars[i] for i in range(ITERS)]
            norm = [scalars[ITERS + i] for i in range(ITERS)]
        else:
            alpha, norm = alphas, norms
        weights = weights_of(alpha, norm, [limits[j] for j in range(points)], coeffs, group, groups)
        reals += [pair[0] for pair in weights]
        imags += [pair[1] for pair in weights]
    real, imag = jnp.concatenate(reals, axis=0), jnp.concatenate(imags, axis=0)
    right = exact_dot(pairs, jnp.concatenate([real, imag], axis=1), ((1,), (0,)))
    half = MOMENTS * SUB * groups
    left = jnp.concatenate([real[:, :half], imag[:, :half]], axis=1)
    joined = exact_dot(left.T, right, ((1,), (0,)))
    scale = 1.0 / (planes * ROWS * LANES)
    width = 2 * half
    real = (joined[:half, :width] + joined[half:, width:]) * scale
    imag = (joined[:half, width:] - joined[half:, :width]) * scale
    out_b[0] = real[:, :half]
    out_b[1] = imag[:, :half]
    out_a[0] = real[:, half:]
    out_a[1] = imag[:, half:]


def exchanged(values, mask, other, parts, points):
    pairs = [
        ((point ^ other) * parts + (part ^ mask), point * parts + part)
        for point in range(points)
        for part in range(parts)
    ]
    return lax.ppermute(values, ("point", "dom"), pairs)


def whole_grid(sources, potential, iter_counts, *, parts, points):
    count, depth, _ = sources.shape
    planes = parts * depth
    groups = count // SUB
    packed = packed_blocks(sources, potential, iter_counts)
    crossing = {(0, 2): 1, (0, 4): 2, (1, 6): 3}
    masks, tails, arrived = [], [], []
    for group in range(groups):
        even = [packed[group]]
        for mask in range(2, parts, 2):
            other = crossing.get((group, mask), 0)
            even.append(exchanged(packed[group], mask, other, parts, points))
            if other:
                masks.append(other)
                tails.append(even[-1])
        odd = [exchanged(value, 1, 0, parts, points) for value in even]
        arrived.append([value for pair in zip(even, odd) for value in pair])
    angles = 2.0 * math.pi * (np.arange(points)[:, None] + 0.5) / points
    turns = np.tile(np.repeat(np.arange(MOMENTS) + 1.0, count), 2)[None, :] * angles
    coeffs = 0.25 * np.stack([np.cos(turns), np.sin(turns)], axis=1).reshape(2 * points, -1)
    vmem = pl.BlockSpec(memory_space=pltpu.VMEM)
    smem = pl.BlockSpec(memory_space=pltpu.SMEM)
    cells = planes * ROWS * LANES
    cost = pl.CostEstimate(
        flops=ITERS * SUB * cells * 30, bytes_accessed=16 * 2**20, transcendentals=0
    )
    basis_shape = (planes, BASIS * SUB, ROWS * LANES)
    first = pl.pallas_call(
        first_kernel,
        out_shape=(
            jax.ShapeDtypeStruct(basis_shape, jnp.float32),
            jax.ShapeDtypeStruct((planes, ROWS, LANES), jnp.float32),
            jax.ShapeDtypeStruct((2 * ITERS, SUB, LANES), jnp.float32),
        ),
        in_specs=[vmem] * parts,
        out_specs=(vmem,) * 3,
        compiler_params=pltpu.CompilerParams(vmem_limit_bytes=16 * 2**20),
        cost_estimate=cost,
        name="first_group",
    )(*arrived[0])
    size = BASIS * count
    width = MOMENTS * count
    out = jax.ShapeDtypeStruct((2, width, width), jnp.float32)
    return pl.pallas_call(
        functools.partial(second_kernel, groups, points, masks),
        out_shape=(out, out),
        in_specs=[smem, vmem] + [vmem] * (3 + len(tails) + parts),
        out_specs=(vmem, vmem),
        scratch_shapes=[
            pltpu.VMEM(basis_shape, jnp.float32),
            pltpu.VMEM((size, 2 * size), jnp.float32),
            pltpu.VMEM((points, SUB, LANES), jnp.float32),
        ],
        compiler_params=pltpu.CompilerParams(vmem_limit_bytes=24 * 2**20),
        cost_estimate=cost,
        name="second_group",
    )(iter_counts, jnp.asarray(coeffs, jnp.float32), *first, *tails, *arrived[1])


def on_device(sources, potential, iter_counts):
    parts, points = lax.axis_size("dom"), lax.axis_size("point")
    count, depth, cells = sources.shape
    held = BASIS * count * parts * depth * cells * 4
    fits = (
        held <= 16 * 2**20
        and parts == 8
        and points == 4
        and count == 2 * SUB
        and 2 * MOMENTS * count == LANES
        and cells == GX * GX == ROWS * LANES
    )
    if not fits:
        return split_grid(sources, potential, iter_counts)
    return whole_grid(sources, potential, iter_counts, parts=parts, points=points)


def solution(mesh):
    placed = (P(None, "dom", None), P("dom", None), P("point"))
    return jax.shard_map(
        on_device, mesh=mesh, in_specs=placed, out_specs=(P(), P()), check_vma=False
    )
```

```python
import functools
import math

import jax
import jax.numpy as jnp
from jax import lax
from jax.experimental import pallas as pl
from jax.experimental.pallas import tpu as pltpu
from jax.sharding import PartitionSpec as P

MOMENTS = 4
ITERS = 6
GX = 32


COEF_NEAR = 4.0 / 3.0
COEF_FAR = -1.0 / 12.0
GAMMA = 2.0
RADIUS = 1.5


def padded_2(block, sides, width):
    for axis, dim in sides:
        count = lax.axis_size(axis)
        forward = [(i, i + 1) for i in range(count - 1)]
        forward.append((count - 1, 0))
        backward = [(target, source) for source, target in forward]
        low = lax.ppermute(
            lax.slice_in_dim(block, block.shape[dim] - width, None, axis=dim), axis, forward
        )
        high = lax.ppermute(lax.slice_in_dim(block, 0, width, axis=dim), axis, backward)
        block = jnp.concatenate([low, block, high], axis=dim)
    return block


def plane_terms(values, side):
    lead = values.shape[:-1]
    planes = values.reshape(lead + (side, side))
    summed = COEF_NEAR * (
        jnp.roll(planes, 1, -2)
        + jnp.roll(planes, -1, -2)
        + jnp.roll(planes, 1, -1)
        + jnp.roll(planes, -1, -1)
    )
    summed = summed + COEF_FAR * (
        jnp.roll(planes, 2, -2)
        + jnp.roll(planes, -2, -2)
        + jnp.roll(planes, 2, -1)
        + jnp.roll(planes, -2, -1)
    )
    return summed.reshape(values.shape)


def complex_mul(first, second):
    return jnp.stack(
        [first[0] * second[0] - first[1] * second[1], first[0] * second[1] + first[1] * second[0]]
    )


def complex_div(first, second):
    denom = second[0] * second[0] + second[1] * second[1]
    return jnp.stack(
        [
            (first[0] * second[0] + first[1] * second[1]) / denom,
            (first[1] * second[0] - first[0] * second[1]) / denom,
        ]
    )


def bilinear(first, second):
    real_part = jnp.sum(first[0] * second[0] - first[1] * second[1], axis=(1, 2))
    imag_part = jnp.sum(first[0] * second[1] + first[1] * second[0], axis=(1, 2))
    return jnp.stack([real_part, imag_part])


def scaled(coeffs, values):
    return complex_mul(coeffs[:, :, None, None], values)


def shifted(values, potential, shift_re, shift_im):
    padded = padded_2(values, (("dom", 2),), 2)
    depth = values.shape[2]
    lap = -7.5 * values + plane_terms(values, GX)
    lap = lap + COEF_NEAR * (padded[:, :, 3 : 3 + depth] + padded[:, :, 1 : 1 + depth])
    lap = lap + COEF_FAR * (padded[:, :, 4 : 4 + depth] + padded[:, :, 0:depth])
    applied = -0.5 * lap + potential * values
    return jnp.stack(
        [
            shift_re * values[0] - shift_im * values[1] - applied[0],
            shift_re * values[1] + shift_im * values[0] - applied[1],
        ]
    )


def residual_sum(values):
    return lax.psum(bilinear(values, values), "dom")


def moment_terms(solution, residual, sources, angle_now, shift_re, shift_im):
    applied = jnp.stack(
        [
            shift_re * solution[0] - shift_im * solution[1] - sources[0] + residual[0],
            shift_re * solution[1] + shift_im * solution[0] - sources[1] + residual[1],
        ]
    )
    angles = (jnp.arange(MOMENTS).astype(jnp.float32) + 1.0) * angle_now
    coeffs = 0.25 * jnp.stack([jnp.cos(angles), jnp.sin(angles)])
    s_terms = complex_mul(coeffs[:, :, None, None, None], solution[:, None])
    h_terms = complex_mul(coeffs[:, :, None, None, None], applied[:, None])
    width = MOMENTS * solution.shape[1]
    return (s_terms.reshape(2, width, -1), h_terms.reshape(2, width, -1))


def gram_of(left, right):
    width = left.shape[1]
    joined = lax.dot_general(
        left.reshape(2 * width, -1),
        right.reshape(2 * width, -1),
        (((1,), (1,)), ((), ())),
        precision=lax.Precision.HIGHEST,
        preferred_element_type=jnp.float32,
    )
    blocks = joined.reshape(2, width, 2, width)
    return jnp.stack([blocks[0, :, 0] + blocks[1, :, 1], blocks[0, :, 1] - blocks[1, :, 0]])


def split_grid(sources, potential, iter_counts):
    complex_src = jnp.stack([sources, jnp.zeros_like(sources)])
    angle_now = (
        2.0 * math.pi * (lax.axis_index("point").astype(jnp.float32) + 0.5) / lax.axis_size("point")
    )
    shift_re = GAMMA + RADIUS * jnp.cos(angle_now)
    shift_im = RADIUS * jnp.sin(angle_now)
    limit = iter_counts[0]
    solution = jnp.zeros_like(complex_src)

    def one_turn(turn_idx, state):
        solution, residual, search, norm_now = state
        product = shifted(search, potential, shift_re, shift_im)
        curve = lax.psum(bilinear(search, product), "dom")
        step_size = complex_div(norm_now, curve)
        new_residual = residual - scaled(step_size, product)
        norm_next = residual_sum(new_residual)
        fresh = (
            solution + scaled(step_size, search),
            new_residual,
            new_residual + scaled(complex_div(norm_next, norm_now), search),
            norm_next,
        )
        keep_mask = turn_idx < limit
        return jax.tree.map(lambda newer, older: jnp.where(keep_mask, newer, older), fresh, state)

    start = (solution, complex_src, complex_src, residual_sum(complex_src))
    solution, residual, search, norm_now = lax.fori_loop(0, ITERS, one_turn, start)
    s_terms, h_terms = moment_terms(solution, residual, complex_src, angle_now, shift_re, shift_im)
    cells = sources.shape[1] * sources.shape[2] * lax.axis_size("dom")
    s_total, h_total = lax.psum((s_terms, h_terms), "point")
    gram_b, gram_a = lax.psum((gram_of(s_total, s_total), gram_of(s_total, h_total)), "dom")
    return (gram_b / cells, gram_a / cells)


Y_IN, X_IN = 2, 4
Y_OUT, X_OUT = GX // Y_IN, GX // X_IN
ROWS = Y_IN * X_IN
LANES = Y_OUT * X_OUT
SUB = 8
BASIS = ITERS + 1
H_SCALE = 2.0 / COEF_NEAR
FAR_SCALED = 0.5 * H_SCALE * COEF_FAR


def pack_kernel(depth, groups, counts, rows, levels, out):
    columns = rows.shape[0] // (SUB * groups * depth)
    source = lax.broadcasted_iota(jnp.int32, (LANES, LANES), 0)
    target = lax.broadcasted_iota(jnp.int32, (LANES, LANES), 1)
    inner = target // (LANES // ROWS)
    outer = target % (LANES // ROWS)
    cell = (outer // X_OUT * Y_IN + inner // X_IN) * GX + outer % X_OUT * X_IN + inner % X_IN
    swap = jnp.where(source == cell, 1.0, 0.0).astype(jnp.float32)
    parts = []
    for deep in range(depth):
        for group in range(groups):
            for column in range(columns):
                start = (group * SUB * columns + column) * depth + deep
                parts.append(rows[pl.ds(start, SUB, stride=columns * depth), :])
        parts.append(levels[pl.ds(deep, columns, stride=depth), :])
    mixed = exact_dot(jnp.concatenate(parts, axis=0), swap, ((1,), (0,)))
    block = LANES // ROWS
    lane_block = lax.broadcasted_iota(jnp.int32, (SUB, LANES), 1) // block
    row = lax.broadcasted_iota(jnp.int32, (SUB, LANES), 0)
    for deep in range(depth):
        base = deep * (groups + 1) * columns * SUB - deep * (columns - 1) * SUB
        for group in range(groups):
            pieces = [
                mixed[base + (group * columns + column) * SUB :][:SUB] for column in range(columns)
            ]
            for m in range(ROWS):
                value = pieces[m]
                for column in range(columns):
                    if column != m:
                        moved = pltpu.roll(pieces[column], (column - m) * block % LANES, 1)
                        value = jnp.where(lane_block == column, moved, value)
                start = ((deep * ROWS + m) * groups + group) * SUB
                out[start : start + SUB, :] = value
        piece = mixed[base + groups * columns * SUB :][:SUB]
        value = piece
        for far in range(1, columns):
            moved = pltpu.roll(pltpu.roll(piece, far * block, 1), columns - far, 0)
            value = jnp.where(lane_block == (row + far) % columns, moved, value)
        start = depth * ROWS * SUB * groups + deep * ROWS
        out[start : start + ROWS, :] = value
    out[out.shape[0] - SUB :, :] = jnp.full((SUB, LANES), counts[0].astype(jnp.float32))


def packed_block(sources, potential, iter_counts):
    count, depth, cells = sources.shape
    columns = cells // LANES
    rows = sources.reshape(count, depth, columns, LANES).transpose(0, 2, 1, 3)
    levels = potential.reshape(depth, columns, LANES).transpose(1, 0, 2)
    vmem = pl.BlockSpec(memory_space=pltpu.VMEM)
    smem = pl.BlockSpec(memory_space=pltpu.SMEM)
    size = depth * ROWS * (count + 1) + SUB
    return pl.pallas_call(
        functools.partial(pack_kernel, depth, count // SUB),
        out_shape=jax.ShapeDtypeStruct((size, LANES), jnp.float32),
        in_specs=[smem, vmem, vmem],
        out_specs=vmem,
        name="pack",
    )(iter_counts, rows.reshape(-1, LANES), levels.reshape(-1, LANES))


def lane_sum(values):
    return jnp.broadcast_to(jnp.sum(values, axis=1, keepdims=True), values.shape)


def ratio(top, bottom):
    return jnp.where(bottom > 0.0, top / jnp.where(bottom > 0.0, bottom, 1.0), 0.0)


def x_next(values, wrap_mask):
    return jnp.where(wrap_mask, pltpu.roll(values, X_OUT - 1, 1), pltpu.roll(values, LANES - 1, 1))


def x_prev(values, wrap_mask):
    return jnp.where(wrap_mask, pltpu.roll(values, LANES - X_OUT + 1, 1), pltpu.roll(values, 1, 1))


def apply_plane(vector, diagonal, plane, planes, group, last_x, first_x):
    rows = pl.ds(group * SUB, SUB)

    def plane_at(index):
        return [vector[index, rows, pl.ds(m * LANES, LANES)] for m in range(ROWS)]

    here = plane_at(plane)
    above, below = (plane_at(lax.rem(plane + far, planes)) for far in (1, planes - 1))
    above_2, below_2 = (plane_at(lax.rem(plane + far, planes)) for far in (2, planes - 2))
    y_up = [pltpu.roll(value, LANES - X_OUT, 1) for value in here]
    y_down = [pltpu.roll(value, X_OUT, 1) for value in here]
    out = []
    for yi in range(Y_IN):
        line = here[yi * X_IN : (yi + 1) * X_IN]
        before = [x_prev(line[X_IN - 2], first_x), x_prev(line[X_IN - 1], first_x)]
        after = [x_next(line[0], last_x), x_next(line[1], last_x)]
        wide = before + line + after
        for xi in range(X_IN):
            m = yi * X_IN + xi
            other = (1 - yi) * X_IN + xi
            y_next = here[other] if yi == 0 else y_up[other]
            y_prev = here[other] if yi == 1 else y_down[other]
            near = (wide[xi + 1] + wide[xi + 3]) + (y_next + y_prev) + (above[m] + below[m])
            far = (wide[xi] + wide[xi + 4]) + (y_up[m] + y_down[m]) + (above_2[m] + below_2[m])
            level = diagonal[plane, pl.ds(m, 1), :]
            out.append(level * here[m] - near - FAR_SCALED * far)
    return here, out


def cmul(first, second):
    return (
        first[0] * second[0] - first[1] * second[1],
        first[0] * second[1] + first[1] * second[0],
    )


def moment_coeffs(point, points, count):
    lane = lax.broadcasted_iota(jnp.int32, (1, LANES), 1)
    moment = lax.rem(lane, MOMENTS * count) // count
    angle = 2.0 * math.pi * (point + 0.5) / points
    parts = []
    for func in (math.cos, math.sin):
        value = jnp.full((1, LANES), 0.25 * func(angle), jnp.float32)
        for k in range(1, MOMENTS):
            value = jnp.where(moment == k, 0.25 * func((k + 1) * angle), value)
        parts.append(value)
    return parts


def weights_of(alphas, norms, limits, count):
    points = len(limits)
    shape = (count, LANES)
    half = MOMENTS * count
    lane = lax.broadcasted_iota(jnp.int32, shape, 1)
    source = lax.broadcasted_iota(jnp.int32, shape, 0)
    own = lax.rem(lane, count) == source
    left_half = lane < half
    betas = [ratio(norms[i + 1], norms[i]) for i in range(ITERS - 1)]
    sums = [[jnp.zeros(shape, jnp.float32)] * 2 for _ in range(BASIS)]
    zero = jnp.zeros(shape, jnp.float32)
    one = jnp.ones(shape, jnp.float32)
    for point in range(points):
        angle = 2.0 * math.pi * (point + 0.5) / points
        shift = (GAMMA + RADIUS * math.cos(angle), RADIUS * math.sin(angle))
        scaled_shift = (H_SCALE * shift[0], H_SCALE * shift[1])
        limit = limits[point]
        product = (one, zero)
        products = [product]
        links = []
        pivot = (scaled_shift[0] - alphas[0], zero + scaled_shift[1])
        for i in range(ITERS):
            size = 1.0 / (pivot[0] * pivot[0] + pivot[1] * pivot[1])
            inverse = (pivot[0] * size, -pivot[1] * size)
            product = cmul(product, inverse)
            products.append(product)
            if i < ITERS - 1:
                link = (betas[i] * inverse[0], betas[i] * inverse[1])
                links.append(link)
                pivot = (scaled_shift[0] - alphas[i + 1] - link[0], scaled_shift[1] - link[1])
        solved = [None] * ITERS
        for i in reversed(range(ITERS)):
            value = (H_SCALE * products[i + 1][0], H_SCALE * products[i + 1][1])
            if i < ITERS - 1:
                step = cmul(links[i], solved[i + 1])
                value = (value[0] + step[0], value[1] + step[1])
            used = limit > i
            solved[i] = (jnp.where(used, value[0], 0.0), jnp.where(used, value[1], 0.0))
        applied = []
        for i in range(BASIS):
            left = limit == i
            rest = (
                jnp.where(left, products[i][0], 0.0),
                jnp.where(left, products[i][1], 0.0),
            )
            if i < ITERS:
                turned = (
                    shift[0] * solved[i][0] - shift[1] * solved[i][1],
                    shift[0] * solved[i][1] + shift[1] * solved[i][0],
                )
                rest = (rest[0] + turned[0], rest[1] + turned[1])
            if i == 0:
                rest = (rest[0] - 1.0, rest[1])
            applied.append(rest)
        tail = applied[ITERS]
        for back, factor in ((1, alphas[ITERS - 1]), (2, betas[ITERS - 2])):
            part = applied[ITERS - back]
            applied[ITERS - back] = (part[0] - factor * tail[0], part[1] - factor * tail[1])
        moment = moment_coeffs(point, points, count)
        for i in range(BASIS):
            left = solved[i] if i < ITERS else (zero, zero)
            both = (
                jnp.where(left_half, left[0], applied[i][0]),
                jnp.where(left_half, left[1], applied[i][1]),
            )
            term = cmul(moment, both)
            sums[i] = [sums[i][0] + term[0], sums[i][1] + term[1]]
    return [[jnp.where(own, part, 0.0) for part in pair] for pair in sums]


def exact_dot(first, second, dims):
    return lax.dot_general(
        first,
        second,
        (dims, ((), ())),
        precision=lax.Precision.HIGHEST,
        preferred_element_type=jnp.float32,
    )


def solve_kernel(parts, points, count, *refs):
    blocks = refs[:parts]
    out_b, out_a = refs[parts : parts + 2]
    vectors = refs[parts + 2 : parts + 2 + BASIS]
    applied, diagonal, gram, limits = refs[parts + 2 + BASIS :]
    planes = diagonal.shape[0]
    depth = planes // parts
    groups = count // SUB
    lane = lax.broadcasted_iota(jnp.int32, (SUB, LANES), 1)
    last_x = lax.rem(lane, X_OUT) == X_OUT - 1
    first_x = lax.rem(lane, X_OUT) == 0
    here = lax.axis_index("dom")
    point_here = lax.axis_index("point")
    core = jnp.bitwise_and(here, 1)

    for turn in range(parts):
        slab = jnp.bitwise_xor(here, turn) * depth
        for deep in range(depth):
            for m in range(ROWS):
                start = (deep * ROWS + m) * count
                lanes = pl.ds(m * LANES, LANES)
                vectors[0][slab + deep, :, lanes] = blocks[turn][start : start + count, :]
            start = depth * ROWS * count + deep * ROWS
            diagonal[slab + deep] = H_SCALE * (blocks[turn][start : start + ROWS, :] + 3.75)

    blank = jnp.zeros((SUB, LANES), jnp.float32)
    alphas, norms = [], []
    for i in range(ITERS):
        source, target = vectors[i], applied if i < ITERS - 1 else vectors[ITERS]

        def apply_turn(plane, sums, i=i, source=source, target=target):
            new_sums = []
            for group in range(groups):
                rows = pl.ds(group * SUB, SUB)
                curve, norm = sums[group]
                value, out = apply_plane(source, diagonal, plane, planes, group, last_x, first_x)
                for m in range(ROWS):
                    target[plane, rows, pl.ds(m * LANES, LANES)] = out[m]
                    curve = curve + value[m] * out[m]
                    if i == 0:
                        norm = norm + value[m] * value[m]
                new_sums.append((curve, norm))
            return tuple(new_sums)

        sums = lax.fori_loop(0, planes, apply_turn, ((blank, blank),) * groups)
        if i == 0:
            norms.append([lane_sum(norm) for _, norm in sums])
        alphas.append([ratio(lane_sum(sums[g][0]), norms[i][g]) for g in range(groups)])
        if i == ITERS - 1:
            break
        betas = [ratio(norms[i][g], norms[i - 1][g]) for g in range(groups)] if i else None

        def step_turn(plane, sums, i=i, alpha=alphas[i], betas=betas):
            new_sums = []
            for group in range(groups):
                rows = pl.ds(group * SUB, SUB)
                norm = sums[group]
                for m in range(ROWS):
                    lanes = pl.ds(m * LANES, LANES)
                    value = applied[plane, rows, lanes]
                    value = value - alpha[group] * vectors[i][plane, rows, lanes]
                    if i:
                        value = value - betas[group] * vectors[i - 1][plane, rows, lanes]
                    vectors[i + 1][plane, rows, lanes] = value
                    norm = norm + value * value
                new_sums.append(norm)
            return tuple(new_sums)

        sums = lax.fori_loop(0, planes, step_turn, (blank,) * groups, unroll=2)
        norms.append([lane_sum(norm) for norm in sums])

    size = BASIS * count
    gram[...] = jnp.zeros_like(gram)

    def gram_turn(plane, carry):
        values = jnp.concatenate([vector[plane] for vector in vectors], axis=0)
        high = values.astype(jnp.bfloat16)
        low = (values - high.astype(jnp.float32)).astype(jnp.bfloat16)
        gram[...] += lax.dot_general(
            high,
            jnp.concatenate([high, low], axis=0),
            (((1,), (1,)), ((), ())),
            preferred_element_type=jnp.float32,
        )
        return carry

    lax.fori_loop(0, planes, gram_turn, 0)
    cross = gram[:, size:]
    pairs = gram[:, :size] + cross + cross.T

    tails = [block[block.shape[0] - SUB :, :] for block in blocks]
    limits[point_here] = tails[0]
    limits[jnp.bitwise_xor(point_here, 1 + core)] = tails[2]
    limits[jnp.bitwise_xor(point_here, 2 - core)] = tails[3]
    limits[jnp.bitwise_xor(point_here, 3)] = jnp.where(core == 0, tails[4], tails[5])
    bounds = [jnp.concatenate([limits[j]] * groups, axis=0) for j in range(points)]
    alphas = [jnp.concatenate(value, axis=0) for value in alphas]
    norms = [jnp.concatenate(value, axis=0) for value in norms]
    weights = weights_of(alphas, norms, bounds, count)
    real = jnp.concatenate([pair[0] for pair in weights], axis=0)
    imag = jnp.concatenate([pair[1] for pair in weights], axis=0)
    right = exact_dot(pairs, jnp.concatenate([real, imag], axis=1), ((1,), (0,)))
    half = MOMENTS * count
    left = jnp.concatenate([real[:, :half], imag[:, :half]], axis=1)
    joined = exact_dot(left.T, right, ((1,), (0,)))
    scale = 1.0 / (planes * ROWS * LANES)
    width = 2 * half
    real = (joined[:half, :width] + joined[half:, width:]) * scale
    imag = (joined[:half, width:] - joined[half:, :width]) * scale
    out_b[0] = real[:, :half]
    out_b[1] = imag[:, :half]
    out_a[0] = real[:, half:]
    out_a[1] = imag[:, half:]


CROSSING = {2: (1, 2), 4: (3, 0), 6: (0, 0)}


def exchanged(values, mask, parts, points):
    pairs = []
    for point in range(points):
        for part in range(parts):
            other = CROSSING[mask][part % 2] if mask in CROSSING else 0
            pairs.append(((point ^ other) * parts + (part ^ mask), point * parts + part))
    return lax.ppermute(values, ("point", "dom"), pairs)


def whole_grid(sources, potential, iter_counts, *, parts, points):
    count, depth, _ = sources.shape
    planes = parts * depth
    block = packed_block(sources, potential, iter_counts)
    even = [block] + [exchanged(block, mask, parts, points) for mask in range(2, parts, 2)]
    odd = [exchanged(value, 1, parts, points) for value in even]
    blocks = [value for pair in zip(even, odd) for value in pair]
    vmem = pl.BlockSpec(memory_space=pltpu.VMEM)
    size = BASIS * count
    width = MOMENTS * count
    out = jax.ShapeDtypeStruct((2, width, width), jnp.float32)
    vector = pltpu.VMEM((planes, count, ROWS * LANES), jnp.float32)
    return pl.pallas_call(
        functools.partial(solve_kernel, parts, points, count),
        out_shape=(out, out),
        in_specs=[vmem] * parts,
        out_specs=(vmem, vmem),
        scratch_shapes=[vector] * (BASIS + 1)
        + [
            pltpu.VMEM((planes, ROWS, LANES), jnp.float32),
            pltpu.VMEM((size, 2 * size), jnp.float32),
            pltpu.VMEM((points, SUB, LANES), jnp.float32),
        ],
        compiler_params=pltpu.CompilerParams(vmem_limit_bytes=32 * 2**20),
        name="solve",
    )(*blocks)


def on_device(sources, potential, iter_counts):
    parts, points = lax.axis_size("dom"), lax.axis_size("point")
    count, depth, cells = sources.shape
    held = BASIS * count * parts * depth * cells * 4
    fits = (
        held <= 16 * 2**20
        and parts == 8
        and points == 4
        and count == 2 * SUB
        and 2 * MOMENTS * count == LANES
        and cells == GX * GX == ROWS * LANES
    )
    if not fits:
        return split_grid(sources, potential, iter_counts)
    return whole_grid(sources, potential, iter_counts, parts=parts, points=points)


def solution(mesh):
    placed = (P(None, "dom", None), P("dom", None), P("point"))
    return jax.shard_map(
        on_device, mesh=mesh, in_specs=placed, out_specs=(P(), P()), check_vma=False
    )
```

```python
import functools
import math

import jax
import jax.numpy as jnp
from jax import lax
from jax.experimental import pallas as pl
from jax.experimental.pallas import tpu as pltpu
from jax.sharding import PartitionSpec as P

MOMENTS = 4
ITERS = 6
GX = 32


COEF_NEAR = 4.0 / 3.0
COEF_FAR = -1.0 / 12.0
GAMMA = 2.0
RADIUS = 1.5


def padded_2(block, sides, width):
    for axis, dim in sides:
        count = lax.axis_size(axis)
        forward = [(i, i + 1) for i in range(count - 1)]
        forward.append((count - 1, 0))
        backward = [(target, source) for source, target in forward]
        low = lax.ppermute(
            lax.slice_in_dim(block, block.shape[dim] - width, None, axis=dim), axis, forward
        )
        high = lax.ppermute(lax.slice_in_dim(block, 0, width, axis=dim), axis, backward)
        block = jnp.concatenate([low, block, high], axis=dim)
    return block


def plane_terms(values, side):
    lead = values.shape[:-1]
    planes = values.reshape(lead + (side, side))
    summed = COEF_NEAR * (
        jnp.roll(planes, 1, -2)
        + jnp.roll(planes, -1, -2)
        + jnp.roll(planes, 1, -1)
        + jnp.roll(planes, -1, -1)
    )
    summed = summed + COEF_FAR * (
        jnp.roll(planes, 2, -2)
        + jnp.roll(planes, -2, -2)
        + jnp.roll(planes, 2, -1)
        + jnp.roll(planes, -2, -1)
    )
    return summed.reshape(values.shape)


def complex_mul(first, second):
    return jnp.stack(
        [first[0] * second[0] - first[1] * second[1], first[0] * second[1] + first[1] * second[0]]
    )


def complex_div(first, second):
    denom = second[0] * second[0] + second[1] * second[1]
    return jnp.stack(
        [
            (first[0] * second[0] + first[1] * second[1]) / denom,
            (first[1] * second[0] - first[0] * second[1]) / denom,
        ]
    )


def bilinear(first, second):
    real_part = jnp.sum(first[0] * second[0] - first[1] * second[1], axis=(1, 2))
    imag_part = jnp.sum(first[0] * second[1] + first[1] * second[0], axis=(1, 2))
    return jnp.stack([real_part, imag_part])


def scaled(coeffs, values):
    return complex_mul(coeffs[:, :, None, None], values)


def shifted(values, potential, shift_re, shift_im):
    padded = padded_2(values, (("dom", 2),), 2)
    depth = values.shape[2]
    lap = -7.5 * values + plane_terms(values, GX)
    lap = lap + COEF_NEAR * (padded[:, :, 3 : 3 + depth] + padded[:, :, 1 : 1 + depth])
    lap = lap + COEF_FAR * (padded[:, :, 4 : 4 + depth] + padded[:, :, 0:depth])
    applied = -0.5 * lap + potential * values
    return jnp.stack(
        [
            shift_re * values[0] - shift_im * values[1] - applied[0],
            shift_re * values[1] + shift_im * values[0] - applied[1],
        ]
    )


def residual_sum(values):
    return lax.psum(bilinear(values, values), "dom")


def moment_terms(solution, residual, sources, angle_now, shift_re, shift_im):
    applied = jnp.stack(
        [
            shift_re * solution[0] - shift_im * solution[1] - sources[0] + residual[0],
            shift_re * solution[1] + shift_im * solution[0] - sources[1] + residual[1],
        ]
    )
    angles = (jnp.arange(MOMENTS).astype(jnp.float32) + 1.0) * angle_now
    coeffs = 0.25 * jnp.stack([jnp.cos(angles), jnp.sin(angles)])
    s_terms = complex_mul(coeffs[:, :, None, None, None], solution[:, None])
    h_terms = complex_mul(coeffs[:, :, None, None, None], applied[:, None])
    width = MOMENTS * solution.shape[1]
    return (s_terms.reshape(2, width, -1), h_terms.reshape(2, width, -1))


def gram_of(left, right):
    width = left.shape[1]
    joined = lax.dot_general(
        left.reshape(2 * width, -1),
        right.reshape(2 * width, -1),
        (((1,), (1,)), ((), ())),
        precision=lax.Precision.HIGHEST,
        preferred_element_type=jnp.float32,
    )
    blocks = joined.reshape(2, width, 2, width)
    return jnp.stack([blocks[0, :, 0] + blocks[1, :, 1], blocks[0, :, 1] - blocks[1, :, 0]])


def split_grid(sources, potential, iter_counts):
    complex_src = jnp.stack([sources, jnp.zeros_like(sources)])
    angle_now = (
        2.0 * math.pi * (lax.axis_index("point").astype(jnp.float32) + 0.5) / lax.axis_size("point")
    )
    shift_re = GAMMA + RADIUS * jnp.cos(angle_now)
    shift_im = RADIUS * jnp.sin(angle_now)
    limit = iter_counts[0]
    solution = jnp.zeros_like(complex_src)

    def one_turn(turn_idx, state):
        solution, residual, search, norm_now = state
        product = shifted(search, potential, shift_re, shift_im)
        curve = lax.psum(bilinear(search, product), "dom")
        step_size = complex_div(norm_now, curve)
        new_residual = residual - scaled(step_size, product)
        norm_next = residual_sum(new_residual)
        fresh = (
            solution + scaled(step_size, search),
            new_residual,
            new_residual + scaled(complex_div(norm_next, norm_now), search),
            norm_next,
        )
        keep_mask = turn_idx < limit
        return jax.tree.map(lambda newer, older: jnp.where(keep_mask, newer, older), fresh, state)

    start = (solution, complex_src, complex_src, residual_sum(complex_src))
    solution, residual, search, norm_now = lax.fori_loop(0, ITERS, one_turn, start)
    s_terms, h_terms = moment_terms(solution, residual, complex_src, angle_now, shift_re, shift_im)
    cells = sources.shape[1] * sources.shape[2] * lax.axis_size("dom")
    s_total, h_total = lax.psum((s_terms, h_terms), "point")
    gram_b, gram_a = lax.psum((gram_of(s_total, s_total), gram_of(s_total, h_total)), "dom")
    return (gram_b / cells, gram_a / cells)


Y_IN, X_IN = 2, 4
Y_OUT, X_OUT = GX // Y_IN, GX // X_IN
ROWS = Y_IN * X_IN
LANES = Y_OUT * X_OUT
SUB = 8
BASIS = ITERS + 1
H_SCALE = 2.0 / COEF_NEAR
FAR_SCALED = 0.5 * H_SCALE * COEF_FAR


def pack_kernel(depth, groups, counts, rows, levels, out):
    columns = rows.shape[0] // (SUB * groups * depth)
    source = lax.broadcasted_iota(jnp.int32, (LANES, LANES), 0)
    target = lax.broadcasted_iota(jnp.int32, (LANES, LANES), 1)
    inner = target // (LANES // ROWS)
    outer = target % (LANES // ROWS)
    cell = (outer // X_OUT * Y_IN + inner // X_IN) * GX + outer % X_OUT * X_IN + inner % X_IN
    swap = jnp.where(source == cell, 1.0, 0.0).astype(jnp.float32)
    parts = []
    for deep in range(depth):
        for group in range(groups):
            for column in range(columns):
                start = (group * SUB * columns + column) * depth + deep
                parts.append(rows[pl.ds(start, SUB, stride=columns * depth), :])
        parts.append(levels[pl.ds(deep, columns, stride=depth), :])
    mixed = exact_dot(jnp.concatenate(parts, axis=0), swap, ((1,), (0,)))
    block = LANES // ROWS
    lane_block = lax.broadcasted_iota(jnp.int32, (SUB, LANES), 1) // block
    row = lax.broadcasted_iota(jnp.int32, (SUB, LANES), 0)
    for deep in range(depth):
        base = deep * (groups + 1) * columns * SUB - deep * (columns - 1) * SUB
        for group in range(groups):
            pieces = [
                mixed[base + (group * columns + column) * SUB :][:SUB] for column in range(columns)
            ]
            for m in range(ROWS):
                value = pieces[m]
                for column in range(columns):
                    if column != m:
                        moved = pltpu.roll(pieces[column], (column - m) * block % LANES, 1)
                        value = jnp.where(lane_block == column, moved, value)
                start = ((deep * ROWS + m) * groups + group) * SUB
                out[start : start + SUB, :] = value
        piece = mixed[base + groups * columns * SUB :][:SUB]
        value = piece
        for far in range(1, columns):
            moved = pltpu.roll(pltpu.roll(piece, far * block, 1), columns - far, 0)
            value = jnp.where(lane_block == (row + far) % columns, moved, value)
        start = depth * ROWS * SUB * groups + deep * ROWS
        out[start : start + ROWS, :] = value
    out[out.shape[0] - SUB :, :] = jnp.full((SUB, LANES), counts[0].astype(jnp.float32))


def packed_block(sources, potential, iter_counts):
    count, depth, cells = sources.shape
    columns = cells // LANES
    rows = sources.reshape(count, depth, columns, LANES).transpose(0, 2, 1, 3)
    levels = potential.reshape(depth, columns, LANES).transpose(1, 0, 2)
    vmem = pl.BlockSpec(memory_space=pltpu.VMEM)
    smem = pl.BlockSpec(memory_space=pltpu.SMEM)
    size = depth * ROWS * (count + 1) + SUB
    return pl.pallas_call(
        functools.partial(pack_kernel, depth, count // SUB),
        out_shape=jax.ShapeDtypeStruct((size, LANES), jnp.float32),
        in_specs=[smem, vmem, vmem],
        out_specs=vmem,
        compiler_params=pltpu.CompilerParams(vmem_limit_bytes=4 * 2**20),
        name="pack",
    )(iter_counts, rows.reshape(-1, LANES), levels.reshape(-1, LANES))


def lane_sum(values):
    return jnp.broadcast_to(jnp.sum(values, axis=1, keepdims=True), values.shape)


def ratio(top, bottom):
    return jnp.where(bottom > 0.0, top / jnp.where(bottom > 0.0, bottom, 1.0), 0.0)


def x_next(values, wrap_mask):
    return jnp.where(wrap_mask, pltpu.roll(values, X_OUT - 1, 1), pltpu.roll(values, LANES - 1, 1))


def x_prev(values, wrap_mask):
    return jnp.where(wrap_mask, pltpu.roll(values, LANES - X_OUT + 1, 1), pltpu.roll(values, 1, 1))


def apply_plane(vector, diagonal, plane, planes, group, last_x, first_x):
    rows = pl.ds(group * SUB, SUB)

    def plane_at(index):
        return [vector[index, rows, pl.ds(m * LANES, LANES)] for m in range(ROWS)]

    here = plane_at(plane)
    above, below = (plane_at(lax.rem(plane + far, planes)) for far in (1, planes - 1))
    above_2, below_2 = (plane_at(lax.rem(plane + far, planes)) for far in (2, planes - 2))
    y_up = [pltpu.roll(value, LANES - X_OUT, 1) for value in here]
    y_down = [pltpu.roll(value, X_OUT, 1) for value in here]
    out = []
    for yi in range(Y_IN):
        line = here[yi * X_IN : (yi + 1) * X_IN]
        before = [x_prev(line[X_IN - 2], first_x), x_prev(line[X_IN - 1], first_x)]
        after = [x_next(line[0], last_x), x_next(line[1], last_x)]
        wide = before + line + after
        for xi in range(X_IN):
            m = yi * X_IN + xi
            other = (1 - yi) * X_IN + xi
            y_next = here[other] if yi == 0 else y_up[other]
            y_prev = here[other] if yi == 1 else y_down[other]
            near = (wide[xi + 1] + wide[xi + 3]) + (y_next + y_prev) + (above[m] + below[m])
            far = (wide[xi] + wide[xi + 4]) + (y_up[m] + y_down[m]) + (above_2[m] + below_2[m])
            level = diagonal[plane, pl.ds(m, 1), :]
            out.append(level * here[m] - near - FAR_SCALED * far)
    return here, out


def cmul(first, second):
    return (
        first[0] * second[0] - first[1] * second[1],
        first[0] * second[1] + first[1] * second[0],
    )


def moment_coeffs(point, points, count):
    lane = lax.broadcasted_iota(jnp.int32, (1, LANES), 1)
    moment = lax.rem(lane, MOMENTS * count) // count
    angle = 2.0 * math.pi * (point + 0.5) / points
    parts = []
    for func in (math.cos, math.sin):
        value = jnp.full((1, LANES), 0.25 * func(angle), jnp.float32)
        for k in range(1, MOMENTS):
            value = jnp.where(moment == k, 0.25 * func((k + 1) * angle), value)
        parts.append(value)
    return parts


def weights_of(alphas, norms, limits, count):
    points = len(limits)
    shape = (count, LANES)
    half = MOMENTS * count
    lane = lax.broadcasted_iota(jnp.int32, shape, 1)
    source = lax.broadcasted_iota(jnp.int32, shape, 0)
    own = lax.rem(lane, count) == source
    left_half = lane < half
    betas = [ratio(norms[i + 1], norms[i]) for i in range(ITERS - 1)]
    sums = [[jnp.zeros(shape, jnp.float32)] * 2 for _ in range(BASIS)]
    zero = jnp.zeros(shape, jnp.float32)
    one = jnp.ones(shape, jnp.float32)
    for point in range(points):
        angle = 2.0 * math.pi * (point + 0.5) / points
        shift = (GAMMA + RADIUS * math.cos(angle), RADIUS * math.sin(angle))
        scaled_shift = (H_SCALE * shift[0], H_SCALE * shift[1])
        limit = limits[point]
        product = (one, zero)
        products = [product]
        links = []
        pivot = (scaled_shift[0] - alphas[0], zero + scaled_shift[1])
        for i in range(ITERS):
            size = 1.0 / (pivot[0] * pivot[0] + pivot[1] * pivot[1])
            inverse = (pivot[0] * size, -pivot[1] * size)
            product = cmul(product, inverse)
            products.append(product)
            if i < ITERS - 1:
                link = (betas[i] * inverse[0], betas[i] * inverse[1])
                links.append(link)
                pivot = (scaled_shift[0] - alphas[i + 1] - link[0], scaled_shift[1] - link[1])
        solved = [None] * ITERS
        for i in reversed(range(ITERS)):
            value = (H_SCALE * products[i + 1][0], H_SCALE * products[i + 1][1])
            if i < ITERS - 1:
                step = cmul(links[i], solved[i + 1])
                value = (value[0] + step[0], value[1] + step[1])
            used = limit > i
            solved[i] = (jnp.where(used, value[0], 0.0), jnp.where(used, value[1], 0.0))
        applied = []
        for i in range(BASIS):
            left = limit == i
            rest = (
                jnp.where(left, products[i][0], 0.0),
                jnp.where(left, products[i][1], 0.0),
            )
            if i < ITERS:
                turned = (
                    shift[0] * solved[i][0] - shift[1] * solved[i][1],
                    shift[0] * solved[i][1] + shift[1] * solved[i][0],
                )
                rest = (rest[0] + turned[0], rest[1] + turned[1])
            if i == 0:
                rest = (rest[0] - 1.0, rest[1])
            applied.append(rest)
        tail = applied[ITERS]
        for back, factor in ((1, alphas[ITERS - 1]), (2, betas[ITERS - 2])):
            part = applied[ITERS - back]
            applied[ITERS - back] = (part[0] - factor * tail[0], part[1] - factor * tail[1])
        moment = moment_coeffs(point, points, count)
        for i in range(BASIS):
            left = solved[i] if i < ITERS else (zero, zero)
            both = (
                jnp.where(left_half, left[0], applied[i][0]),
                jnp.where(left_half, left[1], applied[i][1]),
            )
            term = cmul(moment, both)
            sums[i] = [sums[i][0] + term[0], sums[i][1] + term[1]]
    return [[jnp.where(own, part, 0.0) for part in pair] for pair in sums]


def exact_dot(first, second, dims):
    return lax.dot_general(
        first,
        second,
        (dims, ((), ())),
        precision=lax.Precision.HIGHEST,
        preferred_element_type=jnp.float32,
    )


def solve_kernel(parts, points, count, *refs):
    blocks = refs[:parts]
    out_b, out_a = refs[parts : parts + 2]
    vectors = refs[parts + 2 : parts + 2 + BASIS]
    applied, diagonal, gram, limits = refs[parts + 2 + BASIS :]
    planes = diagonal.shape[0]
    depth = planes // parts
    groups = count // SUB
    lane = lax.broadcasted_iota(jnp.int32, (SUB, LANES), 1)
    last_x = lax.rem(lane, X_OUT) == X_OUT - 1
    first_x = lax.rem(lane, X_OUT) == 0
    here = lax.axis_index("dom")
    point_here = lax.axis_index("point")
    core = jnp.bitwise_and(here, 1)

    for turn in range(parts):
        slab = jnp.bitwise_xor(here, turn) * depth
        for deep in range(depth):
            for m in range(ROWS):
                start = (deep * ROWS + m) * count
                lanes = pl.ds(m * LANES, LANES)
                vectors[0][slab + deep, :, lanes] = blocks[turn][start : start + count, :]
            start = depth * ROWS * count + deep * ROWS
            diagonal[slab + deep] = H_SCALE * (blocks[turn][start : start + ROWS, :] + 3.75)

    blank = jnp.zeros((SUB, LANES), jnp.float32)
    alphas, norms = [], []
    for i in range(ITERS):
        source, target = vectors[i], applied if i < ITERS - 1 else vectors[ITERS]

        def apply_turn(plane, sums, i=i, source=source, target=target):
            new_sums = []
            for group in range(groups):
                rows = pl.ds(group * SUB, SUB)
                curve, norm = sums[group]
                value, out = apply_plane(source, diagonal, plane, planes, group, last_x, first_x)
                for m in range(ROWS):
                    target[plane, rows, pl.ds(m * LANES, LANES)] = out[m]
                    curve = curve + value[m] * out[m]
                    if i == 0:
                        norm = norm + value[m] * value[m]
                new_sums.append((curve, norm))
            return tuple(new_sums)

        sums = lax.fori_loop(0, planes, apply_turn, ((blank, blank),) * groups, unroll=4)
        if i == 0:
            norms.append([lane_sum(norm) for _, norm in sums])
        alphas.append([ratio(lane_sum(sums[g][0]), norms[i][g]) for g in range(groups)])
        if i == ITERS - 1:
            break
        betas = [ratio(norms[i][g], norms[i - 1][g]) for g in range(groups)] if i else None

        def step_turn(plane, sums, i=i, alpha=alphas[i], betas=betas):
            new_sums = []
            for group in range(groups):
                rows = pl.ds(group * SUB, SUB)
                norm = sums[group]
                for m in range(ROWS):
                    lanes = pl.ds(m * LANES, LANES)
                    value = applied[plane, rows, lanes]
                    value = value - alpha[group] * vectors[i][plane, rows, lanes]
                    if i:
                        value = value - betas[group] * vectors[i - 1][plane, rows, lanes]
                    vectors[i + 1][plane, rows, lanes] = value
                    norm = norm + value * value
                new_sums.append(norm)
            return tuple(new_sums)

        sums = lax.fori_loop(0, planes, step_turn, (blank,) * groups, unroll=4)
        norms.append([lane_sum(norm) for norm in sums])

    size = BASIS * count
    gram[...] = jnp.zeros_like(gram)

    def gram_turn(plane, carry):
        values = jnp.concatenate([vector[plane] for vector in vectors], axis=0)
        high = values.astype(jnp.bfloat16)
        low = (values - high.astype(jnp.float32)).astype(jnp.bfloat16)
        gram[...] += lax.dot_general(
            high,
            jnp.concatenate([high, low], axis=0),
            (((1,), (1,)), ((), ())),
            preferred_element_type=jnp.float32,
        )
        return carry

    lax.fori_loop(0, planes, gram_turn, 0, unroll=4)
    cross = gram[:, size:]
    pairs = gram[:, :size] + cross + cross.T

    tails = [block[block.shape[0] - SUB :, :] for block in blocks]
    limits[point_here] = tails[0]
    limits[jnp.bitwise_xor(point_here, 1 + core)] = tails[2]
    limits[jnp.bitwise_xor(point_here, 2 - core)] = tails[3]
    limits[jnp.bitwise_xor(point_here, 3)] = jnp.where(core == 0, tails[4], tails[5])
    bounds = [jnp.concatenate([limits[j]] * groups, axis=0) for j in range(points)]
    alphas = [jnp.concatenate(value, axis=0) for value in alphas]
    norms = [jnp.concatenate(value, axis=0) for value in norms]
    weights = weights_of(alphas, norms, bounds, count)
    real = jnp.concatenate([pair[0] for pair in weights], axis=0)
    imag = jnp.concatenate([pair[1] for pair in weights], axis=0)
    right = exact_dot(pairs, jnp.concatenate([real, imag], axis=1), ((1,), (0,)))
    half = MOMENTS * count
    left = jnp.concatenate([real[:, :half], imag[:, :half]], axis=1)
    joined = exact_dot(left.T, right, ((1,), (0,)))
    scale = 1.0 / (planes * ROWS * LANES)
    width = 2 * half
    real = (joined[:half, :width] + joined[half:, width:]) * scale
    imag = (joined[:half, width:] - joined[half:, :width]) * scale
    out_b[0] = real[:, :half]
    out_b[1] = imag[:, :half]
    out_a[0] = real[:, half:]
    out_a[1] = imag[:, half:]


CROSSING = {2: (1, 2), 4: (3, 0), 6: (0, 0)}


def exchanged(values, mask, parts, points):
    pairs = []
    for point in range(points):
        for part in range(parts):
            other = CROSSING[mask][part % 2] if mask in CROSSING else 0
            pairs.append(((point ^ other) * parts + (part ^ mask), point * parts + part))
    return lax.ppermute(values, ("point", "dom"), pairs)


def whole_grid(sources, potential, iter_counts, *, parts, points):
    count, depth, _ = sources.shape
    planes = parts * depth
    block = packed_block(sources, potential, iter_counts)
    even = [block] + [exchanged(block, mask, parts, points) for mask in range(2, parts, 2)]
    odd = [exchanged(value, 1, parts, points) for value in even]
    blocks = [value for pair in zip(even, odd) for value in pair]
    vmem = pl.BlockSpec(memory_space=pltpu.VMEM)
    size = BASIS * count
    width = MOMENTS * count
    out = jax.ShapeDtypeStruct((2, width, width), jnp.float32)
    vector = pltpu.VMEM((planes, count, ROWS * LANES), jnp.float32)
    return pl.pallas_call(
        functools.partial(solve_kernel, parts, points, count),
        out_shape=(out, out),
        in_specs=[vmem] * parts,
        out_specs=(vmem, vmem),
        scratch_shapes=[vector] * (BASIS + 1)
        + [
            pltpu.VMEM((planes, ROWS, LANES), jnp.float32),
            pltpu.VMEM((size, 2 * size), jnp.float32),
            pltpu.VMEM((points, SUB, LANES), jnp.float32),
        ],
        compiler_params=pltpu.CompilerParams(vmem_limit_bytes=32 * 2**20),
        name="solve",
    )(*blocks)


def on_device(sources, potential, iter_counts):
    parts, points = lax.axis_size("dom"), lax.axis_size("point")
    count, depth, cells = sources.shape
    held = BASIS * count * parts * depth * cells * 4
    fits = (
        held <= 16 * 2**20
        and parts == 8
        and points == 4
        and count == 2 * SUB
        and 2 * MOMENTS * count == LANES
        and cells == GX * GX == ROWS * LANES
    )
    if not fits:
        return split_grid(sources, potential, iter_counts)
    return whole_grid(sources, potential, iter_counts, parts=parts, points=points)


def solution(mesh):
    placed = (P(None, "dom", None), P("dom", None), P("point"))
    return jax.shard_map(
        on_device, mesh=mesh, in_specs=placed, out_specs=(P(), P()), check_vma=False
    )
```

```python
import functools
import math

import jax
import jax.numpy as jnp
from jax import lax
from jax.experimental import pallas as pl
from jax.experimental.pallas import tpu as pltpu
from jax.sharding import PartitionSpec as P

MOMENTS = 4
ITERS = 6
GX = 32


COEF_NEAR = 4.0 / 3.0
COEF_FAR = -1.0 / 12.0
GAMMA = 2.0
RADIUS = 1.5


def padded_2(block, sides, width):
    for axis, dim in sides:
        count = lax.axis_size(axis)
        forward = [(i, i + 1) for i in range(count - 1)]
        forward.append((count - 1, 0))
        backward = [(target, source) for source, target in forward]
        low = lax.ppermute(
            lax.slice_in_dim(block, block.shape[dim] - width, None, axis=dim), axis, forward
        )
        high = lax.ppermute(lax.slice_in_dim(block, 0, width, axis=dim), axis, backward)
        block = jnp.concatenate([low, block, high], axis=dim)
    return block


def plane_terms(values, side):
    lead = values.shape[:-1]
    planes = values.reshape(lead + (side, side))
    summed = COEF_NEAR * (
        jnp.roll(planes, 1, -2)
        + jnp.roll(planes, -1, -2)
        + jnp.roll(planes, 1, -1)
        + jnp.roll(planes, -1, -1)
    )
    summed = summed + COEF_FAR * (
        jnp.roll(planes, 2, -2)
        + jnp.roll(planes, -2, -2)
        + jnp.roll(planes, 2, -1)
        + jnp.roll(planes, -2, -1)
    )
    return summed.reshape(values.shape)


def complex_mul(first, second):
    return jnp.stack(
        [first[0] * second[0] - first[1] * second[1], first[0] * second[1] + first[1] * second[0]]
    )


def complex_div(first, second):
    denom = second[0] * second[0] + second[1] * second[1]
    return jnp.stack(
        [
            (first[0] * second[0] + first[1] * second[1]) / denom,
            (first[1] * second[0] - first[0] * second[1]) / denom,
        ]
    )


def bilinear(first, second):
    real_part = jnp.sum(first[0] * second[0] - first[1] * second[1], axis=(1, 2))
    imag_part = jnp.sum(first[0] * second[1] + first[1] * second[0], axis=(1, 2))
    return jnp.stack([real_part, imag_part])


def scaled(coeffs, values):
    return complex_mul(coeffs[:, :, None, None], values)


def shifted(values, potential, shift_re, shift_im):
    padded = padded_2(values, (("dom", 2),), 2)
    depth = values.shape[2]
    lap = -7.5 * values + plane_terms(values, GX)
    lap = lap + COEF_NEAR * (padded[:, :, 3 : 3 + depth] + padded[:, :, 1 : 1 + depth])
    lap = lap + COEF_FAR * (padded[:, :, 4 : 4 + depth] + padded[:, :, 0:depth])
    applied = -0.5 * lap + potential * values
    return jnp.stack(
        [
            shift_re * values[0] - shift_im * values[1] - applied[0],
            shift_re * values[1] + shift_im * values[0] - applied[1],
        ]
    )


def residual_sum(values):
    return lax.psum(bilinear(values, values), "dom")


def moment_terms(solution, residual, sources, angle_now, shift_re, shift_im):
    applied = jnp.stack(
        [
            shift_re * solution[0] - shift_im * solution[1] - sources[0] + residual[0],
            shift_re * solution[1] + shift_im * solution[0] - sources[1] + residual[1],
        ]
    )
    angles = (jnp.arange(MOMENTS).astype(jnp.float32) + 1.0) * angle_now
    coeffs = 0.25 * jnp.stack([jnp.cos(angles), jnp.sin(angles)])
    s_terms = complex_mul(coeffs[:, :, None, None, None], solution[:, None])
    h_terms = complex_mul(coeffs[:, :, None, None, None], applied[:, None])
    width = MOMENTS * solution.shape[1]
    return (s_terms.reshape(2, width, -1), h_terms.reshape(2, width, -1))


def gram_of(left, right):
    width = left.shape[1]
    joined = lax.dot_general(
        left.reshape(2 * width, -1),
        right.reshape(2 * width, -1),
        (((1,), (1,)), ((), ())),
        precision=lax.Precision.HIGHEST,
        preferred_element_type=jnp.float32,
    )
    blocks = joined.reshape(2, width, 2, width)
    return jnp.stack([blocks[0, :, 0] + blocks[1, :, 1], blocks[0, :, 1] - blocks[1, :, 0]])


def split_grid(sources, potential, iter_counts):
    complex_src = jnp.stack([sources, jnp.zeros_like(sources)])
    angle_now = (
        2.0 * math.pi * (lax.axis_index("point").astype(jnp.float32) + 0.5) / lax.axis_size("point")
    )
    shift_re = GAMMA + RADIUS * jnp.cos(angle_now)
    shift_im = RADIUS * jnp.sin(angle_now)
    limit = iter_counts[0]
    solution = jnp.zeros_like(complex_src)

    def one_turn(turn_idx, state):
        solution, residual, search, norm_now = state
        product = shifted(search, potential, shift_re, shift_im)
        curve = lax.psum(bilinear(search, product), "dom")
        step_size = complex_div(norm_now, curve)
        new_residual = residual - scaled(step_size, product)
        norm_next = residual_sum(new_residual)
        fresh = (
            solution + scaled(step_size, search),
            new_residual,
            new_residual + scaled(complex_div(norm_next, norm_now), search),
            norm_next,
        )
        keep_mask = turn_idx < limit
        return jax.tree.map(lambda newer, older: jnp.where(keep_mask, newer, older), fresh, state)

    start = (solution, complex_src, complex_src, residual_sum(complex_src))
    solution, residual, search, norm_now = lax.fori_loop(0, ITERS, one_turn, start)
    s_terms, h_terms = moment_terms(solution, residual, complex_src, angle_now, shift_re, shift_im)
    cells = sources.shape[1] * sources.shape[2] * lax.axis_size("dom")
    s_total, h_total = lax.psum((s_terms, h_terms), "point")
    gram_b, gram_a = lax.psum((gram_of(s_total, s_total), gram_of(s_total, h_total)), "dom")
    return (gram_b / cells, gram_a / cells)


Y_IN, X_IN = 2, 4
Y_OUT, X_OUT = GX // Y_IN, GX // X_IN
ROWS = Y_IN * X_IN
LANES = Y_OUT * X_OUT
SUB = 8
BASIS = ITERS + 1
CORES = 2
H_SCALE = 2.0 / COEF_NEAR
FAR_SCALED = 0.5 * H_SCALE * COEF_FAR


def pack_kernel(depth, groups, counts, rows, levels, out):
    columns = rows.shape[0] // (SUB * groups * depth)
    source = lax.broadcasted_iota(jnp.int32, (LANES, LANES), 0)
    target = lax.broadcasted_iota(jnp.int32, (LANES, LANES), 1)
    inner = target // (LANES // ROWS)
    outer = target % (LANES // ROWS)
    cell = (outer // X_OUT * Y_IN + inner // X_IN) * GX + outer % X_OUT * X_IN + inner % X_IN
    swap = jnp.where(source == cell, 1.0, 0.0).astype(jnp.float32)
    parts = []
    for deep in range(depth):
        for group in range(groups):
            for column in range(columns):
                start = (group * SUB * columns + column) * depth + deep
                parts.append(rows[pl.ds(start, SUB, stride=columns * depth), :])
        parts.append(levels[pl.ds(deep, columns, stride=depth), :])
    mixed = exact_dot(jnp.concatenate(parts, axis=0), swap, ((1,), (0,)))
    block = LANES // ROWS
    lane_block = lax.broadcasted_iota(jnp.int32, (SUB, LANES), 1) // block
    row = lax.broadcasted_iota(jnp.int32, (SUB, LANES), 0)
    for deep in range(depth):
        base = deep * (groups + 1) * columns * SUB - deep * (columns - 1) * SUB
        for group in range(groups):
            pieces = [
                mixed[base + (group * columns + column) * SUB :][:SUB] for column in range(columns)
            ]
            for m in range(ROWS):
                value = pieces[m]
                for column in range(columns):
                    if column != m:
                        moved = pltpu.roll(pieces[column], (column - m) * block % LANES, 1)
                        value = jnp.where(lane_block == column, moved, value)
                start = ((deep * ROWS + m) * groups + group) * SUB
                out[0, start : start + SUB, :] = value
        piece = mixed[base + groups * columns * SUB :][:SUB]
        value = piece
        for far in range(1, columns):
            moved = pltpu.roll(pltpu.roll(piece, far * block, 1), columns - far, 0)
            value = jnp.where(lane_block == (row + far) % columns, moved, value)
        start = depth * ROWS * SUB * groups + deep * ROWS
        out[0, start : start + ROWS, :] = value
    size = out.shape[1]
    out[0, size - SUB :, :] = jnp.full((SUB, LANES), counts[0].astype(jnp.float32))
    for copy in range(1, out.shape[0]):
        out[copy] = out[0]


def packed_block(sources, potential, iter_counts, copies):
    count, depth, cells = sources.shape
    columns = cells // LANES
    rows = sources.reshape(count, depth, columns, LANES).transpose(0, 2, 1, 3)
    levels = potential.reshape(depth, columns, LANES).transpose(1, 0, 2)
    vmem = pl.BlockSpec(memory_space=pltpu.VMEM)
    smem = pl.BlockSpec(memory_space=pltpu.SMEM)
    size = depth * ROWS * (count + 1) + SUB
    return pl.pallas_call(
        functools.partial(pack_kernel, depth, count // SUB),
        out_shape=jax.ShapeDtypeStruct((copies, size, LANES), jnp.float32),
        in_specs=[smem, vmem, vmem],
        out_specs=vmem,
        compiler_params=pltpu.CompilerParams(vmem_limit_bytes=4 * 2**20),
        name="pack",
    )(iter_counts, rows.reshape(-1, LANES), levels.reshape(-1, LANES))


def lane_sum(values):
    return jnp.broadcast_to(jnp.sum(values, axis=1, keepdims=True), values.shape)


def ratio(top, bottom):
    return jnp.where(bottom > 0.0, top / jnp.where(bottom > 0.0, bottom, 1.0), 0.0)


def x_next(values, wrap_mask):
    return jnp.where(wrap_mask, pltpu.roll(values, X_OUT - 1, 1), pltpu.roll(values, LANES - 1, 1))


def x_prev(values, wrap_mask):
    return jnp.where(wrap_mask, pltpu.roll(values, LANES - X_OUT + 1, 1), pltpu.roll(values, 1, 1))


def apply_plane(vector, diagonal, plane, planes, group, last_x, first_x):
    rows = pl.ds(group * SUB, SUB)

    def plane_at(index):
        return [vector[index, rows, pl.ds(m * LANES, LANES)] for m in range(ROWS)]

    here = plane_at(plane)
    above, below = (plane_at(lax.rem(plane + far, planes)) for far in (1, planes - 1))
    above_2, below_2 = (plane_at(lax.rem(plane + far, planes)) for far in (2, planes - 2))
    y_up = [pltpu.roll(value, LANES - X_OUT, 1) for value in here]
    y_down = [pltpu.roll(value, X_OUT, 1) for value in here]
    out = []
    for yi in range(Y_IN):
        line = here[yi * X_IN : (yi + 1) * X_IN]
        before = [x_prev(line[X_IN - 2], first_x), x_prev(line[X_IN - 1], first_x)]
        after = [x_next(line[0], last_x), x_next(line[1], last_x)]
        wide = before + line + after
        for xi in range(X_IN):
            m = yi * X_IN + xi
            other = (1 - yi) * X_IN + xi
            y_next = here[other] if yi == 0 else y_up[other]
            y_prev = here[other] if yi == 1 else y_down[other]
            near = (wide[xi + 1] + wide[xi + 3]) + (y_next + y_prev) + (above[m] + below[m])
            far = (wide[xi] + wide[xi + 4]) + (y_up[m] + y_down[m]) + (above_2[m] + below_2[m])
            level = diagonal[plane, pl.ds(m, 1), :]
            out.append(level * here[m] - near - FAR_SCALED * far)
    return here, out


def cmul(first, second):
    return (
        first[0] * second[0] - first[1] * second[1],
        first[0] * second[1] + first[1] * second[0],
    )


def moment_coeffs(point, points, count):
    lane = lax.broadcasted_iota(jnp.int32, (1, LANES), 1)
    moment = lax.rem(lane, MOMENTS * count) // count
    angle = 2.0 * math.pi * (point + 0.5) / points
    parts = []
    for func in (math.cos, math.sin):
        value = jnp.full((1, LANES), 0.25 * func(angle), jnp.float32)
        for k in range(1, MOMENTS):
            value = jnp.where(moment == k, 0.25 * func((k + 1) * angle), value)
        parts.append(value)
    return parts


def weights_of(alphas, norms, limits, count):
    points = len(limits)
    shape = (count, LANES)
    half = MOMENTS * count
    lane = lax.broadcasted_iota(jnp.int32, shape, 1)
    source = lax.broadcasted_iota(jnp.int32, shape, 0)
    own = lax.rem(lane, count) == source
    left_half = lane < half
    betas = [ratio(norms[i + 1], norms[i]) for i in range(ITERS - 1)]
    sums = [[jnp.zeros(shape, jnp.float32)] * 2 for _ in range(BASIS)]
    zero = jnp.zeros(shape, jnp.float32)
    one = jnp.ones(shape, jnp.float32)
    for point in range(points):
        angle = 2.0 * math.pi * (point + 0.5) / points
        shift = (GAMMA + RADIUS * math.cos(angle), RADIUS * math.sin(angle))
        scaled_shift = (H_SCALE * shift[0], H_SCALE * shift[1])
        limit = limits[point]
        product = (one, zero)
        products = [product]
        links = []
        pivot = (scaled_shift[0] - alphas[0], zero + scaled_shift[1])
        for i in range(ITERS):
            size = 1.0 / (pivot[0] * pivot[0] + pivot[1] * pivot[1])
            inverse = (pivot[0] * size, -pivot[1] * size)
            product = cmul(product, inverse)
            products.append(product)
            if i < ITERS - 1:
                link = (betas[i] * inverse[0], betas[i] * inverse[1])
                links.append(link)
                pivot = (scaled_shift[0] - alphas[i + 1] - link[0], scaled_shift[1] - link[1])
        solved = [None] * ITERS
        for i in reversed(range(ITERS)):
            value = (H_SCALE * products[i + 1][0], H_SCALE * products[i + 1][1])
            if i < ITERS - 1:
                step = cmul(links[i], solved[i + 1])
                value = (value[0] + step[0], value[1] + step[1])
            used = limit > i
            solved[i] = (jnp.where(used, value[0], 0.0), jnp.where(used, value[1], 0.0))
        applied = []
        for i in range(BASIS):
            left = limit == i
            rest = (
                jnp.where(left, products[i][0], 0.0),
                jnp.where(left, products[i][1], 0.0),
            )
            if i < ITERS:
                turned = (
                    shift[0] * solved[i][0] - shift[1] * solved[i][1],
                    shift[0] * solved[i][1] + shift[1] * solved[i][0],
                )
                rest = (rest[0] + turned[0], rest[1] + turned[1])
            if i == 0:
                rest = (rest[0] - 1.0, rest[1])
            applied.append(rest)
        tail = applied[ITERS]
        for back, factor in ((1, alphas[ITERS - 1]), (2, betas[ITERS - 2])):
            part = applied[ITERS - back]
            applied[ITERS - back] = (part[0] - factor * tail[0], part[1] - factor * tail[1])
        moment = moment_coeffs(point, points, count)
        for i in range(BASIS):
            left = solved[i] if i < ITERS else (zero, zero)
            both = (
                jnp.where(left_half, left[0], applied[i][0]),
                jnp.where(left_half, left[1], applied[i][1]),
            )
            term = cmul(moment, both)
            sums[i] = [sums[i][0] + term[0], sums[i][1] + term[1]]
    return [[jnp.where(own, part, 0.0) for part in pair] for pair in sums]


def exact_dot(first, second, dims):
    return lax.dot_general(
        first,
        second,
        (dims, ((), ())),
        precision=lax.Precision.HIGHEST,
        preferred_element_type=jnp.float32,
    )


def solve_kernel(parts, points, count, mine, other, out_b, out_a, *refs):
    vectors = refs[:BASIS]
    applied, diagonal, gram, limits = refs[BASIS:]
    planes = diagonal.shape[0]
    depth = planes // parts
    groups = count // SUB
    lane = lax.broadcasted_iota(jnp.int32, (SUB, LANES), 1)
    last_x = lax.rem(lane, X_OUT) == X_OUT - 1
    first_x = lax.rem(lane, X_OUT) == 0
    here = lax.axis_index("dom")
    core = jnp.bitwise_and(here, CORES - 1)
    origin = jnp.bitwise_xor(lax.axis_index("point"), here // CORES)

    for chip in range(parts // CORES):
        for block, side in ((mine, core), (other, 1 - core)):
            slab = (chip * CORES + side) * depth
            for deep in range(depth):
                for m in range(ROWS):
                    start = (deep * ROWS + m) * count
                    lanes = pl.ds(m * LANES, LANES)
                    vectors[0][slab + deep, :, lanes] = block[chip, start : start + count, :]
                start = depth * ROWS * count + deep * ROWS
                levels = block[chip, start : start + ROWS, :]
                diagonal[slab + deep] = H_SCALE * (levels + 3.75)

    blank = jnp.zeros((SUB, LANES), jnp.float32)
    alphas, norms = [], []
    for i in range(ITERS):
        source, target = vectors[i], applied if i < ITERS - 1 else vectors[ITERS]

        def apply_turn(plane, sums, i=i, source=source, target=target):
            new_sums = []
            for group in range(groups):
                rows = pl.ds(group * SUB, SUB)
                curve, norm = sums[group]
                value, out = apply_plane(source, diagonal, plane, planes, group, last_x, first_x)
                for m in range(ROWS):
                    target[plane, rows, pl.ds(m * LANES, LANES)] = out[m]
                    curve = curve + value[m] * out[m]
                    if i == 0:
                        norm = norm + value[m] * value[m]
                new_sums.append((curve, norm))
            return tuple(new_sums)

        sums = lax.fori_loop(0, planes, apply_turn, ((blank, blank),) * groups, unroll=4)
        if i == 0:
            norms.append([lane_sum(norm) for _, norm in sums])
        alphas.append([ratio(lane_sum(sums[g][0]), norms[i][g]) for g in range(groups)])
        if i == ITERS - 1:
            break
        betas = [ratio(norms[i][g], norms[i - 1][g]) for g in range(groups)] if i else None

        def step_turn(plane, sums, i=i, alpha=alphas[i], betas=betas):
            new_sums = []
            for group in range(groups):
                rows = pl.ds(group * SUB, SUB)
                norm = sums[group]
                for m in range(ROWS):
                    lanes = pl.ds(m * LANES, LANES)
                    value = applied[plane, rows, lanes]
                    value = value - alpha[group] * vectors[i][plane, rows, lanes]
                    if i:
                        value = value - betas[group] * vectors[i - 1][plane, rows, lanes]
                    vectors[i + 1][plane, rows, lanes] = value
                    norm = norm + value * value
                new_sums.append(norm)
            return tuple(new_sums)

        sums = lax.fori_loop(0, planes, step_turn, (blank,) * groups, unroll=4)
        norms.append([lane_sum(norm) for norm in sums])

    size = BASIS * count
    gram[...] = jnp.zeros_like(gram)

    def gram_turn(plane, carry):
        values = jnp.concatenate([vector[plane] for vector in vectors], axis=0)
        high = values.astype(jnp.bfloat16)
        low = (values - high.astype(jnp.float32)).astype(jnp.bfloat16)
        gram[...] += lax.dot_general(
            high,
            jnp.concatenate([high, low], axis=0),
            (((1,), (1,)), ((), ())),
            preferred_element_type=jnp.float32,
        )
        return carry

    lax.fori_loop(0, planes, gram_turn, 0, unroll=4)
    cross = gram[:, size:]
    pairs = gram[:, :size] + cross + cross.T

    tail = mine.shape[1] - SUB
    for chip in range(parts // CORES):
        limits[jnp.bitwise_xor(origin, chip)] = jnp.where(
            core == 0, mine[chip, tail:, :], other[chip, tail:, :]
        )
    bounds = [jnp.concatenate([limits[j]] * groups, axis=0) for j in range(points)]
    alphas = [jnp.concatenate(value, axis=0) for value in alphas]
    norms = [jnp.concatenate(value, axis=0) for value in norms]
    weights = weights_of(alphas, norms, bounds, count)
    real = jnp.concatenate([pair[0] for pair in weights], axis=0)
    imag = jnp.concatenate([pair[1] for pair in weights], axis=0)
    right = exact_dot(pairs, jnp.concatenate([real, imag], axis=1), ((1,), (0,)))
    half = MOMENTS * count
    left = jnp.concatenate([real[:, :half], imag[:, :half]], axis=1)
    joined = exact_dot(left.T, right, ((1,), (0,)))
    scale = 1.0 / (planes * ROWS * LANES)
    width = 2 * half
    real = (joined[:half, :width] + joined[half:, width:]) * scale
    imag = (joined[:half, width:] - joined[half:, :width]) * scale
    out_b[0] = real[:, :half]
    out_b[1] = imag[:, :half]
    out_a[0] = real[:, half:]
    out_a[1] = imag[:, half:]


def chip_groups(parts, points):
    groups = []
    for core in range(CORES):
        for base in range(points):
            groups.append(
                [
                    ((base ^ chip) if core == 0 else base) * parts + chip * CORES + core
                    for chip in range(parts // CORES)
                ]
            )
    return groups


def whole_grid(sources, potential, iter_counts, *, parts, points):
    count, depth, _ = sources.shape
    planes = parts * depth
    chips = parts // CORES
    copies = packed_block(sources, potential, iter_counts, chips)
    near = lax.all_to_all(
        copies, ("point", "dom"), 0, 0, axis_index_groups=chip_groups(parts, points), tiled=True
    )
    swap = [(part ^ 1, part) for part in range(parts)]
    blocks = [near, lax.ppermute(near, "dom", swap)]
    vmem = pl.BlockSpec(memory_space=pltpu.VMEM)
    size = BASIS * count
    width = MOMENTS * count
    out = jax.ShapeDtypeStruct((2, width, width), jnp.float32)
    vector = pltpu.VMEM((planes, count, ROWS * LANES), jnp.float32)
    return pl.pallas_call(
        functools.partial(solve_kernel, parts, points, count),
        out_shape=(out, out),
        in_specs=[vmem] * CORES,
        out_specs=(vmem, vmem),
        scratch_shapes=[vector] * (BASIS + 1)
        + [
            pltpu.VMEM((planes, ROWS, LANES), jnp.float32),
            pltpu.VMEM((size, 2 * size), jnp.float32),
            pltpu.VMEM((points, SUB, LANES), jnp.float32),
        ],
        compiler_params=pltpu.CompilerParams(vmem_limit_bytes=32 * 2**20),
        name="solve",
    )(*blocks)


def on_device(sources, potential, iter_counts):
    parts, points = lax.axis_size("dom"), lax.axis_size("point")
    count, depth, cells = sources.shape
    held = BASIS * count * parts * depth * cells * 4
    fits = (
        held <= 16 * 2**20
        and parts == 8
        and points == 4
        and count == 2 * SUB
        and 2 * MOMENTS * count == LANES
        and cells == GX * GX == ROWS * LANES
    )
    if not fits:
        return split_grid(sources, potential, iter_counts)
    return whole_grid(sources, potential, iter_counts, parts=parts, points=points)


def solution(mesh):
    placed = (P(None, "dom", None), P("dom", None), P("point"))
    return jax.shard_map(
        on_device, mesh=mesh, in_specs=placed, out_specs=(P(), P()), check_vma=False
    )
```

```python
import functools
import math

import jax
import jax.numpy as jnp
from jax import lax
from jax.experimental import pallas as pl
from jax.experimental.pallas import tpu as pltpu
from jax.sharding import PartitionSpec as P

MOMENTS = 4
ITERS = 6
GX = 32


COEF_NEAR = 4.0 / 3.0
COEF_FAR = -1.0 / 12.0
GAMMA = 2.0
RADIUS = 1.5


def padded_2(block, sides, width):
    for axis, dim in sides:
        count = lax.axis_size(axis)
        forward = [(i, i + 1) for i in range(count - 1)]
        forward.append((count - 1, 0))
        backward = [(target, source) for source, target in forward]
        low = lax.ppermute(
            lax.slice_in_dim(block, block.shape[dim] - width, None, axis=dim), axis, forward
        )
        high = lax.ppermute(lax.slice_in_dim(block, 0, width, axis=dim), axis, backward)
        block = jnp.concatenate([low, block, high], axis=dim)
    return block


def plane_terms(values, side):
    lead = values.shape[:-1]
    planes = values.reshape(lead + (side, side))
    summed = COEF_NEAR * (
        jnp.roll(planes, 1, -2)
        + jnp.roll(planes, -1, -2)
        + jnp.roll(planes, 1, -1)
        + jnp.roll(planes, -1, -1)
    )
    summed = summed + COEF_FAR * (
        jnp.roll(planes, 2, -2)
        + jnp.roll(planes, -2, -2)
        + jnp.roll(planes, 2, -1)
        + jnp.roll(planes, -2, -1)
    )
    return summed.reshape(values.shape)


def complex_mul(first, second):
    return jnp.stack(
        [first[0] * second[0] - first[1] * second[1], first[0] * second[1] + first[1] * second[0]]
    )


def complex_div(first, second):
    denom = second[0] * second[0] + second[1] * second[1]
    return jnp.stack(
        [
            (first[0] * second[0] + first[1] * second[1]) / denom,
            (first[1] * second[0] - first[0] * second[1]) / denom,
        ]
    )


def bilinear(first, second):
    real_part = jnp.sum(first[0] * second[0] - first[1] * second[1], axis=(1, 2))
    imag_part = jnp.sum(first[0] * second[1] + first[1] * second[0], axis=(1, 2))
    return jnp.stack([real_part, imag_part])


def scaled(coeffs, values):
    return complex_mul(coeffs[:, :, None, None], values)


def shifted(values, potential, shift_re, shift_im):
    padded = padded_2(values, (("dom", 2),), 2)
    depth = values.shape[2]
    lap = -7.5 * values + plane_terms(values, GX)
    lap = lap + COEF_NEAR * (padded[:, :, 3 : 3 + depth] + padded[:, :, 1 : 1 + depth])
    lap = lap + COEF_FAR * (padded[:, :, 4 : 4 + depth] + padded[:, :, 0:depth])
    applied = -0.5 * lap + potential * values
    return jnp.stack(
        [
            shift_re * values[0] - shift_im * values[1] - applied[0],
            shift_re * values[1] + shift_im * values[0] - applied[1],
        ]
    )


def residual_sum(values):
    return lax.psum(bilinear(values, values), "dom")


def moment_terms(solution, residual, sources, angle_now, shift_re, shift_im):
    applied = jnp.stack(
        [
            shift_re * solution[0] - shift_im * solution[1] - sources[0] + residual[0],
            shift_re * solution[1] + shift_im * solution[0] - sources[1] + residual[1],
        ]
    )
    angles = (jnp.arange(MOMENTS).astype(jnp.float32) + 1.0) * angle_now
    coeffs = 0.25 * jnp.stack([jnp.cos(angles), jnp.sin(angles)])
    s_terms = complex_mul(coeffs[:, :, None, None, None], solution[:, None])
    h_terms = complex_mul(coeffs[:, :, None, None, None], applied[:, None])
    width = MOMENTS * solution.shape[1]
    return (s_terms.reshape(2, width, -1), h_terms.reshape(2, width, -1))


def gram_of(left, right):
    width = left.shape[1]
    joined = lax.dot_general(
        left.reshape(2 * width, -1),
        right.reshape(2 * width, -1),
        (((1,), (1,)), ((), ())),
        precision=lax.Precision.HIGHEST,
        preferred_element_type=jnp.float32,
    )
    blocks = joined.reshape(2, width, 2, width)
    return jnp.stack([blocks[0, :, 0] + blocks[1, :, 1], blocks[0, :, 1] - blocks[1, :, 0]])


def split_grid(sources, potential, iter_counts):
    complex_src = jnp.stack([sources, jnp.zeros_like(sources)])
    angle_now = (
        2.0 * math.pi * (lax.axis_index("point").astype(jnp.float32) + 0.5) / lax.axis_size("point")
    )
    shift_re = GAMMA + RADIUS * jnp.cos(angle_now)
    shift_im = RADIUS * jnp.sin(angle_now)
    limit = iter_counts[0]
    solution = jnp.zeros_like(complex_src)

    def one_turn(turn_idx, state):
        solution, residual, search, norm_now = state
        product = shifted(search, potential, shift_re, shift_im)
        curve = lax.psum(bilinear(search, product), "dom")
        step_size = complex_div(norm_now, curve)
        new_residual = residual - scaled(step_size, product)
        norm_next = residual_sum(new_residual)
        fresh = (
            solution + scaled(step_size, search),
            new_residual,
            new_residual + scaled(complex_div(norm_next, norm_now), search),
            norm_next,
        )
        keep_mask = turn_idx < limit
        return jax.tree.map(lambda newer, older: jnp.where(keep_mask, newer, older), fresh, state)

    start = (solution, complex_src, complex_src, residual_sum(complex_src))
    solution, residual, search, norm_now = lax.fori_loop(0, ITERS, one_turn, start)
    s_terms, h_terms = moment_terms(solution, residual, complex_src, angle_now, shift_re, shift_im)
    cells = sources.shape[1] * sources.shape[2] * lax.axis_size("dom")
    s_total, h_total = lax.psum((s_terms, h_terms), "point")
    gram_b, gram_a = lax.psum((gram_of(s_total, s_total), gram_of(s_total, h_total)), "dom")
    return (gram_b / cells, gram_a / cells)


Y_IN, X_IN = 2, 4
Y_OUT, X_OUT = GX // Y_IN, GX // X_IN
ROWS = Y_IN * X_IN
LANES = Y_OUT * X_OUT
SUB = 8
BASIS = ITERS + 1
CORES = 2
TOGETHER = 4
H_SCALE = 2.0 / COEF_NEAR
FAR_SCALED = 0.5 * H_SCALE * COEF_FAR


def pack_kernel(depth, groups, counts, rows, levels, out, count_tile):
    columns = rows.shape[0] // (SUB * groups * depth)
    source = lax.broadcasted_iota(jnp.int32, (LANES, LANES), 0)
    target = lax.broadcasted_iota(jnp.int32, (LANES, LANES), 1)
    inner = target // (LANES // ROWS)
    outer = target % (LANES // ROWS)
    cell = (outer // X_OUT * Y_IN + inner // X_IN) * GX + outer % X_OUT * X_IN + inner % X_IN
    swap = jnp.where(source == cell, 1.0, 0.0).astype(jnp.float32)
    parts = []
    for deep in range(depth):
        for group in range(groups):
            for column in range(columns):
                start = (group * SUB * columns + column) * depth + deep
                parts.append(rows[pl.ds(start, SUB, stride=columns * depth), :])
        parts.append(levels[pl.ds(deep, columns, stride=depth), :])
    mixed = exact_dot(jnp.concatenate(parts, axis=0), swap, ((1,), (0,)))
    block = LANES // ROWS
    lane_block = lax.broadcasted_iota(jnp.int32, (SUB, LANES), 1) // block
    row = lax.broadcasted_iota(jnp.int32, (SUB, LANES), 0)
    for deep in range(depth):
        base = deep * (groups + 1) * columns * SUB - deep * (columns - 1) * SUB
        for group in range(groups):
            pieces = [
                mixed[base + (group * columns + column) * SUB :][:SUB] for column in range(columns)
            ]
            for m in range(ROWS):
                value = pieces[m]
                for column in range(columns):
                    if column != m:
                        moved = pltpu.roll(pieces[column], (column - m) * block % LANES, 1)
                        value = jnp.where(lane_block == column, moved, value)
                start = ((deep * ROWS + m) * groups + group) * SUB
                out[0, start : start + SUB, :] = value
        piece = mixed[base + groups * columns * SUB :][:SUB]
        value = piece
        for far in range(1, columns):
            moved = pltpu.roll(pltpu.roll(piece, far * block, 1), columns - far, 0)
            value = jnp.where(lane_block == (row + far) % columns, moved, value)
        start = depth * ROWS * SUB * groups + deep * ROWS
        out[0, start : start + ROWS, :] = value
    count_tile[...] = jnp.full((SUB, LANES), counts[0].astype(jnp.float32))
    for copy in range(1, out.shape[0]):
        out[copy] = out[0]


def packed_block(sources, potential, iter_counts, copies):
    count, depth, cells = sources.shape
    columns = cells // LANES
    rows = sources.reshape(count, depth, columns, LANES).transpose(0, 2, 1, 3)
    levels = potential.reshape(depth, columns, LANES).transpose(1, 0, 2)
    vmem = pl.BlockSpec(memory_space=pltpu.VMEM)
    smem = pl.BlockSpec(memory_space=pltpu.SMEM)
    size = depth * ROWS * (count + 1)
    return pl.pallas_call(
        functools.partial(pack_kernel, depth, count // SUB),
        out_shape=(
            jax.ShapeDtypeStruct((copies, size, LANES), jnp.float32),
            jax.ShapeDtypeStruct((SUB, LANES), jnp.float32),
        ),
        in_specs=[smem, vmem, vmem],
        out_specs=(vmem, vmem),
        compiler_params=pltpu.CompilerParams(vmem_limit_bytes=4 * 2**20),
        name="pack",
    )(iter_counts, rows.reshape(-1, LANES), levels.reshape(-1, LANES))


def lane_sum(values):
    return jnp.broadcast_to(jnp.sum(values, axis=1, keepdims=True), values.shape)


def ratio(top, bottom):
    return jnp.where(bottom > 0.0, top / jnp.where(bottom > 0.0, bottom, 1.0), 0.0)


def x_next(values, wrap_mask):
    return jnp.where(wrap_mask, pltpu.roll(values, X_OUT - 1, 1), pltpu.roll(values, LANES - 1, 1))


def x_prev(values, wrap_mask):
    return jnp.where(wrap_mask, pltpu.roll(values, LANES - X_OUT + 1, 1), pltpu.roll(values, 1, 1))


def apply_planes(vector, diagonal, first, count, group, last_x, first_x):
    planes = vector.shape[0]
    rows = pl.ds(group * SUB, SUB)
    held = {}
    for far in range(-2, count + 2):
        index = jnp.bitwise_and(first + (far + planes), planes - 1)
        held[far] = [vector[index, rows, pl.ds(m * LANES, LANES)] for m in range(ROWS)]
    for plane in range(count):
        here, above, below = held[plane], held[plane + 1], held[plane - 1]
        above_2, below_2 = held[plane + 2], held[plane - 2]
        y_up = [pltpu.roll(value, LANES - X_OUT, 1) for value in here]
        y_down = [pltpu.roll(value, X_OUT, 1) for value in here]
        out = []
        for yi in range(Y_IN):
            line = here[yi * X_IN : (yi + 1) * X_IN]
            before = [x_prev(line[X_IN - 2], first_x), x_prev(line[X_IN - 1], first_x)]
            after = [x_next(line[0], last_x), x_next(line[1], last_x)]
            wide = before + line + after
            for xi in range(X_IN):
                m = yi * X_IN + xi
                other = (1 - yi) * X_IN + xi
                y_next = here[other] if yi == 0 else y_up[other]
                y_prev = here[other] if yi == 1 else y_down[other]
                near = (wide[xi + 1] + wide[xi + 3]) + (y_next + y_prev) + (above[m] + below[m])
                far = (wide[xi] + wide[xi + 4]) + (y_up[m] + y_down[m])
                far = far + (above_2[m] + below_2[m])
                level = diagonal[first + plane, pl.ds(m, 1), :]
                out.append(level * here[m] - near - FAR_SCALED * far)
        yield here, out


def cmul(first, second):
    return (
        first[0] * second[0] - first[1] * second[1],
        first[0] * second[1] + first[1] * second[0],
    )


def moment_coeffs(point, points, count):
    lane = lax.broadcasted_iota(jnp.int32, (1, LANES), 1)
    moment = lax.rem(lane, MOMENTS * count) // count
    angle = 2.0 * math.pi * (point + 0.5) / points
    parts = []
    for func in (math.cos, math.sin):
        value = jnp.full((1, LANES), 0.25 * func(angle), jnp.float32)
        for k in range(1, MOMENTS):
            value = jnp.where(moment == k, 0.25 * func((k + 1) * angle), value)
        parts.append(value)
    return parts


def weights_of(alphas, norms, limits, count):
    points = len(limits)
    shape = (count, LANES)
    half = MOMENTS * count
    lane = lax.broadcasted_iota(jnp.int32, shape, 1)
    source = lax.broadcasted_iota(jnp.int32, shape, 0)
    own = lax.rem(lane, count) == source
    left_half = lane < half
    betas = [ratio(norms[i + 1], norms[i]) for i in range(ITERS - 1)]
    sums = [[jnp.zeros(shape, jnp.float32)] * 2 for _ in range(BASIS)]
    zero = jnp.zeros(shape, jnp.float32)
    one = jnp.ones(shape, jnp.float32)
    for point in range(points):
        angle = 2.0 * math.pi * (point + 0.5) / points
        shift = (GAMMA + RADIUS * math.cos(angle), RADIUS * math.sin(angle))
        scaled_shift = (H_SCALE * shift[0], H_SCALE * shift[1])
        limit = limits[point]
        product = (one, zero)
        products = [product]
        links = []
        pivot = (scaled_shift[0] - alphas[0], zero + scaled_shift[1])
        for i in range(ITERS):
            size = 1.0 / (pivot[0] * pivot[0] + pivot[1] * pivot[1])
            inverse = (pivot[0] * size, -pivot[1] * size)
            product = cmul(product, inverse)
            products.append(product)
            if i < ITERS - 1:
                link = (betas[i] * inverse[0], betas[i] * inverse[1])
                links.append(link)
                pivot = (scaled_shift[0] - alphas[i + 1] - link[0], scaled_shift[1] - link[1])
        solved = [None] * ITERS
        for i in reversed(range(ITERS)):
            value = (H_SCALE * products[i + 1][0], H_SCALE * products[i + 1][1])
            if i < ITERS - 1:
                step = cmul(links[i], solved[i + 1])
                value = (value[0] + step[0], value[1] + step[1])
            used = limit > i
            solved[i] = (jnp.where(used, value[0], 0.0), jnp.where(used, value[1], 0.0))
        applied = []
        for i in range(BASIS):
            left = limit == i
            rest = (
                jnp.where(left, products[i][0], 0.0),
                jnp.where(left, products[i][1], 0.0),
            )
            if i < ITERS:
                turned = (
                    shift[0] * solved[i][0] - shift[1] * solved[i][1],
                    shift[0] * solved[i][1] + shift[1] * solved[i][0],
                )
                rest = (rest[0] + turned[0], rest[1] + turned[1])
            if i == 0:
                rest = (rest[0] - 1.0, rest[1])
            applied.append(rest)
        tail = applied[ITERS]
        for back, factor in ((1, alphas[ITERS - 1]), (2, betas[ITERS - 2])):
            part = applied[ITERS - back]
            applied[ITERS - back] = (part[0] - factor * tail[0], part[1] - factor * tail[1])
        moment = moment_coeffs(point, points, count)
        for i in range(BASIS):
            left = solved[i] if i < ITERS else (zero, zero)
            both = (
                jnp.where(left_half, left[0], applied[i][0]),
                jnp.where(left_half, left[1], applied[i][1]),
            )
            term = cmul(moment, both)
            sums[i] = [sums[i][0] + term[0], sums[i][1] + term[1]]
    return [[jnp.where(own, part, 0.0) for part in pair] for pair in sums]


def exact_dot(first, second, dims):
    return lax.dot_general(
        first,
        second,
        (dims, ((), ())),
        precision=lax.Precision.HIGHEST,
        preferred_element_type=jnp.float32,
    )


def krylov_kernel(parts, count, mine, other, *refs):
    vectors, (scalars, applied, diagonal) = refs[:BASIS], refs[BASIS:]
    planes = diagonal.shape[0]
    depth = planes // parts
    groups = count // SUB
    lane = lax.broadcasted_iota(jnp.int32, (SUB, LANES), 1)
    last_x = lax.rem(lane, X_OUT) == X_OUT - 1
    first_x = lax.rem(lane, X_OUT) == 0
    core = jnp.bitwise_and(lax.axis_index("dom"), CORES - 1)

    for chip in range(parts // CORES):
        for block, side in ((mine, core), (other, 1 - core)):
            slab = (chip * CORES + side) * depth
            for deep in range(depth):
                for m in range(ROWS):
                    start = (deep * ROWS + m) * count
                    lanes = pl.ds(m * LANES, LANES)
                    vectors[0][slab + deep, :, lanes] = block[chip, start : start + count, :]
                start = depth * ROWS * count + deep * ROWS
                levels = block[chip, start : start + ROWS, :]
                diagonal[slab + deep] = H_SCALE * (levels + 3.75)

    blank = jnp.zeros((SUB, LANES), jnp.float32)
    alphas, norms = [], []
    for i in range(ITERS):
        source, target = vectors[i], applied if i < ITERS - 1 else vectors[ITERS]

        def apply_turn(turn, sums, i=i, source=source, target=target):
            first = turn * TOGETHER
            new_sums = []
            for group in range(groups):
                rows = pl.ds(group * SUB, SUB)
                curve, norm = sums[group]
                done = apply_planes(source, diagonal, first, TOGETHER, group, last_x, first_x)
                for plane, (value, out) in enumerate(done):
                    for m in range(ROWS):
                        target[first + plane, rows, pl.ds(m * LANES, LANES)] = out[m]
                        curve = curve + value[m] * out[m]
                        if i == 0:
                            norm = norm + value[m] * value[m]
                new_sums.append((curve, norm))
            return tuple(new_sums)

        sums = lax.fori_loop(0, planes // TOGETHER, apply_turn, ((blank, blank),) * groups)
        if i == 0:
            norms.append([lane_sum(norm) for _, norm in sums])
        alphas.append([ratio(lane_sum(sums[g][0]), norms[i][g]) for g in range(groups)])
        if i == ITERS - 1:
            break
        betas = [ratio(norms[i][g], norms[i - 1][g]) for g in range(groups)] if i else None

        def step_turn(plane, sums, i=i, alpha=alphas[i], betas=betas):
            new_sums = []
            for group in range(groups):
                rows = pl.ds(group * SUB, SUB)
                norm = sums[group]
                for m in range(ROWS):
                    lanes = pl.ds(m * LANES, LANES)
                    value = applied[plane, rows, lanes]
                    value = value - alpha[group] * vectors[i][plane, rows, lanes]
                    if i:
                        value = value - betas[group] * vectors[i - 1][plane, rows, lanes]
                    vectors[i + 1][plane, rows, lanes] = value
                    norm = norm + value * value
                new_sums.append(norm)
            return tuple(new_sums)

        sums = lax.fori_loop(0, planes, step_turn, (blank,) * groups, unroll=TOGETHER)
        norms.append([lane_sum(norm) for norm in sums])
    for i, value in enumerate(alphas + norms):
        scalars[i] = jnp.concatenate(value, axis=0)


def gram_kernel(points, scalars, *refs):
    tiles, vectors = refs[:points], refs[points : points + BASIS]
    out_b, out_a, gram, limits = refs[points + BASIS :]
    planes, count, _ = vectors[0].shape
    groups = count // SUB
    size = BASIS * count
    gram[...] = jnp.zeros_like(gram)

    def gram_turn(plane, carry):
        values = jnp.concatenate([vector[plane] for vector in vectors], axis=0)
        high = values.astype(jnp.bfloat16)
        low = (values - high.astype(jnp.float32)).astype(jnp.bfloat16)
        gram[...] += lax.dot_general(
            high,
            jnp.concatenate([high, low], axis=0),
            (((1,), (1,)), ((), ())),
            preferred_element_type=jnp.float32,
        )
        return carry

    lax.fori_loop(0, planes, gram_turn, 0, unroll=TOGETHER)
    cross = gram[:, size:]
    pairs = gram[:, :size] + cross + cross.T

    here = lax.axis_index("point")
    for far, tile in enumerate(tiles):
        limits[jnp.bitwise_xor(here, far)] = tile[...]
    bounds = [jnp.concatenate([limits[j]] * groups, axis=0) for j in range(points)]
    alphas = [scalars[i] for i in range(ITERS)]
    norms = [scalars[ITERS + i] for i in range(ITERS)]
    weights = weights_of(alphas, norms, bounds, count)
    real = jnp.concatenate([pair[0] for pair in weights], axis=0)
    imag = jnp.concatenate([pair[1] for pair in weights], axis=0)
    right = exact_dot(pairs, jnp.concatenate([real, imag], axis=1), ((1,), (0,)))
    half = MOMENTS * count
    left = jnp.concatenate([real[:, :half], imag[:, :half]], axis=1)
    joined = exact_dot(left.T, right, ((1,), (0,)))
    scale = 1.0 / (planes * ROWS * LANES)
    width = 2 * half
    real = (joined[:half, :width] + joined[half:, width:]) * scale
    imag = (joined[:half, width:] - joined[half:, :width]) * scale
    out_b[0] = real[:, :half]
    out_b[1] = imag[:, :half]
    out_a[0] = real[:, half:]
    out_a[1] = imag[:, half:]


def whole_grid(sources, potential, iter_counts, *, parts, points):
    count, depth, _ = sources.shape
    planes = parts * depth
    chips = parts // CORES
    copies, tile = packed_block(sources, potential, iter_counts, chips)
    same_core = [list(range(core, parts, CORES)) for core in range(CORES)]
    mine = lax.all_to_all(copies, "dom", 0, 0, axis_index_groups=same_core, tiled=True)
    other = lax.ppermute(mine, "dom", [(part ^ 1, part) for part in range(parts)])
    tiles = [tile] + [
        lax.ppermute(tile, "point", [(point ^ far, point) for point in range(points)])
        for far in range(1, points)
    ]
    vmem = pl.BlockSpec(memory_space=pltpu.VMEM)
    vector = (planes, count, ROWS * LANES)
    cells = planes * ROWS * LANES
    *vectors, scalars = pl.pallas_call(
        functools.partial(krylov_kernel, parts, count),
        out_shape=[jax.ShapeDtypeStruct(vector, jnp.float32)] * BASIS
        + [jax.ShapeDtypeStruct((2 * ITERS, count, LANES), jnp.float32)],
        in_specs=[vmem] * CORES,
        out_specs=[vmem] * (BASIS + 1),
        scratch_shapes=[
            pltpu.VMEM(vector, jnp.float32),
            pltpu.VMEM((planes, ROWS, LANES), jnp.float32),
        ],
        compiler_params=pltpu.CompilerParams(vmem_limit_bytes=16 * 2**20),
        cost_estimate=pl.CostEstimate(
            flops=ITERS * count * cells * 30, bytes_accessed=32 * 2**20, transcendentals=0
        ),
        name="krylov",
    )(mine, other)
    size = BASIS * count
    width = MOMENTS * count
    out = jax.ShapeDtypeStruct((2, width, width), jnp.float32)
    return pl.pallas_call(
        functools.partial(gram_kernel, points),
        out_shape=(out, out),
        in_specs=[vmem] * (1 + points + BASIS),
        out_specs=(vmem, vmem),
        scratch_shapes=[
            pltpu.VMEM((size, 2 * size), jnp.float32),
            pltpu.VMEM((points, SUB, LANES), jnp.float32),
        ],
        compiler_params=pltpu.CompilerParams(vmem_limit_bytes=16 * 2**20),
        name="gram",
    )(scalars, *tiles, *vectors)


def on_device(sources, potential, iter_counts):
    parts, points = lax.axis_size("dom"), lax.axis_size("point")
    count, depth, cells = sources.shape
    held = BASIS * count * parts * depth * cells * 4
    fits = (
        held <= 16 * 2**20
        and parts == 8
        and points == 4
        and count == 2 * SUB
        and 2 * MOMENTS * count == LANES
        and parts * depth == 16
        and cells == GX * GX == ROWS * LANES
    )
    if not fits:
        return split_grid(sources, potential, iter_counts)
    return whole_grid(sources, potential, iter_counts, parts=parts, points=points)


def solution(mesh):
    placed = (P(None, "dom", None), P("dom", None), P("point"))
    return jax.shard_map(
        on_device, mesh=mesh, in_specs=placed, out_specs=(P(), P()), check_vma=False
    )
```

```python
import functools
import math

import jax
import jax.numpy as jnp
from jax import lax
from jax.experimental import pallas as pl
from jax.experimental.pallas import tpu as pltpu
from jax.sharding import PartitionSpec as P

MOMENTS = 4
ITERS = 6
GX = 32


COEF_NEAR = 4.0 / 3.0
COEF_FAR = -1.0 / 12.0
GAMMA = 2.0
RADIUS = 1.5


def padded_2(block, sides, width):
    for axis, dim in sides:
        count = lax.axis_size(axis)
        forward = [(i, i + 1) for i in range(count - 1)]
        forward.append((count - 1, 0))
        backward = [(target, source) for source, target in forward]
        low = lax.ppermute(
            lax.slice_in_dim(block, block.shape[dim] - width, None, axis=dim), axis, forward
        )
        high = lax.ppermute(lax.slice_in_dim(block, 0, width, axis=dim), axis, backward)
        block = jnp.concatenate([low, block, high], axis=dim)
    return block


def plane_terms(values, side):
    lead = values.shape[:-1]
    planes = values.reshape(lead + (side, side))
    summed = COEF_NEAR * (
        jnp.roll(planes, 1, -2)
        + jnp.roll(planes, -1, -2)
        + jnp.roll(planes, 1, -1)
        + jnp.roll(planes, -1, -1)
    )
    summed = summed + COEF_FAR * (
        jnp.roll(planes, 2, -2)
        + jnp.roll(planes, -2, -2)
        + jnp.roll(planes, 2, -1)
        + jnp.roll(planes, -2, -1)
    )
    return summed.reshape(values.shape)


def complex_mul(first, second):
    return jnp.stack(
        [first[0] * second[0] - first[1] * second[1], first[0] * second[1] + first[1] * second[0]]
    )


def complex_div(first, second):
    denom = second[0] * second[0] + second[1] * second[1]
    return jnp.stack(
        [
            (first[0] * second[0] + first[1] * second[1]) / denom,
            (first[1] * second[0] - first[0] * second[1]) / denom,
        ]
    )


def bilinear(first, second):
    real_part = jnp.sum(first[0] * second[0] - first[1] * second[1], axis=(1, 2))
    imag_part = jnp.sum(first[0] * second[1] + first[1] * second[0], axis=(1, 2))
    return jnp.stack([real_part, imag_part])


def scaled(coeffs, values):
    return complex_mul(coeffs[:, :, None, None], values)


def shifted(values, potential, shift_re, shift_im):
    padded = padded_2(values, (("dom", 2),), 2)
    depth = values.shape[2]
    lap = -7.5 * values + plane_terms(values, GX)
    lap = lap + COEF_NEAR * (padded[:, :, 3 : 3 + depth] + padded[:, :, 1 : 1 + depth])
    lap = lap + COEF_FAR * (padded[:, :, 4 : 4 + depth] + padded[:, :, 0:depth])
    applied = -0.5 * lap + potential * values
    return jnp.stack(
        [
            shift_re * values[0] - shift_im * values[1] - applied[0],
            shift_re * values[1] + shift_im * values[0] - applied[1],
        ]
    )


def residual_sum(values):
    return lax.psum(bilinear(values, values), "dom")


def moment_terms(solution, residual, sources, angle_now, shift_re, shift_im):
    applied = jnp.stack(
        [
            shift_re * solution[0] - shift_im * solution[1] - sources[0] + residual[0],
            shift_re * solution[1] + shift_im * solution[0] - sources[1] + residual[1],
        ]
    )
    angles = (jnp.arange(MOMENTS).astype(jnp.float32) + 1.0) * angle_now
    coeffs = 0.25 * jnp.stack([jnp.cos(angles), jnp.sin(angles)])
    s_terms = complex_mul(coeffs[:, :, None, None, None], solution[:, None])
    h_terms = complex_mul(coeffs[:, :, None, None, None], applied[:, None])
    width = MOMENTS * solution.shape[1]
    return (s_terms.reshape(2, width, -1), h_terms.reshape(2, width, -1))


def gram_of(left, right):
    width = left.shape[1]
    joined = lax.dot_general(
        left.reshape(2 * width, -1),
        right.reshape(2 * width, -1),
        (((1,), (1,)), ((), ())),
        precision=lax.Precision.HIGHEST,
        preferred_element_type=jnp.float32,
    )
    blocks = joined.reshape(2, width, 2, width)
    return jnp.stack([blocks[0, :, 0] + blocks[1, :, 1], blocks[0, :, 1] - blocks[1, :, 0]])


def split_grid(sources, potential, iter_counts):
    complex_src = jnp.stack([sources, jnp.zeros_like(sources)])
    angle_now = (
        2.0 * math.pi * (lax.axis_index("point").astype(jnp.float32) + 0.5) / lax.axis_size("point")
    )
    shift_re = GAMMA + RADIUS * jnp.cos(angle_now)
    shift_im = RADIUS * jnp.sin(angle_now)
    limit = iter_counts[0]
    solution = jnp.zeros_like(complex_src)

    def one_turn(turn_idx, state):
        solution, residual, search, norm_now = state
        product = shifted(search, potential, shift_re, shift_im)
        curve = lax.psum(bilinear(search, product), "dom")
        step_size = complex_div(norm_now, curve)
        new_residual = residual - scaled(step_size, product)
        norm_next = residual_sum(new_residual)
        fresh = (
            solution + scaled(step_size, search),
            new_residual,
            new_residual + scaled(complex_div(norm_next, norm_now), search),
            norm_next,
        )
        keep_mask = turn_idx < limit
        return jax.tree.map(lambda newer, older: jnp.where(keep_mask, newer, older), fresh, state)

    start = (solution, complex_src, complex_src, residual_sum(complex_src))
    solution, residual, search, norm_now = lax.fori_loop(0, ITERS, one_turn, start)
    s_terms, h_terms = moment_terms(solution, residual, complex_src, angle_now, shift_re, shift_im)
    cells = sources.shape[1] * sources.shape[2] * lax.axis_size("dom")
    s_total, h_total = lax.psum((s_terms, h_terms), "point")
    gram_b, gram_a = lax.psum((gram_of(s_total, s_total), gram_of(s_total, h_total)), "dom")
    return (gram_b / cells, gram_a / cells)


Y_IN, X_IN = 2, 4
Y_OUT, X_OUT = GX // Y_IN, GX // X_IN
ROWS = Y_IN * X_IN
LANES = Y_OUT * X_OUT
SUB = 8
BASIS = ITERS + 1
CORES = 2
TOGETHER = 4
H_SCALE = 2.0 / COEF_NEAR
FAR_SCALED = 0.5 * H_SCALE * COEF_FAR


def pack_kernel(depth, groups, rows, out):
    columns = rows.shape[0] // (SUB * groups * depth + depth)
    first_level = columns * SUB * groups * depth
    source = lax.broadcasted_iota(jnp.int32, (LANES, LANES), 0)
    target = lax.broadcasted_iota(jnp.int32, (LANES, LANES), 1)
    inner = target // (LANES // ROWS)
    outer = target % (LANES // ROWS)
    cell = (outer // X_OUT * Y_IN + inner // X_IN) * GX + outer % X_OUT * X_IN + inner % X_IN
    swap = jnp.where(source == cell, 1.0, 0.0).astype(jnp.float32)
    parts = []
    for deep in range(depth):
        for group in range(groups):
            for column in range(columns):
                start = (group * SUB * columns + column) * depth + deep
                parts.append(rows[pl.ds(start, SUB, stride=columns * depth), :])
        parts.append(rows[pl.ds(first_level + deep, columns, stride=depth), :])
    mixed = exact_dot(jnp.concatenate(parts, axis=0), swap, ((1,), (0,)))
    block = LANES // ROWS
    lane_block = lax.broadcasted_iota(jnp.int32, (SUB, LANES), 1) // block
    row = lax.broadcasted_iota(jnp.int32, (SUB, LANES), 0)
    for deep in range(depth):
        base = deep * (groups + 1) * columns * SUB - deep * (columns - 1) * SUB
        for group in range(groups):
            pieces = [
                mixed[base + (group * columns + column) * SUB :][:SUB] for column in range(columns)
            ]
            for m in range(ROWS):
                value = pieces[m]
                for column in range(columns):
                    if column != m:
                        moved = pltpu.roll(pieces[column], (column - m) * block % LANES, 1)
                        value = jnp.where(lane_block == column, moved, value)
                start = ((deep * ROWS + m) * groups + group) * SUB
                out[start : start + SUB, :] = value
        piece = mixed[base + groups * columns * SUB :][:SUB]
        value = piece
        for far in range(1, columns):
            moved = pltpu.roll(pltpu.roll(piece, far * block, 1), columns - far, 0)
            value = jnp.where(lane_block == (row + far) % columns, moved, value)
        start = depth * ROWS * SUB * groups + deep * ROWS
        out[start : start + ROWS, :] = value


def packed_block(sources, potential):
    count, depth, cells = sources.shape
    columns = cells // LANES
    rows = sources.reshape(count, depth, columns, LANES).transpose(0, 2, 1, 3).reshape(-1, LANES)
    levels = potential.reshape(depth, columns, LANES).transpose(1, 0, 2).reshape(-1, LANES)
    vmem = pl.BlockSpec(memory_space=pltpu.VMEM)
    size = depth * ROWS * (count + 1)
    return pl.pallas_call(
        functools.partial(pack_kernel, depth, count // SUB),
        out_shape=jax.ShapeDtypeStruct((size, LANES), jnp.float32),
        in_specs=[vmem],
        out_specs=vmem,
        compiler_params=pltpu.CompilerParams(vmem_limit_bytes=4 * 2**20),
        name="pack",
    )(jnp.concatenate([rows, levels], axis=0))


def lane_sum(values):
    return jnp.broadcast_to(jnp.sum(values, axis=1, keepdims=True), values.shape)


def ratio(top, bottom):
    return jnp.where(bottom > 0.0, top / jnp.where(bottom > 0.0, bottom, 1.0), 0.0)


def x_next(values, wrap_mask):
    return jnp.where(wrap_mask, pltpu.roll(values, X_OUT - 1, 1), pltpu.roll(values, LANES - 1, 1))


def x_prev(values, wrap_mask):
    return jnp.where(wrap_mask, pltpu.roll(values, LANES - X_OUT + 1, 1), pltpu.roll(values, 1, 1))


def apply_planes(vector, diagonal, first, count, group, last_x, first_x):
    planes = vector.shape[0]
    rows = pl.ds(group * SUB, SUB)
    held = {}
    for far in range(-2, count + 2):
        index = jnp.bitwise_and(first + (far + planes), planes - 1)
        held[far] = [vector[index, rows, pl.ds(m * LANES, LANES)] for m in range(ROWS)]
    for plane in range(count):
        here, above, below = held[plane], held[plane + 1], held[plane - 1]
        above_2, below_2 = held[plane + 2], held[plane - 2]
        y_up = [pltpu.roll(value, LANES - X_OUT, 1) for value in here]
        y_down = [pltpu.roll(value, X_OUT, 1) for value in here]
        out = []
        for yi in range(Y_IN):
            line = here[yi * X_IN : (yi + 1) * X_IN]
            before = [x_prev(line[X_IN - 2], first_x), x_prev(line[X_IN - 1], first_x)]
            after = [x_next(line[0], last_x), x_next(line[1], last_x)]
            wide = before + line + after
            for xi in range(X_IN):
                m = yi * X_IN + xi
                other = (1 - yi) * X_IN + xi
                y_next = here[other] if yi == 0 else y_up[other]
                y_prev = here[other] if yi == 1 else y_down[other]
                near = (wide[xi + 1] + wide[xi + 3]) + (y_next + y_prev) + (above[m] + below[m])
                far = (wide[xi] + wide[xi + 4]) + (y_up[m] + y_down[m])
                far = far + (above_2[m] + below_2[m])
                level = diagonal[first + plane, pl.ds(m, 1), :]
                out.append(level * here[m] - near - FAR_SCALED * far)
        yield here, out


def cmul(first, second):
    return (
        first[0] * second[0] - first[1] * second[1],
        first[0] * second[1] + first[1] * second[0],
    )


def moment_coeffs(point, points, count):
    lane = lax.broadcasted_iota(jnp.int32, (1, LANES), 1)
    moment = lax.rem(lane, MOMENTS * count) // count
    angle = 2.0 * math.pi * (point + 0.5) / points
    parts = []
    for func in (math.cos, math.sin):
        value = jnp.full((1, LANES), 0.25 * func(angle), jnp.float32)
        for k in range(1, MOMENTS):
            value = jnp.where(moment == k, 0.25 * func((k + 1) * angle), value)
        parts.append(value)
    return parts


def weights_of(alphas, norms, limits, count):
    points = len(limits)
    shape = (count, LANES)
    half = MOMENTS * count
    lane = lax.broadcasted_iota(jnp.int32, shape, 1)
    source = lax.broadcasted_iota(jnp.int32, shape, 0)
    own = lax.rem(lane, count) == source
    left_half = lane < half
    betas = [ratio(norms[i + 1], norms[i]) for i in range(ITERS - 1)]
    sums = [[jnp.zeros(shape, jnp.float32)] * 2 for _ in range(BASIS)]
    zero = jnp.zeros(shape, jnp.float32)
    one = jnp.ones(shape, jnp.float32)
    for point in range(points):
        angle = 2.0 * math.pi * (point + 0.5) / points
        shift = (GAMMA + RADIUS * math.cos(angle), RADIUS * math.sin(angle))
        scaled_shift = (H_SCALE * shift[0], H_SCALE * shift[1])
        limit = limits[point]
        product = (one, zero)
        products = [product]
        links = []
        pivot = (scaled_shift[0] - alphas[0], zero + scaled_shift[1])
        for i in range(ITERS):
            size = 1.0 / (pivot[0] * pivot[0] + pivot[1] * pivot[1])
            inverse = (pivot[0] * size, -pivot[1] * size)
            product = cmul(product, inverse)
            products.append(product)
            if i < ITERS - 1:
                link = (betas[i] * inverse[0], betas[i] * inverse[1])
                links.append(link)
                pivot = (scaled_shift[0] - alphas[i + 1] - link[0], scaled_shift[1] - link[1])
        solved = [None] * ITERS
        for i in reversed(range(ITERS)):
            value = (H_SCALE * products[i + 1][0], H_SCALE * products[i + 1][1])
            if i < ITERS - 1:
                step = cmul(links[i], solved[i + 1])
                value = (value[0] + step[0], value[1] + step[1])
            used = limit > i
            solved[i] = (jnp.where(used, value[0], 0.0), jnp.where(used, value[1], 0.0))
        applied = []
        for i in range(BASIS):
            left = limit == i
            rest = (
                jnp.where(left, products[i][0], 0.0),
                jnp.where(left, products[i][1], 0.0),
            )
            if i < ITERS:
                turned = (
                    shift[0] * solved[i][0] - shift[1] * solved[i][1],
                    shift[0] * solved[i][1] + shift[1] * solved[i][0],
                )
                rest = (rest[0] + turned[0], rest[1] + turned[1])
            if i == 0:
                rest = (rest[0] - 1.0, rest[1])
            applied.append(rest)
        tail = applied[ITERS]
        for back, factor in ((1, alphas[ITERS - 1]), (2, betas[ITERS - 2])):
            part = applied[ITERS - back]
            applied[ITERS - back] = (part[0] - factor * tail[0], part[1] - factor * tail[1])
        moment = moment_coeffs(point, points, count)
        for i in range(BASIS):
            left = solved[i] if i < ITERS else (zero, zero)
            both = (
                jnp.where(left_half, left[0], applied[i][0]),
                jnp.where(left_half, left[1], applied[i][1]),
            )
            term = cmul(moment, both)
            sums[i] = [sums[i][0] + term[0], sums[i][1] + term[1]]
    return [[jnp.where(own, part, 0.0) for part in pair] for pair in sums]


def exact_dot(first, second, dims):
    return lax.dot_general(
        first,
        second,
        (dims, ((), ())),
        precision=lax.Precision.HIGHEST,
        preferred_element_type=jnp.float32,
    )


def krylov_kernel(parts, count, *refs):
    blocks, vectors = refs[:parts], refs[parts : parts + BASIS]
    scalars, applied, diagonal = refs[parts + BASIS :]
    planes = diagonal.shape[0]
    depth = planes // parts
    groups = count // SUB
    lane = lax.broadcasted_iota(jnp.int32, (SUB, LANES), 1)
    last_x = lax.rem(lane, X_OUT) == X_OUT - 1
    first_x = lax.rem(lane, X_OUT) == 0
    here = lax.axis_index("dom")
    for turn in range(parts):
        slab = jnp.bitwise_xor(here, turn) * depth
        for deep in range(depth):
            for m in range(ROWS):
                start = (deep * ROWS + m) * count
                lanes = pl.ds(m * LANES, LANES)
                vectors[0][slab + deep, :, lanes] = blocks[turn][start : start + count, :]
            start = depth * ROWS * count + deep * ROWS
            levels = blocks[turn][start : start + ROWS, :]
            diagonal[slab + deep] = H_SCALE * (levels + 3.75)

    blank = jnp.zeros((SUB, LANES), jnp.float32)
    alphas, norms = [], []
    for i in range(ITERS):
        source, target = vectors[i], applied if i < ITERS - 1 else vectors[ITERS]

        def apply_turn(turn, sums, i=i, source=source, target=target):
            first = turn * TOGETHER
            new_sums = []
            for group in range(groups):
                rows = pl.ds(group * SUB, SUB)
                curve, norm = sums[group]
                done = apply_planes(source, diagonal, first, TOGETHER, group, last_x, first_x)
                for plane, (value, out) in enumerate(done):
                    for m in range(ROWS):
                        target[first + plane, rows, pl.ds(m * LANES, LANES)] = out[m]
                        curve = curve + value[m] * out[m]
                        if i == 0:
                            norm = norm + value[m] * value[m]
                new_sums.append((curve, norm))
            return tuple(new_sums)

        sums = lax.fori_loop(0, planes // TOGETHER, apply_turn, ((blank, blank),) * groups)
        if i == 0:
            norms.append([lane_sum(norm) for _, norm in sums])
        alphas.append([ratio(lane_sum(sums[g][0]), norms[i][g]) for g in range(groups)])
        if i == ITERS - 1:
            break
        betas = [ratio(norms[i][g], norms[i - 1][g]) for g in range(groups)] if i else None

        def step_turn(plane, sums, i=i, alpha=alphas[i], betas=betas):
            new_sums = []
            for group in range(groups):
                rows = pl.ds(group * SUB, SUB)
                norm = sums[group]
                for m in range(ROWS):
                    lanes = pl.ds(m * LANES, LANES)
                    value = applied[plane, rows, lanes]
                    value = value - alpha[group] * vectors[i][plane, rows, lanes]
                    if i:
                        value = value - betas[group] * vectors[i - 1][plane, rows, lanes]
                    vectors[i + 1][plane, rows, lanes] = value
                    norm = norm + value * value
                new_sums.append(norm)
            return tuple(new_sums)

        sums = lax.fori_loop(0, planes, step_turn, (blank,) * groups, unroll=TOGETHER)
        norms.append([lane_sum(norm) for norm in sums])
    for i, value in enumerate(alphas + norms):
        scalars[i] = jnp.concatenate(value, axis=0)


def gram_kernel(points, limits, scalars, *refs):
    vectors, (out_b, out_a, gram) = refs[:BASIS], refs[BASIS:]
    planes, count, _ = vectors[0].shape
    groups = count // SUB
    size = BASIS * count
    gram[...] = jnp.zeros_like(gram)

    def gram_turn(plane, carry):
        values = jnp.concatenate([vector[plane] for vector in vectors], axis=0)
        high = values.astype(jnp.bfloat16)
        low = (values - high.astype(jnp.float32)).astype(jnp.bfloat16)
        gram[...] += lax.dot_general(
            high,
            jnp.concatenate([high, low], axis=0),
            (((1,), (1,)), ((), ())),
            preferred_element_type=jnp.float32,
        )
        return carry

    lax.fori_loop(0, planes, gram_turn, 0, unroll=TOGETHER)
    cross = gram[:, size:]
    pairs = gram[:, :size] + cross + cross.T

    bounds = [jnp.concatenate([limits[j]] * groups, axis=0) for j in range(points)]
    alphas = [scalars[i] for i in range(ITERS)]
    norms = [scalars[ITERS + i] for i in range(ITERS)]
    weights = weights_of(alphas, norms, bounds, count)
    real = jnp.concatenate([pair[0] for pair in weights], axis=0)
    imag = jnp.concatenate([pair[1] for pair in weights], axis=0)
    right = exact_dot(pairs, jnp.concatenate([real, imag], axis=1), ((1,), (0,)))
    half = MOMENTS * count
    left = jnp.concatenate([real[:, :half], imag[:, :half]], axis=1)
    joined = exact_dot(left.T, right, ((1,), (0,)))
    scale = 1.0 / (planes * ROWS * LANES)
    width = 2 * half
    real = (joined[:half, :width] + joined[half:, width:]) * scale
    imag = (joined[:half, width:] - joined[half:, :width]) * scale
    out_b[0] = real[:, :half]
    out_b[1] = imag[:, :half]
    out_a[0] = real[:, half:]
    out_a[1] = imag[:, half:]


def swapped(values, parts, mask):
    return lax.ppermute(values, "dom", [(part ^ mask, part) for part in range(parts)])


def whole_grid(sources, potential, iter_counts, *, parts, points):
    count, depth, _ = sources.shape
    planes = parts * depth
    tile = jnp.broadcast_to(iter_counts.astype(jnp.float32), (SUB, LANES))
    limits = lax.all_gather(lax.optimization_barrier(tile), "point")
    block = packed_block(sources, potential)
    even = [block] + [swapped(block, parts, mask) for mask in range(CORES, parts, CORES)]
    odd = [swapped(value, parts, 1) for value in even]
    blocks = [value for pair in zip(even, odd) for value in pair]
    vmem = pl.BlockSpec(memory_space=pltpu.VMEM)
    vector = (planes, count, ROWS * LANES)
    cells = planes * ROWS * LANES
    *vectors, scalars = pl.pallas_call(
        functools.partial(krylov_kernel, parts, count),
        out_shape=[jax.ShapeDtypeStruct(vector, jnp.float32)] * BASIS
        + [jax.ShapeDtypeStruct((2 * ITERS, count, LANES), jnp.float32)],
        in_specs=[vmem] * parts,
        out_specs=[vmem] * (BASIS + 1),
        scratch_shapes=[
            pltpu.VMEM(vector, jnp.float32),
            pltpu.VMEM((planes, ROWS, LANES), jnp.float32),
        ],
        compiler_params=pltpu.CompilerParams(vmem_limit_bytes=16 * 2**20),
        cost_estimate=pl.CostEstimate(
            flops=ITERS * count * cells * 30, bytes_accessed=32 * 2**20, transcendentals=0
        ),
        name="krylov",
    )(*blocks)
    size = BASIS * count
    width = MOMENTS * count
    out = jax.ShapeDtypeStruct((2, width, width), jnp.float32)
    return pl.pallas_call(
        functools.partial(gram_kernel, points),
        out_shape=(out, out),
        in_specs=[vmem] * (2 + BASIS),
        out_specs=(vmem, vmem),
        scratch_shapes=[pltpu.VMEM((size, 2 * size), jnp.float32)],
        compiler_params=pltpu.CompilerParams(vmem_limit_bytes=16 * 2**20),
        name="gram",
    )(limits, scalars, *vectors)


def on_device(sources, potential, iter_counts):
    parts, points = lax.axis_size("dom"), lax.axis_size("point")
    count, depth, cells = sources.shape
    held = BASIS * count * parts * depth * cells * 4
    fits = (
        held <= 16 * 2**20
        and parts == 8
        and points == 4
        and count == 2 * SUB
        and 2 * MOMENTS * count == LANES
        and parts * depth == 16
        and cells == GX * GX == ROWS * LANES
    )
    if not fits:
        return split_grid(sources, potential, iter_counts)
    return whole_grid(sources, potential, iter_counts, parts=parts, points=points)


def solution(mesh):
    placed = (P(None, "dom", None), P("dom", None), P("point"))
    return jax.shard_map(
        on_device, mesh=mesh, in_specs=placed, out_specs=(P(), P()), check_vma=False
    )
```

```python
import functools
import math

import jax
import jax.numpy as jnp
from jax import lax
from jax.experimental import pallas as pl
from jax.experimental.pallas import tpu as pltpu
from jax.sharding import PartitionSpec as P

MOMENTS = 4
ITERS = 6
GX = 32


COEF_NEAR = 4.0 / 3.0
COEF_FAR = -1.0 / 12.0
GAMMA = 2.0
RADIUS = 1.5


def padded_2(block, sides, width):
    for axis, dim in sides:
        count = lax.axis_size(axis)
        forward = [(i, i + 1) for i in range(count - 1)]
        forward.append((count - 1, 0))
        backward = [(target, source) for source, target in forward]
        low = lax.ppermute(
            lax.slice_in_dim(block, block.shape[dim] - width, None, axis=dim), axis, forward
        )
        high = lax.ppermute(lax.slice_in_dim(block, 0, width, axis=dim), axis, backward)
        block = jnp.concatenate([low, block, high], axis=dim)
    return block


def plane_terms(values, side):
    lead = values.shape[:-1]
    planes = values.reshape(lead + (side, side))
    summed = COEF_NEAR * (
        jnp.roll(planes, 1, -2)
        + jnp.roll(planes, -1, -2)
        + jnp.roll(planes, 1, -1)
        + jnp.roll(planes, -1, -1)
    )
    summed = summed + COEF_FAR * (
        jnp.roll(planes, 2, -2)
        + jnp.roll(planes, -2, -2)
        + jnp.roll(planes, 2, -1)
        + jnp.roll(planes, -2, -1)
    )
    return summed.reshape(values.shape)


def complex_mul(first, second):
    return jnp.stack(
        [first[0] * second[0] - first[1] * second[1], first[0] * second[1] + first[1] * second[0]]
    )


def complex_div(first, second):
    denom = second[0] * second[0] + second[1] * second[1]
    return jnp.stack(
        [
            (first[0] * second[0] + first[1] * second[1]) / denom,
            (first[1] * second[0] - first[0] * second[1]) / denom,
        ]
    )


def bilinear(first, second):
    real_part = jnp.sum(first[0] * second[0] - first[1] * second[1], axis=(1, 2))
    imag_part = jnp.sum(first[0] * second[1] + first[1] * second[0], axis=(1, 2))
    return jnp.stack([real_part, imag_part])


def scaled(coeffs, values):
    return complex_mul(coeffs[:, :, None, None], values)


def shifted(values, potential, shift_re, shift_im):
    padded = padded_2(values, (("dom", 2),), 2)
    depth = values.shape[2]
    lap = -7.5 * values + plane_terms(values, GX)
    lap = lap + COEF_NEAR * (padded[:, :, 3 : 3 + depth] + padded[:, :, 1 : 1 + depth])
    lap = lap + COEF_FAR * (padded[:, :, 4 : 4 + depth] + padded[:, :, 0:depth])
    applied = -0.5 * lap + potential * values
    return jnp.stack(
        [
            shift_re * values[0] - shift_im * values[1] - applied[0],
            shift_re * values[1] + shift_im * values[0] - applied[1],
        ]
    )


def residual_sum(values):
    return lax.psum(bilinear(values, values), "dom")


def moment_terms(solution, residual, sources, angle_now, shift_re, shift_im):
    applied = jnp.stack(
        [
            shift_re * solution[0] - shift_im * solution[1] - sources[0] + residual[0],
            shift_re * solution[1] + shift_im * solution[0] - sources[1] + residual[1],
        ]
    )
    angles = (jnp.arange(MOMENTS).astype(jnp.float32) + 1.0) * angle_now
    coeffs = 0.25 * jnp.stack([jnp.cos(angles), jnp.sin(angles)])
    s_terms = complex_mul(coeffs[:, :, None, None, None], solution[:, None])
    h_terms = complex_mul(coeffs[:, :, None, None, None], applied[:, None])
    width = MOMENTS * solution.shape[1]
    return (s_terms.reshape(2, width, -1), h_terms.reshape(2, width, -1))


def gram_of(left, right):
    width = left.shape[1]
    joined = lax.dot_general(
        left.reshape(2 * width, -1),
        right.reshape(2 * width, -1),
        (((1,), (1,)), ((), ())),
        precision=lax.Precision.HIGHEST,
        preferred_element_type=jnp.float32,
    )
    blocks = joined.reshape(2, width, 2, width)
    return jnp.stack([blocks[0, :, 0] + blocks[1, :, 1], blocks[0, :, 1] - blocks[1, :, 0]])


def split_grid(sources, potential, iter_counts):
    complex_src = jnp.stack([sources, jnp.zeros_like(sources)])
    angle_now = (
        2.0 * math.pi * (lax.axis_index("point").astype(jnp.float32) + 0.5) / lax.axis_size("point")
    )
    shift_re = GAMMA + RADIUS * jnp.cos(angle_now)
    shift_im = RADIUS * jnp.sin(angle_now)
    limit = iter_counts[0]
    solution = jnp.zeros_like(complex_src)

    def one_turn(turn_idx, state):
        solution, residual, search, norm_now = state
        product = shifted(search, potential, shift_re, shift_im)
        curve = lax.psum(bilinear(search, product), "dom")
        step_size = complex_div(norm_now, curve)
        new_residual = residual - scaled(step_size, product)
        norm_next = residual_sum(new_residual)
        fresh = (
            solution + scaled(step_size, search),
            new_residual,
            new_residual + scaled(complex_div(norm_next, norm_now), search),
            norm_next,
        )
        keep_mask = turn_idx < limit
        return jax.tree.map(lambda newer, older: jnp.where(keep_mask, newer, older), fresh, state)

    start = (solution, complex_src, complex_src, residual_sum(complex_src))
    solution, residual, search, norm_now = lax.fori_loop(0, ITERS, one_turn, start)
    s_terms, h_terms = moment_terms(solution, residual, complex_src, angle_now, shift_re, shift_im)
    cells = sources.shape[1] * sources.shape[2] * lax.axis_size("dom")
    s_total, h_total = lax.psum((s_terms, h_terms), "point")
    gram_b, gram_a = lax.psum((gram_of(s_total, s_total), gram_of(s_total, h_total)), "dom")
    return (gram_b / cells, gram_a / cells)


Y_IN, X_IN = 2, 4
Y_OUT, X_OUT = GX // Y_IN, GX // X_IN
ROWS = Y_IN * X_IN
LANES = Y_OUT * X_OUT
SUB = 8
BASIS = ITERS + 1
CORES = 2
TOGETHER = 4
H_SCALE = 2.0 / COEF_NEAR
FAR_SCALED = 0.5 * H_SCALE * COEF_FAR


def pack_kernel(depth, groups, counts, rows, out, tile):
    columns = rows.shape[0] // (SUB * groups * depth + depth)
    first_level = columns * SUB * groups * depth
    source = lax.broadcasted_iota(jnp.int32, (LANES, LANES), 0)
    target = lax.broadcasted_iota(jnp.int32, (LANES, LANES), 1)
    inner = target // (LANES // ROWS)
    outer = target % (LANES // ROWS)
    cell = (outer // X_OUT * Y_IN + inner // X_IN) * GX + outer % X_OUT * X_IN + inner % X_IN
    swap = jnp.where(source == cell, 1.0, 0.0).astype(jnp.float32)
    parts = []
    for deep in range(depth):
        for group in range(groups):
            for column in range(columns):
                start = (group * SUB * columns + column) * depth + deep
                parts.append(rows[pl.ds(start, SUB, stride=columns * depth), :])
        parts.append(rows[pl.ds(first_level + deep, columns, stride=depth), :])
    mixed = exact_dot(jnp.concatenate(parts, axis=0), swap, ((1,), (0,)))
    block = LANES // ROWS
    lane_block = lax.broadcasted_iota(jnp.int32, (SUB, LANES), 1) // block
    row = lax.broadcasted_iota(jnp.int32, (SUB, LANES), 0)
    for deep in range(depth):
        base = deep * (groups + 1) * columns * SUB - deep * (columns - 1) * SUB
        for group in range(groups):
            pieces = [
                mixed[base + (group * columns + column) * SUB :][:SUB] for column in range(columns)
            ]
            for m in range(ROWS):
                value = pieces[m]
                for column in range(columns):
                    if column != m:
                        moved = pltpu.roll(pieces[column], (column - m) * block % LANES, 1)
                        value = jnp.where(lane_block == column, moved, value)
                start = ((deep * ROWS + m) * groups + group) * SUB
                out[start : start + SUB, :] = value
        piece = mixed[base + groups * columns * SUB :][:SUB]
        value = piece
        for far in range(1, columns):
            moved = pltpu.roll(pltpu.roll(piece, far * block, 1), columns - far, 0)
            value = jnp.where(lane_block == (row + far) % columns, moved, value)
        start = depth * ROWS * SUB * groups + deep * ROWS
        out[start : start + ROWS, :] = value
    tile[...] = jnp.broadcast_to(counts[...].astype(jnp.float32), (SUB, LANES))


def packed_block(sources, potential, iter_counts):
    count, depth, cells = sources.shape
    columns = cells // LANES
    rows = sources.reshape(count, depth, columns, LANES).transpose(0, 2, 1, 3).reshape(-1, LANES)
    levels = potential.reshape(depth, columns, LANES).transpose(1, 0, 2).reshape(-1, LANES)
    vmem = pl.BlockSpec(memory_space=pltpu.VMEM)
    size = depth * ROWS * (count + 1)
    return pl.pallas_call(
        functools.partial(pack_kernel, depth, count // SUB),
        out_shape=(
            jax.ShapeDtypeStruct((size, LANES), jnp.float32),
            jax.ShapeDtypeStruct((SUB, LANES), jnp.float32),
        ),
        in_specs=[vmem, vmem],
        out_specs=(vmem, vmem),
        compiler_params=pltpu.CompilerParams(vmem_limit_bytes=4 * 2**20),
        name="pack",
    )(iter_counts.reshape(1, 1), jnp.concatenate([rows, levels], axis=0))


def lane_sum(values):
    return jnp.broadcast_to(jnp.sum(values, axis=1, keepdims=True), values.shape)


def ratio(top, bottom):
    return jnp.where(bottom > 0.0, top / jnp.where(bottom > 0.0, bottom, 1.0), 0.0)


def x_next(values, wrap_mask):
    return jnp.where(wrap_mask, pltpu.roll(values, X_OUT - 1, 1), pltpu.roll(values, LANES - 1, 1))


def x_prev(values, wrap_mask):
    return jnp.where(wrap_mask, pltpu.roll(values, LANES - X_OUT + 1, 1), pltpu.roll(values, 1, 1))


def apply_planes(vector, diagonal, first, count, group, last_x, first_x):
    planes = vector.shape[0]
    rows = pl.ds(group * SUB, SUB)
    held = {}
    for far in range(-2, count + 2):
        index = jnp.bitwise_and(first + (far + planes), planes - 1)
        held[far] = [vector[index, rows, pl.ds(m * LANES, LANES)] for m in range(ROWS)]
    for plane in range(count):
        here, above, below = held[plane], held[plane + 1], held[plane - 1]
        above_2, below_2 = held[plane + 2], held[plane - 2]
        y_up = [pltpu.roll(value, LANES - X_OUT, 1) for value in here]
        y_down = [pltpu.roll(value, X_OUT, 1) for value in here]
        out = []
        for yi in range(Y_IN):
            line = here[yi * X_IN : (yi + 1) * X_IN]
            before = [x_prev(line[X_IN - 2], first_x), x_prev(line[X_IN - 1], first_x)]
            after = [x_next(line[0], last_x), x_next(line[1], last_x)]
            wide = before + line + after
            for xi in range(X_IN):
                m = yi * X_IN + xi
                other = (1 - yi) * X_IN + xi
                y_next = here[other] if yi == 0 else y_up[other]
                y_prev = here[other] if yi == 1 else y_down[other]
                near = (wide[xi + 1] + wide[xi + 3]) + (y_next + y_prev) + (above[m] + below[m])
                far = (wide[xi] + wide[xi + 4]) + (y_up[m] + y_down[m])
                far = far + (above_2[m] + below_2[m])
                level = diagonal[first + plane, :, pl.ds(m * LANES, LANES)]
                out.append(level * here[m] - near - FAR_SCALED * far)
        yield here, out


def cmul(first, second):
    return (
        first[0] * second[0] - first[1] * second[1],
        first[0] * second[1] + first[1] * second[0],
    )


def moment_coeffs(point, points, count):
    lane = lax.broadcasted_iota(jnp.int32, (1, LANES), 1)
    moment = lax.rem(lane, MOMENTS * count) // count
    angle = 2.0 * math.pi * (point + 0.5) / points
    parts = []
    for func in (math.cos, math.sin):
        value = jnp.full((1, LANES), 0.25 * func(angle), jnp.float32)
        for k in range(1, MOMENTS):
            value = jnp.where(moment == k, 0.25 * func((k + 1) * angle), value)
        parts.append(value)
    return parts


def weights_of(alphas, norms, limits, count):
    points = len(limits)
    shape = (count, LANES)
    half = MOMENTS * count
    lane = lax.broadcasted_iota(jnp.int32, shape, 1)
    source = lax.broadcasted_iota(jnp.int32, shape, 0)
    own = lax.rem(lane, count) == source
    left_half = lane < half
    betas = [ratio(norms[i + 1], norms[i]) for i in range(ITERS - 1)]
    sums = [[jnp.zeros(shape, jnp.float32)] * 2 for _ in range(BASIS)]
    zero = jnp.zeros(shape, jnp.float32)
    one = jnp.ones(shape, jnp.float32)
    for point in range(points):
        angle = 2.0 * math.pi * (point + 0.5) / points
        shift = (GAMMA + RADIUS * math.cos(angle), RADIUS * math.sin(angle))
        scaled_shift = (H_SCALE * shift[0], H_SCALE * shift[1])
        limit = limits[point]
        product = (one, zero)
        products = [product]
        links = []
        pivot = (scaled_shift[0] - alphas[0], zero + scaled_shift[1])
        for i in range(ITERS):
            size = 1.0 / (pivot[0] * pivot[0] + pivot[1] * pivot[1])
            inverse = (pivot[0] * size, -pivot[1] * size)
            product = cmul(product, inverse)
            products.append(product)
            if i < ITERS - 1:
                link = (betas[i] * inverse[0], betas[i] * inverse[1])
                links.append(link)
                pivot = (scaled_shift[0] - alphas[i + 1] - link[0], scaled_shift[1] - link[1])
        solved = [None] * ITERS
        for i in reversed(range(ITERS)):
            value = (H_SCALE * products[i + 1][0], H_SCALE * products[i + 1][1])
            if i < ITERS - 1:
                step = cmul(links[i], solved[i + 1])
                value = (value[0] + step[0], value[1] + step[1])
            used = limit > i
            solved[i] = (jnp.where(used, value[0], 0.0), jnp.where(used, value[1], 0.0))
        applied = []
        for i in range(BASIS):
            left = limit == i
            rest = (
                jnp.where(left, products[i][0], 0.0),
                jnp.where(left, products[i][1], 0.0),
            )
            if i < ITERS:
                turned = (
                    shift[0] * solved[i][0] - shift[1] * solved[i][1],
                    shift[0] * solved[i][1] + shift[1] * solved[i][0],
                )
                rest = (rest[0] + turned[0], rest[1] + turned[1])
            if i == 0:
                rest = (rest[0] - 1.0, rest[1])
            applied.append(rest)
        tail = applied[ITERS]
        for back, factor in ((1, alphas[ITERS - 1]), (2, betas[ITERS - 2])):
            part = applied[ITERS - back]
            applied[ITERS - back] = (part[0] - factor * tail[0], part[1] - factor * tail[1])
        moment = moment_coeffs(point, points, count)
        for i in range(BASIS):
            left = solved[i] if i < ITERS else (zero, zero)
            both = (
                jnp.where(left_half, left[0], applied[i][0]),
                jnp.where(left_half, left[1], applied[i][1]),
            )
            term = cmul(moment, both)
            sums[i] = [sums[i][0] + term[0], sums[i][1] + term[1]]
    return [[jnp.where(own, part, 0.0) for part in pair] for pair in sums]


def exact_dot(first, second, dims):
    return lax.dot_general(
        first,
        second,
        (dims, ((), ())),
        precision=lax.Precision.HIGHEST,
        preferred_element_type=jnp.float32,
    )


def krylov_kernel(parts, count, *refs):
    blocks, vectors = refs[:parts], refs[parts : parts + BASIS]
    scalars, applied, diagonal = refs[parts + BASIS :]
    planes = diagonal.shape[0]
    depth = planes // parts
    groups = count // SUB
    lane = lax.broadcasted_iota(jnp.int32, (SUB, LANES), 1)
    last_x = lax.rem(lane, X_OUT) == X_OUT - 1
    first_x = lax.rem(lane, X_OUT) == 0
    here = lax.axis_index("dom")
    for turn in range(parts):
        slab = jnp.bitwise_xor(here, turn) * depth
        for deep in range(depth):
            for m in range(ROWS):
                start = (deep * ROWS + m) * count
                lanes = pl.ds(m * LANES, LANES)
                vectors[0][slab + deep, :, lanes] = blocks[turn][start : start + count, :]
            start = depth * ROWS * count + deep * ROWS
            levels = H_SCALE * (blocks[turn][start : start + ROWS, :] + 3.75)
            for m in range(ROWS):
                level = jnp.broadcast_to(levels[m : m + 1, :], (SUB, LANES))
                diagonal[slab + deep, :, m * LANES : (m + 1) * LANES] = level

    blank = jnp.zeros((SUB, LANES), jnp.float32)
    alphas, norms = [], []
    for i in range(ITERS):
        source, target = vectors[i], applied if i < ITERS - 1 else vectors[ITERS]

        def apply_turn(turn, sums, i=i, source=source, target=target):
            first = turn * TOGETHER
            new_sums = []
            for group in range(groups):
                rows = pl.ds(group * SUB, SUB)
                curve, norm = sums[group]
                done = apply_planes(source, diagonal, first, TOGETHER, group, last_x, first_x)
                for plane, (value, out) in enumerate(done):
                    for m in range(ROWS):
                        target[first + plane, rows, pl.ds(m * LANES, LANES)] = out[m]
                        curve = curve + value[m] * out[m]
                        if i == 0:
                            norm = norm + value[m] * value[m]
                new_sums.append((curve, norm))
            return tuple(new_sums)

        sums = lax.fori_loop(0, planes // TOGETHER, apply_turn, ((blank, blank),) * groups)
        if i == 0:
            norms.append([lane_sum(norm) for _, norm in sums])
        alphas.append([ratio(lane_sum(sums[g][0]), norms[i][g]) for g in range(groups)])
        if i == ITERS - 1:
            break
        betas = [ratio(norms[i][g], norms[i - 1][g]) for g in range(groups)] if i else None

        def step_turn(plane, sums, i=i, alpha=alphas[i], betas=betas):
            new_sums = []
            for group in range(groups):
                rows = pl.ds(group * SUB, SUB)
                norm = sums[group]
                for m in range(ROWS):
                    lanes = pl.ds(m * LANES, LANES)
                    value = applied[plane, rows, lanes]
                    value = value - alpha[group] * vectors[i][plane, rows, lanes]
                    if i:
                        value = value - betas[group] * vectors[i - 1][plane, rows, lanes]
                    vectors[i + 1][plane, rows, lanes] = value
                    norm = norm + value * value
                new_sums.append(norm)
            return tuple(new_sums)

        sums = lax.fori_loop(0, planes, step_turn, (blank,) * groups, unroll=TOGETHER)
        norms.append([lane_sum(norm) for norm in sums])
    for i, value in enumerate(alphas + norms):
        scalars[i] = jnp.concatenate(value, axis=0)


def gram_kernel(points, scalars, *refs):
    tiles, vectors = refs[:points], refs[points : points + BASIS]
    out_b, out_a, gram, limits = refs[points + BASIS :]
    planes, count, _ = vectors[0].shape
    groups = count // SUB
    size = BASIS * count
    gram[...] = jnp.zeros_like(gram)

    def gram_turn(plane, carry):
        values = jnp.concatenate([vector[plane] for vector in vectors], axis=0)
        high = values.astype(jnp.bfloat16)
        low = (values - high.astype(jnp.float32)).astype(jnp.bfloat16)
        gram[...] += lax.dot_general(
            high,
            jnp.concatenate([high, low], axis=0),
            (((1,), (1,)), ((), ())),
            preferred_element_type=jnp.float32,
        )
        return carry

    lax.fori_loop(0, planes, gram_turn, 0, unroll=TOGETHER)
    cross = gram[:, size:]
    pairs = gram[:, :size] + cross + cross.T

    here = lax.axis_index("point")
    for far, tile in enumerate(tiles):
        limits[jnp.bitwise_xor(here, far)] = tile[...]
    bounds = [jnp.concatenate([limits[j]] * groups, axis=0) for j in range(points)]
    alphas = [scalars[i] for i in range(ITERS)]
    norms = [scalars[ITERS + i] for i in range(ITERS)]
    weights = weights_of(alphas, norms, bounds, count)
    real = jnp.concatenate([pair[0] for pair in weights], axis=0)
    imag = jnp.concatenate([pair[1] for pair in weights], axis=0)
    right = exact_dot(pairs, jnp.concatenate([real, imag], axis=1), ((1,), (0,)))
    half = MOMENTS * count
    left = jnp.concatenate([real[:, :half], imag[:, :half]], axis=1)
    joined = exact_dot(left.T, right, ((1,), (0,)))
    scale = 1.0 / (planes * ROWS * LANES)
    width = 2 * half
    real = (joined[:half, :width] + joined[half:, width:]) * scale
    imag = (joined[:half, width:] - joined[half:, :width]) * scale
    out_b[0] = real[:, :half]
    out_b[1] = imag[:, :half]
    out_a[0] = real[:, half:]
    out_a[1] = imag[:, half:]


def swapped(values, axis, size, mask):
    return lax.ppermute(values, axis, [(index ^ mask, index) for index in range(size)])


def whole_grid(sources, potential, iter_counts, *, parts, points):
    count, depth, _ = sources.shape
    planes = parts * depth
    block, tile = packed_block(sources, potential, iter_counts)
    even = [block] + [swapped(block, "dom", parts, mask) for mask in range(CORES, parts, CORES)]
    tiles = [swapped(tile, "point", points, far) for far in range(1, points)]
    even[2], *tiles = lax.optimization_barrier((even[2], *tiles))
    odd = [swapped(value, "dom", parts, 1) for value in even]
    blocks = [value for pair in zip(even, odd) for value in pair]
    vmem = pl.BlockSpec(memory_space=pltpu.VMEM)
    vector = (planes, count, ROWS * LANES)
    cells = planes * ROWS * LANES
    *vectors, scalars = pl.pallas_call(
        functools.partial(krylov_kernel, parts, count),
        out_shape=[jax.ShapeDtypeStruct(vector, jnp.float32)] * BASIS
        + [jax.ShapeDtypeStruct((2 * ITERS, count, LANES), jnp.float32)],
        in_specs=[vmem] * parts,
        out_specs=[vmem] * (BASIS + 1),
        scratch_shapes=[
            pltpu.VMEM(vector, jnp.float32),
            pltpu.VMEM((planes, SUB, ROWS * LANES), jnp.float32),
        ],
        compiler_params=pltpu.CompilerParams(vmem_limit_bytes=16 * 2**20),
        cost_estimate=pl.CostEstimate(
            flops=ITERS * count * cells * 30, bytes_accessed=32 * 2**20, transcendentals=0
        ),
        name="krylov",
    )(*blocks)
    size = BASIS * count
    width = MOMENTS * count
    out = jax.ShapeDtypeStruct((2, width, width), jnp.float32)
    return pl.pallas_call(
        functools.partial(gram_kernel, points),
        out_shape=(out, out),
        in_specs=[vmem] * (1 + points + BASIS),
        out_specs=(vmem, vmem),
        scratch_shapes=[
            pltpu.VMEM((size, 2 * size), jnp.float32),
            pltpu.VMEM((points, SUB, LANES), jnp.float32),
        ],
        compiler_params=pltpu.CompilerParams(vmem_limit_bytes=16 * 2**20),
        name="gram",
    )(scalars, tile, *tiles, *vectors)


def on_device(sources, potential, iter_counts):
    parts, points = lax.axis_size("dom"), lax.axis_size("point")
    count, depth, cells = sources.shape
    held = BASIS * count * parts * depth * cells * 4
    fits = (
        held <= 16 * 2**20
        and parts == 8
        and points == 4
        and count == 2 * SUB
        and 2 * MOMENTS * count == LANES
        and parts * depth == 16
        and cells == GX * GX == ROWS * LANES
    )
    if not fits:
        return split_grid(sources, potential, iter_counts)
    return whole_grid(sources, potential, iter_counts, parts=parts, points=points)


def solution(mesh):
    placed = (P(None, "dom", None), P("dom", None), P("point"))
    return jax.shard_map(
        on_device, mesh=mesh, in_specs=placed, out_specs=(P(), P()), check_vma=False
    )
```

```python
import functools
import math

import jax
import jax.numpy as jnp
from jax import lax
from jax.experimental import pallas as pl
from jax.experimental.pallas import tpu as pltpu
from jax.sharding import PartitionSpec as P

MOMENTS = 4
ITERS = 6
GX = 32


COEF_NEAR = 4.0 / 3.0
COEF_FAR = -1.0 / 12.0
GAMMA = 2.0
RADIUS = 1.5


def padded_2(block, sides, width):
    for axis, dim in sides:
        count = lax.axis_size(axis)
        forward = [(i, i + 1) for i in range(count - 1)]
        forward.append((count - 1, 0))
        backward = [(target, source) for source, target in forward]
        low = lax.ppermute(
            lax.slice_in_dim(block, block.shape[dim] - width, None, axis=dim), axis, forward
        )
        high = lax.ppermute(lax.slice_in_dim(block, 0, width, axis=dim), axis, backward)
        block = jnp.concatenate([low, block, high], axis=dim)
    return block


def plane_terms(values, side):
    lead = values.shape[:-1]
    planes = values.reshape(lead + (side, side))
    summed = COEF_NEAR * (
        jnp.roll(planes, 1, -2)
        + jnp.roll(planes, -1, -2)
        + jnp.roll(planes, 1, -1)
        + jnp.roll(planes, -1, -1)
    )
    summed = summed + COEF_FAR * (
        jnp.roll(planes, 2, -2)
        + jnp.roll(planes, -2, -2)
        + jnp.roll(planes, 2, -1)
        + jnp.roll(planes, -2, -1)
    )
    return summed.reshape(values.shape)


def complex_mul(first, second):
    return jnp.stack(
        [first[0] * second[0] - first[1] * second[1], first[0] * second[1] + first[1] * second[0]]
    )


def complex_div(first, second):
    denom = second[0] * second[0] + second[1] * second[1]
    return jnp.stack(
        [
            (first[0] * second[0] + first[1] * second[1]) / denom,
            (first[1] * second[0] - first[0] * second[1]) / denom,
        ]
    )


def bilinear(first, second):
    real_part = jnp.sum(first[0] * second[0] - first[1] * second[1], axis=(1, 2))
    imag_part = jnp.sum(first[0] * second[1] + first[1] * second[0], axis=(1, 2))
    return jnp.stack([real_part, imag_part])


def scaled(coeffs, values):
    return complex_mul(coeffs[:, :, None, None], values)


def shifted(values, potential, shift_re, shift_im):
    padded = padded_2(values, (("dom", 2),), 2)
    depth = values.shape[2]
    lap = -7.5 * values + plane_terms(values, GX)
    lap = lap + COEF_NEAR * (padded[:, :, 3 : 3 + depth] + padded[:, :, 1 : 1 + depth])
    lap = lap + COEF_FAR * (padded[:, :, 4 : 4 + depth] + padded[:, :, 0:depth])
    applied = -0.5 * lap + potential * values
    return jnp.stack(
        [
            shift_re * values[0] - shift_im * values[1] - applied[0],
            shift_re * values[1] + shift_im * values[0] - applied[1],
        ]
    )


def residual_sum(values):
    return lax.psum(bilinear(values, values), "dom")


def moment_terms(solution, residual, sources, angle_now, shift_re, shift_im):
    applied = jnp.stack(
        [
            shift_re * solution[0] - shift_im * solution[1] - sources[0] + residual[0],
            shift_re * solution[1] + shift_im * solution[0] - sources[1] + residual[1],
        ]
    )
    angles = (jnp.arange(MOMENTS).astype(jnp.float32) + 1.0) * angle_now
    coeffs = 0.25 * jnp.stack([jnp.cos(angles), jnp.sin(angles)])
    s_terms = complex_mul(coeffs[:, :, None, None, None], solution[:, None])
    h_terms = complex_mul(coeffs[:, :, None, None, None], applied[:, None])
    width = MOMENTS * solution.shape[1]
    return (s_terms.reshape(2, width, -1), h_terms.reshape(2, width, -1))


def gram_of(left, right):
    width = left.shape[1]
    joined = lax.dot_general(
        left.reshape(2 * width, -1),
        right.reshape(2 * width, -1),
        (((1,), (1,)), ((), ())),
        precision=lax.Precision.HIGHEST,
        preferred_element_type=jnp.float32,
    )
    blocks = joined.reshape(2, width, 2, width)
    return jnp.stack([blocks[0, :, 0] + blocks[1, :, 1], blocks[0, :, 1] - blocks[1, :, 0]])


def split_grid(sources, potential, iter_counts):
    complex_src = jnp.stack([sources, jnp.zeros_like(sources)])
    angle_now = (
        2.0 * math.pi * (lax.axis_index("point").astype(jnp.float32) + 0.5) / lax.axis_size("point")
    )
    shift_re = GAMMA + RADIUS * jnp.cos(angle_now)
    shift_im = RADIUS * jnp.sin(angle_now)
    limit = iter_counts[0]
    solution = jnp.zeros_like(complex_src)

    def one_turn(turn_idx, state):
        solution, residual, search, norm_now = state
        product = shifted(search, potential, shift_re, shift_im)
        curve = lax.psum(bilinear(search, product), "dom")
        step_size = complex_div(norm_now, curve)
        new_residual = residual - scaled(step_size, product)
        norm_next = residual_sum(new_residual)
        fresh = (
            solution + scaled(step_size, search),
            new_residual,
            new_residual + scaled(complex_div(norm_next, norm_now), search),
            norm_next,
        )
        keep_mask = turn_idx < limit
        return jax.tree.map(lambda newer, older: jnp.where(keep_mask, newer, older), fresh, state)

    start = (solution, complex_src, complex_src, residual_sum(complex_src))
    solution, residual, search, norm_now = lax.fori_loop(0, ITERS, one_turn, start)
    s_terms, h_terms = moment_terms(solution, residual, complex_src, angle_now, shift_re, shift_im)
    cells = sources.shape[1] * sources.shape[2] * lax.axis_size("dom")
    s_total, h_total = lax.psum((s_terms, h_terms), "point")
    gram_b, gram_a = lax.psum((gram_of(s_total, s_total), gram_of(s_total, h_total)), "dom")
    return (gram_b / cells, gram_a / cells)


Y_IN, X_IN = 2, 4
Y_OUT, X_OUT = GX // Y_IN, GX // X_IN
ROWS = Y_IN * X_IN
LANES = Y_OUT * X_OUT
SUB = 8
BASIS = ITERS + 1
CORES = 2
TOGETHER = 4
H_SCALE = 2.0 / COEF_NEAR
FAR_SCALED = 0.5 * H_SCALE * COEF_FAR


def pack_kernel(depth, groups, counts, rows, out, tile):
    columns = rows.shape[0] // (SUB * groups * depth + depth)
    first_level = columns * SUB * groups * depth
    source = lax.broadcasted_iota(jnp.int32, (LANES, LANES), 0)
    target = lax.broadcasted_iota(jnp.int32, (LANES, LANES), 1)
    inner = target // (LANES // ROWS)
    outer = target % (LANES // ROWS)
    cell = (outer // X_OUT * Y_IN + inner // X_IN) * GX + outer % X_OUT * X_IN + inner % X_IN
    swap = jnp.where(source == cell, 1.0, 0.0).astype(jnp.float32)
    parts = []
    for deep in range(depth):
        for group in range(groups):
            for column in range(columns):
                start = (group * SUB * columns + column) * depth + deep
                parts.append(rows[pl.ds(start, SUB, stride=columns * depth), :])
        parts.append(rows[pl.ds(first_level + deep, columns, stride=depth), :])
    mixed = exact_dot(jnp.concatenate(parts, axis=0), swap, ((1,), (0,)))
    block = LANES // ROWS
    lane_block = lax.broadcasted_iota(jnp.int32, (SUB, LANES), 1) // block
    row = lax.broadcasted_iota(jnp.int32, (SUB, LANES), 0)
    for deep in range(depth):
        base = deep * (groups + 1) * columns * SUB - deep * (columns - 1) * SUB
        for group in range(groups):
            pieces = [
                mixed[base + (group * columns + column) * SUB :][:SUB] for column in range(columns)
            ]
            for m in range(ROWS):
                value = pieces[m]
                for column in range(columns):
                    if column != m:
                        moved = pltpu.roll(pieces[column], (column - m) * block % LANES, 1)
                        value = jnp.where(lane_block == column, moved, value)
                start = ((deep * ROWS + m) * groups + group) * SUB
                out[start : start + SUB, :] = value
        piece = mixed[base + groups * columns * SUB :][:SUB]
        value = piece
        for far in range(1, columns):
            moved = pltpu.roll(pltpu.roll(piece, far * block, 1), columns - far, 0)
            value = jnp.where(lane_block == (row + far) % columns, moved, value)
        start = depth * ROWS * SUB * groups + deep * ROWS
        out[start : start + ROWS, :] = value
    tile[...] = jnp.broadcast_to(counts[...].astype(jnp.float32), (SUB, LANES))


def packed_block(sources, potential, iter_counts):
    count, depth, cells = sources.shape
    columns = cells // LANES
    rows = sources.reshape(count, depth, columns, LANES).transpose(0, 2, 1, 3).reshape(-1, LANES)
    levels = potential.reshape(depth, columns, LANES).transpose(1, 0, 2).reshape(-1, LANES)
    vmem = pl.BlockSpec(memory_space=pltpu.VMEM)
    size = depth * ROWS * (count + 1)
    return pl.pallas_call(
        functools.partial(pack_kernel, depth, count // SUB),
        out_shape=(
            jax.ShapeDtypeStruct((size, LANES), jnp.float32),
            jax.ShapeDtypeStruct((SUB, LANES), jnp.float32),
        ),
        in_specs=[vmem, vmem],
        out_specs=(vmem, vmem),
        compiler_params=pltpu.CompilerParams(vmem_limit_bytes=4 * 2**20),
        name="pack",
    )(iter_counts.reshape(1, 1), jnp.concatenate([rows, levels], axis=0))


def lane_sum(values):
    return jnp.broadcast_to(jnp.sum(values, axis=1, keepdims=True), values.shape)


def ratio(top, bottom):
    return jnp.where(bottom > 0.0, top / jnp.where(bottom > 0.0, bottom, 1.0), 0.0)


def lane_moved(values, lanes):
    return jnp.take_along_axis(values, lanes, axis=1)


def apply_planes(vector, diagonal, first, count, group, x_after, x_before):
    planes = vector.shape[0]
    rows = pl.ds(group * SUB, SUB)
    held = {}
    for far in range(-2, count + 2):
        index = jnp.bitwise_and(first + (far + planes), planes - 1)
        held[far] = [vector[index, rows, pl.ds(m * LANES, LANES)] for m in range(ROWS)]
    for plane in range(count):
        here, above, below = held[plane], held[plane + 1], held[plane - 1]
        above_2, below_2 = held[plane + 2], held[plane - 2]
        y_up = [pltpu.roll(value, LANES - X_OUT, 1) for value in here]
        y_down = [pltpu.roll(value, X_OUT, 1) for value in here]
        out = []
        for yi in range(Y_IN):
            line = here[yi * X_IN : (yi + 1) * X_IN]
            before = [lane_moved(value, x_before) for value in line[X_IN - 2 :]]
            after = [lane_moved(value, x_after) for value in line[:2]]
            wide = before + line + after
            for xi in range(X_IN):
                m = yi * X_IN + xi
                other = (1 - yi) * X_IN + xi
                y_next = here[other] if yi == 0 else y_up[other]
                y_prev = here[other] if yi == 1 else y_down[other]
                near = (wide[xi + 1] + wide[xi + 3]) + (y_next + y_prev) + (above[m] + below[m])
                far = (wide[xi] + wide[xi + 4]) + (y_up[m] + y_down[m])
                far = far + (above_2[m] + below_2[m])
                level = diagonal[first + plane, :, pl.ds(m * LANES, LANES)]
                out.append(level * here[m] - near - FAR_SCALED * far)
        yield here, out


def cmul(first, second):
    return (
        first[0] * second[0] - first[1] * second[1],
        first[0] * second[1] + first[1] * second[0],
    )


def moment_coeffs(point, points, count):
    lane = lax.broadcasted_iota(jnp.int32, (1, LANES), 1)
    moment = lax.rem(lane, MOMENTS * count) // count
    angle = 2.0 * math.pi * (point + 0.5) / points
    parts = []
    for func in (math.cos, math.sin):
        value = jnp.full((1, LANES), 0.25 * func(angle), jnp.float32)
        for k in range(1, MOMENTS):
            value = jnp.where(moment == k, 0.25 * func((k + 1) * angle), value)
        parts.append(value)
    return parts


def weights_of(alphas, norms, limits, count):
    points = len(limits)
    shape = (count, LANES)
    half = MOMENTS * count
    lane = lax.broadcasted_iota(jnp.int32, shape, 1)
    source = lax.broadcasted_iota(jnp.int32, shape, 0)
    own = lax.rem(lane, count) == source
    left_half = lane < half
    betas = [ratio(norms[i + 1], norms[i]) for i in range(ITERS - 1)]
    sums = [[jnp.zeros(shape, jnp.float32)] * 2 for _ in range(BASIS)]
    zero = jnp.zeros(shape, jnp.float32)
    one = jnp.ones(shape, jnp.float32)
    for point in range(points):
        angle = 2.0 * math.pi * (point + 0.5) / points
        shift = (GAMMA + RADIUS * math.cos(angle), RADIUS * math.sin(angle))
        scaled_shift = (H_SCALE * shift[0], H_SCALE * shift[1])
        limit = limits[point]
        product = (one, zero)
        products = [product]
        links = []
        pivot = (scaled_shift[0] - alphas[0], zero + scaled_shift[1])
        for i in range(ITERS):
            size = 1.0 / (pivot[0] * pivot[0] + pivot[1] * pivot[1])
            inverse = (pivot[0] * size, -pivot[1] * size)
            product = cmul(product, inverse)
            products.append(product)
            if i < ITERS - 1:
                link = (betas[i] * inverse[0], betas[i] * inverse[1])
                links.append(link)
                pivot = (scaled_shift[0] - alphas[i + 1] - link[0], scaled_shift[1] - link[1])
        solved = [None] * ITERS
        for i in reversed(range(ITERS)):
            value = (H_SCALE * products[i + 1][0], H_SCALE * products[i + 1][1])
            if i < ITERS - 1:
                step = cmul(links[i], solved[i + 1])
                value = (value[0] + step[0], value[1] + step[1])
            used = limit > i
            solved[i] = (jnp.where(used, value[0], 0.0), jnp.where(used, value[1], 0.0))
        applied = []
        for i in range(BASIS):
            left = limit == i
            rest = (
                jnp.where(left, products[i][0], 0.0),
                jnp.where(left, products[i][1], 0.0),
            )
            if i < ITERS:
                turned = (
                    shift[0] * solved[i][0] - shift[1] * solved[i][1],
                    shift[0] * solved[i][1] + shift[1] * solved[i][0],
                )
                rest = (rest[0] + turned[0], rest[1] + turned[1])
            if i == 0:
                rest = (rest[0] - 1.0, rest[1])
            applied.append(rest)
        tail = applied[ITERS]
        for back, factor in ((1, alphas[ITERS - 1]), (2, betas[ITERS - 2])):
            part = applied[ITERS - back]
            applied[ITERS - back] = (part[0] - factor * tail[0], part[1] - factor * tail[1])
        moment = moment_coeffs(point, points, count)
        for i in range(BASIS):
            left = solved[i] if i < ITERS else (zero, zero)
            both = (
                jnp.where(left_half, left[0], applied[i][0]),
                jnp.where(left_half, left[1], applied[i][1]),
            )
            term = cmul(moment, both)
            sums[i] = [sums[i][0] + term[0], sums[i][1] + term[1]]
    return [[jnp.where(own, part, 0.0) for part in pair] for pair in sums]


def exact_dot(first, second, dims):
    return lax.dot_general(
        first,
        second,
        (dims, ((), ())),
        precision=lax.Precision.HIGHEST,
        preferred_element_type=jnp.float32,
    )


def krylov_kernel(parts, count, *refs):
    blocks, vectors = refs[:parts], refs[parts : parts + BASIS]
    scalars, applied, diagonal = refs[parts + BASIS :]
    planes = diagonal.shape[0]
    depth = planes // parts
    groups = count // SUB
    lane = lax.broadcasted_iota(jnp.int32, (SUB, LANES), 1)
    x_out = jnp.bitwise_and(lane, X_OUT - 1)
    x_after = lane - x_out + jnp.bitwise_and(x_out + 1, X_OUT - 1)
    x_before = lane - x_out + jnp.bitwise_and(x_out + X_OUT - 1, X_OUT - 1)
    here = lax.axis_index("dom")
    for turn in range(parts):
        slab = jnp.bitwise_xor(here, turn) * depth
        for deep in range(depth):
            for m in range(ROWS):
                start = (deep * ROWS + m) * count
                lanes = pl.ds(m * LANES, LANES)
                vectors[0][slab + deep, :, lanes] = blocks[turn][start : start + count, :]
            start = depth * ROWS * count + deep * ROWS
            levels = H_SCALE * (blocks[turn][start : start + ROWS, :] + 3.75)
            for m in range(ROWS):
                level = jnp.broadcast_to(levels[m : m + 1, :], (SUB, LANES))
                diagonal[slab + deep, :, m * LANES : (m + 1) * LANES] = level

    blank = jnp.zeros((SUB, LANES), jnp.float32)
    alphas, norms = [], []
    for i in range(ITERS):
        source, target = vectors[i], applied if i < ITERS - 1 else vectors[ITERS]

        def apply_turn(turn, sums, i=i, source=source, target=target):
            first = turn * TOGETHER
            new_sums = []
            for group in range(groups):
                rows = pl.ds(group * SUB, SUB)
                curve, norm = sums[group]
                done = apply_planes(source, diagonal, first, TOGETHER, group, x_after, x_before)
                for plane, (value, out) in enumerate(done):
                    for m in range(ROWS):
                        target[first + plane, rows, pl.ds(m * LANES, LANES)] = out[m]
                        curve = curve + value[m] * out[m]
                        if i == 0:
                            norm = norm + value[m] * value[m]
                new_sums.append((curve, norm))
            return tuple(new_sums)

        sums = lax.fori_loop(0, planes // TOGETHER, apply_turn, ((blank, blank),) * groups)
        if i == 0:
            norms.append([lane_sum(norm) for _, norm in sums])
        alphas.append([ratio(lane_sum(sums[g][0]), norms[i][g]) for g in range(groups)])
        if i == ITERS - 1:
            break
        betas = [ratio(norms[i][g], norms[i - 1][g]) for g in range(groups)] if i else None

        def step_turn(plane, sums, i=i, alpha=alphas[i], betas=betas):
            new_sums = []
            for group in range(groups):
                rows = pl.ds(group * SUB, SUB)
                norm = sums[group]
                for m in range(ROWS):
                    lanes = pl.ds(m * LANES, LANES)
                    value = applied[plane, rows, lanes]
                    value = value - alpha[group] * vectors[i][plane, rows, lanes]
                    if i:
                        value = value - betas[group] * vectors[i - 1][plane, rows, lanes]
                    vectors[i + 1][plane, rows, lanes] = value
                    norm = norm + value * value
                new_sums.append(norm)
            return tuple(new_sums)

        sums = lax.fori_loop(0, planes, step_turn, (blank,) * groups, unroll=TOGETHER)
        norms.append([lane_sum(norm) for norm in sums])
    for i, value in enumerate(alphas + norms):
        scalars[i] = jnp.concatenate(value, axis=0)


def gram_kernel(points, scalars, *refs):
    tiles, vectors = refs[:points], refs[points : points + BASIS]
    out_b, out_a, gram, limits = refs[points + BASIS :]
    planes, count, _ = vectors[0].shape
    groups = count // SUB
    size = BASIS * count
    gram[...] = jnp.zeros_like(gram)

    def gram_turn(plane, carry):
        values = jnp.concatenate([vector[plane] for vector in vectors], axis=0)
        high = values.astype(jnp.bfloat16)
        low = (values - high.astype(jnp.float32)).astype(jnp.bfloat16)
        gram[...] += lax.dot_general(
            jnp.concatenate([high, low], axis=0),
            high,
            (((1,), (1,)), ((), ())),
            preferred_element_type=jnp.float32,
        )
        return carry

    lax.fori_loop(0, planes, gram_turn, 0, unroll=TOGETHER)
    cross = gram[size:, :]
    pairs = gram[:size, :] + cross + cross.T

    here = lax.axis_index("point")
    for far, tile in enumerate(tiles):
        limits[jnp.bitwise_xor(here, far)] = tile[...]
    bounds = [jnp.concatenate([limits[j]] * groups, axis=0) for j in range(points)]
    alphas = [scalars[i] for i in range(ITERS)]
    norms = [scalars[ITERS + i] for i in range(ITERS)]
    weights = weights_of(alphas, norms, bounds, count)
    real = jnp.concatenate([pair[0] for pair in weights], axis=0)
    imag = jnp.concatenate([pair[1] for pair in weights], axis=0)
    right = exact_dot(pairs, jnp.concatenate([real, imag], axis=1), ((1,), (0,)))
    half = MOMENTS * count
    left = jnp.concatenate([real[:, :half], imag[:, :half]], axis=1)
    joined = exact_dot(left.T, right, ((1,), (0,)))
    scale = 1.0 / (planes * ROWS * LANES)
    width = 2 * half
    real = (joined[:half, :width] + joined[half:, width:]) * scale
    imag = (joined[:half, width:] - joined[half:, :width]) * scale
    out_b[0] = real[:, :half]
    out_b[1] = imag[:, :half]
    out_a[0] = real[:, half:]
    out_a[1] = imag[:, half:]


def swapped(values, axis, size, mask):
    return lax.ppermute(values, axis, [(index ^ mask, index) for index in range(size)])


def whole_grid(sources, potential, iter_counts, *, parts, points):
    count, depth, _ = sources.shape
    planes = parts * depth
    block, tile = packed_block(sources, potential, iter_counts)
    even = [block] + [swapped(block, "dom", parts, mask) for mask in range(CORES, parts, CORES)]
    tiles = [swapped(tile, "point", points, far) for far in range(1, points)]
    odd = [swapped(value, "dom", parts, 1) for value in even]
    blocks = [value for pair in zip(even, odd) for value in pair]
    vmem = pl.BlockSpec(memory_space=pltpu.VMEM)
    vector = (planes, count, ROWS * LANES)
    cells = planes * ROWS * LANES
    *vectors, scalars = pl.pallas_call(
        functools.partial(krylov_kernel, parts, count),
        out_shape=[jax.ShapeDtypeStruct(vector, jnp.float32)] * BASIS
        + [jax.ShapeDtypeStruct((2 * ITERS, count, LANES), jnp.float32)],
        in_specs=[vmem] * parts,
        out_specs=[vmem] * (BASIS + 1),
        scratch_shapes=[
            pltpu.VMEM(vector, jnp.float32),
            pltpu.VMEM((planes, SUB, ROWS * LANES), jnp.float32),
        ],
        compiler_params=pltpu.CompilerParams(vmem_limit_bytes=16 * 2**20),
        name="krylov",
    )(*blocks)
    size = BASIS * count
    width = MOMENTS * count
    out = jax.ShapeDtypeStruct((2, width, width), jnp.float32)
    return pl.pallas_call(
        functools.partial(gram_kernel, points),
        out_shape=(out, out),
        in_specs=[vmem] * (1 + points + BASIS),
        out_specs=(vmem, vmem),
        scratch_shapes=[
            pltpu.VMEM((2 * size, size), jnp.float32),
            pltpu.VMEM((points, SUB, LANES), jnp.float32),
        ],
        compiler_params=pltpu.CompilerParams(vmem_limit_bytes=16 * 2**20),
        name="gram",
    )(scalars, tile, *tiles, *vectors)


def on_device(sources, potential, iter_counts):
    parts, points = lax.axis_size("dom"), lax.axis_size("point")
    count, depth, cells = sources.shape
    held = BASIS * count * parts * depth * cells * 4
    fits = (
        held <= 16 * 2**20
        and parts == 8
        and points == 4
        and count == 2 * SUB
        and 2 * MOMENTS * count == LANES
        and parts * depth == 16
        and cells == GX * GX == ROWS * LANES
    )
    if not fits:
        return split_grid(sources, potential, iter_counts)
    return whole_grid(sources, potential, iter_counts, parts=parts, points=points)


def solution(mesh):
    placed = (P(None, "dom", None), P("dom", None), P("point"))
    return jax.shard_map(
        on_device, mesh=mesh, in_specs=placed, out_specs=(P(), P()), check_vma=False
    )
```

```python
import functools
import math

import jax
import jax.numpy as jnp
from jax import lax
from jax.experimental import pallas as pl
from jax.experimental.pallas import tpu as pltpu
from jax.sharding import PartitionSpec as P

MOMENTS = 4
ITERS = 6
GX = 32


COEF_NEAR = 4.0 / 3.0
COEF_FAR = -1.0 / 12.0
GAMMA = 2.0
RADIUS = 1.5


def padded_2(block, sides, width):
    for axis, dim in sides:
        count = lax.axis_size(axis)
        forward = [(i, i + 1) for i in range(count - 1)]
        forward.append((count - 1, 0))
        backward = [(target, source) for source, target in forward]
        low = lax.ppermute(
            lax.slice_in_dim(block, block.shape[dim] - width, None, axis=dim), axis, forward
        )
        high = lax.ppermute(lax.slice_in_dim(block, 0, width, axis=dim), axis, backward)
        block = jnp.concatenate([low, block, high], axis=dim)
    return block


def plane_terms(values, side):
    lead = values.shape[:-1]
    planes = values.reshape(lead + (side, side))
    summed = COEF_NEAR * (
        jnp.roll(planes, 1, -2)
        + jnp.roll(planes, -1, -2)
        + jnp.roll(planes, 1, -1)
        + jnp.roll(planes, -1, -1)
    )
    summed = summed + COEF_FAR * (
        jnp.roll(planes, 2, -2)
        + jnp.roll(planes, -2, -2)
        + jnp.roll(planes, 2, -1)
        + jnp.roll(planes, -2, -1)
    )
    return summed.reshape(values.shape)


def complex_mul(first, second):
    return jnp.stack(
        [first[0] * second[0] - first[1] * second[1], first[0] * second[1] + first[1] * second[0]]
    )


def complex_div(first, second):
    denom = second[0] * second[0] + second[1] * second[1]
    return jnp.stack(
        [
            (first[0] * second[0] + first[1] * second[1]) / denom,
            (first[1] * second[0] - first[0] * second[1]) / denom,
        ]
    )


def bilinear(first, second):
    real_part = jnp.sum(first[0] * second[0] - first[1] * second[1], axis=(1, 2))
    imag_part = jnp.sum(first[0] * second[1] + first[1] * second[0], axis=(1, 2))
    return jnp.stack([real_part, imag_part])


def scaled(coeffs, values):
    return complex_mul(coeffs[:, :, None, None], values)


def shifted(values, potential, shift_re, shift_im):
    padded = padded_2(values, (("dom", 2),), 2)
    depth = values.shape[2]
    lap = -7.5 * values + plane_terms(values, GX)
    lap = lap + COEF_NEAR * (padded[:, :, 3 : 3 + depth] + padded[:, :, 1 : 1 + depth])
    lap = lap + COEF_FAR * (padded[:, :, 4 : 4 + depth] + padded[:, :, 0:depth])
    applied = -0.5 * lap + potential * values
    return jnp.stack(
        [
            shift_re * values[0] - shift_im * values[1] - applied[0],
            shift_re * values[1] + shift_im * values[0] - applied[1],
        ]
    )


def residual_sum(values):
    return lax.psum(bilinear(values, values), "dom")


def moment_terms(solution, residual, sources, angle_now, shift_re, shift_im):
    applied = jnp.stack(
        [
            shift_re * solution[0] - shift_im * solution[1] - sources[0] + residual[0],
            shift_re * solution[1] + shift_im * solution[0] - sources[1] + residual[1],
        ]
    )
    angles = (jnp.arange(MOMENTS).astype(jnp.float32) + 1.0) * angle_now
    coeffs = 0.25 * jnp.stack([jnp.cos(angles), jnp.sin(angles)])
    s_terms = complex_mul(coeffs[:, :, None, None, None], solution[:, None])
    h_terms = complex_mul(coeffs[:, :, None, None, None], applied[:, None])
    width = MOMENTS * solution.shape[1]
    return (s_terms.reshape(2, width, -1), h_terms.reshape(2, width, -1))


def gram_of(left, right):
    width = left.shape[1]
    joined = lax.dot_general(
        left.reshape(2 * width, -1),
        right.reshape(2 * width, -1),
        (((1,), (1,)), ((), ())),
        precision=lax.Precision.HIGHEST,
        preferred_element_type=jnp.float32,
    )
    blocks = joined.reshape(2, width, 2, width)
    return jnp.stack([blocks[0, :, 0] + blocks[1, :, 1], blocks[0, :, 1] - blocks[1, :, 0]])


def split_grid(sources, potential, iter_counts):
    complex_src = jnp.stack([sources, jnp.zeros_like(sources)])
    angle_now = (
        2.0 * math.pi * (lax.axis_index("point").astype(jnp.float32) + 0.5) / lax.axis_size("point")
    )
    shift_re = GAMMA + RADIUS * jnp.cos(angle_now)
    shift_im = RADIUS * jnp.sin(angle_now)
    limit = iter_counts[0]
    solution = jnp.zeros_like(complex_src)

    def one_turn(turn_idx, state):
        solution, residual, search, norm_now = state
        product = shifted(search, potential, shift_re, shift_im)
        curve = lax.psum(bilinear(search, product), "dom")
        step_size = complex_div(norm_now, curve)
        new_residual = residual - scaled(step_size, product)
        norm_next = residual_sum(new_residual)
        fresh = (
            solution + scaled(step_size, search),
            new_residual,
            new_residual + scaled(complex_div(norm_next, norm_now), search),
            norm_next,
        )
        keep_mask = turn_idx < limit
        return jax.tree.map(lambda newer, older: jnp.where(keep_mask, newer, older), fresh, state)

    start = (solution, complex_src, complex_src, residual_sum(complex_src))
    solution, residual, search, norm_now = lax.fori_loop(0, ITERS, one_turn, start)
    s_terms, h_terms = moment_terms(solution, residual, complex_src, angle_now, shift_re, shift_im)
    cells = sources.shape[1] * sources.shape[2] * lax.axis_size("dom")
    s_total, h_total = lax.psum((s_terms, h_terms), "point")
    gram_b, gram_a = lax.psum((gram_of(s_total, s_total), gram_of(s_total, h_total)), "dom")
    return (gram_b / cells, gram_a / cells)


Y_IN, X_IN = 2, 4
Y_OUT, X_OUT = GX // Y_IN, GX // X_IN
ROWS = Y_IN * X_IN
LANES = Y_OUT * X_OUT
SUB = 8
BASIS = ITERS + 1
CORES = 2
TOGETHER = 4
TILE = 128
H_SCALE = 2.0 / COEF_NEAR
FAR_SCALED = 0.5 * H_SCALE * COEF_FAR


def pack_kernel(depth, groups, counts, rows, out, tile):
    columns = rows.shape[0] // (SUB * groups * depth + depth)
    first_level = columns * SUB * groups * depth
    source = lax.broadcasted_iota(jnp.int32, (LANES, LANES), 0)
    target = lax.broadcasted_iota(jnp.int32, (LANES, LANES), 1)
    inner = target // (LANES // ROWS)
    outer = target % (LANES // ROWS)
    cell = (outer // X_OUT * Y_IN + inner // X_IN) * GX + outer % X_OUT * X_IN + inner % X_IN
    swap = jnp.where(source == cell, 1.0, 0.0).astype(jnp.float32)
    parts = []
    for deep in range(depth):
        for group in range(groups):
            for column in range(columns):
                start = (group * SUB * columns + column) * depth + deep
                parts.append(rows[pl.ds(start, SUB, stride=columns * depth), :])
        parts.append(rows[pl.ds(first_level + deep, columns, stride=depth), :])
    mixed = exact_dot(jnp.concatenate(parts, axis=0), swap, ((1,), (0,)))
    block = LANES // ROWS
    lane_block = lax.broadcasted_iota(jnp.int32, (SUB, LANES), 1) // block
    row = lax.broadcasted_iota(jnp.int32, (SUB, LANES), 0)
    for deep in range(depth):
        base = deep * (groups + 1) * columns * SUB - deep * (columns - 1) * SUB
        for group in range(groups):
            pieces = [
                mixed[base + (group * columns + column) * SUB :][:SUB] for column in range(columns)
            ]
            for m in range(ROWS):
                value = pieces[m]
                for column in range(columns):
                    if column != m:
                        moved = pltpu.roll(pieces[column], (column - m) * block % LANES, 1)
                        value = jnp.where(lane_block == column, moved, value)
                start = ((deep * ROWS + m) * groups + group) * SUB
                out[start : start + SUB, :] = value
        piece = mixed[base + groups * columns * SUB :][:SUB]
        value = piece
        for far in range(1, columns):
            moved = pltpu.roll(pltpu.roll(piece, far * block, 1), columns - far, 0)
            value = jnp.where(lane_block == (row + far) % columns, moved, value)
        start = depth * ROWS * SUB * groups + deep * ROWS
        out[start : start + ROWS, :] = value
    tile[...] = jnp.broadcast_to(counts[...].astype(jnp.float32), tile.shape)


def packed_block(sources, potential, iter_counts):
    count, depth, cells = sources.shape
    columns = cells // LANES
    rows = sources.reshape(count, depth, columns, LANES).transpose(0, 2, 1, 3).reshape(-1, LANES)
    levels = potential.reshape(depth, columns, LANES).transpose(1, 0, 2).reshape(-1, LANES)
    vmem = pl.BlockSpec(memory_space=pltpu.VMEM)
    size = depth * ROWS * (count + 1)
    return pl.pallas_call(
        functools.partial(pack_kernel, depth, count // SUB),
        out_shape=(
            jax.ShapeDtypeStruct((size, LANES), jnp.float32),
            jax.ShapeDtypeStruct((TILE, LANES), jnp.float32),
        ),
        in_specs=[vmem, vmem],
        out_specs=(vmem, vmem),
        compiler_params=pltpu.CompilerParams(vmem_limit_bytes=4 * 2**20),
        name="pack",
    )(iter_counts.reshape(1, 1), jnp.concatenate([rows, levels], axis=0))


def lane_sum(values):
    return jnp.broadcast_to(jnp.sum(values, axis=1, keepdims=True), values.shape)


def ratio(top, bottom):
    return jnp.where(bottom > 0.0, top / jnp.where(bottom > 0.0, bottom, 1.0), 0.0)


def x_next(values, wrap_mask):
    return jnp.where(wrap_mask, pltpu.roll(values, X_OUT - 1, 1), pltpu.roll(values, LANES - 1, 1))


def x_prev(values, wrap_mask):
    return jnp.where(wrap_mask, pltpu.roll(values, LANES - X_OUT + 1, 1), pltpu.roll(values, 1, 1))


def apply_planes(vector, diagonal, first, count, group, last_x, first_x):
    planes = vector.shape[0]
    rows = pl.ds(group * SUB, SUB)
    held = {}
    for far in range(-2, count + 2):
        index = jnp.bitwise_and(first + (far + planes), planes - 1)
        held[far] = [vector[index, rows, pl.ds(m * LANES, LANES)] for m in range(ROWS)]
    for plane in range(count):
        here, above, below = held[plane], held[plane + 1], held[plane - 1]
        above_2, below_2 = held[plane + 2], held[plane - 2]
        y_up = [pltpu.roll(value, LANES - X_OUT, 1) for value in here]
        y_down = [pltpu.roll(value, X_OUT, 1) for value in here]
        out = []
        for yi in range(Y_IN):
            line = here[yi * X_IN : (yi + 1) * X_IN]
            before = [x_prev(value, first_x) for value in line[X_IN - 2 :]]
            after = [x_next(value, last_x) for value in line[:2]]
            wide = before + line + after
            for xi in range(X_IN):
                m = yi * X_IN + xi
                other = (1 - yi) * X_IN + xi
                y_next = here[other] if yi == 0 else y_up[other]
                y_prev = here[other] if yi == 1 else y_down[other]
                near = (wide[xi + 1] + wide[xi + 3]) + (y_next + y_prev) + (above[m] + below[m])
                far = (wide[xi] + wide[xi + 4]) + (y_up[m] + y_down[m])
                far = far + (above_2[m] + below_2[m])
                level = diagonal[first + plane, :, pl.ds(m * LANES, LANES)]
                out.append(level * here[m] - near - FAR_SCALED * far)
        yield here, out


def cmul(first, second):
    return (
        first[0] * second[0] - first[1] * second[1],
        first[0] * second[1] + first[1] * second[0],
    )


def moment_coeffs(point, points, count):
    lane = lax.broadcasted_iota(jnp.int32, (1, LANES), 1)
    moment = lax.rem(lane, MOMENTS * count) // count
    angle = 2.0 * math.pi * (point + 0.5) / points
    parts = []
    for func in (math.cos, math.sin):
        value = jnp.full((1, LANES), 0.25 * func(angle), jnp.float32)
        for k in range(1, MOMENTS):
            value = jnp.where(moment == k, 0.25 * func((k + 1) * angle), value)
        parts.append(value)
    return parts


def weights_of(alphas, norms, limits, count):
    points = len(limits)
    shape = (count, LANES)
    half = MOMENTS * count
    lane = lax.broadcasted_iota(jnp.int32, shape, 1)
    source = lax.broadcasted_iota(jnp.int32, shape, 0)
    own = lax.rem(lane, count) == source
    left_half = lane < half
    betas = [ratio(norms[i + 1], norms[i]) for i in range(ITERS - 1)]
    sums = [[jnp.zeros(shape, jnp.float32)] * 2 for _ in range(BASIS)]
    zero = jnp.zeros(shape, jnp.float32)
    one = jnp.ones(shape, jnp.float32)
    for point in range(points):
        angle = 2.0 * math.pi * (point + 0.5) / points
        shift = (GAMMA + RADIUS * math.cos(angle), RADIUS * math.sin(angle))
        scaled_shift = (H_SCALE * shift[0], H_SCALE * shift[1])
        limit = limits[point]
        product = (one, zero)
        products = [product]
        links = []
        pivot = (scaled_shift[0] - alphas[0], zero + scaled_shift[1])
        for i in range(ITERS):
            size = 1.0 / (pivot[0] * pivot[0] + pivot[1] * pivot[1])
            inverse = (pivot[0] * size, -pivot[1] * size)
            product = cmul(product, inverse)
            products.append(product)
            if i < ITERS - 1:
                link = (betas[i] * inverse[0], betas[i] * inverse[1])
                links.append(link)
                pivot = (scaled_shift[0] - alphas[i + 1] - link[0], scaled_shift[1] - link[1])
        solved = [None] * ITERS
        for i in reversed(range(ITERS)):
            value = (H_SCALE * products[i + 1][0], H_SCALE * products[i + 1][1])
            if i < ITERS - 1:
                step = cmul(links[i], solved[i + 1])
                value = (value[0] + step[0], value[1] + step[1])
            used = limit > i
            solved[i] = (jnp.where(used, value[0], 0.0), jnp.where(used, value[1], 0.0))
        applied = []
        for i in range(BASIS):
            left = limit == i
            rest = (
                jnp.where(left, products[i][0], 0.0),
                jnp.where(left, products[i][1], 0.0),
            )
            if i < ITERS:
                turned = (
                    shift[0] * solved[i][0] - shift[1] * solved[i][1],
                    shift[0] * solved[i][1] + shift[1] * solved[i][0],
                )
                rest = (rest[0] + turned[0], rest[1] + turned[1])
            if i == 0:
                rest = (rest[0] - 1.0, rest[1])
            applied.append(rest)
        tail = applied[ITERS]
        for back, factor in ((1, alphas[ITERS - 1]), (2, betas[ITERS - 2])):
            part = applied[ITERS - back]
            applied[ITERS - back] = (part[0] - factor * tail[0], part[1] - factor * tail[1])
        moment = moment_coeffs(point, points, count)
        for i in range(BASIS):
            left = solved[i] if i < ITERS else (zero, zero)
            both = (
                jnp.where(left_half, left[0], applied[i][0]),
                jnp.where(left_half, left[1], applied[i][1]),
            )
            term = cmul(moment, both)
            sums[i] = [sums[i][0] + term[0], sums[i][1] + term[1]]
    return [[jnp.where(own, part, 0.0) for part in pair] for pair in sums]


def exact_dot(first, second, dims):
    return lax.dot_general(
        first,
        second,
        (dims, ((), ())),
        precision=lax.Precision.HIGHEST,
        preferred_element_type=jnp.float32,
    )


def krylov_kernel(parts, count, *refs):
    blocks, vectors = refs[:parts], refs[parts : parts + BASIS]
    scalars, applied, diagonal = refs[parts + BASIS :]
    planes = diagonal.shape[0]
    depth = planes // parts
    groups = count // SUB
    lane = lax.broadcasted_iota(jnp.int32, (SUB, LANES), 1)
    last_x = lax.rem(lane, X_OUT) == X_OUT - 1
    first_x = lax.rem(lane, X_OUT) == 0
    here = lax.axis_index("dom")
    for turn in range(parts):
        slab = jnp.bitwise_xor(here, turn) * depth
        for deep in range(depth):
            for m in range(ROWS):
                start = (deep * ROWS + m) * count
                lanes = pl.ds(m * LANES, LANES)
                vectors[0][slab + deep, :, lanes] = blocks[turn][start : start + count, :]
            start = depth * ROWS * count + deep * ROWS
            levels = H_SCALE * (blocks[turn][start : start + ROWS, :] + 3.75)
            for m in range(ROWS):
                level = jnp.broadcast_to(levels[m : m + 1, :], (SUB, LANES))
                diagonal[slab + deep, :, m * LANES : (m + 1) * LANES] = level

    blank = jnp.zeros((SUB, LANES), jnp.float32)
    alphas, norms = [], []
    for i in range(ITERS):
        source, target = vectors[i], applied if i < ITERS - 1 else vectors[ITERS]

        def apply_turn(turn, sums, i=i, source=source, target=target):
            first = turn * TOGETHER
            new_sums = []
            for group in range(groups):
                rows = pl.ds(group * SUB, SUB)
                curve, norm = sums[group]
                done = apply_planes(source, diagonal, first, TOGETHER, group, last_x, first_x)
                for plane, (value, out) in enumerate(done):
                    for m in range(ROWS):
                        target[first + plane, rows, pl.ds(m * LANES, LANES)] = out[m]
                        curve = curve + value[m] * out[m]
                        if i == 0:
                            norm = norm + value[m] * value[m]
                new_sums.append((curve, norm))
            return tuple(new_sums)

        sums = lax.fori_loop(0, planes // TOGETHER, apply_turn, ((blank, blank),) * groups)
        if i == 0:
            norms.append([lane_sum(norm) for _, norm in sums])
        alphas.append([ratio(lane_sum(sums[g][0]), norms[i][g]) for g in range(groups)])
        if i == ITERS - 1:
            break
        betas = [ratio(norms[i][g], norms[i - 1][g]) for g in range(groups)] if i else None

        def step_turn(plane, sums, i=i, alpha=alphas[i], betas=betas):
            new_sums = []
            for group in range(groups):
                rows = pl.ds(group * SUB, SUB)
                norm = sums[group]
                for m in range(ROWS):
                    lanes = pl.ds(m * LANES, LANES)
                    value = applied[plane, rows, lanes]
                    value = value - alpha[group] * vectors[i][plane, rows, lanes]
                    if i:
                        value = value - betas[group] * vectors[i - 1][plane, rows, lanes]
                    vectors[i + 1][plane, rows, lanes] = value
                    norm = norm + value * value
                new_sums.append(norm)
            return tuple(new_sums)

        sums = lax.fori_loop(0, planes, step_turn, (blank,) * groups, unroll=TOGETHER)
        norms.append([lane_sum(norm) for norm in sums])
    for i, value in enumerate(alphas + norms):
        scalars[i] = jnp.concatenate(value, axis=0)


def gram_kernel(points, limits, scalars, *refs):
    vectors, (out_b, out_a, gram) = refs[:BASIS], refs[BASIS:]
    planes, count, _ = vectors[0].shape
    groups = count // SUB
    size = BASIS * count
    gram[...] = jnp.zeros_like(gram)

    def gram_turn(plane, carry):
        values = jnp.concatenate([vector[plane] for vector in vectors], axis=0)
        high = values.astype(jnp.bfloat16)
        low = (values - high.astype(jnp.float32)).astype(jnp.bfloat16)
        gram[...] += lax.dot_general(
            jnp.concatenate([high, low], axis=0),
            high,
            (((1,), (1,)), ((), ())),
            preferred_element_type=jnp.float32,
        )
        return carry

    lax.fori_loop(0, planes, gram_turn, 0, unroll=TOGETHER)
    cross = gram[size:, :]
    pairs = gram[:size, :] + cross + cross.T

    bounds = [jnp.concatenate([limits[j]] * groups, axis=0) for j in range(points)]
    alphas = [scalars[i] for i in range(ITERS)]
    norms = [scalars[ITERS + i] for i in range(ITERS)]
    weights = weights_of(alphas, norms, bounds, count)
    real = jnp.concatenate([pair[0] for pair in weights], axis=0)
    imag = jnp.concatenate([pair[1] for pair in weights], axis=0)
    right = exact_dot(pairs, jnp.concatenate([real, imag], axis=1), ((1,), (0,)))
    half = MOMENTS * count
    left = jnp.concatenate([real[:, :half], imag[:, :half]], axis=1)
    joined = exact_dot(left.T, right, ((1,), (0,)))
    scale = 1.0 / (planes * ROWS * LANES)
    width = 2 * half
    real = (joined[:half, :width] + joined[half:, width:]) * scale
    imag = (joined[:half, width:] - joined[half:, :width]) * scale
    out_b[0] = real[:, :half]
    out_b[1] = imag[:, :half]
    out_a[0] = real[:, half:]
    out_a[1] = imag[:, half:]


def swapped(values, axis, size, mask):
    return lax.ppermute(values, axis, [(index ^ mask, index) for index in range(size)])


def whole_grid(sources, potential, iter_counts, *, parts, points):
    count, depth, _ = sources.shape
    planes = parts * depth
    block, tile = packed_block(sources, potential, iter_counts)
    even = [block] + [swapped(block, "dom", parts, mask) for mask in range(CORES, parts, CORES)]
    limits = lax.all_gather(tile, "point")[:, :SUB]
    odd = [swapped(value, "dom", parts, 1) for value in even]
    blocks = [value for pair in zip(even, odd) for value in pair]
    vmem = pl.BlockSpec(memory_space=pltpu.VMEM)
    vector = (planes, count, ROWS * LANES)
    cells = planes * ROWS * LANES
    *vectors, scalars = pl.pallas_call(
        functools.partial(krylov_kernel, parts, count),
        out_shape=[jax.ShapeDtypeStruct(vector, jnp.float32)] * BASIS
        + [jax.ShapeDtypeStruct((2 * ITERS, count, LANES), jnp.float32)],
        in_specs=[vmem] * parts,
        out_specs=[vmem] * (BASIS + 1),
        scratch_shapes=[
            pltpu.VMEM(vector, jnp.float32),
            pltpu.VMEM((planes, SUB, ROWS * LANES), jnp.float32),
        ],
        compiler_params=pltpu.CompilerParams(vmem_limit_bytes=16 * 2**20),
        name="krylov",
    )(*blocks)
    size = BASIS * count
    width = MOMENTS * count
    out = jax.ShapeDtypeStruct((2, width, width), jnp.float32)
    return pl.pallas_call(
        functools.partial(gram_kernel, points),
        out_shape=(out, out),
        in_specs=[vmem] * (2 + BASIS),
        out_specs=(vmem, vmem),
        scratch_shapes=[pltpu.VMEM((2 * size, size), jnp.float32)],
        compiler_params=pltpu.CompilerParams(vmem_limit_bytes=16 * 2**20),
        name="gram",
    )(limits, scalars, *vectors)


def on_device(sources, potential, iter_counts):
    parts, points = lax.axis_size("dom"), lax.axis_size("point")
    count, depth, cells = sources.shape
    held = BASIS * count * parts * depth * cells * 4
    fits = (
        held <= 16 * 2**20
        and parts == 8
        and points == 4
        and count == 2 * SUB
        and 2 * MOMENTS * count == LANES
        and parts * depth == 16
        and cells == GX * GX == ROWS * LANES
    )
    if not fits:
        return split_grid(sources, potential, iter_counts)
    return whole_grid(sources, potential, iter_counts, parts=parts, points=points)


def solution(mesh):
    placed = (P(None, "dom", None), P("dom", None), P("point"))
    return jax.shard_map(
        on_device, mesh=mesh, in_specs=placed, out_specs=(P(), P()), check_vma=False
    )
```

```python
import functools
import math

import jax
import jax.numpy as jnp
from jax import lax
from jax.experimental import pallas as pl
from jax.experimental.pallas import tpu as pltpu
from jax.sharding import PartitionSpec as P

MOMENTS = 4
ITERS = 6
GX = 32


COEF_NEAR = 4.0 / 3.0
COEF_FAR = -1.0 / 12.0
GAMMA = 2.0
RADIUS = 1.5


def padded_2(block, sides, width):
    for axis, dim in sides:
        count = lax.axis_size(axis)
        forward = [(i, i + 1) for i in range(count - 1)]
        forward.append((count - 1, 0))
        backward = [(target, source) for source, target in forward]
        low = lax.ppermute(
            lax.slice_in_dim(block, block.shape[dim] - width, None, axis=dim), axis, forward
        )
        high = lax.ppermute(lax.slice_in_dim(block, 0, width, axis=dim), axis, backward)
        block = jnp.concatenate([low, block, high], axis=dim)
    return block


def plane_terms(values, side):
    lead = values.shape[:-1]
    planes = values.reshape(lead + (side, side))
    summed = COEF_NEAR * (
        jnp.roll(planes, 1, -2)
        + jnp.roll(planes, -1, -2)
        + jnp.roll(planes, 1, -1)
        + jnp.roll(planes, -1, -1)
    )
    summed = summed + COEF_FAR * (
        jnp.roll(planes, 2, -2)
        + jnp.roll(planes, -2, -2)
        + jnp.roll(planes, 2, -1)
        + jnp.roll(planes, -2, -1)
    )
    return summed.reshape(values.shape)


def complex_mul(first, second):
    return jnp.stack(
        [first[0] * second[0] - first[1] * second[1], first[0] * second[1] + first[1] * second[0]]
    )


def complex_div(first, second):
    denom = second[0] * second[0] + second[1] * second[1]
    return jnp.stack(
        [
            (first[0] * second[0] + first[1] * second[1]) / denom,
            (first[1] * second[0] - first[0] * second[1]) / denom,
        ]
    )


def bilinear(first, second):
    real_part = jnp.sum(first[0] * second[0] - first[1] * second[1], axis=(1, 2))
    imag_part = jnp.sum(first[0] * second[1] + first[1] * second[0], axis=(1, 2))
    return jnp.stack([real_part, imag_part])


def scaled(coeffs, values):
    return complex_mul(coeffs[:, :, None, None], values)


def shifted(values, potential, shift_re, shift_im):
    padded = padded_2(values, (("dom", 2),), 2)
    depth = values.shape[2]
    lap = -7.5 * values + plane_terms(values, GX)
    lap = lap + COEF_NEAR * (padded[:, :, 3 : 3 + depth] + padded[:, :, 1 : 1 + depth])
    lap = lap + COEF_FAR * (padded[:, :, 4 : 4 + depth] + padded[:, :, 0:depth])
    applied = -0.5 * lap + potential * values
    return jnp.stack(
        [
            shift_re * values[0] - shift_im * values[1] - applied[0],
            shift_re * values[1] + shift_im * values[0] - applied[1],
        ]
    )


def residual_sum(values):
    return lax.psum(bilinear(values, values), "dom")


def moment_terms(solution, residual, sources, angle_now, shift_re, shift_im):
    applied = jnp.stack(
        [
            shift_re * solution[0] - shift_im * solution[1] - sources[0] + residual[0],
            shift_re * solution[1] + shift_im * solution[0] - sources[1] + residual[1],
        ]
    )
    angles = (jnp.arange(MOMENTS).astype(jnp.float32) + 1.0) * angle_now
    coeffs = 0.25 * jnp.stack([jnp.cos(angles), jnp.sin(angles)])
    s_terms = complex_mul(coeffs[:, :, None, None, None], solution[:, None])
    h_terms = complex_mul(coeffs[:, :, None, None, None], applied[:, None])
    width = MOMENTS * solution.shape[1]
    return (s_terms.reshape(2, width, -1), h_terms.reshape(2, width, -1))


def gram_of(left, right):
    width = left.shape[1]
    joined = lax.dot_general(
        left.reshape(2 * width, -1),
        right.reshape(2 * width, -1),
        (((1,), (1,)), ((), ())),
        precision=lax.Precision.HIGHEST,
        preferred_element_type=jnp.float32,
    )
    blocks = joined.reshape(2, width, 2, width)
    return jnp.stack([blocks[0, :, 0] + blocks[1, :, 1], blocks[0, :, 1] - blocks[1, :, 0]])


def split_grid(sources, potential, iter_counts):
    complex_src = jnp.stack([sources, jnp.zeros_like(sources)])
    angle_now = (
        2.0 * math.pi * (lax.axis_index("point").astype(jnp.float32) + 0.5) / lax.axis_size("point")
    )
    shift_re = GAMMA + RADIUS * jnp.cos(angle_now)
    shift_im = RADIUS * jnp.sin(angle_now)
    limit = iter_counts[0]
    solution = jnp.zeros_like(complex_src)

    def one_turn(turn_idx, state):
        solution, residual, search, norm_now = state
        product = shifted(search, potential, shift_re, shift_im)
        curve = lax.psum(bilinear(search, product), "dom")
        step_size = complex_div(norm_now, curve)
        new_residual = residual - scaled(step_size, product)
        norm_next = residual_sum(new_residual)
        fresh = (
            solution + scaled(step_size, search),
            new_residual,
            new_residual + scaled(complex_div(norm_next, norm_now), search),
            norm_next,
        )
        keep_mask = turn_idx < limit
        return jax.tree.map(lambda newer, older: jnp.where(keep_mask, newer, older), fresh, state)

    start = (solution, complex_src, complex_src, residual_sum(complex_src))
    solution, residual, search, norm_now = lax.fori_loop(0, ITERS, one_turn, start)
    s_terms, h_terms = moment_terms(solution, residual, complex_src, angle_now, shift_re, shift_im)
    cells = sources.shape[1] * sources.shape[2] * lax.axis_size("dom")
    s_total, h_total = lax.psum((s_terms, h_terms), "point")
    gram_b, gram_a = lax.psum((gram_of(s_total, s_total), gram_of(s_total, h_total)), "dom")
    return (gram_b / cells, gram_a / cells)


Y_IN, X_IN = 2, 4
Y_OUT, X_OUT = GX // Y_IN, GX // X_IN
ROWS = Y_IN * X_IN
LANES = Y_OUT * X_OUT
SUB = 8
BASIS = ITERS + 1
CORES = 2
TOGETHER = 2
UNROLL = 4
H_SCALE = 2.0 / COEF_NEAR
FAR_SCALED = 0.5 * H_SCALE * COEF_FAR


def pack_kernel(depth, groups, counts, rows, out, tile):
    columns = rows.shape[0] // (SUB * groups * depth + depth)
    first_level = columns * SUB * groups * depth
    source = lax.broadcasted_iota(jnp.int32, (LANES, LANES), 0)
    target = lax.broadcasted_iota(jnp.int32, (LANES, LANES), 1)
    inner = target // (LANES // ROWS)
    outer = target % (LANES // ROWS)
    cell = (outer // X_OUT * Y_IN + inner // X_IN) * GX + outer % X_OUT * X_IN + inner % X_IN
    swap = jnp.where(source == cell, 1.0, 0.0).astype(jnp.float32)
    parts = []
    for deep in range(depth):
        for group in range(groups):
            for column in range(columns):
                start = (group * SUB * columns + column) * depth + deep
                parts.append(rows[pl.ds(start, SUB, stride=columns * depth), :])
        parts.append(rows[pl.ds(first_level + deep, columns, stride=depth), :])
    mixed = exact_dot(jnp.concatenate(parts, axis=0), swap, ((1,), (0,)))
    block = LANES // ROWS
    lane_block = lax.broadcasted_iota(jnp.int32, (SUB, LANES), 1) // block
    row = lax.broadcasted_iota(jnp.int32, (SUB, LANES), 0)
    for deep in range(depth):
        base = deep * (groups + 1) * columns * SUB - deep * (columns - 1) * SUB
        for group in range(groups):
            pieces = [
                mixed[base + (group * columns + column) * SUB :][:SUB] for column in range(columns)
            ]
            for m in range(ROWS):
                value = pieces[m]
                for column in range(columns):
                    if column != m:
                        moved = pltpu.roll(pieces[column], (column - m) * block % LANES, 1)
                        value = jnp.where(lane_block == column, moved, value)
                start = ((deep * ROWS + m) * groups + group) * SUB
                out[start : start + SUB, :] = value
        piece = mixed[base + groups * columns * SUB :][:SUB]
        value = piece
        for far in range(1, columns):
            moved = pltpu.roll(pltpu.roll(piece, far * block, 1), columns - far, 0)
            value = jnp.where(lane_block == (row + far) % columns, moved, value)
        start = depth * ROWS * SUB * groups + deep * ROWS
        out[start : start + ROWS, :] = value
    tile[...] = jnp.broadcast_to(counts[...].astype(jnp.float32), (SUB, LANES))


def packed_block(sources, potential, iter_counts):
    count, depth, cells = sources.shape
    columns = cells // LANES
    rows = sources.reshape(count, depth, columns, LANES).transpose(0, 2, 1, 3).reshape(-1, LANES)
    levels = potential.reshape(depth, columns, LANES).transpose(1, 0, 2).reshape(-1, LANES)
    vmem = pl.BlockSpec(memory_space=pltpu.VMEM)
    size = depth * ROWS * (count + 1)
    return pl.pallas_call(
        functools.partial(pack_kernel, depth, count // SUB),
        out_shape=(
            jax.ShapeDtypeStruct((size, LANES), jnp.float32),
            jax.ShapeDtypeStruct((SUB, LANES), jnp.float32),
        ),
        in_specs=[vmem, vmem],
        out_specs=(vmem, vmem),
        compiler_params=pltpu.CompilerParams(vmem_limit_bytes=4 * 2**20),
        name="pack",
    )(iter_counts.reshape(1, 1), jnp.concatenate([rows, levels], axis=0))


def lane_sum(values):
    return jnp.broadcast_to(jnp.sum(values, axis=1, keepdims=True), values.shape)


def ratio(top, bottom):
    return jnp.where(bottom > 0.0, top / jnp.where(bottom > 0.0, bottom, 1.0), 0.0)


def x_next(values, wrap_mask):
    return jnp.where(wrap_mask, pltpu.roll(values, X_OUT - 1, 1), pltpu.roll(values, LANES - 1, 1))


def x_prev(values, wrap_mask):
    return jnp.where(wrap_mask, pltpu.roll(values, LANES - X_OUT + 1, 1), pltpu.roll(values, 1, 1))


def apply_planes(vector, diagonal, first, count, group, last_x, first_x):
    planes = vector.shape[0]
    rows = pl.ds(group * SUB, SUB)
    held = {}
    for far in range(-2, count + 2):
        index = jnp.bitwise_and(first + (far + planes), planes - 1)
        held[far] = [vector[index, rows, pl.ds(m * LANES, LANES)] for m in range(ROWS)]
    for plane in range(count):
        here, above, below = held[plane], held[plane + 1], held[plane - 1]
        above_2, below_2 = held[plane + 2], held[plane - 2]
        y_up = [pltpu.roll(value, LANES - X_OUT, 1) for value in here]
        y_down = [pltpu.roll(value, X_OUT, 1) for value in here]
        out = []
        for yi in range(Y_IN):
            line = here[yi * X_IN : (yi + 1) * X_IN]
            before = [x_prev(value, first_x) for value in line[X_IN - 2 :]]
            after = [x_next(value, last_x) for value in line[:2]]
            wide = before + line + after
            for xi in range(X_IN):
                m = yi * X_IN + xi
                other = (1 - yi) * X_IN + xi
                y_next = here[other] if yi == 0 else y_up[other]
                y_prev = here[other] if yi == 1 else y_down[other]
                near = (wide[xi + 1] + wide[xi + 3]) + (y_next + y_prev) + (above[m] + below[m])
                far = (wide[xi] + wide[xi + 4]) + (y_up[m] + y_down[m])
                far = far + (above_2[m] + below_2[m])
                level = diagonal[first + plane, :, pl.ds(m * LANES, LANES)]
                out.append(level * here[m] - near - FAR_SCALED * far)
        yield here, out


def cmul(first, second):
    return (
        first[0] * second[0] - first[1] * second[1],
        first[0] * second[1] + first[1] * second[0],
    )


def moment_coeffs(point, points, count):
    lane = lax.broadcasted_iota(jnp.int32, (1, LANES), 1)
    moment = lax.rem(lane, MOMENTS * count) // count
    angle = 2.0 * math.pi * (point + 0.5) / points
    parts = []
    for func in (math.cos, math.sin):
        value = jnp.full((1, LANES), 0.25 * func(angle), jnp.float32)
        for k in range(1, MOMENTS):
            value = jnp.where(moment == k, 0.25 * func((k + 1) * angle), value)
        parts.append(value)
    return parts


def weights_of(alphas, norms, limits, count):
    points = len(limits)
    shape = (count, LANES)
    half = MOMENTS * count
    lane = lax.broadcasted_iota(jnp.int32, shape, 1)
    source = lax.broadcasted_iota(jnp.int32, shape, 0)
    own = lax.rem(lane, count) == source
    left_half = lane < half
    betas = [ratio(norms[i + 1], norms[i]) for i in range(ITERS - 1)]
    sums = [[jnp.zeros(shape, jnp.float32)] * 2 for _ in range(BASIS)]
    zero = jnp.zeros(shape, jnp.float32)
    one = jnp.ones(shape, jnp.float32)
    for point in range(points):
        angle = 2.0 * math.pi * (point + 0.5) / points
        shift = (GAMMA + RADIUS * math.cos(angle), RADIUS * math.sin(angle))
        scaled_shift = (H_SCALE * shift[0], H_SCALE * shift[1])
        limit = limits[point]
        product = (one, zero)
        products = [product]
        links = []
        pivot = (scaled_shift[0] - alphas[0], zero + scaled_shift[1])
        for i in range(ITERS):
            size = 1.0 / (pivot[0] * pivot[0] + pivot[1] * pivot[1])
            inverse = (pivot[0] * size, -pivot[1] * size)
            product = cmul(product, inverse)
            products.append(product)
            if i < ITERS - 1:
                link = (betas[i] * inverse[0], betas[i] * inverse[1])
                links.append(link)
                pivot = (scaled_shift[0] - alphas[i + 1] - link[0], scaled_shift[1] - link[1])
        solved = [None] * ITERS
        for i in reversed(range(ITERS)):
            value = (H_SCALE * products[i + 1][0], H_SCALE * products[i + 1][1])
            if i < ITERS - 1:
                step = cmul(links[i], solved[i + 1])
                value = (value[0] + step[0], value[1] + step[1])
            used = limit > i
            solved[i] = (jnp.where(used, value[0], 0.0), jnp.where(used, value[1], 0.0))
        applied = []
        for i in range(BASIS):
            left = limit == i
            rest = (
                jnp.where(left, products[i][0], 0.0),
                jnp.where(left, products[i][1], 0.0),
            )
            if i < ITERS:
                turned = (
                    shift[0] * solved[i][0] - shift[1] * solved[i][1],
                    shift[0] * solved[i][1] + shift[1] * solved[i][0],
                )
                rest = (rest[0] + turned[0], rest[1] + turned[1])
            if i == 0:
                rest = (rest[0] - 1.0, rest[1])
            applied.append(rest)
        tail = applied[ITERS]
        for back, factor in ((1, alphas[ITERS - 1]), (2, betas[ITERS - 2])):
            part = applied[ITERS - back]
            applied[ITERS - back] = (part[0] - factor * tail[0], part[1] - factor * tail[1])
        moment = moment_coeffs(point, points, count)
        for i in range(BASIS):
            left = solved[i] if i < ITERS else (zero, zero)
            both = (
                jnp.where(left_half, left[0], applied[i][0]),
                jnp.where(left_half, left[1], applied[i][1]),
            )
            term = cmul(moment, both)
            sums[i] = [sums[i][0] + term[0], sums[i][1] + term[1]]
    return [[jnp.where(own, part, 0.0) for part in pair] for pair in sums]


def exact_dot(first, second, dims):
    return lax.dot_general(
        first,
        second,
        (dims, ((), ())),
        precision=lax.Precision.HIGHEST,
        preferred_element_type=jnp.float32,
    )


def krylov_kernel(parts, count, *refs):
    blocks, vectors = refs[:parts], refs[parts : parts + BASIS]
    scalars, applied, diagonal = refs[parts + BASIS :]
    planes = diagonal.shape[0]
    depth = planes // parts
    groups = count // SUB
    lane = lax.broadcasted_iota(jnp.int32, (SUB, LANES), 1)
    last_x = lax.rem(lane, X_OUT) == X_OUT - 1
    first_x = lax.rem(lane, X_OUT) == 0
    here = lax.axis_index("dom")
    for turn in range(parts):
        slab = jnp.bitwise_xor(here, turn) * depth
        for deep in range(depth):
            for m in range(ROWS):
                start = (deep * ROWS + m) * count
                lanes = pl.ds(m * LANES, LANES)
                vectors[0][slab + deep, :, lanes] = blocks[turn][start : start + count, :]
            start = depth * ROWS * count + deep * ROWS
            levels = H_SCALE * (blocks[turn][start : start + ROWS, :] + 3.75)
            for m in range(ROWS):
                level = jnp.broadcast_to(levels[m : m + 1, :], (SUB, LANES))
                diagonal[slab + deep, :, m * LANES : (m + 1) * LANES] = level

    blank = jnp.zeros((SUB, LANES), jnp.float32)
    alphas, norms = [], []
    for i in range(ITERS):
        source, target = vectors[i], applied if i < ITERS - 1 else vectors[ITERS]

        def apply_turn(turn, sums, i=i, source=source, target=target):
            first = turn * TOGETHER
            new_sums = []
            for group in range(groups):
                rows = pl.ds(group * SUB, SUB)
                curve, norm = sums[group]
                done = apply_planes(source, diagonal, first, TOGETHER, group, last_x, first_x)
                for plane, (value, out) in enumerate(done):
                    for m in range(ROWS):
                        target[first + plane, rows, pl.ds(m * LANES, LANES)] = out[m]
                        curve = curve + value[m] * out[m]
                        if i == 0:
                            norm = norm + value[m] * value[m]
                new_sums.append((curve, norm))
            return tuple(new_sums)

        start = ((blank, blank),) * groups
        sums = lax.fori_loop(0, planes // TOGETHER, apply_turn, start, unroll=2)
        if i == 0:
            norms.append([lane_sum(norm) for _, norm in sums])
        alphas.append([ratio(lane_sum(sums[g][0]), norms[i][g]) for g in range(groups)])
        if i == ITERS - 1:
            break
        betas = [ratio(norms[i][g], norms[i - 1][g]) for g in range(groups)] if i else None

        def step_turn(plane, sums, i=i, alpha=alphas[i], betas=betas):
            new_sums = []
            for group in range(groups):
                rows = pl.ds(group * SUB, SUB)
                norm = sums[group]
                for m in range(ROWS):
                    lanes = pl.ds(m * LANES, LANES)
                    value = applied[plane, rows, lanes]
                    value = value - alpha[group] * vectors[i][plane, rows, lanes]
                    if i:
                        value = value - betas[group] * vectors[i - 1][plane, rows, lanes]
                    vectors[i + 1][plane, rows, lanes] = value
                    norm = norm + value * value
                new_sums.append(norm)
            return tuple(new_sums)

        sums = lax.fori_loop(0, planes, step_turn, (blank,) * groups, unroll=UNROLL)
        norms.append([lane_sum(norm) for norm in sums])
    for i, value in enumerate(alphas + norms):
        scalars[i] = jnp.concatenate(value, axis=0)


def gram_kernel(points, scalars, *refs):
    tiles, vectors = refs[:points], refs[points : points + BASIS]
    out_b, out_a, gram, limits = refs[points + BASIS :]
    planes, count, _ = vectors[0].shape
    groups = count // SUB
    size = BASIS * count
    gram[...] = jnp.zeros_like(gram)

    def gram_turn(plane, carry):
        values = jnp.concatenate([vector[plane] for vector in vectors], axis=0)
        high = values.astype(jnp.bfloat16)
        low = (values - high.astype(jnp.float32)).astype(jnp.bfloat16)
        gram[...] += lax.dot_general(
            jnp.concatenate([high, low], axis=0),
            high,
            (((1,), (1,)), ((), ())),
            preferred_element_type=jnp.float32,
        )
        return carry

    lax.fori_loop(0, planes, gram_turn, 0, unroll=UNROLL)
    cross = gram[size:, :]
    pairs = gram[:size, :] + cross + cross.T

    here = lax.axis_index("point")
    core = jnp.bitwise_and(lax.axis_index("dom"), CORES - 1)
    for far, tile in zip((0, 1 + core, 3, 2 - core), tiles):
        limits[jnp.bitwise_xor(here, far)] = tile[...]
    bounds = [jnp.concatenate([limits[j]] * groups, axis=0) for j in range(points)]
    alphas = [scalars[i] for i in range(ITERS)]
    norms = [scalars[ITERS + i] for i in range(ITERS)]
    weights = weights_of(alphas, norms, bounds, count)
    real = jnp.concatenate([pair[0] for pair in weights], axis=0)
    imag = jnp.concatenate([pair[1] for pair in weights], axis=0)
    right = exact_dot(pairs, jnp.concatenate([real, imag], axis=1), ((1,), (0,)))
    half = MOMENTS * count
    left = jnp.concatenate([real[:, :half], imag[:, :half]], axis=1)
    joined = exact_dot(left.T, right, ((1,), (0,)))
    scale = 1.0 / (planes * ROWS * LANES)
    width = 2 * half
    real = (joined[:half, :width] + joined[half:, width:]) * scale
    imag = (joined[:half, width:] - joined[half:, :width]) * scale
    out_b[0] = real[:, :half]
    out_b[1] = imag[:, :half]
    out_a[0] = real[:, half:]
    out_a[1] = imag[:, half:]


def swapped(values, axis, size, mask):
    return lax.ppermute(values, axis, [(index ^ mask, index) for index in range(size)])


def whole_grid(sources, potential, iter_counts, *, parts, points):
    count, depth, _ = sources.shape
    planes = parts * depth
    block, tile = packed_block(sources, potential, iter_counts)
    even = [block] + [swapped(block, "dom", parts, mask) for mask in range(CORES, parts, CORES)]
    mixed = [
        ((point ^ (1 + part % CORES)) * parts + part, point * parts + part)
        for point in range(points)
        for part in range(parts)
    ]
    tiles = [lax.ppermute(tile, ("point", "dom"), mixed), swapped(tile, "point", points, 3)]
    even[1], *tiles = lax.optimization_barrier((even[1], *tiles))
    tiles.append(swapped(tiles[0], "dom", parts, 1))
    odd = [swapped(value, "dom", parts, 1) for value in even]
    blocks = [value for pair in zip(even, odd) for value in pair]
    vmem = pl.BlockSpec(memory_space=pltpu.VMEM)
    vector = (planes, count, ROWS * LANES)
    cells = planes * ROWS * LANES
    *vectors, scalars = pl.pallas_call(
        functools.partial(krylov_kernel, parts, count),
        out_shape=[jax.ShapeDtypeStruct(vector, jnp.float32)] * BASIS
        + [jax.ShapeDtypeStruct((2 * ITERS, count, LANES), jnp.float32)],
        in_specs=[vmem] * parts,
        out_specs=[vmem] * (BASIS + 1),
        scratch_shapes=[
            pltpu.VMEM(vector, jnp.float32),
            pltpu.VMEM((planes, SUB, ROWS * LANES), jnp.float32),
        ],
        compiler_params=pltpu.CompilerParams(vmem_limit_bytes=16 * 2**20),
        name="krylov",
    )(*blocks)
    size = BASIS * count
    width = MOMENTS * count
    out = jax.ShapeDtypeStruct((2, width, width), jnp.float32)
    return pl.pallas_call(
        functools.partial(gram_kernel, points),
        out_shape=(out, out),
        in_specs=[vmem] * (1 + points + BASIS),
        out_specs=(vmem, vmem),
        scratch_shapes=[
            pltpu.VMEM((2 * size, size), jnp.float32),
            pltpu.VMEM((points, SUB, LANES), jnp.float32),
        ],
        compiler_params=pltpu.CompilerParams(vmem_limit_bytes=16 * 2**20),
        name="gram",
    )(scalars, tile, *tiles, *vectors)


def on_device(sources, potential, iter_counts):
    parts, points = lax.axis_size("dom"), lax.axis_size("point")
    count, depth, cells = sources.shape
    held = BASIS * count * parts * depth * cells * 4
    fits = (
        held <= 16 * 2**20
        and parts == 8
        and points == 4
        and count == 2 * SUB
        and 2 * MOMENTS * count == LANES
        and parts * depth == 16
        and cells == GX * GX == ROWS * LANES
    )
    if not fits:
        return split_grid(sources, potential, iter_counts)
    return whole_grid(sources, potential, iter_counts, parts=parts, points=points)


def solution(mesh):
    placed = (P(None, "dom", None), P("dom", None), P("point"))
    return jax.shard_map(
        on_device, mesh=mesh, in_specs=placed, out_specs=(P(), P()), check_vma=False
    )
```

```python
import functools
import math

import jax
import jax.numpy as jnp
from jax import lax
from jax.experimental import pallas as pl
from jax.experimental.pallas import tpu as pltpu
from jax.sharding import PartitionSpec as P

MOMENTS = 4
ITERS = 6
GX = 32


COEF_NEAR = 4.0 / 3.0
COEF_FAR = -1.0 / 12.0
GAMMA = 2.0
RADIUS = 1.5


def padded_2(block, sides, width):
    for axis, dim in sides:
        count = lax.axis_size(axis)
        forward = [(i, i + 1) for i in range(count - 1)]
        forward.append((count - 1, 0))
        backward = [(target, source) for source, target in forward]
        low = lax.ppermute(
            lax.slice_in_dim(block, block.shape[dim] - width, None, axis=dim), axis, forward
        )
        high = lax.ppermute(lax.slice_in_dim(block, 0, width, axis=dim), axis, backward)
        block = jnp.concatenate([low, block, high], axis=dim)
    return block


def plane_terms(values, side):
    lead = values.shape[:-1]
    planes = values.reshape(lead + (side, side))
    summed = COEF_NEAR * (
        jnp.roll(planes, 1, -2)
        + jnp.roll(planes, -1, -2)
        + jnp.roll(planes, 1, -1)
        + jnp.roll(planes, -1, -1)
    )
    summed = summed + COEF_FAR * (
        jnp.roll(planes, 2, -2)
        + jnp.roll(planes, -2, -2)
        + jnp.roll(planes, 2, -1)
        + jnp.roll(planes, -2, -1)
    )
    return summed.reshape(values.shape)


def complex_mul(first, second):
    return jnp.stack(
        [first[0] * second[0] - first[1] * second[1], first[0] * second[1] + first[1] * second[0]]
    )


def complex_div(first, second):
    denom = second[0] * second[0] + second[1] * second[1]
    return jnp.stack(
        [
            (first[0] * second[0] + first[1] * second[1]) / denom,
            (first[1] * second[0] - first[0] * second[1]) / denom,
        ]
    )


def bilinear(first, second):
    real_part = jnp.sum(first[0] * second[0] - first[1] * second[1], axis=(1, 2))
    imag_part = jnp.sum(first[0] * second[1] + first[1] * second[0], axis=(1, 2))
    return jnp.stack([real_part, imag_part])


def scaled(coeffs, values):
    return complex_mul(coeffs[:, :, None, None], values)


def shifted(values, potential, shift_re, shift_im):
    padded = padded_2(values, (("dom", 2),), 2)
    depth = values.shape[2]
    lap = -7.5 * values + plane_terms(values, GX)
    lap = lap + COEF_NEAR * (padded[:, :, 3 : 3 + depth] + padded[:, :, 1 : 1 + depth])
    lap = lap + COEF_FAR * (padded[:, :, 4 : 4 + depth] + padded[:, :, 0:depth])
    applied = -0.5 * lap + potential * values
    return jnp.stack(
        [
            shift_re * values[0] - shift_im * values[1] - applied[0],
            shift_re * values[1] + shift_im * values[0] - applied[1],
        ]
    )


def residual_sum(values):
    return lax.psum(bilinear(values, values), "dom")


def moment_terms(solution, residual, sources, angle_now, shift_re, shift_im):
    applied = jnp.stack(
        [
            shift_re * solution[0] - shift_im * solution[1] - sources[0] + residual[0],
            shift_re * solution[1] + shift_im * solution[0] - sources[1] + residual[1],
        ]
    )
    angles = (jnp.arange(MOMENTS).astype(jnp.float32) + 1.0) * angle_now
    coeffs = 0.25 * jnp.stack([jnp.cos(angles), jnp.sin(angles)])
    s_terms = complex_mul(coeffs[:, :, None, None, None], solution[:, None])
    h_terms = complex_mul(coeffs[:, :, None, None, None], applied[:, None])
    width = MOMENTS * solution.shape[1]
    return (s_terms.reshape(2, width, -1), h_terms.reshape(2, width, -1))


def gram_of(left, right):
    width = left.shape[1]
    joined = lax.dot_general(
        left.reshape(2 * width, -1),
        right.reshape(2 * width, -1),
        (((1,), (1,)), ((), ())),
        precision=lax.Precision.HIGHEST,
        preferred_element_type=jnp.float32,
    )
    blocks = joined.reshape(2, width, 2, width)
    return jnp.stack([blocks[0, :, 0] + blocks[1, :, 1], blocks[0, :, 1] - blocks[1, :, 0]])


def split_grid(sources, potential, iter_counts):
    complex_src = jnp.stack([sources, jnp.zeros_like(sources)])
    angle_now = (
        2.0 * math.pi * (lax.axis_index("point").astype(jnp.float32) + 0.5) / lax.axis_size("point")
    )
    shift_re = GAMMA + RADIUS * jnp.cos(angle_now)
    shift_im = RADIUS * jnp.sin(angle_now)
    limit = iter_counts[0]
    solution = jnp.zeros_like(complex_src)

    def one_turn(turn_idx, state):
        solution, residual, search, norm_now = state
        product = shifted(search, potential, shift_re, shift_im)
        curve = lax.psum(bilinear(search, product), "dom")
        step_size = complex_div(norm_now, curve)
        new_residual = residual - scaled(step_size, product)
        norm_next = residual_sum(new_residual)
        fresh = (
            solution + scaled(step_size, search),
            new_residual,
            new_residual + scaled(complex_div(norm_next, norm_now), search),
            norm_next,
        )
        keep_mask = turn_idx < limit
        return jax.tree.map(lambda newer, older: jnp.where(keep_mask, newer, older), fresh, state)

    start = (solution, complex_src, complex_src, residual_sum(complex_src))
    solution, residual, search, norm_now = lax.fori_loop(0, ITERS, one_turn, start)
    s_terms, h_terms = moment_terms(solution, residual, complex_src, angle_now, shift_re, shift_im)
    cells = sources.shape[1] * sources.shape[2] * lax.axis_size("dom")
    s_total, h_total = lax.psum((s_terms, h_terms), "point")
    gram_b, gram_a = lax.psum((gram_of(s_total, s_total), gram_of(s_total, h_total)), "dom")
    return (gram_b / cells, gram_a / cells)


Y_IN, X_IN = 2, 4
Y_OUT, X_OUT = GX // Y_IN, GX // X_IN
ROWS = Y_IN * X_IN
LANES = Y_OUT * X_OUT
SUB = 8
BASIS = ITERS + 1
CORES = 2
TOGETHER = 2
UNROLL = 4
H_SCALE = 2.0 / COEF_NEAR
FAR_SCALED = 0.5 * H_SCALE * COEF_FAR


def pack_kernel(depth, groups, counts, rows, out, tile):
    columns = rows.shape[0] // (SUB * groups * depth + depth)
    first_level = columns * SUB * groups * depth
    source = lax.broadcasted_iota(jnp.int32, (LANES, LANES), 0)
    target = lax.broadcasted_iota(jnp.int32, (LANES, LANES), 1)
    inner = target // (LANES // ROWS)
    outer = target % (LANES // ROWS)
    cell = (outer // X_OUT * Y_IN + inner // X_IN) * GX + outer % X_OUT * X_IN + inner % X_IN
    swap = jnp.where(source == cell, 1.0, 0.0).astype(jnp.float32)
    parts = []
    for deep in range(depth):
        for group in range(groups):
            for column in range(columns):
                start = (group * SUB * columns + column) * depth + deep
                parts.append(rows[pl.ds(start, SUB, stride=columns * depth), :])
        parts.append(rows[pl.ds(first_level + deep, columns, stride=depth), :])
    mixed = exact_dot(jnp.concatenate(parts, axis=0), swap, ((1,), (0,)))
    block = LANES // ROWS
    lane_block = lax.broadcasted_iota(jnp.int32, (SUB, LANES), 1) // block
    row = lax.broadcasted_iota(jnp.int32, (SUB, LANES), 0)
    for deep in range(depth):
        base = deep * (groups + 1) * columns * SUB - deep * (columns - 1) * SUB
        for group in range(groups):
            pieces = [
                mixed[base + (group * columns + column) * SUB :][:SUB] for column in range(columns)
            ]
            for m in range(ROWS):
                value = pieces[m]
                for column in range(columns):
                    if column != m:
                        moved = pltpu.roll(pieces[column], (column - m) * block % LANES, 1)
                        value = jnp.where(lane_block == column, moved, value)
                start = ((deep * ROWS + m) * groups + group) * SUB
                out[start : start + SUB, :] = value
        piece = mixed[base + groups * columns * SUB :][:SUB]
        value = piece
        for far in range(1, columns):
            moved = pltpu.roll(pltpu.roll(piece, far * block, 1), columns - far, 0)
            value = jnp.where(lane_block == (row + far) % columns, moved, value)
        start = depth * ROWS * SUB * groups + deep * ROWS
        out[start : start + ROWS, :] = value
    tile[...] = jnp.broadcast_to(counts[...].astype(jnp.float32), (SUB, LANES))


def packed_block(sources, potential, iter_counts):
    count, depth, cells = sources.shape
    columns = cells // LANES
    rows = sources.reshape(count, depth, columns, LANES).transpose(0, 2, 1, 3).reshape(-1, LANES)
    levels = potential.reshape(depth, columns, LANES).transpose(1, 0, 2).reshape(-1, LANES)
    vmem = pl.BlockSpec(memory_space=pltpu.VMEM)
    size = depth * ROWS * (count + 1)
    return pl.pallas_call(
        functools.partial(pack_kernel, depth, count // SUB),
        out_shape=(
            jax.ShapeDtypeStruct((size, LANES), jnp.float32),
            jax.ShapeDtypeStruct((SUB, LANES), jnp.float32),
        ),
        in_specs=[vmem, vmem],
        out_specs=(vmem, vmem),
        compiler_params=pltpu.CompilerParams(vmem_limit_bytes=4 * 2**20),
        name="pack",
    )(iter_counts.reshape(1, 1), jnp.concatenate([rows, levels], axis=0))


def lane_sum(values):
    return jnp.broadcast_to(jnp.sum(values, axis=1, keepdims=True), values.shape)


def ratio(top, bottom):
    return jnp.where(bottom > 0.0, top / jnp.where(bottom > 0.0, bottom, 1.0), 0.0)


def tree_sum(values):
    while len(values) > 1:
        values = [sum(values[i : i + 2][1:], values[i]) for i in range(0, len(values), 2)]
    return values[0]


def apply_planes(vector, diagonal, first, count, group, last_x, first_x):
    planes = vector.shape[0]
    rows = pl.ds(group * SUB, SUB)
    held = {}
    for far in range(-2, count + 2):
        index = jnp.bitwise_and(first + (far + planes), planes - 1)
        held[far] = [vector[index, rows, pl.ds(m * LANES, LANES)] for m in range(ROWS)]
    for plane in range(count):
        here, above, below = held[plane], held[plane + 1], held[plane - 1]
        above_2, below_2 = held[plane + 2], held[plane - 2]
        y_up = [pltpu.roll(value, LANES - X_OUT, 1) for value in here]
        y_down = [pltpu.roll(value, X_OUT, 1) for value in here]
        out = []
        for yi in range(Y_IN):
            line = here[yi * X_IN : (yi + 1) * X_IN]
            before = [
                pltpu.roll(jnp.where(last_x, y_up[yi * X_IN + xi], line[xi]), 1, 1)
                for xi in range(X_IN - 2, X_IN)
            ]
            after = [
                pltpu.roll(jnp.where(first_x, y_down[yi * X_IN + xi], line[xi]), LANES - 1, 1)
                for xi in range(2)
            ]
            wide = before + line + after
            for xi in range(X_IN):
                m = yi * X_IN + xi
                other = (1 - yi) * X_IN + xi
                y_next = here[other] if yi == 0 else y_up[other]
                y_prev = here[other] if yi == 1 else y_down[other]
                near = (wide[xi + 1] + wide[xi + 3]) + (y_next + y_prev) + (above[m] + below[m])
                far = (wide[xi] + wide[xi + 4]) + (y_up[m] + y_down[m])
                far = far + (above_2[m] + below_2[m])
                level = diagonal[first + plane, :, pl.ds(m * LANES, LANES)]
                out.append(level * here[m] - near - FAR_SCALED * far)
        yield here, out


def cmul(first, second):
    return (
        first[0] * second[0] - first[1] * second[1],
        first[0] * second[1] + first[1] * second[0],
    )


def moment_coeffs(point, points, count):
    lane = lax.broadcasted_iota(jnp.int32, (1, LANES), 1)
    moment = lax.rem(lane, MOMENTS * count) // count
    angle = 2.0 * math.pi * (point + 0.5) / points
    parts = []
    for func in (math.cos, math.sin):
        value = jnp.full((1, LANES), 0.25 * func(angle), jnp.float32)
        for k in range(1, MOMENTS):
            value = jnp.where(moment == k, 0.25 * func((k + 1) * angle), value)
        parts.append(value)
    return parts


def weights_of(alphas, norms, limits, count):
    points = len(limits)
    shape = (count, LANES)
    half = MOMENTS * count
    lane = lax.broadcasted_iota(jnp.int32, shape, 1)
    source = lax.broadcasted_iota(jnp.int32, shape, 0)
    own = lax.rem(lane, count) == source
    left_half = lane < half
    betas = [ratio(norms[i + 1], norms[i]) for i in range(ITERS - 1)]
    sums = [[jnp.zeros(shape, jnp.float32)] * 2 for _ in range(BASIS)]
    zero = jnp.zeros(shape, jnp.float32)
    one = jnp.ones(shape, jnp.float32)
    for point in range(points):
        angle = 2.0 * math.pi * (point + 0.5) / points
        shift = (GAMMA + RADIUS * math.cos(angle), RADIUS * math.sin(angle))
        scaled_shift = (H_SCALE * shift[0], H_SCALE * shift[1])
        limit = limits[point]
        product = (one, zero)
        products = [product]
        links = []
        pivot = (scaled_shift[0] - alphas[0], zero + scaled_shift[1])
        for i in range(ITERS):
            size = 1.0 / (pivot[0] * pivot[0] + pivot[1] * pivot[1])
            inverse = (pivot[0] * size, -pivot[1] * size)
            product = cmul(product, inverse)
            products.append(product)
            if i < ITERS - 1:
                link = (betas[i] * inverse[0], betas[i] * inverse[1])
                links.append(link)
                pivot = (scaled_shift[0] - alphas[i + 1] - link[0], scaled_shift[1] - link[1])
        solved = [None] * ITERS
        for i in reversed(range(ITERS)):
            value = (H_SCALE * products[i + 1][0], H_SCALE * products[i + 1][1])
            if i < ITERS - 1:
                step = cmul(links[i], solved[i + 1])
                value = (value[0] + step[0], value[1] + step[1])
            used = limit > i
            solved[i] = (jnp.where(used, value[0], 0.0), jnp.where(used, value[1], 0.0))
        applied = []
        for i in range(BASIS):
            left = limit == i
            rest = (
                jnp.where(left, products[i][0], 0.0),
                jnp.where(left, products[i][1], 0.0),
            )
            if i < ITERS:
                turned = (
                    shift[0] * solved[i][0] - shift[1] * solved[i][1],
                    shift[0] * solved[i][1] + shift[1] * solved[i][0],
                )
                rest = (rest[0] + turned[0], rest[1] + turned[1])
            if i == 0:
                rest = (rest[0] - 1.0, rest[1])
            applied.append(rest)
        tail = applied[ITERS]
        for back, factor in ((1, alphas[ITERS - 1]), (2, betas[ITERS - 2])):
            part = applied[ITERS - back]
            applied[ITERS - back] = (part[0] - factor * tail[0], part[1] - factor * tail[1])
        moment = moment_coeffs(point, points, count)
        for i in range(BASIS):
            left = solved[i] if i < ITERS else (zero, zero)
            both = (
                jnp.where(left_half, left[0], applied[i][0]),
                jnp.where(left_half, left[1], applied[i][1]),
            )
            term = cmul(moment, both)
            sums[i] = [sums[i][0] + term[0], sums[i][1] + term[1]]
    return [[jnp.where(own, part, 0.0) for part in pair] for pair in sums]


def exact_dot(first, second, dims):
    return lax.dot_general(
        first,
        second,
        (dims, ((), ())),
        precision=lax.Precision.HIGHEST,
        preferred_element_type=jnp.float32,
    )


def krylov_kernel(parts, count, *refs):
    blocks, vectors = refs[:parts], refs[parts : parts + BASIS]
    scalars, applied, diagonal = refs[parts + BASIS :]
    planes = diagonal.shape[0]
    depth = planes // parts
    groups = count // SUB
    lane = lax.broadcasted_iota(jnp.int32, (SUB, LANES), 1)
    last_x = lax.rem(lane, X_OUT) == X_OUT - 1
    first_x = lax.rem(lane, X_OUT) == 0
    here = lax.axis_index("dom")
    for turn in range(parts):
        slab = jnp.bitwise_xor(here, turn) * depth
        for deep in range(depth):
            for m in range(ROWS):
                start = (deep * ROWS + m) * count
                lanes = pl.ds(m * LANES, LANES)
                vectors[0][slab + deep, :, lanes] = blocks[turn][start : start + count, :]
            start = depth * ROWS * count + deep * ROWS
            levels = H_SCALE * (blocks[turn][start : start + ROWS, :] + 3.75)
            for m in range(ROWS):
                level = jnp.broadcast_to(levels[m : m + 1, :], (SUB, LANES))
                diagonal[slab + deep, :, m * LANES : (m + 1) * LANES] = level

    blank = jnp.zeros((SUB, LANES), jnp.float32)
    alphas, norms = [], []
    for i in range(ITERS):
        source, target = vectors[i], applied if i < ITERS - 1 else vectors[ITERS]

        def apply_turn(turn, sums, i=i, source=source, target=target):
            first = turn * TOGETHER
            new_sums = []
            for group in range(groups):
                rows = pl.ds(group * SUB, SUB)
                curve, norm = sums[group]
                done = apply_planes(source, diagonal, first, TOGETHER, group, last_x, first_x)
                for plane, (value, out) in enumerate(done):
                    for m in range(ROWS):
                        target[first + plane, rows, pl.ds(m * LANES, LANES)] = out[m]
                    curve = curve + tree_sum([value[m] * out[m] for m in range(ROWS)])
                    if i == 0:
                        norm = norm + tree_sum([value[m] * value[m] for m in range(ROWS)])
                new_sums.append((curve, norm))
            return tuple(new_sums)

        start = ((blank, blank),) * groups
        sums = lax.fori_loop(0, planes // TOGETHER, apply_turn, start, unroll=2)
        if i == 0:
            norms.append([lane_sum(norm) for _, norm in sums])
        alphas.append([ratio(lane_sum(sums[g][0]), norms[i][g]) for g in range(groups)])
        if i == ITERS - 1:
            break
        betas = [ratio(norms[i][g], norms[i - 1][g]) for g in range(groups)] if i else None

        def step_turn(plane, sums, i=i, alpha=alphas[i], betas=betas):
            new_sums = []
            for group in range(groups):
                rows = pl.ds(group * SUB, SUB)
                squares = []
                for m in range(ROWS):
                    lanes = pl.ds(m * LANES, LANES)
                    value = applied[plane, rows, lanes]
                    value = value - alpha[group] * vectors[i][plane, rows, lanes]
                    if i:
                        value = value - betas[group] * vectors[i - 1][plane, rows, lanes]
                    vectors[i + 1][plane, rows, lanes] = value
                    squares.append(value * value)
                new_sums.append(sums[group] + tree_sum(squares))
            return tuple(new_sums)

        sums = lax.fori_loop(0, planes, step_turn, (blank,) * groups, unroll=UNROLL)
        norms.append([lane_sum(norm) for norm in sums])
    for i, value in enumerate(alphas + norms):
        scalars[i] = jnp.concatenate(value, axis=0)


def gram_kernel(points, scalars, *refs):
    tiles, vectors = refs[:points], refs[points : points + BASIS]
    out_b, out_a, gram, limits = refs[points + BASIS :]
    planes, count, _ = vectors[0].shape
    groups = count // SUB
    size = BASIS * count
    gram[...] = jnp.zeros_like(gram)

    def gram_turn(plane, carry):
        values = jnp.concatenate([vector[plane] for vector in vectors], axis=0)
        high = values.astype(jnp.bfloat16)
        low = (values - high.astype(jnp.float32)).astype(jnp.bfloat16)
        gram[...] += lax.dot_general(
            jnp.concatenate([high, low], axis=0),
            high,
            (((1,), (1,)), ((), ())),
            preferred_element_type=jnp.float32,
        )
        return carry

    lax.fori_loop(0, planes, gram_turn, 0, unroll=UNROLL)
    cross = gram[size:, :]
    pairs = gram[:size, :] + cross + cross.T

    here = lax.axis_index("point")
    core = jnp.bitwise_and(lax.axis_index("dom"), CORES - 1)
    for far, tile in zip((0, 1 + core, 3, 2 - core), tiles):
        limits[jnp.bitwise_xor(here, far)] = tile[...]
    bounds = [jnp.concatenate([limits[j]] * groups, axis=0) for j in range(points)]
    alphas = [scalars[i] for i in range(ITERS)]
    norms = [scalars[ITERS + i] for i in range(ITERS)]
    weights = weights_of(alphas, norms, bounds, count)
    real = jnp.concatenate([pair[0] for pair in weights], axis=0)
    imag = jnp.concatenate([pair[1] for pair in weights], axis=0)
    right = exact_dot(pairs, jnp.concatenate([real, imag], axis=1), ((1,), (0,)))
    half = MOMENTS * count
    left = jnp.concatenate([real[:, :half], imag[:, :half]], axis=1)
    joined = exact_dot(left.T, right, ((1,), (0,)))
    scale = 1.0 / (planes * ROWS * LANES)
    width = 2 * half
    real = (joined[:half, :width] + joined[half:, width:]) * scale
    imag = (joined[:half, width:] - joined[half:, :width]) * scale
    out_b[0] = real[:, :half]
    out_b[1] = imag[:, :half]
    out_a[0] = real[:, half:]
    out_a[1] = imag[:, half:]


def swapped(values, axis, size, mask):
    return lax.ppermute(values, axis, [(index ^ mask, index) for index in range(size)])


def whole_grid(sources, potential, iter_counts, *, parts, points):
    count, depth, _ = sources.shape
    planes = parts * depth
    block, tile = packed_block(sources, potential, iter_counts)
    even = [block] + [swapped(block, "dom", parts, mask) for mask in range(CORES, parts, CORES)]
    mixed = [
        ((point ^ (1 + part % CORES)) * parts + part, point * parts + part)
        for point in range(points)
        for part in range(parts)
    ]
    tiles = [lax.ppermute(tile, ("point", "dom"), mixed), swapped(tile, "point", points, 3)]
    even[1], *tiles = lax.optimization_barrier((even[1], *tiles))
    tiles.append(swapped(tiles[0], "dom", parts, 1))
    odd = [swapped(value, "dom", parts, 1) for value in even]
    blocks = [value for pair in zip(even, odd) for value in pair]
    vmem = pl.BlockSpec(memory_space=pltpu.VMEM)
    vector = (planes, count, ROWS * LANES)
    cells = planes * ROWS * LANES
    *vectors, scalars = pl.pallas_call(
        functools.partial(krylov_kernel, parts, count),
        out_shape=[jax.ShapeDtypeStruct(vector, jnp.float32)] * BASIS
        + [jax.ShapeDtypeStruct((2 * ITERS, count, LANES), jnp.float32)],
        in_specs=[vmem] * parts,
        out_specs=[vmem] * (BASIS + 1),
        scratch_shapes=[
            pltpu.VMEM(vector, jnp.float32),
            pltpu.VMEM((planes, SUB, ROWS * LANES), jnp.float32),
        ],
        compiler_params=pltpu.CompilerParams(vmem_limit_bytes=16 * 2**20),
        name="krylov",
    )(*blocks)
    size = BASIS * count
    width = MOMENTS * count
    out = jax.ShapeDtypeStruct((2, width, width), jnp.float32)
    return pl.pallas_call(
        functools.partial(gram_kernel, points),
        out_shape=(out, out),
        in_specs=[vmem] * (1 + points + BASIS),
        out_specs=(vmem, vmem),
        scratch_shapes=[
            pltpu.VMEM((2 * size, size), jnp.float32),
            pltpu.VMEM((points, SUB, LANES), jnp.float32),
        ],
        compiler_params=pltpu.CompilerParams(vmem_limit_bytes=16 * 2**20),
        name="gram",
    )(scalars, tile, *tiles, *vectors)


def on_device(sources, potential, iter_counts):
    parts, points = lax.axis_size("dom"), lax.axis_size("point")
    count, depth, cells = sources.shape
    held = BASIS * count * parts * depth * cells * 4
    fits = (
        held <= 16 * 2**20
        and parts == 8
        and points == 4
        and count == 2 * SUB
        and 2 * MOMENTS * count == LANES
        and parts * depth == 16
        and cells == GX * GX == ROWS * LANES
    )
    if not fits:
        return split_grid(sources, potential, iter_counts)
    return whole_grid(sources, potential, iter_counts, parts=parts, points=points)


def solution(mesh):
    placed = (P(None, "dom", None), P("dom", None), P("point"))
    return jax.shard_map(
        on_device, mesh=mesh, in_specs=placed, out_specs=(P(), P()), check_vma=False
    )
```

```python
import functools
import math

import jax
import jax.numpy as jnp
from jax import lax
from jax.experimental import pallas as pl
from jax.experimental.pallas import tpu as pltpu
from jax.sharding import PartitionSpec as P

MOMENTS = 4
ITERS = 6
GX = 32


COEF_NEAR = 4.0 / 3.0
COEF_FAR = -1.0 / 12.0
GAMMA = 2.0
RADIUS = 1.5


def padded_2(block, sides, width):
    for axis, dim in sides:
        count = lax.axis_size(axis)
        forward = [(i, i + 1) for i in range(count - 1)]
        forward.append((count - 1, 0))
        backward = [(target, source) for source, target in forward]
        low = lax.ppermute(
            lax.slice_in_dim(block, block.shape[dim] - width, None, axis=dim), axis, forward
        )
        high = lax.ppermute(lax.slice_in_dim(block, 0, width, axis=dim), axis, backward)
        block = jnp.concatenate([low, block, high], axis=dim)
    return block


def plane_terms(values, side):
    lead = values.shape[:-1]
    planes = values.reshape(lead + (side, side))
    summed = COEF_NEAR * (
        jnp.roll(planes, 1, -2)
        + jnp.roll(planes, -1, -2)
        + jnp.roll(planes, 1, -1)
        + jnp.roll(planes, -1, -1)
    )
    summed = summed + COEF_FAR * (
        jnp.roll(planes, 2, -2)
        + jnp.roll(planes, -2, -2)
        + jnp.roll(planes, 2, -1)
        + jnp.roll(planes, -2, -1)
    )
    return summed.reshape(values.shape)


def complex_mul(first, second):
    return jnp.stack(
        [first[0] * second[0] - first[1] * second[1], first[0] * second[1] + first[1] * second[0]]
    )


def complex_div(first, second):
    denom = second[0] * second[0] + second[1] * second[1]
    return jnp.stack(
        [
            (first[0] * second[0] + first[1] * second[1]) / denom,
            (first[1] * second[0] - first[0] * second[1]) / denom,
        ]
    )


def bilinear(first, second):
    real_part = jnp.sum(first[0] * second[0] - first[1] * second[1], axis=(1, 2))
    imag_part = jnp.sum(first[0] * second[1] + first[1] * second[0], axis=(1, 2))
    return jnp.stack([real_part, imag_part])


def scaled(coeffs, values):
    return complex_mul(coeffs[:, :, None, None], values)


def shifted(values, potential, shift_re, shift_im):
    padded = padded_2(values, (("dom", 2),), 2)
    depth = values.shape[2]
    lap = -7.5 * values + plane_terms(values, GX)
    lap = lap + COEF_NEAR * (padded[:, :, 3 : 3 + depth] + padded[:, :, 1 : 1 + depth])
    lap = lap + COEF_FAR * (padded[:, :, 4 : 4 + depth] + padded[:, :, 0:depth])
    applied = -0.5 * lap + potential * values
    return jnp.stack(
        [
            shift_re * values[0] - shift_im * values[1] - applied[0],
            shift_re * values[1] + shift_im * values[0] - applied[1],
        ]
    )


def residual_sum(values):
    return lax.psum(bilinear(values, values), "dom")


def moment_terms(solution, residual, sources, angle_now, shift_re, shift_im):
    applied = jnp.stack(
        [
            shift_re * solution[0] - shift_im * solution[1] - sources[0] + residual[0],
            shift_re * solution[1] + shift_im * solution[0] - sources[1] + residual[1],
        ]
    )
    angles = (jnp.arange(MOMENTS).astype(jnp.float32) + 1.0) * angle_now
    coeffs = 0.25 * jnp.stack([jnp.cos(angles), jnp.sin(angles)])
    s_terms = complex_mul(coeffs[:, :, None, None, None], solution[:, None])
    h_terms = complex_mul(coeffs[:, :, None, None, None], applied[:, None])
    width = MOMENTS * solution.shape[1]
    return (s_terms.reshape(2, width, -1), h_terms.reshape(2, width, -1))


def gram_of(left, right):
    width = left.shape[1]
    joined = lax.dot_general(
        left.reshape(2 * width, -1),
        right.reshape(2 * width, -1),
        (((1,), (1,)), ((), ())),
        precision=lax.Precision.HIGHEST,
        preferred_element_type=jnp.float32,
    )
    blocks = joined.reshape(2, width, 2, width)
    return jnp.stack([blocks[0, :, 0] + blocks[1, :, 1], blocks[0, :, 1] - blocks[1, :, 0]])


def split_grid(sources, potential, iter_counts):
    complex_src = jnp.stack([sources, jnp.zeros_like(sources)])
    angle_now = (
        2.0 * math.pi * (lax.axis_index("point").astype(jnp.float32) + 0.5) / lax.axis_size("point")
    )
    shift_re = GAMMA + RADIUS * jnp.cos(angle_now)
    shift_im = RADIUS * jnp.sin(angle_now)
    limit = iter_counts[0]
    solution = jnp.zeros_like(complex_src)

    def one_turn(turn_idx, state):
        solution, residual, search, norm_now = state
        product = shifted(search, potential, shift_re, shift_im)
        curve = lax.psum(bilinear(search, product), "dom")
        step_size = complex_div(norm_now, curve)
        new_residual = residual - scaled(step_size, product)
        norm_next = residual_sum(new_residual)
        fresh = (
            solution + scaled(step_size, search),
            new_residual,
            new_residual + scaled(complex_div(norm_next, norm_now), search),
            norm_next,
        )
        keep_mask = turn_idx < limit
        return jax.tree.map(lambda newer, older: jnp.where(keep_mask, newer, older), fresh, state)

    start = (solution, complex_src, complex_src, residual_sum(complex_src))
    solution, residual, search, norm_now = lax.fori_loop(0, ITERS, one_turn, start)
    s_terms, h_terms = moment_terms(solution, residual, complex_src, angle_now, shift_re, shift_im)
    cells = sources.shape[1] * sources.shape[2] * lax.axis_size("dom")
    s_total, h_total = lax.psum((s_terms, h_terms), "point")
    gram_b, gram_a = lax.psum((gram_of(s_total, s_total), gram_of(s_total, h_total)), "dom")
    return (gram_b / cells, gram_a / cells)


Y_IN, X_IN = 2, 4
Y_OUT, X_OUT = GX // Y_IN, GX // X_IN
ROWS = Y_IN * X_IN
LANES = Y_OUT * X_OUT
SUB = 8
BASIS = ITERS + 1
CORES = 2
TOGETHER = 2
UNROLL = 4
H_SCALE = 2.0 / COEF_NEAR
FAR_SCALED = 0.5 * H_SCALE * COEF_FAR


def pack_kernel(depth, groups, counts, rows, out, tile):
    columns = rows.shape[0] // (SUB * groups * depth + depth)
    first_level = columns * SUB * groups * depth
    source = lax.broadcasted_iota(jnp.int32, (LANES, LANES), 0)
    target = lax.broadcasted_iota(jnp.int32, (LANES, LANES), 1)
    inner = target // (LANES // ROWS)
    outer = target % (LANES // ROWS)
    cell = (outer // X_OUT * Y_IN + inner // X_IN) * GX + outer % X_OUT * X_IN + inner % X_IN
    swap = jnp.where(source == cell, 1.0, 0.0).astype(jnp.float32)
    parts = []
    for deep in range(depth):
        for group in range(groups):
            for column in range(columns):
                start = (group * SUB * columns + column) * depth + deep
                parts.append(rows[pl.ds(start, SUB, stride=columns * depth), :])
        parts.append(rows[pl.ds(first_level + deep, columns, stride=depth), :])
    mixed = exact_dot(jnp.concatenate(parts, axis=0), swap, ((1,), (0,)))
    block = LANES // ROWS
    lane_block = lax.broadcasted_iota(jnp.int32, (SUB, LANES), 1) // block
    row = lax.broadcasted_iota(jnp.int32, (SUB, LANES), 0)
    for deep in range(depth):
        base = deep * (groups + 1) * columns * SUB - deep * (columns - 1) * SUB
        for group in range(groups):
            pieces = [
                mixed[base + (group * columns + column) * SUB :][:SUB] for column in range(columns)
            ]
            for m in range(ROWS):
                value = pieces[m]
                for column in range(columns):
                    if column != m:
                        moved = pltpu.roll(pieces[column], (column - m) * block % LANES, 1)
                        value = jnp.where(lane_block == column, moved, value)
                start = ((deep * ROWS + m) * groups + group) * SUB
                out[start : start + SUB, :] = value
        piece = mixed[base + groups * columns * SUB :][:SUB]
        value = piece
        for far in range(1, columns):
            moved = pltpu.roll(pltpu.roll(piece, far * block, 1), columns - far, 0)
            value = jnp.where(lane_block == (row + far) % columns, moved, value)
        start = depth * ROWS * SUB * groups + deep * ROWS
        out[start : start + ROWS, :] = value
    tile[...] = jnp.broadcast_to(counts[...].astype(jnp.float32), (SUB, LANES))


def packed_block(sources, potential, iter_counts):
    count, depth, cells = sources.shape
    columns = cells // LANES
    rows = sources.reshape(count, depth, columns, LANES).transpose(0, 2, 1, 3).reshape(-1, LANES)
    levels = potential.reshape(depth, columns, LANES).transpose(1, 0, 2).reshape(-1, LANES)
    vmem = pl.BlockSpec(memory_space=pltpu.VMEM)
    size = depth * ROWS * (count + 1)
    return pl.pallas_call(
        functools.partial(pack_kernel, depth, count // SUB),
        out_shape=(
            jax.ShapeDtypeStruct((size, LANES), jnp.float32),
            jax.ShapeDtypeStruct((SUB, LANES), jnp.float32),
        ),
        in_specs=[vmem, vmem],
        out_specs=(vmem, vmem),
        compiler_params=pltpu.CompilerParams(vmem_limit_bytes=4 * 2**20),
        name="pack",
    )(iter_counts.reshape(1, 1), jnp.concatenate([rows, levels], axis=0))


def lane_sum(values):
    return jnp.broadcast_to(jnp.sum(values, axis=1, keepdims=True), values.shape)


def ratio(top, bottom):
    return jnp.where(bottom > 0.0, top / jnp.where(bottom > 0.0, bottom, 1.0), 0.0)


def tree_sum(values):
    while len(values) > 1:
        values = [sum(values[i : i + 2][1:], values[i]) for i in range(0, len(values), 2)]
    return values[0]


def x_next(values, wrap_mask):
    return jnp.where(wrap_mask, pltpu.roll(values, X_OUT - 1, 1), pltpu.roll(values, LANES - 1, 1))


def x_prev(values, wrap_mask):
    return jnp.where(wrap_mask, pltpu.roll(values, LANES - X_OUT + 1, 1), pltpu.roll(values, 1, 1))


def halo_sums(here, last_x, first_x):
    y_up = [pltpu.roll(value, LANES - X_OUT, 1) for value in here]
    y_down = [pltpu.roll(value, X_OUT, 1) for value in here]
    sums = []
    for yi in range(Y_IN):
        line = here[yi * X_IN : (yi + 1) * X_IN]
        before = [x_prev(value, first_x) for value in line[X_IN - 2 :]]
        after = [x_next(value, last_x) for value in line[:2]]
        far_x = before + after
        near_x = [before[1], None, None, after[0]]
        for xi in range(X_IN):
            m = yi * X_IN + xi
            other = (1 - yi) * X_IN + xi
            near = y_down[other] if yi == 0 else y_up[other]
            if near_x[xi] is not None:
                near = near + near_x[xi]
            sums.append(near + FAR_SCALED * ((y_up[m] + y_down[m]) + far_x[xi]))
    return sums


def apply_planes(vector, halo, diagonal, first, count, group):
    planes = vector.shape[0]
    rows = pl.ds(group * SUB, SUB)
    held = {}
    for far in range(-2, count + 2):
        index = jnp.bitwise_and(first + (far + planes), planes - 1)
        held[far] = [vector[index, rows, pl.ds(m * LANES, LANES)] for m in range(ROWS)]
    for plane in range(count):
        here, above, below = held[plane], held[plane + 1], held[plane - 1]
        above_2, below_2 = held[plane + 2], held[plane - 2]
        out = []
        for m in range(ROWS):
            lanes = pl.ds(m * LANES, LANES)
            yi, xi = m // X_IN, m % X_IN
            near = [here[(1 - yi) * X_IN + xi] + (above[m] + below[m])]
            near += [here[yi * X_IN + x] for x in (xi - 1, xi + 1) if 0 <= x < X_IN]
            far = [above_2[m] + below_2[m]]
            far += [here[yi * X_IN + x] for x in (xi - 2, xi + 2) if 0 <= x < X_IN]
            value = diagonal[first + plane, :, lanes] * here[m] - halo[first + plane, rows, lanes]
            out.append((value - sum(near[1:], near[0])) - FAR_SCALED * sum(far[1:], far[0]))
        yield here, out


def cmul(first, second):
    return (
        first[0] * second[0] - first[1] * second[1],
        first[0] * second[1] + first[1] * second[0],
    )


def moment_coeffs(point, points, count):
    lane = lax.broadcasted_iota(jnp.int32, (1, LANES), 1)
    moment = lax.rem(lane, MOMENTS * count) // count
    angle = 2.0 * math.pi * (point + 0.5) / points
    parts = []
    for func in (math.cos, math.sin):
        value = jnp.full((1, LANES), 0.25 * func(angle), jnp.float32)
        for k in range(1, MOMENTS):
            value = jnp.where(moment == k, 0.25 * func((k + 1) * angle), value)
        parts.append(value)
    return parts


def weights_of(alphas, norms, limits, count):
    points = len(limits)
    shape = (count, LANES)
    half = MOMENTS * count
    lane = lax.broadcasted_iota(jnp.int32, shape, 1)
    source = lax.broadcasted_iota(jnp.int32, shape, 0)
    own = lax.rem(lane, count) == source
    left_half = lane < half
    betas = [ratio(norms[i + 1], norms[i]) for i in range(ITERS - 1)]
    sums = [[jnp.zeros(shape, jnp.float32)] * 2 for _ in range(BASIS)]
    zero = jnp.zeros(shape, jnp.float32)
    one = jnp.ones(shape, jnp.float32)
    for point in range(points):
        angle = 2.0 * math.pi * (point + 0.5) / points
        shift = (GAMMA + RADIUS * math.cos(angle), RADIUS * math.sin(angle))
        scaled_shift = (H_SCALE * shift[0], H_SCALE * shift[1])
        limit = limits[point]
        product = (one, zero)
        products = [product]
        links = []
        pivot = (scaled_shift[0] - alphas[0], zero + scaled_shift[1])
        for i in range(ITERS):
            size = 1.0 / (pivot[0] * pivot[0] + pivot[1] * pivot[1])
            inverse = (pivot[0] * size, -pivot[1] * size)
            product = cmul(product, inverse)
            products.append(product)
            if i < ITERS - 1:
                link = (betas[i] * inverse[0], betas[i] * inverse[1])
                links.append(link)
                pivot = (scaled_shift[0] - alphas[i + 1] - link[0], scaled_shift[1] - link[1])
        solved = [None] * ITERS
        for i in reversed(range(ITERS)):
            value = (H_SCALE * products[i + 1][0], H_SCALE * products[i + 1][1])
            if i < ITERS - 1:
                step = cmul(links[i], solved[i + 1])
                value = (value[0] + step[0], value[1] + step[1])
            used = limit > i
            solved[i] = (jnp.where(used, value[0], 0.0), jnp.where(used, value[1], 0.0))
        applied = []
        for i in range(BASIS):
            left = limit == i
            rest = (
                jnp.where(left, products[i][0], 0.0),
                jnp.where(left, products[i][1], 0.0),
            )
            if i < ITERS:
                turned = (
                    shift[0] * solved[i][0] - shift[1] * solved[i][1],
                    shift[0] * solved[i][1] + shift[1] * solved[i][0],
                )
                rest = (rest[0] + turned[0], rest[1] + turned[1])
            if i == 0:
                rest = (rest[0] - 1.0, rest[1])
            applied.append(rest)
        tail = applied[ITERS]
        for back, factor in ((1, alphas[ITERS - 1]), (2, betas[ITERS - 2])):
            part = applied[ITERS - back]
            applied[ITERS - back] = (part[0] - factor * tail[0], part[1] - factor * tail[1])
        moment = moment_coeffs(point, points, count)
        for i in range(BASIS):
            left = solved[i] if i < ITERS else (zero, zero)
            both = (
                jnp.where(left_half, left[0], applied[i][0]),
                jnp.where(left_half, left[1], applied[i][1]),
            )
            term = cmul(moment, both)
            sums[i] = [sums[i][0] + term[0], sums[i][1] + term[1]]
    return [[jnp.where(own, part, 0.0) for part in pair] for pair in sums]


def exact_dot(first, second, dims):
    return lax.dot_general(
        first,
        second,
        (dims, ((), ())),
        precision=lax.Precision.HIGHEST,
        preferred_element_type=jnp.float32,
    )


def krylov_kernel(parts, count, *refs):
    blocks, vectors = refs[:parts], refs[parts : parts + BASIS]
    scalars, applied, halo, diagonal = refs[parts + BASIS :]
    planes = diagonal.shape[0]
    depth = planes // parts
    groups = count // SUB
    lane = lax.broadcasted_iota(jnp.int32, (SUB, LANES), 1)
    last_x = lax.rem(lane, X_OUT) == X_OUT - 1
    first_x = lax.rem(lane, X_OUT) == 0
    here = lax.axis_index("dom")
    for turn in range(parts):
        slab = jnp.bitwise_xor(here, turn) * depth
        for deep in range(depth):
            for group in range(groups):
                rows = pl.ds(group * SUB, SUB)
                values = []
                for m in range(ROWS):
                    start = (deep * ROWS + m) * count + group * SUB
                    values.append(blocks[turn][start : start + SUB, :])
                    vectors[0][slab + deep, rows, m * LANES : (m + 1) * LANES] = values[m]
                for m, value in enumerate(halo_sums(values, last_x, first_x)):
                    halo[slab + deep, rows, m * LANES : (m + 1) * LANES] = value
            start = depth * ROWS * count + deep * ROWS
            levels = H_SCALE * (blocks[turn][start : start + ROWS, :] + 3.75)
            for m in range(ROWS):
                level = jnp.broadcast_to(levels[m : m + 1, :], (SUB, LANES))
                diagonal[slab + deep, :, m * LANES : (m + 1) * LANES] = level

    blank = jnp.zeros((SUB, LANES), jnp.float32)
    alphas, norms = [], []
    for i in range(ITERS):
        source, target = vectors[i], applied if i < ITERS - 1 else vectors[ITERS]

        def apply_turn(turn, sums, i=i, source=source, target=target):
            first = turn * TOGETHER
            new_sums = []
            for group in range(groups):
                rows = pl.ds(group * SUB, SUB)
                curve, norm = sums[group]
                done = apply_planes(source, halo, diagonal, first, TOGETHER, group)
                for plane, (value, out) in enumerate(done):
                    for m in range(ROWS):
                        target[first + plane, rows, pl.ds(m * LANES, LANES)] = out[m]
                    curve = curve + tree_sum([value[m] * out[m] for m in range(ROWS)])
                    if i == 0:
                        norm = norm + tree_sum([value[m] * value[m] for m in range(ROWS)])
                new_sums.append((curve, norm))
            return tuple(new_sums)

        start = ((blank, blank),) * groups
        sums = lax.fori_loop(0, planes // TOGETHER, apply_turn, start, unroll=2)
        if i == 0:
            norms.append([lane_sum(norm) for _, norm in sums])
        alphas.append([ratio(lane_sum(sums[g][0]), norms[i][g]) for g in range(groups)])
        if i == ITERS - 1:
            break
        betas = [ratio(norms[i][g], norms[i - 1][g]) for g in range(groups)] if i else None

        def step_turn(plane, sums, i=i, alpha=alphas[i], betas=betas):
            new_sums = []
            for group in range(groups):
                rows = pl.ds(group * SUB, SUB)
                values = []
                for m in range(ROWS):
                    lanes = pl.ds(m * LANES, LANES)
                    value = applied[plane, rows, lanes]
                    value = value - alpha[group] * vectors[i][plane, rows, lanes]
                    if i:
                        value = value - betas[group] * vectors[i - 1][plane, rows, lanes]
                    vectors[i + 1][plane, rows, lanes] = value
                    values.append(value)
                for m, value in enumerate(halo_sums(values, last_x, first_x)):
                    halo[plane, rows, pl.ds(m * LANES, LANES)] = value
                new_sums.append(sums[group] + tree_sum([value * value for value in values]))
            return tuple(new_sums)

        sums = lax.fori_loop(0, planes, step_turn, (blank,) * groups, unroll=UNROLL)
        norms.append([lane_sum(norm) for norm in sums])
    for i, value in enumerate(alphas + norms):
        scalars[i] = jnp.concatenate(value, axis=0)


def gram_kernel(points, scalars, *refs):
    tiles, vectors = refs[:points], refs[points : points + BASIS]
    out_b, out_a, gram, limits = refs[points + BASIS :]
    planes, count, _ = vectors[0].shape
    groups = count // SUB
    size = BASIS * count
    gram[...] = jnp.zeros_like(gram)

    def gram_turn(plane, carry):
        values = jnp.concatenate([vector[plane] for vector in vectors], axis=0)
        high = values.astype(jnp.bfloat16)
        low = (values - high.astype(jnp.float32)).astype(jnp.bfloat16)
        gram[...] += lax.dot_general(
            jnp.concatenate([high, low], axis=0),
            high,
            (((1,), (1,)), ((), ())),
            preferred_element_type=jnp.float32,
        )
        return carry

    lax.fori_loop(0, planes, gram_turn, 0, unroll=UNROLL)
    cross = gram[size:, :]
    pairs = gram[:size, :] + cross + cross.T

    here = lax.axis_index("point")
    core = jnp.bitwise_and(lax.axis_index("dom"), CORES - 1)
    for far, tile in zip((0, 1 + core, 3, 2 - core), tiles):
        limits[jnp.bitwise_xor(here, far)] = tile[...]
    bounds = [jnp.concatenate([limits[j]] * groups, axis=0) for j in range(points)]
    alphas = [scalars[i] for i in range(ITERS)]
    norms = [scalars[ITERS + i] for i in range(ITERS)]
    weights = weights_of(alphas, norms, bounds, count)
    real = jnp.concatenate([pair[0] for pair in weights], axis=0)
    imag = jnp.concatenate([pair[1] for pair in weights], axis=0)
    right = exact_dot(pairs, jnp.concatenate([real, imag], axis=1), ((1,), (0,)))
    half = MOMENTS * count
    left = jnp.concatenate([real[:, :half], imag[:, :half]], axis=1)
    joined = exact_dot(left.T, right, ((1,), (0,)))
    scale = 1.0 / (planes * ROWS * LANES)
    width = 2 * half
    real = (joined[:half, :width] + joined[half:, width:]) * scale
    imag = (joined[:half, width:] - joined[half:, :width]) * scale
    out_b[0] = real[:, :half]
    out_b[1] = imag[:, :half]
    out_a[0] = real[:, half:]
    out_a[1] = imag[:, half:]


def swapped(values, axis, size, mask):
    return lax.ppermute(values, axis, [(index ^ mask, index) for index in range(size)])


def whole_grid(sources, potential, iter_counts, *, parts, points):
    count, depth, _ = sources.shape
    planes = parts * depth
    block, tile = packed_block(sources, potential, iter_counts)
    even = [block] + [swapped(block, "dom", parts, mask) for mask in range(CORES, parts, CORES)]
    mixed = [
        ((point ^ (1 + part % CORES)) * parts + part, point * parts + part)
        for point in range(points)
        for part in range(parts)
    ]
    tiles = [lax.ppermute(tile, ("point", "dom"), mixed), swapped(tile, "point", points, 3)]
    even[1], *tiles = lax.optimization_barrier((even[1], *tiles))
    tiles.append(swapped(tiles[0], "dom", parts, 1))
    odd = [swapped(value, "dom", parts, 1) for value in even]
    blocks = [value for pair in zip(even, odd) for value in pair]
    vmem = pl.BlockSpec(memory_space=pltpu.VMEM)
    vector = (planes, count, ROWS * LANES)
    cells = planes * ROWS * LANES
    *vectors, scalars = pl.pallas_call(
        functools.partial(krylov_kernel, parts, count),
        out_shape=[jax.ShapeDtypeStruct(vector, jnp.float32)] * BASIS
        + [jax.ShapeDtypeStruct((2 * ITERS, count, LANES), jnp.float32)],
        in_specs=[vmem] * parts,
        out_specs=[vmem] * (BASIS + 1),
        scratch_shapes=[
            pltpu.VMEM(vector, jnp.float32),
            pltpu.VMEM(vector, jnp.float32),
            pltpu.VMEM((planes, SUB, ROWS * LANES), jnp.float32),
        ],
        compiler_params=pltpu.CompilerParams(vmem_limit_bytes=16 * 2**20),
        name="krylov",
    )(*blocks)
    size = BASIS * count
    width = MOMENTS * count
    out = jax.ShapeDtypeStruct((2, width, width), jnp.float32)
    return pl.pallas_call(
        functools.partial(gram_kernel, points),
        out_shape=(out, out),
        in_specs=[vmem] * (1 + points + BASIS),
        out_specs=(vmem, vmem),
        scratch_shapes=[
            pltpu.VMEM((2 * size, size), jnp.float32),
            pltpu.VMEM((points, SUB, LANES), jnp.float32),
        ],
        compiler_params=pltpu.CompilerParams(vmem_limit_bytes=16 * 2**20),
        name="gram",
    )(scalars, tile, *tiles, *vectors)


def on_device(sources, potential, iter_counts):
    parts, points = lax.axis_size("dom"), lax.axis_size("point")
    count, depth, cells = sources.shape
    held = BASIS * count * parts * depth * cells * 4
    fits = (
        held <= 16 * 2**20
        and parts == 8
        and points == 4
        and count == 2 * SUB
        and 2 * MOMENTS * count == LANES
        and parts * depth == 16
        and cells == GX * GX == ROWS * LANES
    )
    if not fits:
        return split_grid(sources, potential, iter_counts)
    return whole_grid(sources, potential, iter_counts, parts=parts, points=points)


def solution(mesh):
    placed = (P(None, "dom", None), P("dom", None), P("point"))
    return jax.shard_map(
        on_device, mesh=mesh, in_specs=placed, out_specs=(P(), P()), check_vma=False
    )
```

```python
import functools
import math

import jax
import jax.numpy as jnp
from jax import lax
from jax.experimental import pallas as pl
from jax.experimental.pallas import tpu as pltpu
from jax.sharding import PartitionSpec as P

MOMENTS = 4
ITERS = 6
GX = 32


COEF_NEAR = 4.0 / 3.0
COEF_FAR = -1.0 / 12.0
GAMMA = 2.0
RADIUS = 1.5


def padded_2(block, sides, width):
    for axis, dim in sides:
        count = lax.axis_size(axis)
        forward = [(i, i + 1) for i in range(count - 1)]
        forward.append((count - 1, 0))
        backward = [(target, source) for source, target in forward]
        low = lax.ppermute(
            lax.slice_in_dim(block, block.shape[dim] - width, None, axis=dim), axis, forward
        )
        high = lax.ppermute(lax.slice_in_dim(block, 0, width, axis=dim), axis, backward)
        block = jnp.concatenate([low, block, high], axis=dim)
    return block


def plane_terms(values, side):
    lead = values.shape[:-1]
    planes = values.reshape(lead + (side, side))
    summed = COEF_NEAR * (
        jnp.roll(planes, 1, -2)
        + jnp.roll(planes, -1, -2)
        + jnp.roll(planes, 1, -1)
        + jnp.roll(planes, -1, -1)
    )
    summed = summed + COEF_FAR * (
        jnp.roll(planes, 2, -2)
        + jnp.roll(planes, -2, -2)
        + jnp.roll(planes, 2, -1)
        + jnp.roll(planes, -2, -1)
    )
    return summed.reshape(values.shape)


def complex_mul(first, second):
    return jnp.stack(
        [first[0] * second[0] - first[1] * second[1], first[0] * second[1] + first[1] * second[0]]
    )


def complex_div(first, second):
    denom = second[0] * second[0] + second[1] * second[1]
    return jnp.stack(
        [
            (first[0] * second[0] + first[1] * second[1]) / denom,
            (first[1] * second[0] - first[0] * second[1]) / denom,
        ]
    )


def bilinear(first, second):
    real_part = jnp.sum(first[0] * second[0] - first[1] * second[1], axis=(1, 2))
    imag_part = jnp.sum(first[0] * second[1] + first[1] * second[0], axis=(1, 2))
    return jnp.stack([real_part, imag_part])


def scaled(coeffs, values):
    return complex_mul(coeffs[:, :, None, None], values)


def shifted(values, potential, shift_re, shift_im):
    padded = padded_2(values, (("dom", 2),), 2)
    depth = values.shape[2]
    lap = -7.5 * values + plane_terms(values, GX)
    lap = lap + COEF_NEAR * (padded[:, :, 3 : 3 + depth] + padded[:, :, 1 : 1 + depth])
    lap = lap + COEF_FAR * (padded[:, :, 4 : 4 + depth] + padded[:, :, 0:depth])
    applied = -0.5 * lap + potential * values
    return jnp.stack(
        [
            shift_re * values[0] - shift_im * values[1] - applied[0],
            shift_re * values[1] + shift_im * values[0] - applied[1],
        ]
    )


def residual_sum(values):
    return lax.psum(bilinear(values, values), "dom")


def moment_terms(solution, residual, sources, angle_now, shift_re, shift_im):
    applied = jnp.stack(
        [
            shift_re * solution[0] - shift_im * solution[1] - sources[0] + residual[0],
            shift_re * solution[1] + shift_im * solution[0] - sources[1] + residual[1],
        ]
    )
    angles = (jnp.arange(MOMENTS).astype(jnp.float32) + 1.0) * angle_now
    coeffs = 0.25 * jnp.stack([jnp.cos(angles), jnp.sin(angles)])
    s_terms = complex_mul(coeffs[:, :, None, None, None], solution[:, None])
    h_terms = complex_mul(coeffs[:, :, None, None, None], applied[:, None])
    width = MOMENTS * solution.shape[1]
    return (s_terms.reshape(2, width, -1), h_terms.reshape(2, width, -1))


def gram_of(left, right):
    width = left.shape[1]
    joined = lax.dot_general(
        left.reshape(2 * width, -1),
        right.reshape(2 * width, -1),
        (((1,), (1,)), ((), ())),
        precision=lax.Precision.HIGHEST,
        preferred_element_type=jnp.float32,
    )
    blocks = joined.reshape(2, width, 2, width)
    return jnp.stack([blocks[0, :, 0] + blocks[1, :, 1], blocks[0, :, 1] - blocks[1, :, 0]])


def split_grid(sources, potential, iter_counts):
    complex_src = jnp.stack([sources, jnp.zeros_like(sources)])
    angle_now = (
        2.0 * math.pi * (lax.axis_index("point").astype(jnp.float32) + 0.5) / lax.axis_size("point")
    )
    shift_re = GAMMA + RADIUS * jnp.cos(angle_now)
    shift_im = RADIUS * jnp.sin(angle_now)
    limit = iter_counts[0]
    solution = jnp.zeros_like(complex_src)

    def one_turn(turn_idx, state):
        solution, residual, search, norm_now = state
        product = shifted(search, potential, shift_re, shift_im)
        curve = lax.psum(bilinear(search, product), "dom")
        step_size = complex_div(norm_now, curve)
        new_residual = residual - scaled(step_size, product)
        norm_next = residual_sum(new_residual)
        fresh = (
            solution + scaled(step_size, search),
            new_residual,
            new_residual + scaled(complex_div(norm_next, norm_now), search),
            norm_next,
        )
        keep_mask = turn_idx < limit
        return jax.tree.map(lambda newer, older: jnp.where(keep_mask, newer, older), fresh, state)

    start = (solution, complex_src, complex_src, residual_sum(complex_src))
    solution, residual, search, norm_now = lax.fori_loop(0, ITERS, one_turn, start)
    s_terms, h_terms = moment_terms(solution, residual, complex_src, angle_now, shift_re, shift_im)
    cells = sources.shape[1] * sources.shape[2] * lax.axis_size("dom")
    s_total, h_total = lax.psum((s_terms, h_terms), "point")
    gram_b, gram_a = lax.psum((gram_of(s_total, s_total), gram_of(s_total, h_total)), "dom")
    return (gram_b / cells, gram_a / cells)


Y_IN, X_IN = 2, 4
Y_OUT, X_OUT = GX // Y_IN, GX // X_IN
ROWS = Y_IN * X_IN
LANES = Y_OUT * X_OUT
SUB = 8
BASIS = ITERS + 1
CORES = 2
UNROLL = 4
H_SCALE = 2.0 / COEF_NEAR
FAR_SCALED = 0.5 * H_SCALE * COEF_FAR


def pack_kernel(depth, groups, counts, rows, out, tile):
    columns = rows.shape[0] // (SUB * groups * depth + depth)
    first_level = columns * SUB * groups * depth
    source = lax.broadcasted_iota(jnp.int32, (LANES, LANES), 0)
    target = lax.broadcasted_iota(jnp.int32, (LANES, LANES), 1)
    inner = target // (LANES // ROWS)
    outer = target % (LANES // ROWS)
    cell = (outer // X_OUT * Y_IN + inner // X_IN) * GX + outer % X_OUT * X_IN + inner % X_IN
    swap = jnp.where(source == cell, 1.0, 0.0).astype(jnp.float32)
    parts = []
    for deep in range(depth):
        for group in range(groups):
            for column in range(columns):
                start = (group * SUB * columns + column) * depth + deep
                parts.append(rows[pl.ds(start, SUB, stride=columns * depth), :])
        parts.append(rows[pl.ds(first_level + deep, columns, stride=depth), :])
    mixed = exact_dot(jnp.concatenate(parts, axis=0), swap, ((1,), (0,)))
    block = LANES // ROWS
    lane_block = lax.broadcasted_iota(jnp.int32, (SUB, LANES), 1) // block
    row = lax.broadcasted_iota(jnp.int32, (SUB, LANES), 0)
    for deep in range(depth):
        base = deep * (groups + 1) * columns * SUB - deep * (columns - 1) * SUB
        for group in range(groups):
            pieces = [
                mixed[base + (group * columns + column) * SUB :][:SUB] for column in range(columns)
            ]
            for m in range(ROWS):
                value = pieces[m]
                for column in range(columns):
                    if column != m:
                        moved = pltpu.roll(pieces[column], (column - m) * block % LANES, 1)
                        value = jnp.where(lane_block == column, moved, value)
                start = ((deep * ROWS + m) * groups + group) * SUB
                out[start : start + SUB, :] = value
        piece = mixed[base + groups * columns * SUB :][:SUB]
        value = piece
        for far in range(1, columns):
            moved = pltpu.roll(pltpu.roll(piece, far * block, 1), columns - far, 0)
            value = jnp.where(lane_block == (row + far) % columns, moved, value)
        start = depth * ROWS * SUB * groups + deep * ROWS
        out[start : start + ROWS, :] = value
    tile[...] = jnp.broadcast_to(counts[...].astype(jnp.float32), (SUB, LANES))


def packed_block(sources, potential, iter_counts):
    count, depth, cells = sources.shape
    columns = cells // LANES
    rows = sources.reshape(count, depth, columns, LANES).transpose(0, 2, 1, 3).reshape(-1, LANES)
    levels = potential.reshape(depth, columns, LANES).transpose(1, 0, 2).reshape(-1, LANES)
    vmem = pl.BlockSpec(memory_space=pltpu.VMEM)
    size = depth * ROWS * (count + 1)
    return pl.pallas_call(
        functools.partial(pack_kernel, depth, count // SUB),
        out_shape=(
            jax.ShapeDtypeStruct((size, LANES), jnp.float32),
            jax.ShapeDtypeStruct((SUB, LANES), jnp.float32),
        ),
        in_specs=[vmem, vmem],
        out_specs=(vmem, vmem),
        compiler_params=pltpu.CompilerParams(vmem_limit_bytes=4 * 2**20),
        name="pack",
    )(iter_counts.reshape(1, 1), jnp.concatenate([rows, levels], axis=0))


def lane_sum(values):
    return jnp.broadcast_to(jnp.sum(values, axis=1, keepdims=True), values.shape)


def ratio(top, bottom):
    return jnp.where(bottom > 0.0, top / jnp.where(bottom > 0.0, bottom, 1.0), 0.0)


def x_next(values, wrap_mask):
    return jnp.where(wrap_mask, pltpu.roll(values, X_OUT - 1, 1), pltpu.roll(values, LANES - 1, 1))


def x_prev(values, wrap_mask):
    return jnp.where(wrap_mask, pltpu.roll(values, LANES - X_OUT + 1, 1), pltpu.roll(values, 1, 1))


def tree_sum(values):
    while len(values) > 1:
        values = [sum(values[i : i + 2][1:], values[i]) for i in range(0, len(values), 2)]
    return values[0]


def apply_plane(vector, diagonal, plane, group, last_x, first_x):
    planes = vector.shape[0]
    rows = pl.ds(group * SUB, SUB)

    def plane_at(index):
        return [vector[index % planes, rows, m * LANES : (m + 1) * LANES] for m in range(ROWS)]

    here, above, below = (plane_at(plane + far) for far in (0, 1, -1))
    above_2, below_2 = (plane_at(plane + far) for far in (2, -2))
    y_up = [pltpu.roll(value, LANES - X_OUT, 1) for value in here]
    y_down = [pltpu.roll(value, X_OUT, 1) for value in here]
    out = []
    for yi in range(Y_IN):
        line = here[yi * X_IN : (yi + 1) * X_IN]
        before = [x_prev(line[X_IN - 2], first_x), x_prev(line[X_IN - 1], first_x)]
        after = [x_next(line[0], last_x), x_next(line[1], last_x)]
        wide = before + line + after
        for xi in range(X_IN):
            m = yi * X_IN + xi
            other = (1 - yi) * X_IN + xi
            y_next = here[other] if yi == 0 else y_up[other]
            y_prev = here[other] if yi == 1 else y_down[other]
            near = (wide[xi + 1] + wide[xi + 3]) + (y_next + y_prev) + (above[m] + below[m])
            far = (wide[xi] + wide[xi + 4]) + (y_up[m] + y_down[m]) + (above_2[m] + below_2[m])
            level = diagonal[plane, :, m * LANES : (m + 1) * LANES]
            out.append(level * here[m] - near - FAR_SCALED * far)
    return here, out


def cmul(first, second):
    return (
        first[0] * second[0] - first[1] * second[1],
        first[0] * second[1] + first[1] * second[0],
    )


def moment_coeffs(point, points, count):
    lane = lax.broadcasted_iota(jnp.int32, (1, LANES), 1)
    moment = lax.rem(lane, MOMENTS * count) // count
    angle = 2.0 * math.pi * (point + 0.5) / points
    parts = []
    for func in (math.cos, math.sin):
        value = jnp.full((1, LANES), 0.25 * func(angle), jnp.float32)
        for k in range(1, MOMENTS):
            value = jnp.where(moment == k, 0.25 * func((k + 1) * angle), value)
        parts.append(value)
    return parts


def weights_of(alphas, norms, limits, count):
    points = len(limits)
    shape = (count, LANES)
    half = MOMENTS * count
    lane = lax.broadcasted_iota(jnp.int32, shape, 1)
    source = lax.broadcasted_iota(jnp.int32, shape, 0)
    own = lax.rem(lane, count) == source
    left_half = lane < half
    betas = [ratio(norms[i + 1], norms[i]) for i in range(ITERS - 1)]
    sums = [[jnp.zeros(shape, jnp.float32)] * 2 for _ in range(BASIS)]
    zero = jnp.zeros(shape, jnp.float32)
    one = jnp.ones(shape, jnp.float32)
    for point in range(points):
        angle = 2.0 * math.pi * (point + 0.5) / points
        shift = (GAMMA + RADIUS * math.cos(angle), RADIUS * math.sin(angle))
        scaled_shift = (H_SCALE * shift[0], H_SCALE * shift[1])
        limit = limits[point]
        product = (one, zero)
        products = [product]
        links = []
        pivot = (scaled_shift[0] - alphas[0], zero + scaled_shift[1])
        for i in range(ITERS):
            size = 1.0 / (pivot[0] * pivot[0] + pivot[1] * pivot[1])
            inverse = (pivot[0] * size, -pivot[1] * size)
            product = cmul(product, inverse)
            products.append(product)
            if i < ITERS - 1:
                link = (betas[i] * inverse[0], betas[i] * inverse[1])
                links.append(link)
                pivot = (scaled_shift[0] - alphas[i + 1] - link[0], scaled_shift[1] - link[1])
        solved = [None] * ITERS
        for i in reversed(range(ITERS)):
            value = (H_SCALE * products[i + 1][0], H_SCALE * products[i + 1][1])
            if i < ITERS - 1:
                step = cmul(links[i], solved[i + 1])
                value = (value[0] + step[0], value[1] + step[1])
            used = limit > i
            solved[i] = (jnp.where(used, value[0], 0.0), jnp.where(used, value[1], 0.0))
        applied = []
        for i in range(BASIS):
            left = limit == i
            rest = (
                jnp.where(left, products[i][0], 0.0),
                jnp.where(left, products[i][1], 0.0),
            )
            if i < ITERS:
                turned = (
                    shift[0] * solved[i][0] - shift[1] * solved[i][1],
                    shift[0] * solved[i][1] + shift[1] * solved[i][0],
                )
                rest = (rest[0] + turned[0], rest[1] + turned[1])
            if i == 0:
                rest = (rest[0] - 1.0, rest[1])
            applied.append(rest)
        tail = applied[ITERS]
        for back, factor in ((1, alphas[ITERS - 1]), (2, betas[ITERS - 2])):
            part = applied[ITERS - back]
            applied[ITERS - back] = (part[0] - factor * tail[0], part[1] - factor * tail[1])
        moment = moment_coeffs(point, points, count)
        for i in range(BASIS):
            left = solved[i] if i < ITERS else (zero, zero)
            both = (
                jnp.where(left_half, left[0], applied[i][0]),
                jnp.where(left_half, left[1], applied[i][1]),
            )
            term = cmul(moment, both)
            sums[i] = [sums[i][0] + term[0], sums[i][1] + term[1]]
    return [[jnp.where(own, part, 0.0) for part in pair] for pair in sums]


def exact_dot(first, second, dims):
    return lax.dot_general(
        first,
        second,
        (dims, ((), ())),
        precision=lax.Precision.HIGHEST,
        preferred_element_type=jnp.float32,
    )


def krylov_kernel(parts, count, *refs):
    blocks, (vectors, applied, scalars, first_work, second_work, diagonal) = refs[:parts], refs[parts:]
    planes = diagonal.shape[0]
    depth = planes // parts
    groups = count // SUB
    lane = lax.broadcasted_iota(jnp.int32, (SUB, LANES), 1)
    last_x = lax.rem(lane, X_OUT) == X_OUT - 1
    first_x = lax.rem(lane, X_OUT) == 0
    here = lax.axis_index("dom")
    for turn in range(parts):
        slab = jnp.bitwise_xor(here, turn) * depth
        for deep in range(depth):
            for m in range(ROWS):
                start = (deep * ROWS + m) * count
                lanes = slice(m * LANES, (m + 1) * LANES)
                value = blocks[turn][start : start + count, :]
                first_work[slab + deep, :, lanes] = value
                vectors[0, slab + deep, :, lanes] = value
            start = depth * ROWS * count + deep * ROWS
            levels = H_SCALE * (blocks[turn][start : start + ROWS, :] + 3.75)
            for m in range(ROWS):
                level = jnp.broadcast_to(levels[m : m + 1, :], (SUB, LANES))
                diagonal[slab + deep, :, m * LANES : (m + 1) * LANES] = level
    second_work[...] = jnp.zeros_like(second_work)
    scalars[ITERS] = jnp.zeros((count, LANES), jnp.float32)

    all_rows = [pl.ds(group * SUB, SUB) for group in range(groups)]
    all_lanes = [slice(m * LANES, (m + 1) * LANES) for m in range(ROWS)]
    for group, rows in enumerate(all_rows):
        norm = []
        for plane in range(planes):
            values = [first_work[plane, rows, lanes] for lanes in all_lanes]
            norm.append(tree_sum([value * value for value in values]))
        scalars[ITERS + 1, rows, :] = lane_sum(tree_sum(norm))

    def half_turn(i, work, before):
        curves = []
        for group, rows in enumerate(all_rows):
            curve = []
            for plane in range(planes):
                value, out = apply_plane(work, diagonal, plane, group, last_x, first_x)
                for m, lanes in enumerate(all_lanes):
                    applied[plane, rows, lanes] = out[m]
                curve.append(tree_sum([value[m] * out[m] for m in range(ROWS)]))
            curves.append(lane_sum(tree_sum(curve)))
        alphas = []
        for group, rows in enumerate(all_rows):
            alphas.append(ratio(curves[group], scalars[ITERS + 1 + i, rows, :]))
            scalars[i, rows, :] = alphas[group]

        @pl.when(i < ITERS - 1)
        def _():
            norms = []
            for group, rows in enumerate(all_rows):
                beta = ratio(scalars[ITERS + 1 + i, rows, :], scalars[ITERS + i, rows, :])
                norm = []
                for plane in range(planes):
                    values = []
                    for lanes in all_lanes:
                        value = applied[plane, rows, lanes]
                        value = value - alphas[group] * work[plane, rows, lanes]
                        value = value - beta * before[plane, rows, lanes]
                        before[plane, rows, lanes] = value
                        vectors[i + 1, plane, rows, lanes] = value
                        values.append(value * value)
                    norm.append(tree_sum(values))
                norms.append(lane_sum(tree_sum(norm)))
            for group, rows in enumerate(all_rows):
                scalars[ITERS + 2 + i, rows, :] = norms[group]

    def turn(step, carry):
        half_turn(2 * step, first_work, second_work)
        half_turn(2 * step + 1, second_work, first_work)
        return carry

    lax.fori_loop(0, ITERS // 2, turn, 0)


def gram_kernel(points, scalars, *refs):
    tiles = refs[:points]
    archive, applied, out_b, out_a, gram, limits = refs[points:]
    planes, count, _ = applied.shape
    groups = count // SUB
    size = BASIS * count
    gram[...] = jnp.zeros_like(gram)

    def gram_turn(plane, carry):
        values = [archive[i, plane] for i in range(ITERS)] + [applied[plane]]
        values = jnp.concatenate(values, axis=0)
        high = values.astype(jnp.bfloat16)
        low = (values - high.astype(jnp.float32)).astype(jnp.bfloat16)
        gram[...] += lax.dot_general(
            jnp.concatenate([high, low], axis=0),
            high,
            (((1,), (1,)), ((), ())),
            preferred_element_type=jnp.float32,
        )
        return carry

    lax.fori_loop(0, planes, gram_turn, 0, unroll=UNROLL)
    cross = gram[size:, :]
    pairs = gram[:size, :] + cross + cross.T

    here = lax.axis_index("point")
    core = jnp.bitwise_and(lax.axis_index("dom"), CORES - 1)
    for far, tile in zip((0, 1 + core, 3, 2 - core), tiles):
        limits[jnp.bitwise_xor(here, far)] = tile[...]
    bounds = [jnp.concatenate([limits[j]] * groups, axis=0) for j in range(points)]
    alphas = [scalars[i] for i in range(ITERS)]
    norms = [scalars[ITERS + 1 + i] for i in range(ITERS)]
    weights = weights_of(alphas, norms, bounds, count)
    real = jnp.concatenate([pair[0] for pair in weights], axis=0)
    imag = jnp.concatenate([pair[1] for pair in weights], axis=0)
    right = exact_dot(pairs, jnp.concatenate([real, imag], axis=1), ((1,), (0,)))
    half = MOMENTS * count
    left = jnp.concatenate([real[:, :half], imag[:, :half]], axis=1)
    joined = exact_dot(left.T, right, ((1,), (0,)))
    scale = 1.0 / (planes * ROWS * LANES)
    width = 2 * half
    real = (joined[:half, :width] + joined[half:, width:]) * scale
    imag = (joined[:half, width:] - joined[half:, :width]) * scale
    out_b[0] = real[:, :half]
    out_b[1] = imag[:, :half]
    out_a[0] = real[:, half:]
    out_a[1] = imag[:, half:]


def swapped(values, axis, size, mask):
    return lax.ppermute(values, axis, [(index ^ mask, index) for index in range(size)])


def whole_grid(sources, potential, iter_counts, *, parts, points):
    count, depth, _ = sources.shape
    planes = parts * depth
    block, tile = packed_block(sources, potential, iter_counts)
    even = [block] + [swapped(block, "dom", parts, mask) for mask in range(CORES, parts, CORES)]
    mixed = [
        ((point ^ (1 + part % CORES)) * parts + part, point * parts + part)
        for point in range(points)
        for part in range(parts)
    ]
    tiles = [lax.ppermute(tile, ("point", "dom"), mixed), swapped(tile, "point", points, 3)]
    even[1], *tiles = lax.optimization_barrier((even[1], *tiles))
    tiles.append(swapped(tiles[0], "dom", parts, 1))
    odd = [swapped(value, "dom", parts, 1) for value in even]
    blocks = [value for pair in zip(even, odd) for value in pair]
    vmem = pl.BlockSpec(memory_space=pltpu.VMEM)
    vector = (planes, count, ROWS * LANES)
    cells = planes * ROWS * LANES
    vectors, applied, scalars = pl.pallas_call(
        functools.partial(krylov_kernel, parts, count),
        out_shape=(
            jax.ShapeDtypeStruct((ITERS,) + vector, jnp.float32),
            jax.ShapeDtypeStruct(vector, jnp.float32),
            jax.ShapeDtypeStruct((2 * ITERS + 1, count, LANES), jnp.float32),
        ),
        in_specs=[vmem] * parts,
        out_specs=(vmem,) * 3,
        scratch_shapes=[
            pltpu.VMEM(vector, jnp.float32),
            pltpu.VMEM(vector, jnp.float32),
            pltpu.VMEM((planes, SUB, ROWS * LANES), jnp.float32),
        ],
        compiler_params=pltpu.CompilerParams(vmem_limit_bytes=16 * 2**20),
        name="krylov",
    )(*blocks)
    size = BASIS * count
    width = MOMENTS * count
    out = jax.ShapeDtypeStruct((2, width, width), jnp.float32)
    return pl.pallas_call(
        functools.partial(gram_kernel, points),
        out_shape=(out, out),
        in_specs=[vmem] * (3 + points),
        out_specs=(vmem, vmem),
        scratch_shapes=[
            pltpu.VMEM((2 * size, size), jnp.float32),
            pltpu.VMEM((points, SUB, LANES), jnp.float32),
        ],
        compiler_params=pltpu.CompilerParams(vmem_limit_bytes=16 * 2**20),
        name="gram",
    )(scalars, tile, *tiles, vectors, applied)


def on_device(sources, potential, iter_counts):
    parts, points = lax.axis_size("dom"), lax.axis_size("point")
    count, depth, cells = sources.shape
    held = BASIS * count * parts * depth * cells * 4
    fits = (
        held <= 16 * 2**20
        and parts == 8
        and points == 4
        and count == 2 * SUB
        and 2 * MOMENTS * count == LANES
        and parts * depth == 16
        and cells == GX * GX == ROWS * LANES
    )
    if not fits:
        return split_grid(sources, potential, iter_counts)
    return whole_grid(sources, potential, iter_counts, parts=parts, points=points)


def solution(mesh):
    placed = (P(None, "dom", None), P("dom", None), P("point"))
    return jax.shard_map(
        on_device, mesh=mesh, in_specs=placed, out_specs=(P(), P()), check_vma=False
    )
```

```python
import functools
import math

import jax
import jax.numpy as jnp
from jax import lax
from jax.experimental import pallas as pl
from jax.experimental.pallas import tpu as pltpu
from jax.sharding import PartitionSpec as P

MOMENTS = 4
ITERS = 6
GX = 32


COEF_NEAR = 4.0 / 3.0
COEF_FAR = -1.0 / 12.0
GAMMA = 2.0
RADIUS = 1.5


def padded_2(block, sides, width):
    for axis, dim in sides:
        count = lax.axis_size(axis)
        forward = [(i, i + 1) for i in range(count - 1)]
        forward.append((count - 1, 0))
        backward = [(target, source) for source, target in forward]
        low = lax.ppermute(
            lax.slice_in_dim(block, block.shape[dim] - width, None, axis=dim), axis, forward
        )
        high = lax.ppermute(lax.slice_in_dim(block, 0, width, axis=dim), axis, backward)
        block = jnp.concatenate([low, block, high], axis=dim)
    return block


def plane_terms(values, side):
    lead = values.shape[:-1]
    planes = values.reshape(lead + (side, side))
    summed = COEF_NEAR * (
        jnp.roll(planes, 1, -2)
        + jnp.roll(planes, -1, -2)
        + jnp.roll(planes, 1, -1)
        + jnp.roll(planes, -1, -1)
    )
    summed = summed + COEF_FAR * (
        jnp.roll(planes, 2, -2)
        + jnp.roll(planes, -2, -2)
        + jnp.roll(planes, 2, -1)
        + jnp.roll(planes, -2, -1)
    )
    return summed.reshape(values.shape)


def complex_mul(first, second):
    return jnp.stack(
        [first[0] * second[0] - first[1] * second[1], first[0] * second[1] + first[1] * second[0]]
    )


def complex_div(first, second):
    denom = second[0] * second[0] + second[1] * second[1]
    return jnp.stack(
        [
            (first[0] * second[0] + first[1] * second[1]) / denom,
            (first[1] * second[0] - first[0] * second[1]) / denom,
        ]
    )


def bilinear(first, second):
    real_part = jnp.sum(first[0] * second[0] - first[1] * second[1], axis=(1, 2))
    imag_part = jnp.sum(first[0] * second[1] + first[1] * second[0], axis=(1, 2))
    return jnp.stack([real_part, imag_part])


def scaled(coeffs, values):
    return complex_mul(coeffs[:, :, None, None], values)


def shifted(values, potential, shift_re, shift_im):
    padded = padded_2(values, (("dom", 2),), 2)
    depth = values.shape[2]
    lap = -7.5 * values + plane_terms(values, GX)
    lap = lap + COEF_NEAR * (padded[:, :, 3 : 3 + depth] + padded[:, :, 1 : 1 + depth])
    lap = lap + COEF_FAR * (padded[:, :, 4 : 4 + depth] + padded[:, :, 0:depth])
    applied = -0.5 * lap + potential * values
    return jnp.stack(
        [
            shift_re * values[0] - shift_im * values[1] - applied[0],
            shift_re * values[1] + shift_im * values[0] - applied[1],
        ]
    )


def residual_sum(values):
    return lax.psum(bilinear(values, values), "dom")


def moment_terms(solution, residual, sources, angle_now, shift_re, shift_im):
    applied = jnp.stack(
        [
            shift_re * solution[0] - shift_im * solution[1] - sources[0] + residual[0],
            shift_re * solution[1] + shift_im * solution[0] - sources[1] + residual[1],
        ]
    )
    angles = (jnp.arange(MOMENTS).astype(jnp.float32) + 1.0) * angle_now
    coeffs = 0.25 * jnp.stack([jnp.cos(angles), jnp.sin(angles)])
    s_terms = complex_mul(coeffs[:, :, None, None, None], solution[:, None])
    h_terms = complex_mul(coeffs[:, :, None, None, None], applied[:, None])
    width = MOMENTS * solution.shape[1]
    return (s_terms.reshape(2, width, -1), h_terms.reshape(2, width, -1))


def gram_of(left, right):
    width = left.shape[1]
    joined = lax.dot_general(
        left.reshape(2 * width, -1),
        right.reshape(2 * width, -1),
        (((1,), (1,)), ((), ())),
        precision=lax.Precision.HIGHEST,
        preferred_element_type=jnp.float32,
    )
    blocks = joined.reshape(2, width, 2, width)
    return jnp.stack([blocks[0, :, 0] + blocks[1, :, 1], blocks[0, :, 1] - blocks[1, :, 0]])


def split_grid(sources, potential, iter_counts):
    complex_src = jnp.stack([sources, jnp.zeros_like(sources)])
    angle_now = (
        2.0 * math.pi * (lax.axis_index("point").astype(jnp.float32) + 0.5) / lax.axis_size("point")
    )
    shift_re = GAMMA + RADIUS * jnp.cos(angle_now)
    shift_im = RADIUS * jnp.sin(angle_now)
    limit = iter_counts[0]
    solution = jnp.zeros_like(complex_src)

    def one_turn(turn_idx, state):
        solution, residual, search, norm_now = state
        product = shifted(search, potential, shift_re, shift_im)
        curve = lax.psum(bilinear(search, product), "dom")
        step_size = complex_div(norm_now, curve)
        new_residual = residual - scaled(step_size, product)
        norm_next = residual_sum(new_residual)
        fresh = (
            solution + scaled(step_size, search),
            new_residual,
            new_residual + scaled(complex_div(norm_next, norm_now), search),
            norm_next,
        )
        keep_mask = turn_idx < limit
        return jax.tree.map(lambda newer, older: jnp.where(keep_mask, newer, older), fresh, state)

    start = (solution, complex_src, complex_src, residual_sum(complex_src))
    solution, residual, search, norm_now = lax.fori_loop(0, ITERS, one_turn, start)
    s_terms, h_terms = moment_terms(solution, residual, complex_src, angle_now, shift_re, shift_im)
    cells = sources.shape[1] * sources.shape[2] * lax.axis_size("dom")
    s_total, h_total = lax.psum((s_terms, h_terms), "point")
    gram_b, gram_a = lax.psum((gram_of(s_total, s_total), gram_of(s_total, h_total)), "dom")
    return (gram_b / cells, gram_a / cells)


Y_IN, X_IN = 2, 4
Y_OUT, X_OUT = GX // Y_IN, GX // X_IN
ROWS = Y_IN * X_IN
LANES = Y_OUT * X_OUT
SUB = 8
BASIS = ITERS + 1
CORES = 2
UNROLL = 4
H_SCALE = 2.0 / COEF_NEAR
FAR_SCALED = 0.5 * H_SCALE * COEF_FAR


def pack_kernel(depth, groups, counts, rows, out, tile):
    columns = rows.shape[0] // (SUB * groups * depth + depth)
    first_level = columns * SUB * groups * depth
    source = lax.broadcasted_iota(jnp.int32, (LANES, LANES), 0)
    target = lax.broadcasted_iota(jnp.int32, (LANES, LANES), 1)
    inner = target // (LANES // ROWS)
    outer = target % (LANES // ROWS)
    cell = (outer // X_OUT * Y_IN + inner // X_IN) * GX + outer % X_OUT * X_IN + inner % X_IN
    swap = jnp.where(source == cell, 1.0, 0.0).astype(jnp.float32)
    parts = []
    for deep in range(depth):
        for group in range(groups):
            for column in range(columns):
                start = (group * SUB * columns + column) * depth + deep
                parts.append(rows[pl.ds(start, SUB, stride=columns * depth), :])
        parts.append(rows[pl.ds(first_level + deep, columns, stride=depth), :])
    mixed = exact_dot(jnp.concatenate(parts, axis=0), swap, ((1,), (0,)))
    block = LANES // ROWS
    lane_block = lax.broadcasted_iota(jnp.int32, (SUB, LANES), 1) // block
    row = lax.broadcasted_iota(jnp.int32, (SUB, LANES), 0)
    for deep in range(depth):
        base = deep * (groups + 1) * columns * SUB - deep * (columns - 1) * SUB
        for group in range(groups):
            pieces = [
                mixed[base + (group * columns + column) * SUB :][:SUB] for column in range(columns)
            ]
            for m in range(ROWS):
                value = pieces[m]
                for column in range(columns):
                    if column != m:
                        moved = pltpu.roll(pieces[column], (column - m) * block % LANES, 1)
                        value = jnp.where(lane_block == column, moved, value)
                start = ((deep * ROWS + m) * groups + group) * SUB
                out[start : start + SUB, :] = value
        piece = mixed[base + groups * columns * SUB :][:SUB]
        value = piece
        for far in range(1, columns):
            moved = pltpu.roll(pltpu.roll(piece, far * block, 1), columns - far, 0)
            value = jnp.where(lane_block == (row + far) % columns, moved, value)
        start = depth * ROWS * SUB * groups + deep * ROWS
        out[start : start + ROWS, :] = value
    tile[...] = jnp.broadcast_to(counts[...].astype(jnp.float32), (SUB, LANES))


def packed_block(sources, potential, iter_counts):
    count, depth, cells = sources.shape
    columns = cells // LANES
    rows = sources.reshape(count, depth, columns, LANES).transpose(0, 2, 1, 3).reshape(-1, LANES)
    levels = potential.reshape(depth, columns, LANES).transpose(1, 0, 2).reshape(-1, LANES)
    vmem = pl.BlockSpec(memory_space=pltpu.VMEM)
    size = depth * ROWS * (count + 1)
    return pl.pallas_call(
        functools.partial(pack_kernel, depth, count // SUB),
        out_shape=(
            jax.ShapeDtypeStruct((size, LANES), jnp.float32),
            jax.ShapeDtypeStruct((SUB, LANES), jnp.float32),
        ),
        in_specs=[vmem, vmem],
        out_specs=(vmem, vmem),
        compiler_params=pltpu.CompilerParams(vmem_limit_bytes=4 * 2**20),
        name="pack",
    )(iter_counts.reshape(1, 1), jnp.concatenate([rows, levels], axis=0))


def lane_sum(values):
    return jnp.broadcast_to(jnp.sum(values, axis=1, keepdims=True), values.shape)


def ratio(top, bottom):
    return jnp.where(bottom > 0.0, top / jnp.where(bottom > 0.0, bottom, 1.0), 0.0)


def tree_sum(values):
    while len(values) > 1:
        values = [sum(values[i : i + 2][1:], values[i]) for i in range(0, len(values), 2)]
    return values[0]


def apply_plane(vector, diagonal, plane, group, last_x, first_x):
    planes = vector.shape[0]
    rows = pl.ds(group * SUB, SUB)

    def plane_at(index):
        return [vector[index % planes, rows, m * LANES : (m + 1) * LANES] for m in range(ROWS)]

    here, above, below = (plane_at(plane + far) for far in (0, 1, -1))
    above_2, below_2 = (plane_at(plane + far) for far in (2, -2))
    y_up = [pltpu.roll(value, LANES - X_OUT, 1) for value in here]
    y_down = [pltpu.roll(value, X_OUT, 1) for value in here]
    out = []
    for yi in range(Y_IN):
        line = here[yi * X_IN : (yi + 1) * X_IN]
        before = [
            pltpu.roll(jnp.where(last_x, y_up[yi * X_IN + xi], line[xi]), 1, 1)
            for xi in range(X_IN - 2, X_IN)
        ]
        after = [
            pltpu.roll(jnp.where(first_x, y_down[yi * X_IN + xi], line[xi]), LANES - 1, 1)
            for xi in range(2)
        ]
        wide = before + line + after
        for xi in range(X_IN):
            m = yi * X_IN + xi
            other = (1 - yi) * X_IN + xi
            y_next = here[other] if yi == 0 else y_up[other]
            y_prev = here[other] if yi == 1 else y_down[other]
            near = (wide[xi + 1] + wide[xi + 3]) + (y_next + y_prev) + (above[m] + below[m])
            far = (wide[xi] + wide[xi + 4]) + (y_up[m] + y_down[m]) + (above_2[m] + below_2[m])
            level = diagonal[plane, :, m * LANES : (m + 1) * LANES]
            out.append(level * here[m] - near - FAR_SCALED * far)
    return here, out


def cmul(first, second):
    return (
        first[0] * second[0] - first[1] * second[1],
        first[0] * second[1] + first[1] * second[0],
    )


def moment_coeffs(point, points, count):
    lane = lax.broadcasted_iota(jnp.int32, (1, LANES), 1)
    moment = lax.rem(lane, MOMENTS * count) // count
    angle = 2.0 * math.pi * (point + 0.5) / points
    parts = []
    for func in (math.cos, math.sin):
        value = jnp.full((1, LANES), 0.25 * func(angle), jnp.float32)
        for k in range(1, MOMENTS):
            value = jnp.where(moment == k, 0.25 * func((k + 1) * angle), value)
        parts.append(value)
    return parts


def weights_of(alphas, norms, limits, count):
    points = len(limits)
    shape = (count, LANES)
    half = MOMENTS * count
    lane = lax.broadcasted_iota(jnp.int32, shape, 1)
    source = lax.broadcasted_iota(jnp.int32, shape, 0)
    own = lax.rem(lane, count) == source
    left_half = lane < half
    betas = [ratio(norms[i + 1], norms[i]) for i in range(ITERS - 1)]
    sums = [[jnp.zeros(shape, jnp.float32)] * 2 for _ in range(BASIS)]
    zero = jnp.zeros(shape, jnp.float32)
    one = jnp.ones(shape, jnp.float32)
    for point in range(points):
        angle = 2.0 * math.pi * (point + 0.5) / points
        shift = (GAMMA + RADIUS * math.cos(angle), RADIUS * math.sin(angle))
        scaled_shift = (H_SCALE * shift[0], H_SCALE * shift[1])
        limit = limits[point]
        product = (one, zero)
        products = [product]
        links = []
        pivot = (scaled_shift[0] - alphas[0], zero + scaled_shift[1])
        for i in range(ITERS):
            size = 1.0 / (pivot[0] * pivot[0] + pivot[1] * pivot[1])
            inverse = (pivot[0] * size, -pivot[1] * size)
            product = cmul(product, inverse)
            products.append(product)
            if i < ITERS - 1:
                link = (betas[i] * inverse[0], betas[i] * inverse[1])
                links.append(link)
                pivot = (scaled_shift[0] - alphas[i + 1] - link[0], scaled_shift[1] - link[1])
        solved = [None] * ITERS
        for i in reversed(range(ITERS)):
            value = (H_SCALE * products[i + 1][0], H_SCALE * products[i + 1][1])
            if i < ITERS - 1:
                step = cmul(links[i], solved[i + 1])
                value = (value[0] + step[0], value[1] + step[1])
            used = limit > i
            solved[i] = (jnp.where(used, value[0], 0.0), jnp.where(used, value[1], 0.0))
        applied = []
        for i in range(BASIS):
            left = limit == i
            rest = (
                jnp.where(left, products[i][0], 0.0),
                jnp.where(left, products[i][1], 0.0),
            )
            if i < ITERS:
                turned = (
                    shift[0] * solved[i][0] - shift[1] * solved[i][1],
                    shift[0] * solved[i][1] + shift[1] * solved[i][0],
                )
                rest = (rest[0] + turned[0], rest[1] + turned[1])
            if i == 0:
                rest = (rest[0] - 1.0, rest[1])
            applied.append(rest)
        tail = applied[ITERS]
        for back, factor in ((1, alphas[ITERS - 1]), (2, betas[ITERS - 2])):
            part = applied[ITERS - back]
            applied[ITERS - back] = (part[0] - factor * tail[0], part[1] - factor * tail[1])
        moment = moment_coeffs(point, points, count)
        for i in range(BASIS):
            left = solved[i] if i < ITERS else (zero, zero)
            both = (
                jnp.where(left_half, left[0], applied[i][0]),
                jnp.where(left_half, left[1], applied[i][1]),
            )
            term = cmul(moment, both)
            sums[i] = [sums[i][0] + term[0], sums[i][1] + term[1]]
    return [[jnp.where(own, part, 0.0) for part in pair] for pair in sums]


def exact_dot(first, second, dims):
    return lax.dot_general(
        first,
        second,
        (dims, ((), ())),
        precision=lax.Precision.HIGHEST,
        preferred_element_type=jnp.float32,
    )


def krylov_kernel(parts, count, *refs):
    blocks, (vectors, applied, scalars, first_work, second_work, diagonal) = refs[:parts], refs[parts:]
    planes = diagonal.shape[0]
    depth = planes // parts
    groups = count // SUB
    lane = lax.broadcasted_iota(jnp.int32, (SUB, LANES), 1)
    last_x = lax.rem(lane, X_OUT) == X_OUT - 1
    first_x = lax.rem(lane, X_OUT) == 0
    here = lax.axis_index("dom")
    for turn in range(parts):
        slab = jnp.bitwise_xor(here, turn) * depth
        for deep in range(depth):
            for m in range(ROWS):
                start = (deep * ROWS + m) * count
                lanes = slice(m * LANES, (m + 1) * LANES)
                value = blocks[turn][start : start + count, :]
                first_work[slab + deep, :, lanes] = value
                vectors[0, slab + deep, :, lanes] = value
            start = depth * ROWS * count + deep * ROWS
            levels = H_SCALE * (blocks[turn][start : start + ROWS, :] + 3.75)
            for m in range(ROWS):
                level = jnp.broadcast_to(levels[m : m + 1, :], (SUB, LANES))
                diagonal[slab + deep, :, m * LANES : (m + 1) * LANES] = level
    second_work[...] = jnp.zeros_like(second_work)
    scalars[ITERS] = jnp.zeros((count, LANES), jnp.float32)

    all_rows = [pl.ds(group * SUB, SUB) for group in range(groups)]
    all_lanes = [slice(m * LANES, (m + 1) * LANES) for m in range(ROWS)]
    for group, rows in enumerate(all_rows):
        norm = []
        for plane in range(planes):
            values = [first_work[plane, rows, lanes] for lanes in all_lanes]
            norm.append(tree_sum([value * value for value in values]))
        scalars[ITERS + 1, rows, :] = lane_sum(tree_sum(norm))

    def half_turn(i, work, before):
        curves = []
        for group, rows in enumerate(all_rows):
            curve = []
            for plane in range(planes):
                value, out = apply_plane(work, diagonal, plane, group, last_x, first_x)
                for m, lanes in enumerate(all_lanes):
                    applied[plane, rows, lanes] = out[m]
                curve.append(tree_sum([value[m] * out[m] for m in range(ROWS)]))
            curves.append(lane_sum(tree_sum(curve)))
        alphas = []
        for group, rows in enumerate(all_rows):
            alphas.append(ratio(curves[group], scalars[ITERS + 1 + i, rows, :]))
            scalars[i, rows, :] = alphas[group]

        @pl.when(i < ITERS - 1)
        def _():
            norms = []
            for group, rows in enumerate(all_rows):
                beta = ratio(scalars[ITERS + 1 + i, rows, :], scalars[ITERS + i, rows, :])
                norm = []
                for plane in range(planes):
                    values = []
                    for lanes in all_lanes:
                        value = applied[plane, rows, lanes]
                        value = value - alphas[group] * work[plane, rows, lanes]
                        value = value - beta * before[plane, rows, lanes]
                        before[plane, rows, lanes] = value
                        vectors[i + 1, plane, rows, lanes] = value
                        values.append(value * value)
                    norm.append(tree_sum(values))
                norms.append(lane_sum(tree_sum(norm)))
            for group, rows in enumerate(all_rows):
                scalars[ITERS + 2 + i, rows, :] = norms[group]

    def turn(step, carry):
        half_turn(2 * step, first_work, second_work)
        half_turn(2 * step + 1, second_work, first_work)
        return carry

    lax.fori_loop(0, ITERS // 2, turn, 0)


def gram_kernel(points, scalars, *refs):
    tiles = refs[:points]
    archive, applied, out_b, out_a, gram, limits = refs[points:]
    planes, count, _ = applied.shape
    groups = count // SUB
    size = BASIS * count
    gram[...] = jnp.zeros_like(gram)

    def gram_turn(plane, carry):
        values = [archive[i, plane] for i in range(ITERS)] + [applied[plane]]
        values = jnp.concatenate(values, axis=0)
        high = values.astype(jnp.bfloat16)
        low = (values - high.astype(jnp.float32)).astype(jnp.bfloat16)
        gram[...] += lax.dot_general(
            jnp.concatenate([high, low], axis=0),
            high,
            (((1,), (1,)), ((), ())),
            preferred_element_type=jnp.float32,
        )
        return carry

    lax.fori_loop(0, planes, gram_turn, 0, unroll=UNROLL)
    cross = gram[size:, :]
    pairs = gram[:size, :] + cross + cross.T

    here = lax.axis_index("point")
    core = jnp.bitwise_and(lax.axis_index("dom"), CORES - 1)
    for far, tile in zip((0, 1 + core, 3, 2 - core), tiles):
        limits[jnp.bitwise_xor(here, far)] = tile[...]
    bounds = [jnp.concatenate([limits[j]] * groups, axis=0) for j in range(points)]
    alphas = [scalars[i] for i in range(ITERS)]
    norms = [scalars[ITERS + 1 + i] for i in range(ITERS)]
    weights = weights_of(alphas, norms, bounds, count)
    real = jnp.concatenate([pair[0] for pair in weights], axis=0)
    imag = jnp.concatenate([pair[1] for pair in weights], axis=0)
    right = exact_dot(pairs, jnp.concatenate([real, imag], axis=1), ((1,), (0,)))
    half = MOMENTS * count
    left = jnp.concatenate([real[:, :half], imag[:, :half]], axis=1)
    joined = exact_dot(left.T, right, ((1,), (0,)))
    scale = 1.0 / (planes * ROWS * LANES)
    width = 2 * half
    real = (joined[:half, :width] + joined[half:, width:]) * scale
    imag = (joined[:half, width:] - joined[half:, :width]) * scale
    out_b[0] = real[:, :half]
    out_b[1] = imag[:, :half]
    out_a[0] = real[:, half:]
    out_a[1] = imag[:, half:]


def swapped(values, axis, size, mask):
    return lax.ppermute(values, axis, [(index ^ mask, index) for index in range(size)])


def whole_grid(sources, potential, iter_counts, *, parts, points):
    count, depth, _ = sources.shape
    planes = parts * depth
    block, tile = packed_block(sources, potential, iter_counts)
    even = [block] + [swapped(block, "dom", parts, mask) for mask in range(CORES, parts, CORES)]
    mixed = [
        ((point ^ (1 + part % CORES)) * parts + part, point * parts + part)
        for point in range(points)
        for part in range(parts)
    ]
    tiles = [lax.ppermute(tile, ("point", "dom"), mixed), swapped(tile, "point", points, 3)]
    even[1], *tiles = lax.optimization_barrier((even[1], *tiles))
    tiles.append(swapped(tiles[0], "dom", parts, 1))
    odd = [swapped(value, "dom", parts, 1) for value in even]
    blocks = [value for pair in zip(even, odd) for value in pair]
    vmem = pl.BlockSpec(memory_space=pltpu.VMEM)
    vector = (planes, count, ROWS * LANES)
    cells = planes * ROWS * LANES
    vectors, applied, scalars = pl.pallas_call(
        functools.partial(krylov_kernel, parts, count),
        out_shape=(
            jax.ShapeDtypeStruct((ITERS,) + vector, jnp.float32),
            jax.ShapeDtypeStruct(vector, jnp.float32),
            jax.ShapeDtypeStruct((2 * ITERS + 1, count, LANES), jnp.float32),
        ),
        in_specs=[vmem] * parts,
        out_specs=(vmem,) * 3,
        scratch_shapes=[
            pltpu.VMEM(vector, jnp.float32),
            pltpu.VMEM(vector, jnp.float32),
            pltpu.VMEM((planes, SUB, ROWS * LANES), jnp.float32),
        ],
        compiler_params=pltpu.CompilerParams(vmem_limit_bytes=16 * 2**20),
        name="krylov",
    )(*blocks)
    size = BASIS * count
    width = MOMENTS * count
    out = jax.ShapeDtypeStruct((2, width, width), jnp.float32)
    return pl.pallas_call(
        functools.partial(gram_kernel, points),
        out_shape=(out, out),
        in_specs=[vmem] * (3 + points),
        out_specs=(vmem, vmem),
        scratch_shapes=[
            pltpu.VMEM((2 * size, size), jnp.float32),
            pltpu.VMEM((points, SUB, LANES), jnp.float32),
        ],
        compiler_params=pltpu.CompilerParams(vmem_limit_bytes=16 * 2**20),
        name="gram",
    )(scalars, tile, *tiles, vectors, applied)


def on_device(sources, potential, iter_counts):
    parts, points = lax.axis_size("dom"), lax.axis_size("point")
    count, depth, cells = sources.shape
    held = BASIS * count * parts * depth * cells * 4
    fits = (
        held <= 16 * 2**20
        and parts == 8
        and points == 4
        and count == 2 * SUB
        and 2 * MOMENTS * count == LANES
        and parts * depth == 16
        and cells == GX * GX == ROWS * LANES
    )
    if not fits:
        return split_grid(sources, potential, iter_counts)
    return whole_grid(sources, potential, iter_counts, parts=parts, points=points)


def solution(mesh):
    placed = (P(None, "dom", None), P("dom", None), P("point"))
    return jax.shard_map(
        on_device, mesh=mesh, in_specs=placed, out_specs=(P(), P()), check_vma=False
    )
```

```python
import functools
import math

import jax
import jax.numpy as jnp
from jax import lax
from jax.experimental import pallas as pl
from jax.experimental.pallas import tpu as pltpu
from jax.sharding import PartitionSpec as P

MOMENTS = 4
ITERS = 6
GX = 32


COEF_NEAR = 4.0 / 3.0
COEF_FAR = -1.0 / 12.0
GAMMA = 2.0
RADIUS = 1.5


def padded_2(block, sides, width):
    for axis, dim in sides:
        count = lax.axis_size(axis)
        forward = [(i, i + 1) for i in range(count - 1)]
        forward.append((count - 1, 0))
        backward = [(target, source) for source, target in forward]
        low = lax.ppermute(
            lax.slice_in_dim(block, block.shape[dim] - width, None, axis=dim), axis, forward
        )
        high = lax.ppermute(lax.slice_in_dim(block, 0, width, axis=dim), axis, backward)
        block = jnp.concatenate([low, block, high], axis=dim)
    return block


def plane_terms(values, side):
    lead = values.shape[:-1]
    planes = values.reshape(lead + (side, side))
    summed = COEF_NEAR * (
        jnp.roll(planes, 1, -2)
        + jnp.roll(planes, -1, -2)
        + jnp.roll(planes, 1, -1)
        + jnp.roll(planes, -1, -1)
    )
    summed = summed + COEF_FAR * (
        jnp.roll(planes, 2, -2)
        + jnp.roll(planes, -2, -2)
        + jnp.roll(planes, 2, -1)
        + jnp.roll(planes, -2, -1)
    )
    return summed.reshape(values.shape)


def complex_mul(first, second):
    return jnp.stack(
        [first[0] * second[0] - first[1] * second[1], first[0] * second[1] + first[1] * second[0]]
    )


def complex_div(first, second):
    denom = second[0] * second[0] + second[1] * second[1]
    return jnp.stack(
        [
            (first[0] * second[0] + first[1] * second[1]) / denom,
            (first[1] * second[0] - first[0] * second[1]) / denom,
        ]
    )


def bilinear(first, second):
    real_part = jnp.sum(first[0] * second[0] - first[1] * second[1], axis=(1, 2))
    imag_part = jnp.sum(first[0] * second[1] + first[1] * second[0], axis=(1, 2))
    return jnp.stack([real_part, imag_part])


def scaled(coeffs, values):
    return complex_mul(coeffs[:, :, None, None], values)


def shifted(values, potential, shift_re, shift_im):
    padded = padded_2(values, (("dom", 2),), 2)
    depth = values.shape[2]
    lap = -7.5 * values + plane_terms(values, GX)
    lap = lap + COEF_NEAR * (padded[:, :, 3 : 3 + depth] + padded[:, :, 1 : 1 + depth])
    lap = lap + COEF_FAR * (padded[:, :, 4 : 4 + depth] + padded[:, :, 0:depth])
    applied = -0.5 * lap + potential * values
    return jnp.stack(
        [
            shift_re * values[0] - shift_im * values[1] - applied[0],
            shift_re * values[1] + shift_im * values[0] - applied[1],
        ]
    )


def residual_sum(values):
    return lax.psum(bilinear(values, values), "dom")


def moment_terms(solution, residual, sources, angle_now, shift_re, shift_im):
    applied = jnp.stack(
        [
            shift_re * solution[0] - shift_im * solution[1] - sources[0] + residual[0],
            shift_re * solution[1] + shift_im * solution[0] - sources[1] + residual[1],
        ]
    )
    angles = (jnp.arange(MOMENTS).astype(jnp.float32) + 1.0) * angle_now
    coeffs = 0.25 * jnp.stack([jnp.cos(angles), jnp.sin(angles)])
    s_terms = complex_mul(coeffs[:, :, None, None, None], solution[:, None])
    h_terms = complex_mul(coeffs[:, :, None, None, None], applied[:, None])
    width = MOMENTS * solution.shape[1]
    return (s_terms.reshape(2, width, -1), h_terms.reshape(2, width, -1))


def gram_of(left, right):
    width = left.shape[1]
    joined = lax.dot_general(
        left.reshape(2 * width, -1),
        right.reshape(2 * width, -1),
        (((1,), (1,)), ((), ())),
        precision=lax.Precision.HIGHEST,
        preferred_element_type=jnp.float32,
    )
    blocks = joined.reshape(2, width, 2, width)
    return jnp.stack([blocks[0, :, 0] + blocks[1, :, 1], blocks[0, :, 1] - blocks[1, :, 0]])


def split_grid(sources, potential, iter_counts):
    complex_src = jnp.stack([sources, jnp.zeros_like(sources)])
    angle_now = (
        2.0 * math.pi * (lax.axis_index("point").astype(jnp.float32) + 0.5) / lax.axis_size("point")
    )
    shift_re = GAMMA + RADIUS * jnp.cos(angle_now)
    shift_im = RADIUS * jnp.sin(angle_now)
    limit = iter_counts[0]
    solution = jnp.zeros_like(complex_src)

    def one_turn(turn_idx, state):
        solution, residual, search, norm_now = state
        product = shifted(search, potential, shift_re, shift_im)
        curve = lax.psum(bilinear(search, product), "dom")
        step_size = complex_div(norm_now, curve)
        new_residual = residual - scaled(step_size, product)
        norm_next = residual_sum(new_residual)
        fresh = (
            solution + scaled(step_size, search),
            new_residual,
            new_residual + scaled(complex_div(norm_next, norm_now), search),
            norm_next,
        )
        keep_mask = turn_idx < limit
        return jax.tree.map(lambda newer, older: jnp.where(keep_mask, newer, older), fresh, state)

    start = (solution, complex_src, complex_src, residual_sum(complex_src))
    solution, residual, search, norm_now = lax.fori_loop(0, ITERS, one_turn, start)
    s_terms, h_terms = moment_terms(solution, residual, complex_src, angle_now, shift_re, shift_im)
    cells = sources.shape[1] * sources.shape[2] * lax.axis_size("dom")
    s_total, h_total = lax.psum((s_terms, h_terms), "point")
    gram_b, gram_a = lax.psum((gram_of(s_total, s_total), gram_of(s_total, h_total)), "dom")
    return (gram_b / cells, gram_a / cells)


Y_IN, X_IN = 2, 4
Y_OUT, X_OUT = GX // Y_IN, GX // X_IN
ROWS = Y_IN * X_IN
LANES = Y_OUT * X_OUT
SUB = 8
BASIS = ITERS + 1
CORES = 2
UNROLL = 4
H_SCALE = 2.0 / COEF_NEAR
FAR_SCALED = 0.5 * H_SCALE * COEF_FAR


def pack_kernel(depth, groups, counts, rows, out, tile):
    columns = rows.shape[0] // (SUB * groups * depth + depth)
    first_level = columns * SUB * groups * depth
    source = lax.broadcasted_iota(jnp.int32, (LANES, LANES), 0)
    target = lax.broadcasted_iota(jnp.int32, (LANES, LANES), 1)
    inner = target // (LANES // ROWS)
    outer = target % (LANES // ROWS)
    cell = (outer // X_OUT * Y_IN + inner // X_IN) * GX + outer % X_OUT * X_IN + inner % X_IN
    swap = jnp.where(source == cell, 1.0, 0.0).astype(jnp.float32)
    parts = []
    for deep in range(depth):
        for group in range(groups):
            for column in range(columns):
                start = (group * SUB * columns + column) * depth + deep
                parts.append(rows[pl.ds(start, SUB, stride=columns * depth), :])
        parts.append(rows[pl.ds(first_level + deep, columns, stride=depth), :])
    mixed = exact_dot(jnp.concatenate(parts, axis=0), swap, ((1,), (0,)))
    block = LANES // ROWS
    lane_block = lax.broadcasted_iota(jnp.int32, (SUB, LANES), 1) // block
    row = lax.broadcasted_iota(jnp.int32, (SUB, LANES), 0)
    for deep in range(depth):
        base = deep * (groups + 1) * columns * SUB - deep * (columns - 1) * SUB
        for group in range(groups):
            pieces = [
                mixed[base + (group * columns + column) * SUB :][:SUB] for column in range(columns)
            ]
            for m in range(ROWS):
                value = pieces[m]
                for column in range(columns):
                    if column != m:
                        moved = pltpu.roll(pieces[column], (column - m) * block % LANES, 1)
                        value = jnp.where(lane_block == column, moved, value)
                start = ((deep * ROWS + m) * groups + group) * SUB
                out[start : start + SUB, :] = value
        piece = mixed[base + groups * columns * SUB :][:SUB]
        value = piece
        for far in range(1, columns):
            moved = pltpu.roll(pltpu.roll(piece, far * block, 1), columns - far, 0)
            value = jnp.where(lane_block == (row + far) % columns, moved, value)
        start = depth * ROWS * SUB * groups + deep * ROWS
        out[start : start + ROWS, :] = value
    tile[...] = jnp.broadcast_to(counts[...].astype(jnp.float32), (SUB, LANES))


def packed_block(sources, potential, iter_counts):
    count, depth, cells = sources.shape
    columns = cells // LANES
    rows = sources.reshape(count, depth, columns, LANES).transpose(0, 2, 1, 3).reshape(-1, LANES)
    levels = potential.reshape(depth, columns, LANES).transpose(1, 0, 2).reshape(-1, LANES)
    vmem = pl.BlockSpec(memory_space=pltpu.VMEM)
    size = depth * ROWS * (count + 1)
    return pl.pallas_call(
        functools.partial(pack_kernel, depth, count // SUB),
        out_shape=(
            jax.ShapeDtypeStruct((size, LANES), jnp.float32),
            jax.ShapeDtypeStruct((SUB, LANES), jnp.float32),
        ),
        in_specs=[vmem, vmem],
        out_specs=(vmem, vmem),
        compiler_params=pltpu.CompilerParams(vmem_limit_bytes=4 * 2**20),
        name="pack",
    )(iter_counts.reshape(1, 1), jnp.concatenate([rows, levels], axis=0))


def lane_sum(values):
    return jnp.broadcast_to(jnp.sum(values, axis=1, keepdims=True), values.shape)


def ratio(top, bottom):
    return jnp.where(bottom > 0.0, top / jnp.where(bottom > 0.0, bottom, 1.0), 0.0)


def tree_sum(values):
    while len(values) > 1:
        values = [sum(values[i : i + 2][1:], values[i]) for i in range(0, len(values), 2)]
    return values[0]


def plane_rows(vector, plane, rows):
    return [vector[plane, rows, m * LANES : (m + 1) * LANES] for m in range(ROWS)]


def plane_rolls(here):
    y_up = [pltpu.roll(value, LANES - X_OUT, 1) for value in here]
    y_down = [pltpu.roll(value, X_OUT, 1) for value in here]
    before, after = [], []
    for yi in range(Y_IN):
        line = here[yi * X_IN : (yi + 1) * X_IN]
        for value in line[X_IN - 2 :]:
            before.append((pltpu.roll(value, LANES - X_OUT + 1, 1), pltpu.roll(value, 1, 1)))
        for value in line[:2]:
            after.append((pltpu.roll(value, X_OUT - 1, 1), pltpu.roll(value, LANES - 1, 1)))
    return y_up, y_down, before, after


def apply_plane(vector, diagonal, plane, rows, rolls, last_x, first_x):
    planes = vector.shape[0]
    here = plane_rows(vector, plane, rows)
    above, below, above_2, below_2 = (
        plane_rows(vector, (plane + far) % planes, rows) for far in (1, -1, 2, -2)
    )
    y_up, y_down, before, after = rolls
    out = []
    for yi in range(Y_IN):
        line = here[yi * X_IN : (yi + 1) * X_IN]
        low = [jnp.where(first_x, *pair) for pair in before[2 * yi : 2 * yi + 2]]
        high = [jnp.where(last_x, *pair) for pair in after[2 * yi : 2 * yi + 2]]
        wide = low + line + high
        for xi in range(X_IN):
            m = yi * X_IN + xi
            other = (1 - yi) * X_IN + xi
            y_next = here[other] if yi == 0 else y_up[other]
            y_prev = here[other] if yi == 1 else y_down[other]
            near = (wide[xi + 1] + wide[xi + 3]) + (y_next + y_prev) + (above[m] + below[m])
            far = (wide[xi] + wide[xi + 4]) + (y_up[m] + y_down[m]) + (above_2[m] + below_2[m])
            level = diagonal[plane, :, m * LANES : (m + 1) * LANES]
            out.append(level * here[m] - near - FAR_SCALED * far)
    return here, out


def cmul(first, second):
    return (
        first[0] * second[0] - first[1] * second[1],
        first[0] * second[1] + first[1] * second[0],
    )


def moment_coeffs(point, points, count):
    lane = lax.broadcasted_iota(jnp.int32, (1, LANES), 1)
    moment = lax.rem(lane, MOMENTS * count) // count
    angle = 2.0 * math.pi * (point + 0.5) / points
    parts = []
    for func in (math.cos, math.sin):
        value = jnp.full((1, LANES), 0.25 * func(angle), jnp.float32)
        for k in range(1, MOMENTS):
            value = jnp.where(moment == k, 0.25 * func((k + 1) * angle), value)
        parts.append(value)
    return parts


def weights_of(alphas, norms, limits, count):
    points = len(limits)
    shape = (count, LANES)
    half = MOMENTS * count
    lane = lax.broadcasted_iota(jnp.int32, shape, 1)
    source = lax.broadcasted_iota(jnp.int32, shape, 0)
    own = lax.rem(lane, count) == source
    left_half = lane < half
    betas = [ratio(norms[i + 1], norms[i]) for i in range(ITERS - 1)]
    sums = [[jnp.zeros(shape, jnp.float32)] * 2 for _ in range(BASIS)]
    zero = jnp.zeros(shape, jnp.float32)
    one = jnp.ones(shape, jnp.float32)
    for point in range(points):
        angle = 2.0 * math.pi * (point + 0.5) / points
        shift = (GAMMA + RADIUS * math.cos(angle), RADIUS * math.sin(angle))
        scaled_shift = (H_SCALE * shift[0], H_SCALE * shift[1])
        limit = limits[point]
        product = (one, zero)
        products = [product]
        links = []
        pivot = (scaled_shift[0] - alphas[0], zero + scaled_shift[1])
        for i in range(ITERS):
            size = 1.0 / (pivot[0] * pivot[0] + pivot[1] * pivot[1])
            inverse = (pivot[0] * size, -pivot[1] * size)
            product = cmul(product, inverse)
            products.append(product)
            if i < ITERS - 1:
                link = (betas[i] * inverse[0], betas[i] * inverse[1])
                links.append(link)
                pivot = (scaled_shift[0] - alphas[i + 1] - link[0], scaled_shift[1] - link[1])
        solved = [None] * ITERS
        for i in reversed(range(ITERS)):
            value = (H_SCALE * products[i + 1][0], H_SCALE * products[i + 1][1])
            if i < ITERS - 1:
                step = cmul(links[i], solved[i + 1])
                value = (value[0] + step[0], value[1] + step[1])
            used = limit > i
            solved[i] = (jnp.where(used, value[0], 0.0), jnp.where(used, value[1], 0.0))
        applied = []
        for i in range(BASIS):
            left = limit == i
            rest = (
                jnp.where(left, products[i][0], 0.0),
                jnp.where(left, products[i][1], 0.0),
            )
            if i < ITERS:
                turned = (
                    shift[0] * solved[i][0] - shift[1] * solved[i][1],
                    shift[0] * solved[i][1] + shift[1] * solved[i][0],
                )
                rest = (rest[0] + turned[0], rest[1] + turned[1])
            if i == 0:
                rest = (rest[0] - 1.0, rest[1])
            applied.append(rest)
        tail = applied[ITERS]
        for back, factor in ((1, alphas[ITERS - 1]), (2, betas[ITERS - 2])):
            part = applied[ITERS - back]
            applied[ITERS - back] = (part[0] - factor * tail[0], part[1] - factor * tail[1])
        moment = moment_coeffs(point, points, count)
        for i in range(BASIS):
            left = solved[i] if i < ITERS else (zero, zero)
            both = (
                jnp.where(left_half, left[0], applied[i][0]),
                jnp.where(left_half, left[1], applied[i][1]),
            )
            term = cmul(moment, both)
            sums[i] = [sums[i][0] + term[0], sums[i][1] + term[1]]
    return [[jnp.where(own, part, 0.0) for part in pair] for pair in sums]


def exact_dot(first, second, dims):
    return lax.dot_general(
        first,
        second,
        (dims, ((), ())),
        precision=lax.Precision.HIGHEST,
        preferred_element_type=jnp.float32,
    )


def krylov_kernel(parts, count, *refs):
    blocks, (vectors, applied, scalars, first_work, second_work, diagonal) = refs[:parts], refs[parts:]
    planes = diagonal.shape[0]
    depth = planes // parts
    groups = count // SUB
    lane = lax.broadcasted_iota(jnp.int32, (SUB, LANES), 1)
    last_x = lax.rem(lane, X_OUT) == X_OUT - 1
    first_x = lax.rem(lane, X_OUT) == 0
    here = lax.axis_index("dom")
    for turn in range(parts):
        slab = jnp.bitwise_xor(here, turn) * depth
        for deep in range(depth):
            for m in range(ROWS):
                start = (deep * ROWS + m) * count
                lanes = slice(m * LANES, (m + 1) * LANES)
                value = blocks[turn][start : start + count, :]
                first_work[slab + deep, :, lanes] = value
                vectors[0, slab + deep, :, lanes] = value
            start = depth * ROWS * count + deep * ROWS
            levels = H_SCALE * (blocks[turn][start : start + ROWS, :] + 3.75)
            for m in range(ROWS):
                level = jnp.broadcast_to(levels[m : m + 1, :], (SUB, LANES))
                diagonal[slab + deep, :, m * LANES : (m + 1) * LANES] = level
    second_work[...] = jnp.zeros_like(second_work)
    scalars[ITERS] = jnp.zeros((count, LANES), jnp.float32)

    all_rows = [pl.ds(group * SUB, SUB) for group in range(groups)]
    all_lanes = [slice(m * LANES, (m + 1) * LANES) for m in range(ROWS)]
    for group, rows in enumerate(all_rows):
        norm = []
        for plane in range(planes):
            values = [first_work[plane, rows, lanes] for lanes in all_lanes]
            norm.append(tree_sum([value * value for value in values]))
        scalars[ITERS + 1, rows, :] = lane_sum(tree_sum(norm))

    def half_turn(i, work, before):
        units = [(plane, group) for plane in range(planes) for group in range(groups)]
        curve = [[] for _ in range(groups)]
        ahead = plane_rolls(plane_rows(work, 0, all_rows[0]))
        for (plane, group), coming in zip(units, units[1:] + [None]):
            rolls = ahead
            if coming is not None:
                ahead = plane_rolls(plane_rows(work, coming[0], all_rows[coming[1]]))
            rows = all_rows[group]
            value, out = apply_plane(work, diagonal, plane, rows, rolls, last_x, first_x)
            for m, lanes in enumerate(all_lanes):
                applied[plane, rows, lanes] = out[m]
            curve[group].append(tree_sum([value[m] * out[m] for m in range(ROWS)]))
        curves = [lane_sum(tree_sum(parts_of)) for parts_of in curve]
        alphas = []
        for group, rows in enumerate(all_rows):
            alphas.append(ratio(curves[group], scalars[ITERS + 1 + i, rows, :]))
            scalars[i, rows, :] = alphas[group]

        @pl.when(i < ITERS - 1)
        def _():
            norms = []
            for group, rows in enumerate(all_rows):
                beta = ratio(scalars[ITERS + 1 + i, rows, :], scalars[ITERS + i, rows, :])
                norm = []
                for plane in range(planes):
                    values = []
                    for lanes in all_lanes:
                        value = applied[plane, rows, lanes]
                        value = value - alphas[group] * work[plane, rows, lanes]
                        value = value - beta * before[plane, rows, lanes]
                        before[plane, rows, lanes] = value
                        vectors[i + 1, plane, rows, lanes] = value
                        values.append(value * value)
                    norm.append(tree_sum(values))
                norms.append(lane_sum(tree_sum(norm)))
            for group, rows in enumerate(all_rows):
                scalars[ITERS + 2 + i, rows, :] = norms[group]

    def turn(step, carry):
        half_turn(2 * step, first_work, second_work)
        half_turn(2 * step + 1, second_work, first_work)
        return carry

    lax.fori_loop(0, ITERS // 2, turn, 0)


def gram_kernel(points, scalars, *refs):
    tiles = refs[:points]
    archive, applied, out_b, out_a, gram, limits = refs[points:]
    planes, count, _ = applied.shape
    groups = count // SUB
    size = BASIS * count
    gram[...] = jnp.zeros_like(gram)

    def gram_turn(plane, carry):
        values = [archive[i, plane] for i in range(ITERS)] + [applied[plane]]
        values = jnp.concatenate(values, axis=0)
        high = values.astype(jnp.bfloat16)
        low = (values - high.astype(jnp.float32)).astype(jnp.bfloat16)
        gram[...] += lax.dot_general(
            jnp.concatenate([high, low], axis=0),
            high,
            (((1,), (1,)), ((), ())),
            preferred_element_type=jnp.float32,
        )
        return carry

    lax.fori_loop(0, planes, gram_turn, 0, unroll=UNROLL)
    cross = gram[size:, :]
    pairs = gram[:size, :] + cross + cross.T

    here = lax.axis_index("point")
    core = jnp.bitwise_and(lax.axis_index("dom"), CORES - 1)
    for far, tile in zip((0, 1 + core, 3, 2 - core), tiles):
        limits[jnp.bitwise_xor(here, far)] = tile[...]
    bounds = [jnp.concatenate([limits[j]] * groups, axis=0) for j in range(points)]
    alphas = [scalars[i] for i in range(ITERS)]
    norms = [scalars[ITERS + 1 + i] for i in range(ITERS)]
    weights = weights_of(alphas, norms, bounds, count)
    real = jnp.concatenate([pair[0] for pair in weights], axis=0)
    imag = jnp.concatenate([pair[1] for pair in weights], axis=0)
    right = exact_dot(pairs, jnp.concatenate([real, imag], axis=1), ((1,), (0,)))
    half = MOMENTS * count
    left = jnp.concatenate([real[:, :half], imag[:, :half]], axis=1)
    joined = exact_dot(left.T, right, ((1,), (0,)))
    scale = 1.0 / (planes * ROWS * LANES)
    width = 2 * half
    real = (joined[:half, :width] + joined[half:, width:]) * scale
    imag = (joined[:half, width:] - joined[half:, :width]) * scale
    out_b[0] = real[:, :half]
    out_b[1] = imag[:, :half]
    out_a[0] = real[:, half:]
    out_a[1] = imag[:, half:]


def swapped(values, axis, size, mask):
    return lax.ppermute(values, axis, [(index ^ mask, index) for index in range(size)])


def whole_grid(sources, potential, iter_counts, *, parts, points):
    count, depth, _ = sources.shape
    planes = parts * depth
    block, tile = packed_block(sources, potential, iter_counts)
    even = [block] + [swapped(block, "dom", parts, mask) for mask in range(CORES, parts, CORES)]
    mixed = [
        ((point ^ (1 + part % CORES)) * parts + part, point * parts + part)
        for point in range(points)
        for part in range(parts)
    ]
    tiles = [lax.ppermute(tile, ("point", "dom"), mixed), swapped(tile, "point", points, 3)]
    even[1], *tiles = lax.optimization_barrier((even[1], *tiles))
    tiles.append(swapped(tiles[0], "dom", parts, 1))
    odd = [swapped(value, "dom", parts, 1) for value in even]
    blocks = [value for pair in zip(even, odd) for value in pair]
    vmem = pl.BlockSpec(memory_space=pltpu.VMEM)
    vector = (planes, count, ROWS * LANES)
    cells = planes * ROWS * LANES
    vectors, applied, scalars = pl.pallas_call(
        functools.partial(krylov_kernel, parts, count),
        out_shape=(
            jax.ShapeDtypeStruct((ITERS,) + vector, jnp.float32),
            jax.ShapeDtypeStruct(vector, jnp.float32),
            jax.ShapeDtypeStruct((2 * ITERS + 1, count, LANES), jnp.float32),
        ),
        in_specs=[vmem] * parts,
        out_specs=(vmem,) * 3,
        scratch_shapes=[
            pltpu.VMEM(vector, jnp.float32),
            pltpu.VMEM(vector, jnp.float32),
            pltpu.VMEM((planes, SUB, ROWS * LANES), jnp.float32),
        ],
        compiler_params=pltpu.CompilerParams(vmem_limit_bytes=16 * 2**20),
        name="krylov",
    )(*blocks)
    size = BASIS * count
    width = MOMENTS * count
    out = jax.ShapeDtypeStruct((2, width, width), jnp.float32)
    return pl.pallas_call(
        functools.partial(gram_kernel, points),
        out_shape=(out, out),
        in_specs=[vmem] * (3 + points),
        out_specs=(vmem, vmem),
        scratch_shapes=[
            pltpu.VMEM((2 * size, size), jnp.float32),
            pltpu.VMEM((points, SUB, LANES), jnp.float32),
        ],
        compiler_params=pltpu.CompilerParams(vmem_limit_bytes=16 * 2**20),
        name="gram",
    )(scalars, tile, *tiles, vectors, applied)


def on_device(sources, potential, iter_counts):
    parts, points = lax.axis_size("dom"), lax.axis_size("point")
    count, depth, cells = sources.shape
    held = BASIS * count * parts * depth * cells * 4
    fits = (
        held <= 16 * 2**20
        and parts == 8
        and points == 4
        and count == 2 * SUB
        and 2 * MOMENTS * count == LANES
        and parts * depth == 16
        and cells == GX * GX == ROWS * LANES
    )
    if not fits:
        return split_grid(sources, potential, iter_counts)
    return whole_grid(sources, potential, iter_counts, parts=parts, points=points)


def solution(mesh):
    placed = (P(None, "dom", None), P("dom", None), P("point"))
    return jax.shard_map(
        on_device, mesh=mesh, in_specs=placed, out_specs=(P(), P()), check_vma=False
    )
```

```python
import functools
import math

import jax
import jax.numpy as jnp
from jax import lax
from jax.experimental import pallas as pl
from jax.experimental.pallas import tpu as pltpu
from jax.sharding import PartitionSpec as P

MOMENTS = 4
ITERS = 6
GX = 32


COEF_NEAR = 4.0 / 3.0
COEF_FAR = -1.0 / 12.0
GAMMA = 2.0
RADIUS = 1.5


def padded_2(block, sides, width):
    for axis, dim in sides:
        count = lax.axis_size(axis)
        forward = [(i, i + 1) for i in range(count - 1)]
        forward.append((count - 1, 0))
        backward = [(target, source) for source, target in forward]
        low = lax.ppermute(
            lax.slice_in_dim(block, block.shape[dim] - width, None, axis=dim), axis, forward
        )
        high = lax.ppermute(lax.slice_in_dim(block, 0, width, axis=dim), axis, backward)
        block = jnp.concatenate([low, block, high], axis=dim)
    return block


def plane_terms(values, side):
    lead = values.shape[:-1]
    planes = values.reshape(lead + (side, side))
    summed = COEF_NEAR * (
        jnp.roll(planes, 1, -2)
        + jnp.roll(planes, -1, -2)
        + jnp.roll(planes, 1, -1)
        + jnp.roll(planes, -1, -1)
    )
    summed = summed + COEF_FAR * (
        jnp.roll(planes, 2, -2)
        + jnp.roll(planes, -2, -2)
        + jnp.roll(planes, 2, -1)
        + jnp.roll(planes, -2, -1)
    )
    return summed.reshape(values.shape)


def complex_mul(first, second):
    return jnp.stack(
        [first[0] * second[0] - first[1] * second[1], first[0] * second[1] + first[1] * second[0]]
    )


def complex_div(first, second):
    denom = second[0] * second[0] + second[1] * second[1]
    return jnp.stack(
        [
            (first[0] * second[0] + first[1] * second[1]) / denom,
            (first[1] * second[0] - first[0] * second[1]) / denom,
        ]
    )


def bilinear(first, second):
    real_part = jnp.sum(first[0] * second[0] - first[1] * second[1], axis=(1, 2))
    imag_part = jnp.sum(first[0] * second[1] + first[1] * second[0], axis=(1, 2))
    return jnp.stack([real_part, imag_part])


def scaled(coeffs, values):
    return complex_mul(coeffs[:, :, None, None], values)


def shifted(values, potential, shift_re, shift_im):
    padded = padded_2(values, (("dom", 2),), 2)
    depth = values.shape[2]
    lap = -7.5 * values + plane_terms(values, GX)
    lap = lap + COEF_NEAR * (padded[:, :, 3 : 3 + depth] + padded[:, :, 1 : 1 + depth])
    lap = lap + COEF_FAR * (padded[:, :, 4 : 4 + depth] + padded[:, :, 0:depth])
    applied = -0.5 * lap + potential * values
    return jnp.stack(
        [
            shift_re * values[0] - shift_im * values[1] - applied[0],
            shift_re * values[1] + shift_im * values[0] - applied[1],
        ]
    )


def residual_sum(values):
    return lax.psum(bilinear(values, values), "dom")


def moment_terms(solution, residual, sources, angle_now, shift_re, shift_im):
    applied = jnp.stack(
        [
            shift_re * solution[0] - shift_im * solution[1] - sources[0] + residual[0],
            shift_re * solution[1] + shift_im * solution[0] - sources[1] + residual[1],
        ]
    )
    angles = (jnp.arange(MOMENTS).astype(jnp.float32) + 1.0) * angle_now
    coeffs = 0.25 * jnp.stack([jnp.cos(angles), jnp.sin(angles)])
    s_terms = complex_mul(coeffs[:, :, None, None, None], solution[:, None])
    h_terms = complex_mul(coeffs[:, :, None, None, None], applied[:, None])
    width = MOMENTS * solution.shape[1]
    return (s_terms.reshape(2, width, -1), h_terms.reshape(2, width, -1))


def gram_of(left, right):
    width = left.shape[1]
    joined = lax.dot_general(
        left.reshape(2 * width, -1),
        right.reshape(2 * width, -1),
        (((1,), (1,)), ((), ())),
        precision=lax.Precision.HIGHEST,
        preferred_element_type=jnp.float32,
    )
    blocks = joined.reshape(2, width, 2, width)
    return jnp.stack([blocks[0, :, 0] + blocks[1, :, 1], blocks[0, :, 1] - blocks[1, :, 0]])


def split_grid(sources, potential, iter_counts):
    complex_src = jnp.stack([sources, jnp.zeros_like(sources)])
    angle_now = (
        2.0 * math.pi * (lax.axis_index("point").astype(jnp.float32) + 0.5) / lax.axis_size("point")
    )
    shift_re = GAMMA + RADIUS * jnp.cos(angle_now)
    shift_im = RADIUS * jnp.sin(angle_now)
    limit = iter_counts[0]
    solution = jnp.zeros_like(complex_src)

    def one_turn(turn_idx, state):
        solution, residual, search, norm_now = state
        product = shifted(search, potential, shift_re, shift_im)
        curve = lax.psum(bilinear(search, product), "dom")
        step_size = complex_div(norm_now, curve)
        new_residual = residual - scaled(step_size, product)
        norm_next = residual_sum(new_residual)
        fresh = (
            solution + scaled(step_size, search),
            new_residual,
            new_residual + scaled(complex_div(norm_next, norm_now), search),
            norm_next,
        )
        keep_mask = turn_idx < limit
        return jax.tree.map(lambda newer, older: jnp.where(keep_mask, newer, older), fresh, state)

    start = (solution, complex_src, complex_src, residual_sum(complex_src))
    solution, residual, search, norm_now = lax.fori_loop(0, ITERS, one_turn, start)
    s_terms, h_terms = moment_terms(solution, residual, complex_src, angle_now, shift_re, shift_im)
    cells = sources.shape[1] * sources.shape[2] * lax.axis_size("dom")
    s_total, h_total = lax.psum((s_terms, h_terms), "point")
    gram_b, gram_a = lax.psum((gram_of(s_total, s_total), gram_of(s_total, h_total)), "dom")
    return (gram_b / cells, gram_a / cells)


Y_IN, X_IN = 2, 4
Y_OUT, X_OUT = GX // Y_IN, GX // X_IN
ROWS = Y_IN * X_IN
LANES = Y_OUT * X_OUT
SUB = 8
BASIS = ITERS + 1
CORES = 2
UNROLL = 4
H_SCALE = 2.0 / COEF_NEAR
FAR_SCALED = 0.5 * H_SCALE * COEF_FAR


def pack_kernel(depth, groups, counts, rows, out, tile):
    columns = rows.shape[0] // (SUB * groups * depth + depth)
    first_level = columns * SUB * groups * depth
    source = lax.broadcasted_iota(jnp.int32, (LANES, LANES), 0)
    target = lax.broadcasted_iota(jnp.int32, (LANES, LANES), 1)
    inner = target // (LANES // ROWS)
    outer = target % (LANES // ROWS)
    cell = (outer // X_OUT * Y_IN + inner // X_IN) * GX + outer % X_OUT * X_IN + inner % X_IN
    swap = jnp.where(source == cell, 1.0, 0.0).astype(jnp.float32)
    parts = []
    for deep in range(depth):
        for group in range(groups):
            for column in range(columns):
                start = (group * SUB * columns + column) * depth + deep
                parts.append(rows[pl.ds(start, SUB, stride=columns * depth), :])
        parts.append(rows[pl.ds(first_level + deep, columns, stride=depth), :])
    mixed = exact_dot(jnp.concatenate(parts, axis=0), swap, ((1,), (0,)))
    block = LANES // ROWS
    lane_block = lax.broadcasted_iota(jnp.int32, (SUB, LANES), 1) // block
    row = lax.broadcasted_iota(jnp.int32, (SUB, LANES), 0)
    for deep in range(depth):
        base = deep * (groups + 1) * columns * SUB - deep * (columns - 1) * SUB
        for group in range(groups):
            pieces = [
                mixed[base + (group * columns + column) * SUB :][:SUB] for column in range(columns)
            ]
            for m in range(ROWS):
                value = pieces[m]
                for column in range(columns):
                    if column != m:
                        moved = pltpu.roll(pieces[column], (column - m) * block % LANES, 1)
                        value = jnp.where(lane_block == column, moved, value)
                start = ((deep * ROWS + m) * groups + group) * SUB
                out[start : start + SUB, :] = value
        piece = mixed[base + groups * columns * SUB :][:SUB]
        value = piece
        for far in range(1, columns):
            moved = pltpu.roll(pltpu.roll(piece, far * block, 1), columns - far, 0)
            value = jnp.where(lane_block == (row + far) % columns, moved, value)
        start = depth * ROWS * SUB * groups + deep * ROWS
        out[start : start + ROWS, :] = value
    tile[...] = jnp.broadcast_to(counts[...].astype(jnp.float32), (SUB, LANES))


def packed_block(sources, potential, iter_counts):
    count, depth, cells = sources.shape
    columns = cells // LANES
    rows = sources.reshape(count, depth, columns, LANES).transpose(0, 2, 1, 3).reshape(-1, LANES)
    levels = potential.reshape(depth, columns, LANES).transpose(1, 0, 2).reshape(-1, LANES)
    vmem = pl.BlockSpec(memory_space=pltpu.VMEM)
    size = depth * ROWS * (count + 1)
    return pl.pallas_call(
        functools.partial(pack_kernel, depth, count // SUB),
        out_shape=(
            jax.ShapeDtypeStruct((size, LANES), jnp.float32),
            jax.ShapeDtypeStruct((SUB, LANES), jnp.float32),
        ),
        in_specs=[vmem, vmem],
        out_specs=(vmem, vmem),
        compiler_params=pltpu.CompilerParams(vmem_limit_bytes=4 * 2**20),
        name="pack",
    )(iter_counts.reshape(1, 1), jnp.concatenate([rows, levels], axis=0))


def lane_sum(values):
    return jnp.broadcast_to(jnp.sum(values, axis=1, keepdims=True), values.shape)


def ratio(top, bottom):
    return jnp.where(bottom > 0.0, top / jnp.where(bottom > 0.0, bottom, 1.0), 0.0)


def tree_sum(values):
    while len(values) > 1:
        values = [sum(values[i : i + 2][1:], values[i]) for i in range(0, len(values), 2)]
    return values[0]


def plane_rows(vector, plane, rows):
    return [vector[plane, rows, m * LANES : (m + 1) * LANES] for m in range(ROWS)]


def plane_rolls(here):
    y_up = [pltpu.roll(value, LANES - X_OUT, 1) for value in here]
    y_down = [pltpu.roll(value, X_OUT, 1) for value in here]
    before, after = [], []
    for yi in range(Y_IN):
        line = here[yi * X_IN : (yi + 1) * X_IN]
        for value in line[X_IN - 2 :]:
            before.append((pltpu.roll(value, LANES - X_OUT + 1, 1), pltpu.roll(value, 1, 1)))
        for value in line[:2]:
            after.append((pltpu.roll(value, X_OUT - 1, 1), pltpu.roll(value, LANES - 1, 1)))
    return y_up, y_down, before, after


def apply_plane(vector, diagonal, plane, rows, rolls, last_x, first_x):
    planes = vector.shape[0]
    here = plane_rows(vector, plane, rows)
    above, below, above_2, below_2 = (
        plane_rows(vector, (plane + far) % planes, rows) for far in (1, -1, 2, -2)
    )
    y_up, y_down, before, after = rolls
    out = []
    for yi in range(Y_IN):
        line = here[yi * X_IN : (yi + 1) * X_IN]
        low = [jnp.where(first_x, *pair) for pair in before[2 * yi : 2 * yi + 2]]
        high = [jnp.where(last_x, *pair) for pair in after[2 * yi : 2 * yi + 2]]
        wide = low + line + high
        for xi in range(X_IN):
            m = yi * X_IN + xi
            other = (1 - yi) * X_IN + xi
            y_next = here[other] if yi == 0 else y_up[other]
            y_prev = here[other] if yi == 1 else y_down[other]
            near = (wide[xi + 1] + wide[xi + 3]) + (y_next + y_prev) + (above[m] + below[m])
            far = (wide[xi] + wide[xi + 4]) + (y_up[m] + y_down[m]) + (above_2[m] + below_2[m])
            level = diagonal[plane, :, m * LANES : (m + 1) * LANES]
            out.append(level * here[m] - near - FAR_SCALED * far)
    return here, out


def cmul(first, second):
    return (
        first[0] * second[0] - first[1] * second[1],
        first[0] * second[1] + first[1] * second[0],
    )


def moment_coeffs(point, points, count):
    lane = lax.broadcasted_iota(jnp.int32, (1, LANES), 1)
    moment = lax.rem(lane, MOMENTS * count) // count
    angle = 2.0 * math.pi * (point + 0.5) / points
    parts = []
    for func in (math.cos, math.sin):
        value = jnp.full((1, LANES), 0.25 * func(angle), jnp.float32)
        for k in range(1, MOMENTS):
            value = jnp.where(moment == k, 0.25 * func((k + 1) * angle), value)
        parts.append(value)
    return parts


def weights_of(alphas, norms, limits, count):
    points = len(limits)
    shape = (count, LANES)
    half = MOMENTS * count
    lane = lax.broadcasted_iota(jnp.int32, shape, 1)
    source = lax.broadcasted_iota(jnp.int32, shape, 0)
    own = lax.rem(lane, count) == source
    left_half = lane < half
    betas = [ratio(norms[i + 1], norms[i]) for i in range(ITERS - 1)]
    sums = [[jnp.zeros(shape, jnp.float32)] * 2 for _ in range(BASIS)]
    zero = jnp.zeros(shape, jnp.float32)
    one = jnp.ones(shape, jnp.float32)
    for point in range(points):
        angle = 2.0 * math.pi * (point + 0.5) / points
        shift = (GAMMA + RADIUS * math.cos(angle), RADIUS * math.sin(angle))
        scaled_shift = (H_SCALE * shift[0], H_SCALE * shift[1])
        limit = limits[point]
        product = (one, zero)
        products = [product]
        links = []
        pivot = (scaled_shift[0] - alphas[0], zero + scaled_shift[1])
        for i in range(ITERS):
            size = 1.0 / (pivot[0] * pivot[0] + pivot[1] * pivot[1])
            inverse = (pivot[0] * size, -pivot[1] * size)
            product = cmul(product, inverse)
            products.append(product)
            if i < ITERS - 1:
                link = (betas[i] * inverse[0], betas[i] * inverse[1])
                links.append(link)
                pivot = (scaled_shift[0] - alphas[i + 1] - link[0], scaled_shift[1] - link[1])
        solved = [None] * ITERS
        for i in reversed(range(ITERS)):
            value = (H_SCALE * products[i + 1][0], H_SCALE * products[i + 1][1])
            if i < ITERS - 1:
                step = cmul(links[i], solved[i + 1])
                value = (value[0] + step[0], value[1] + step[1])
            used = limit > i
            solved[i] = (jnp.where(used, value[0], 0.0), jnp.where(used, value[1], 0.0))
        applied = []
        for i in range(BASIS):
            left = limit == i
            rest = (
                jnp.where(left, products[i][0], 0.0),
                jnp.where(left, products[i][1], 0.0),
            )
            if i < ITERS:
                turned = (
                    shift[0] * solved[i][0] - shift[1] * solved[i][1],
                    shift[0] * solved[i][1] + shift[1] * solved[i][0],
                )
                rest = (rest[0] + turned[0], rest[1] + turned[1])
            if i == 0:
                rest = (rest[0] - 1.0, rest[1])
            applied.append(rest)
        tail = applied[ITERS]
        for back, factor in ((1, alphas[ITERS - 1]), (2, betas[ITERS - 2])):
            part = applied[ITERS - back]
            applied[ITERS - back] = (part[0] - factor * tail[0], part[1] - factor * tail[1])
        moment = moment_coeffs(point, points, count)
        for i in range(BASIS):
            left = solved[i] if i < ITERS else (zero, zero)
            both = (
                jnp.where(left_half, left[0], applied[i][0]),
                jnp.where(left_half, left[1], applied[i][1]),
            )
            term = cmul(moment, both)
            sums[i] = [sums[i][0] + term[0], sums[i][1] + term[1]]
    return [[jnp.where(own, part, 0.0) for part in pair] for pair in sums]


def exact_dot(first, second, dims):
    return lax.dot_general(
        first,
        second,
        (dims, ((), ())),
        precision=lax.Precision.HIGHEST,
        preferred_element_type=jnp.float32,
    )


def krylov_kernel(parts, count, *refs):
    blocks = refs[:parts]
    vectors, applied, scalars, first_work, second_work, diagonal, partial = refs[parts:]
    planes = diagonal.shape[0]
    depth = planes // parts
    groups = count // SUB
    lane = lax.broadcasted_iota(jnp.int32, (SUB, LANES), 1)
    last_x = lax.rem(lane, X_OUT) == X_OUT - 1
    first_x = lax.rem(lane, X_OUT) == 0
    here = lax.axis_index("dom")
    for turn in range(parts):
        slab = jnp.bitwise_xor(here, turn) * depth
        for deep in range(depth):
            for m in range(ROWS):
                start = (deep * ROWS + m) * count
                lanes = slice(m * LANES, (m + 1) * LANES)
                value = blocks[turn][start : start + count, :]
                first_work[slab + deep, :, lanes] = value
                vectors[0, slab + deep, :, lanes] = value
            start = depth * ROWS * count + deep * ROWS
            levels = H_SCALE * (blocks[turn][start : start + ROWS, :] + 3.75)
            for m in range(ROWS):
                level = jnp.broadcast_to(levels[m : m + 1, :], (SUB, LANES))
                diagonal[slab + deep, :, m * LANES : (m + 1) * LANES] = level
    second_work[...] = jnp.zeros_like(second_work)
    scalars[ITERS] = jnp.zeros((count, LANES), jnp.float32)

    all_rows = [pl.ds(group * SUB, SUB) for group in range(groups)]
    all_lanes = [slice(m * LANES, (m + 1) * LANES) for m in range(ROWS)]
    for group, rows in enumerate(all_rows):
        norm = []
        for plane in range(planes):
            values = plane_rows(first_work, plane, rows)
            norm.append(tree_sum([value * value for value in values]))
        partial[rows, :] = tree_sum(norm)

    def stencil_pass(work, group, between):
        rows = all_rows[group]
        curve = []
        ahead = plane_rolls(plane_rows(work, 0, rows))
        for plane in range(planes):
            rolls = ahead
            if plane + 1 < planes:
                ahead = plane_rolls(plane_rows(work, plane + 1, rows))
            value, out = apply_plane(work, diagonal, plane, rows, rolls, last_x, first_x)
            for m, lanes in enumerate(all_lanes):
                applied[plane, rows, lanes] = out[m]
            curve.append(tree_sum([value[m] * out[m] for m in range(ROWS)]))
            if plane == planes // 2:
                between()
        return tree_sum(curve)

    def update_pass(i, work, before, group, alpha, beta, between):
        rows = all_rows[group]
        norm = []
        for plane in range(planes):
            values = []
            for lanes in all_lanes:
                value = applied[plane, rows, lanes]
                value = value - alpha * work[plane, rows, lanes]
                value = value - beta * before[plane, rows, lanes]
                before[plane, rows, lanes] = value
                vectors[i + 1, plane, rows, lanes] = value
                values.append(value * value)
            norm.append(tree_sum(values))
            if plane == planes // 2:
                between()
        partial[rows, :] = tree_sum(norm)

    def half_turn(i, work, before, may_end):
        norms = [lane_sum(partial[rows, :]) for rows in all_rows]
        last_norms = [scalars[ITERS + i, rows, :] for rows in all_rows]
        alphas, betas = [], []

        def finish_norms():
            for group, rows in enumerate(all_rows):
                scalars[ITERS + 1 + i, rows, :] = norms[group]
                betas.append(ratio(norms[group], last_norms[group]))

        def finish_alpha(group, curve):
            alphas.append(ratio(curve, norms[group]))
            scalars[i, all_rows[group], :] = alphas[group]

        curves = [lane_sum(stencil_pass(work, 0, finish_norms))]
        curves.append(lane_sum(stencil_pass(work, 1, lambda: finish_alpha(0, curves[0]))))
        if may_end:
            finish_alpha(1, curves[1])

            @pl.when(i < ITERS - 1)
            def _():
                for group in range(groups):
                    update_pass(
                        i, work, before, group, alphas[group], betas[group], lambda: None
                    )
        else:
            later = [lambda: finish_alpha(1, curves[1]), lambda: None]
            for group in range(groups):
                update_pass(i, work, before, group, alphas[group], betas[group], later[group])

    def turn(step, carry):
        half_turn(2 * step, first_work, second_work, False)
        half_turn(2 * step + 1, second_work, first_work, True)
        return carry

    lax.fori_loop(0, ITERS // 2, turn, 0)


def gram_kernel(points, scalars, *refs):
    tiles = refs[:points]
    archive, applied, out_b, out_a, gram, limits = refs[points:]
    planes, count, _ = applied.shape
    groups = count // SUB
    size = BASIS * count
    gram[...] = jnp.zeros_like(gram)

    def gram_turn(plane, carry):
        values = [archive[i, plane] for i in range(ITERS)] + [applied[plane]]
        values = jnp.concatenate(values, axis=0)
        high = values.astype(jnp.bfloat16)
        low = (values - high.astype(jnp.float32)).astype(jnp.bfloat16)
        gram[...] += lax.dot_general(
            jnp.concatenate([high, low], axis=0),
            high,
            (((1,), (1,)), ((), ())),
            preferred_element_type=jnp.float32,
        )
        return carry

    lax.fori_loop(0, planes, gram_turn, 0, unroll=UNROLL)
    cross = gram[size:, :]
    pairs = gram[:size, :] + cross + cross.T

    here = lax.axis_index("point")
    core = jnp.bitwise_and(lax.axis_index("dom"), CORES - 1)
    for far, tile in zip((0, 1 + core, 3, 2 - core), tiles):
        limits[jnp.bitwise_xor(here, far)] = tile[...]
    bounds = [jnp.concatenate([limits[j]] * groups, axis=0) for j in range(points)]
    alphas = [scalars[i] for i in range(ITERS)]
    norms = [scalars[ITERS + 1 + i] for i in range(ITERS)]
    weights = weights_of(alphas, norms, bounds, count)
    real = jnp.concatenate([pair[0] for pair in weights], axis=0)
    imag = jnp.concatenate([pair[1] for pair in weights], axis=0)
    right = exact_dot(pairs, jnp.concatenate([real, imag], axis=1), ((1,), (0,)))
    half = MOMENTS * count
    left = jnp.concatenate([real[:, :half], imag[:, :half]], axis=1)
    joined = exact_dot(left.T, right, ((1,), (0,)))
    scale = 1.0 / (planes * ROWS * LANES)
    width = 2 * half
    real = (joined[:half, :width] + joined[half:, width:]) * scale
    imag = (joined[:half, width:] - joined[half:, :width]) * scale
    out_b[0] = real[:, :half]
    out_b[1] = imag[:, :half]
    out_a[0] = real[:, half:]
    out_a[1] = imag[:, half:]


def swapped(values, axis, size, mask):
    return lax.ppermute(values, axis, [(index ^ mask, index) for index in range(size)])


def whole_grid(sources, potential, iter_counts, *, parts, points):
    count, depth, _ = sources.shape
    planes = parts * depth
    block, tile = packed_block(sources, potential, iter_counts)
    even = [block] + [swapped(block, "dom", parts, mask) for mask in range(CORES, parts, CORES)]
    mixed = [
        ((point ^ (1 + part % CORES)) * parts + part, point * parts + part)
        for point in range(points)
        for part in range(parts)
    ]
    tiles = [lax.ppermute(tile, ("point", "dom"), mixed), swapped(tile, "point", points, 3)]
    odd = [swapped(value, "dom", parts, 1) for value in even[1:]]
    own, _, *tiles = lax.optimization_barrier((block, odd[0], *tiles))
    tiles.append(swapped(tiles[0], "dom", parts, 1))
    odd.insert(0, swapped(own, "dom", parts, 1))
    blocks = [value for pair in zip(even, odd) for value in pair]
    vmem = pl.BlockSpec(memory_space=pltpu.VMEM)
    vector = (planes, count, ROWS * LANES)
    cells = planes * ROWS * LANES
    vectors, applied, scalars = pl.pallas_call(
        functools.partial(krylov_kernel, parts, count),
        out_shape=(
            jax.ShapeDtypeStruct((ITERS,) + vector, jnp.float32),
            jax.ShapeDtypeStruct(vector, jnp.float32),
            jax.ShapeDtypeStruct((2 * ITERS + 1, count, LANES), jnp.float32),
        ),
        in_specs=[vmem] * parts,
        out_specs=(vmem,) * 3,
        scratch_shapes=[
            pltpu.VMEM(vector, jnp.float32),
            pltpu.VMEM(vector, jnp.float32),
            pltpu.VMEM((planes, SUB, ROWS * LANES), jnp.float32),
            pltpu.VMEM((count, LANES), jnp.float32),
        ],
        compiler_params=pltpu.CompilerParams(vmem_limit_bytes=16 * 2**20),
        name="krylov",
    )(*blocks)
    size = BASIS * count
    width = MOMENTS * count
    out = jax.ShapeDtypeStruct((2, width, width), jnp.float32)
    return pl.pallas_call(
        functools.partial(gram_kernel, points),
        out_shape=(out, out),
        in_specs=[vmem] * (3 + points),
        out_specs=(vmem, vmem),
        scratch_shapes=[
            pltpu.VMEM((2 * size, size), jnp.float32),
            pltpu.VMEM((points, SUB, LANES), jnp.float32),
        ],
        compiler_params=pltpu.CompilerParams(vmem_limit_bytes=16 * 2**20),
        name="gram",
    )(scalars, tile, *tiles, vectors, applied)


def on_device(sources, potential, iter_counts):
    parts, points = lax.axis_size("dom"), lax.axis_size("point")
    count, depth, cells = sources.shape
    held = BASIS * count * parts * depth * cells * 4
    fits = (
        held <= 16 * 2**20
        and parts == 8
        and points == 4
        and count == 2 * SUB
        and 2 * MOMENTS * count == LANES
        and parts * depth == 16
        and cells == GX * GX == ROWS * LANES
    )
    if not fits:
        return split_grid(sources, potential, iter_counts)
    return whole_grid(sources, potential, iter_counts, parts=parts, points=points)


def solution(mesh):
    placed = (P(None, "dom", None), P("dom", None), P("point"))
    return jax.shard_map(
        on_device, mesh=mesh, in_specs=placed, out_specs=(P(), P()), check_vma=False
    )
```

```python
import functools
import math

import jax
import jax.numpy as jnp
from jax import lax
from jax.experimental import pallas as pl
from jax.experimental.pallas import tpu as pltpu
from jax.sharding import PartitionSpec as P

MOMENTS = 4
ITERS = 6
GX = 32


COEF_NEAR = 4.0 / 3.0
COEF_FAR = -1.0 / 12.0
GAMMA = 2.0
RADIUS = 1.5


def padded_2(block, sides, width):
    for axis, dim in sides:
        count = lax.axis_size(axis)
        forward = [(i, i + 1) for i in range(count - 1)]
        forward.append((count - 1, 0))
        backward = [(target, source) for source, target in forward]
        low = lax.ppermute(
            lax.slice_in_dim(block, block.shape[dim] - width, None, axis=dim), axis, forward
        )
        high = lax.ppermute(lax.slice_in_dim(block, 0, width, axis=dim), axis, backward)
        block = jnp.concatenate([low, block, high], axis=dim)
    return block


def plane_terms(values, side):
    lead = values.shape[:-1]
    planes = values.reshape(lead + (side, side))
    summed = COEF_NEAR * (
        jnp.roll(planes, 1, -2)
        + jnp.roll(planes, -1, -2)
        + jnp.roll(planes, 1, -1)
        + jnp.roll(planes, -1, -1)
    )
    summed = summed + COEF_FAR * (
        jnp.roll(planes, 2, -2)
        + jnp.roll(planes, -2, -2)
        + jnp.roll(planes, 2, -1)
        + jnp.roll(planes, -2, -1)
    )
    return summed.reshape(values.shape)


def complex_mul(first, second):
    return jnp.stack(
        [first[0] * second[0] - first[1] * second[1], first[0] * second[1] + first[1] * second[0]]
    )


def complex_div(first, second):
    denom = second[0] * second[0] + second[1] * second[1]
    return jnp.stack(
        [
            (first[0] * second[0] + first[1] * second[1]) / denom,
            (first[1] * second[0] - first[0] * second[1]) / denom,
        ]
    )


def bilinear(first, second):
    real_part = jnp.sum(first[0] * second[0] - first[1] * second[1], axis=(1, 2))
    imag_part = jnp.sum(first[0] * second[1] + first[1] * second[0], axis=(1, 2))
    return jnp.stack([real_part, imag_part])


def scaled(coeffs, values):
    return complex_mul(coeffs[:, :, None, None], values)


def shifted(values, potential, shift_re, shift_im):
    padded = padded_2(values, (("dom", 2),), 2)
    depth = values.shape[2]
    lap = -7.5 * values + plane_terms(values, GX)
    lap = lap + COEF_NEAR * (padded[:, :, 3 : 3 + depth] + padded[:, :, 1 : 1 + depth])
    lap = lap + COEF_FAR * (padded[:, :, 4 : 4 + depth] + padded[:, :, 0:depth])
    applied = -0.5 * lap + potential * values
    return jnp.stack(
        [
            shift_re * values[0] - shift_im * values[1] - applied[0],
            shift_re * values[1] + shift_im * values[0] - applied[1],
        ]
    )


def residual_sum(values):
    return lax.psum(bilinear(values, values), "dom")


def moment_terms(solution, residual, sources, angle_now, shift_re, shift_im):
    applied = jnp.stack(
        [
            shift_re * solution[0] - shift_im * solution[1] - sources[0] + residual[0],
            shift_re * solution[1] + shift_im * solution[0] - sources[1] + residual[1],
        ]
    )
    angles = (jnp.arange(MOMENTS).astype(jnp.float32) + 1.0) * angle_now
    coeffs = 0.25 * jnp.stack([jnp.cos(angles), jnp.sin(angles)])
    s_terms = complex_mul(coeffs[:, :, None, None, None], solution[:, None])
    h_terms = complex_mul(coeffs[:, :, None, None, None], applied[:, None])
    width = MOMENTS * solution.shape[1]
    return (s_terms.reshape(2, width, -1), h_terms.reshape(2, width, -1))


def gram_of(left, right):
    width = left.shape[1]
    joined = lax.dot_general(
        left.reshape(2 * width, -1),
        right.reshape(2 * width, -1),
        (((1,), (1,)), ((), ())),
        precision=lax.Precision.HIGHEST,
        preferred_element_type=jnp.float32,
    )
    blocks = joined.reshape(2, width, 2, width)
    return jnp.stack([blocks[0, :, 0] + blocks[1, :, 1], blocks[0, :, 1] - blocks[1, :, 0]])


def split_grid(sources, potential, iter_counts):
    complex_src = jnp.stack([sources, jnp.zeros_like(sources)])
    angle_now = (
        2.0 * math.pi * (lax.axis_index("point").astype(jnp.float32) + 0.5) / lax.axis_size("point")
    )
    shift_re = GAMMA + RADIUS * jnp.cos(angle_now)
    shift_im = RADIUS * jnp.sin(angle_now)
    limit = iter_counts[0]
    solution = jnp.zeros_like(complex_src)

    def one_turn(turn_idx, state):
        solution, residual, search, norm_now = state
        product = shifted(search, potential, shift_re, shift_im)
        curve = lax.psum(bilinear(search, product), "dom")
        step_size = complex_div(norm_now, curve)
        new_residual = residual - scaled(step_size, product)
        norm_next = residual_sum(new_residual)
        fresh = (
            solution + scaled(step_size, search),
            new_residual,
            new_residual + scaled(complex_div(norm_next, norm_now), search),
            norm_next,
        )
        keep_mask = turn_idx < limit
        return jax.tree.map(lambda newer, older: jnp.where(keep_mask, newer, older), fresh, state)

    start = (solution, complex_src, complex_src, residual_sum(complex_src))
    solution, residual, search, norm_now = lax.fori_loop(0, ITERS, one_turn, start)
    s_terms, h_terms = moment_terms(solution, residual, complex_src, angle_now, shift_re, shift_im)
    cells = sources.shape[1] * sources.shape[2] * lax.axis_size("dom")
    s_total, h_total = lax.psum((s_terms, h_terms), "point")
    gram_b, gram_a = lax.psum((gram_of(s_total, s_total), gram_of(s_total, h_total)), "dom")
    return (gram_b / cells, gram_a / cells)


Y_IN, X_IN = 2, 4
Y_OUT, X_OUT = GX // Y_IN, GX // X_IN
ROWS = Y_IN * X_IN
LANES = Y_OUT * X_OUT
SUB = 8
BASIS = ITERS + 1
CORES = 2
UNROLL = 4
H_SCALE = 2.0 / COEF_NEAR
FAR_SCALED = 0.5 * H_SCALE * COEF_FAR


def pack_kernel(depth, groups, counts, rows, out, tile):
    columns = rows.shape[0] // (SUB * groups * depth + depth)
    first_level = columns * SUB * groups * depth
    source = lax.broadcasted_iota(jnp.int32, (LANES, LANES), 0)
    target = lax.broadcasted_iota(jnp.int32, (LANES, LANES), 1)
    inner = target // (LANES // ROWS)
    outer = target % (LANES // ROWS)
    cell = (outer // X_OUT * Y_IN + inner // X_IN) * GX + outer % X_OUT * X_IN + inner % X_IN
    swap = jnp.where(source == cell, 1.0, 0.0).astype(jnp.float32)
    parts = []
    for deep in range(depth):
        for group in range(groups):
            for column in range(columns):
                start = (group * SUB * columns + column) * depth + deep
                parts.append(rows[pl.ds(start, SUB, stride=columns * depth), :])
        parts.append(rows[pl.ds(first_level + deep, columns, stride=depth), :])
    mixed = exact_dot(jnp.concatenate(parts, axis=0), swap, ((1,), (0,)))
    block = LANES // ROWS
    lane_block = lax.broadcasted_iota(jnp.int32, (SUB, LANES), 1) // block
    row = lax.broadcasted_iota(jnp.int32, (SUB, LANES), 0)
    for deep in range(depth):
        base = deep * (groups + 1) * columns * SUB - deep * (columns - 1) * SUB
        for group in range(groups):
            pieces = [
                mixed[base + (group * columns + column) * SUB :][:SUB] for column in range(columns)
            ]
            for m in range(ROWS):
                value = pieces[m]
                for column in range(columns):
                    if column != m:
                        moved = pltpu.roll(pieces[column], (column - m) * block % LANES, 1)
                        value = jnp.where(lane_block == column, moved, value)
                start = ((deep * ROWS + m) * groups + group) * SUB
                out[start : start + SUB, :] = value
        piece = mixed[base + groups * columns * SUB :][:SUB]
        value = piece
        for far in range(1, columns):
            moved = pltpu.roll(pltpu.roll(piece, far * block, 1), columns - far, 0)
            value = jnp.where(lane_block == (row + far) % columns, moved, value)
        start = depth * ROWS * SUB * groups + deep * ROWS
        out[start : start + ROWS, :] = value
    tile[...] = jnp.broadcast_to(counts[...].astype(jnp.float32), (SUB, LANES))


def packed_block(sources, potential, iter_counts):
    count, depth, cells = sources.shape
    columns = cells // LANES
    rows = sources.reshape(count, depth, columns, LANES).transpose(0, 2, 1, 3).reshape(-1, LANES)
    levels = potential.reshape(depth, columns, LANES).transpose(1, 0, 2).reshape(-1, LANES)
    vmem = pl.BlockSpec(memory_space=pltpu.VMEM)
    size = depth * ROWS * (count + 1)
    return pl.pallas_call(
        functools.partial(pack_kernel, depth, count // SUB),
        out_shape=(
            jax.ShapeDtypeStruct((size, LANES), jnp.float32),
            jax.ShapeDtypeStruct((SUB, LANES), jnp.float32),
        ),
        in_specs=[vmem, vmem],
        out_specs=(vmem, vmem),
        compiler_params=pltpu.CompilerParams(vmem_limit_bytes=4 * 2**20),
        name="pack",
    )(iter_counts.reshape(1, 1), jnp.concatenate([rows, levels], axis=0))


def lane_sum(values):
    return jnp.broadcast_to(jnp.sum(values, axis=1, keepdims=True), values.shape)


def ratio(top, bottom):
    return jnp.where(bottom > 0.0, top / jnp.where(bottom > 0.0, bottom, 1.0), 0.0)


def tree_sum(values):
    while len(values) > 1:
        values = [sum(values[i : i + 2][1:], values[i]) for i in range(0, len(values), 2)]
    return values[0]


def plane_rows(vector, plane, rows):
    return [vector[plane, rows, m * LANES : (m + 1) * LANES] for m in range(ROWS)]


def y_rolls(here):
    return [
        (pltpu.roll(value, LANES - X_OUT, 1), pltpu.roll(value, X_OUT, 1)) for value in here
    ]


def x_rolls(here):
    halos = []
    for yi in range(Y_IN):
        line = here[yi * X_IN : (yi + 1) * X_IN]
        halo = [
            (pltpu.roll(value, LANES - X_OUT + 1, 1), pltpu.roll(value, 1, 1))
            for value in line[X_IN - 2 :]
        ]
        halo += [
            (pltpu.roll(value, X_OUT - 1, 1), pltpu.roll(value, LANES - 1, 1))
            for value in line[:2]
        ]
        halos.append(halo)
    return halos


def apply_plane(vector, diagonal, plane, rows, here, rolled, ahead, last_x, first_x):
    planes = vector.shape[0]
    above, below, above_2, below_2 = (
        plane_rows(vector, (plane + far) % planes, rows) for far in (1, -1, 2, -2)
    )
    near = [above[m] + below[m] for m in range(ROWS)]
    far = [above_2[m] + below_2[m] for m in range(ROWS)]
    halos = x_rolls(here)
    for m in range(ROWS):
        other = m + X_IN if m < X_IN else m - X_IN
        near[m] = near[m] + (here[other] + rolled[other][1 if m < X_IN else 0])
        far[m] = far[m] + (rolled[m][0] + rolled[m][1])
    for m in range(ROWS):
        yi, xi = m // X_IN, m % X_IN
        for x in (xi - 1, xi + 1):
            if 0 <= x < X_IN:
                near[m] = near[m] + here[yi * X_IN + x]
        for x in (xi - 2, xi + 2):
            if 0 <= x < X_IN:
                far[m] = far[m] + here[yi * X_IN + x]
    coming = ahead()
    out = []
    for yi in range(Y_IN):
        low = [jnp.where(first_x, *pair) for pair in halos[yi][:2]]
        high = [jnp.where(last_x, *pair) for pair in halos[yi][2:]]
        first, last = yi * X_IN, (yi + 1) * X_IN - 1
        near[first] = near[first] + low[1]
        near[last] = near[last] + high[0]
        for m, halo in zip((first, first + 1, last - 1, last), low + high):
            far[m] = far[m] + halo
        for m in range(first, last + 1):
            level = diagonal[plane, :, m * LANES : (m + 1) * LANES]
            out.append(level * here[m] - near[m] - FAR_SCALED * far[m])
    return out, coming


def cmul(first, second):
    return (
        first[0] * second[0] - first[1] * second[1],
        first[0] * second[1] + first[1] * second[0],
    )


def moment_coeffs(point, points, count):
    lane = lax.broadcasted_iota(jnp.int32, (1, LANES), 1)
    moment = lax.rem(lane, MOMENTS * count) // count
    angle = 2.0 * math.pi * (point + 0.5) / points
    parts = []
    for func in (math.cos, math.sin):
        value = jnp.full((1, LANES), 0.25 * func(angle), jnp.float32)
        for k in range(1, MOMENTS):
            value = jnp.where(moment == k, 0.25 * func((k + 1) * angle), value)
        parts.append(value)
    return parts


def weights_of(alphas, norms, limits, count):
    points = len(limits)
    shape = (count, LANES)
    half = MOMENTS * count
    lane = lax.broadcasted_iota(jnp.int32, shape, 1)
    source = lax.broadcasted_iota(jnp.int32, shape, 0)
    own = lax.rem(lane, count) == source
    left_half = lane < half
    betas = [ratio(norms[i + 1], norms[i]) for i in range(ITERS - 1)]
    sums = [[jnp.zeros(shape, jnp.float32)] * 2 for _ in range(BASIS)]
    zero = jnp.zeros(shape, jnp.float32)
    one = jnp.ones(shape, jnp.float32)
    for point in range(points):
        angle = 2.0 * math.pi * (point + 0.5) / points
        shift = (GAMMA + RADIUS * math.cos(angle), RADIUS * math.sin(angle))
        scaled_shift = (H_SCALE * shift[0], H_SCALE * shift[1])
        limit = limits[point]
        product = (one, zero)
        products = [product]
        links = []
        pivot = (scaled_shift[0] - alphas[0], zero + scaled_shift[1])
        for i in range(ITERS):
            size = 1.0 / (pivot[0] * pivot[0] + pivot[1] * pivot[1])
            inverse = (pivot[0] * size, -pivot[1] * size)
            product = cmul(product, inverse)
            products.append(product)
            if i < ITERS - 1:
                link = (betas[i] * inverse[0], betas[i] * inverse[1])
                links.append(link)
                pivot = (scaled_shift[0] - alphas[i + 1] - link[0], scaled_shift[1] - link[1])
        solved = [None] * ITERS
        for i in reversed(range(ITERS)):
            value = (H_SCALE * products[i + 1][0], H_SCALE * products[i + 1][1])
            if i < ITERS - 1:
                step = cmul(links[i], solved[i + 1])
                value = (value[0] + step[0], value[1] + step[1])
            used = limit > i
            solved[i] = (jnp.where(used, value[0], 0.0), jnp.where(used, value[1], 0.0))
        applied = []
        for i in range(BASIS):
            left = limit == i
            rest = (
                jnp.where(left, products[i][0], 0.0),
                jnp.where(left, products[i][1], 0.0),
            )
            if i < ITERS:
                turned = (
                    shift[0] * solved[i][0] - shift[1] * solved[i][1],
                    shift[0] * solved[i][1] + shift[1] * solved[i][0],
                )
                rest = (rest[0] + turned[0], rest[1] + turned[1])
            if i == 0:
                rest = (rest[0] - 1.0, rest[1])
            applied.append(rest)
        tail = applied[ITERS]
        for back, factor in ((1, alphas[ITERS - 1]), (2, betas[ITERS - 2])):
            part = applied[ITERS - back]
            applied[ITERS - back] = (part[0] - factor * tail[0], part[1] - factor * tail[1])
        moment = moment_coeffs(point, points, count)
        for i in range(BASIS):
            left = solved[i] if i < ITERS else (zero, zero)
            both = (
                jnp.where(left_half, left[0], applied[i][0]),
                jnp.where(left_half, left[1], applied[i][1]),
            )
            term = cmul(moment, both)
            sums[i] = [sums[i][0] + term[0], sums[i][1] + term[1]]
    return [[jnp.where(own, part, 0.0) for part in pair] for pair in sums]


def exact_dot(first, second, dims):
    return lax.dot_general(
        first,
        second,
        (dims, ((), ())),
        precision=lax.Precision.HIGHEST,
        preferred_element_type=jnp.float32,
    )


def krylov_kernel(parts, count, *refs):
    blocks, (vectors, applied, scalars, first_work, second_work, diagonal) = refs[:parts], refs[parts:]
    planes = diagonal.shape[0]
    depth = planes // parts
    groups = count // SUB
    lane = lax.broadcasted_iota(jnp.int32, (SUB, LANES), 1)
    last_x = lax.rem(lane, X_OUT) == X_OUT - 1
    first_x = lax.rem(lane, X_OUT) == 0
    here = lax.axis_index("dom")
    for turn in range(parts):
        slab = jnp.bitwise_xor(here, turn) * depth
        for deep in range(depth):
            for m in range(ROWS):
                start = (deep * ROWS + m) * count
                lanes = slice(m * LANES, (m + 1) * LANES)
                value = blocks[turn][start : start + count, :]
                first_work[slab + deep, :, lanes] = value
                vectors[0, slab + deep, :, lanes] = value
            start = depth * ROWS * count + deep * ROWS
            levels = H_SCALE * (blocks[turn][start : start + ROWS, :] + 3.75)
            for m in range(ROWS):
                level = jnp.broadcast_to(levels[m : m + 1, :], (SUB, LANES))
                diagonal[slab + deep, :, m * LANES : (m + 1) * LANES] = level
    second_work[...] = jnp.zeros_like(second_work)
    scalars[ITERS] = jnp.zeros((count, LANES), jnp.float32)

    all_rows = [pl.ds(group * SUB, SUB) for group in range(groups)]
    all_lanes = [slice(m * LANES, (m + 1) * LANES) for m in range(ROWS)]
    for group, rows in enumerate(all_rows):
        norm = []
        for plane in range(planes):
            values = [first_work[plane, rows, lanes] for lanes in all_lanes]
            norm.append(tree_sum([value * value for value in values]))
        scalars[ITERS + 1, rows, :] = lane_sum(tree_sum(norm))

    def half_turn(i, work, before):
        units = [(plane, group) for plane in range(planes) for group in range(groups)]
        curve = [[] for _ in range(groups)]
        here = plane_rows(work, 0, all_rows[0])
        state = (here, y_rolls(here))
        for (plane, group), coming in zip(units, units[1:] + [None]):

            def ahead(coming=coming):
                if coming is None:
                    return None
                here = plane_rows(work, coming[0], all_rows[coming[1]])
                return here, y_rolls(here)

            rows = all_rows[group]
            value = state[0]
            out, state = apply_plane(
                work, diagonal, plane, rows, *state, ahead, last_x, first_x
            )
            for m, lanes in enumerate(all_lanes):
                applied[plane, rows, lanes] = out[m]
            curve[group].append(tree_sum([value[m] * out[m] for m in range(ROWS)]))
        curves = [lane_sum(tree_sum(parts_of)) for parts_of in curve]
        alphas = []
        for group, rows in enumerate(all_rows):
            alphas.append(ratio(curves[group], scalars[ITERS + 1 + i, rows, :]))
            scalars[i, rows, :] = alphas[group]

        @pl.when(i < ITERS - 1)
        def _():
            norms = []
            for group, rows in enumerate(all_rows):
                beta = ratio(scalars[ITERS + 1 + i, rows, :], scalars[ITERS + i, rows, :])
                norm = []
                for plane in range(planes):
                    values = []
                    for lanes in all_lanes:
                        value = applied[plane, rows, lanes]
                        value = value - alphas[group] * work[plane, rows, lanes]
                        value = value - beta * before[plane, rows, lanes]
                        before[plane, rows, lanes] = value
                        vectors[i + 1, plane, rows, lanes] = value
                        values.append(value * value)
                    norm.append(tree_sum(values))
                norms.append(lane_sum(tree_sum(norm)))
            for group, rows in enumerate(all_rows):
                scalars[ITERS + 2 + i, rows, :] = norms[group]

    def turn(step, carry):
        half_turn(2 * step, first_work, second_work)
        half_turn(2 * step + 1, second_work, first_work)
        return carry

    lax.fori_loop(0, ITERS // 2, turn, 0)


def gram_kernel(points, scalars, *refs):
    tiles = refs[:points]
    archive, applied, out_b, out_a, gram, limits = refs[points:]
    planes, count, _ = applied.shape
    groups = count // SUB
    size = BASIS * count
    gram[...] = jnp.zeros_like(gram)

    def gram_turn(plane, carry):
        values = [archive[i, plane] for i in range(ITERS)] + [applied[plane]]
        values = jnp.concatenate(values, axis=0)
        high = values.astype(jnp.bfloat16)
        low = (values - high.astype(jnp.float32)).astype(jnp.bfloat16)
        gram[...] += lax.dot_general(
            jnp.concatenate([high, low], axis=0),
            high,
            (((1,), (1,)), ((), ())),
            preferred_element_type=jnp.float32,
        )
        return carry

    lax.fori_loop(0, planes, gram_turn, 0, unroll=UNROLL)
    cross = gram[size:, :]
    pairs = gram[:size, :] + cross + cross.T

    here = lax.axis_index("point")
    core = jnp.bitwise_and(lax.axis_index("dom"), CORES - 1)
    for far, tile in zip((0, 1 + core, 3, 2 - core), tiles):
        limits[jnp.bitwise_xor(here, far)] = tile[...]
    bounds = [jnp.concatenate([limits[j]] * groups, axis=0) for j in range(points)]
    alphas = [scalars[i] for i in range(ITERS)]
    norms = [scalars[ITERS + 1 + i] for i in range(ITERS)]
    weights = weights_of(alphas, norms, bounds, count)
    real = jnp.concatenate([pair[0] for pair in weights], axis=0)
    imag = jnp.concatenate([pair[1] for pair in weights], axis=0)
    right = exact_dot(pairs, jnp.concatenate([real, imag], axis=1), ((1,), (0,)))
    half = MOMENTS * count
    left = jnp.concatenate([real[:, :half], imag[:, :half]], axis=1)
    joined = exact_dot(left.T, right, ((1,), (0,)))
    scale = 1.0 / (planes * ROWS * LANES)
    width = 2 * half
    real = (joined[:half, :width] + joined[half:, width:]) * scale
    imag = (joined[:half, width:] - joined[half:, :width]) * scale
    out_b[0] = real[:, :half]
    out_b[1] = imag[:, :half]
    out_a[0] = real[:, half:]
    out_a[1] = imag[:, half:]


def swapped(values, axis, size, mask):
    return lax.ppermute(values, axis, [(index ^ mask, index) for index in range(size)])


def whole_grid(sources, potential, iter_counts, *, parts, points):
    count, depth, _ = sources.shape
    planes = parts * depth
    block, tile = packed_block(sources, potential, iter_counts)
    even = [block] + [swapped(block, "dom", parts, mask) for mask in range(CORES, parts, CORES)]
    mixed = [
        ((point ^ (1 + part % CORES)) * parts + part, point * parts + part)
        for point in range(points)
        for part in range(parts)
    ]
    tiles = [lax.ppermute(tile, ("point", "dom"), mixed), swapped(tile, "point", points, 3)]
    even[1], *tiles = lax.optimization_barrier((even[1], *tiles))
    tiles.append(swapped(tiles[0], "dom", parts, 1))
    odd = [swapped(value, "dom", parts, 1) for value in even]
    blocks = [value for pair in zip(even, odd) for value in pair]
    vmem = pl.BlockSpec(memory_space=pltpu.VMEM)
    vector = (planes, count, ROWS * LANES)
    cells = planes * ROWS * LANES
    vectors, applied, scalars = pl.pallas_call(
        functools.partial(krylov_kernel, parts, count),
        out_shape=(
            jax.ShapeDtypeStruct((ITERS,) + vector, jnp.float32),
            jax.ShapeDtypeStruct(vector, jnp.float32),
            jax.ShapeDtypeStruct((2 * ITERS + 1, count, LANES), jnp.float32),
        ),
        in_specs=[vmem] * parts,
        out_specs=(vmem,) * 3,
        scratch_shapes=[
            pltpu.VMEM(vector, jnp.float32),
            pltpu.VMEM(vector, jnp.float32),
            pltpu.VMEM((planes, SUB, ROWS * LANES), jnp.float32),
        ],
        compiler_params=pltpu.CompilerParams(vmem_limit_bytes=16 * 2**20),
        name="krylov",
    )(*blocks)
    size = BASIS * count
    width = MOMENTS * count
    out = jax.ShapeDtypeStruct((2, width, width), jnp.float32)
    return pl.pallas_call(
        functools.partial(gram_kernel, points),
        out_shape=(out, out),
        in_specs=[vmem] * (3 + points),
        out_specs=(vmem, vmem),
        scratch_shapes=[
            pltpu.VMEM((2 * size, size), jnp.float32),
            pltpu.VMEM((points, SUB, LANES), jnp.float32),
        ],
        compiler_params=pltpu.CompilerParams(vmem_limit_bytes=16 * 2**20),
        name="gram",
    )(scalars, tile, *tiles, vectors, applied)


def on_device(sources, potential, iter_counts):
    parts, points = lax.axis_size("dom"), lax.axis_size("point")
    count, depth, cells = sources.shape
    held = BASIS * count * parts * depth * cells * 4
    fits = (
        held <= 16 * 2**20
        and parts == 8
        and points == 4
        and count == 2 * SUB
        and 2 * MOMENTS * count == LANES
        and parts * depth == 16
        and cells == GX * GX == ROWS * LANES
    )
    if not fits:
        return split_grid(sources, potential, iter_counts)
    return whole_grid(sources, potential, iter_counts, parts=parts, points=points)


def solution(mesh):
    placed = (P(None, "dom", None), P("dom", None), P("point"))
    return jax.shard_map(
        on_device, mesh=mesh, in_specs=placed, out_specs=(P(), P()), check_vma=False
    )
```

```python
import functools
import math

import jax
import jax.numpy as jnp
from jax import lax
from jax.experimental import pallas as pl
from jax.experimental.pallas import tpu as pltpu
from jax.sharding import PartitionSpec as P

MOMENTS = 4
ITERS = 6
GX = 32


COEF_NEAR = 4.0 / 3.0
COEF_FAR = -1.0 / 12.0
GAMMA = 2.0
RADIUS = 1.5


def padded_2(block, sides, width):
    for axis, dim in sides:
        count = lax.axis_size(axis)
        forward = [(i, i + 1) for i in range(count - 1)]
        forward.append((count - 1, 0))
        backward = [(target, source) for source, target in forward]
        low = lax.ppermute(
            lax.slice_in_dim(block, block.shape[dim] - width, None, axis=dim), axis, forward
        )
        high = lax.ppermute(lax.slice_in_dim(block, 0, width, axis=dim), axis, backward)
        block = jnp.concatenate([low, block, high], axis=dim)
    return block


def plane_terms(values, side):
    lead = values.shape[:-1]
    planes = values.reshape(lead + (side, side))
    summed = COEF_NEAR * (
        jnp.roll(planes, 1, -2)
        + jnp.roll(planes, -1, -2)
        + jnp.roll(planes, 1, -1)
        + jnp.roll(planes, -1, -1)
    )
    summed = summed + COEF_FAR * (
        jnp.roll(planes, 2, -2)
        + jnp.roll(planes, -2, -2)
        + jnp.roll(planes, 2, -1)
        + jnp.roll(planes, -2, -1)
    )
    return summed.reshape(values.shape)


def complex_mul(first, second):
    return jnp.stack(
        [first[0] * second[0] - first[1] * second[1], first[0] * second[1] + first[1] * second[0]]
    )


def complex_div(first, second):
    denom = second[0] * second[0] + second[1] * second[1]
    return jnp.stack(
        [
            (first[0] * second[0] + first[1] * second[1]) / denom,
            (first[1] * second[0] - first[0] * second[1]) / denom,
        ]
    )


def bilinear(first, second):
    real_part = jnp.sum(first[0] * second[0] - first[1] * second[1], axis=(1, 2))
    imag_part = jnp.sum(first[0] * second[1] + first[1] * second[0], axis=(1, 2))
    return jnp.stack([real_part, imag_part])


def scaled(coeffs, values):
    return complex_mul(coeffs[:, :, None, None], values)


def shifted(values, potential, shift_re, shift_im):
    padded = padded_2(values, (("dom", 2),), 2)
    depth = values.shape[2]
    lap = -7.5 * values + plane_terms(values, GX)
    lap = lap + COEF_NEAR * (padded[:, :, 3 : 3 + depth] + padded[:, :, 1 : 1 + depth])
    lap = lap + COEF_FAR * (padded[:, :, 4 : 4 + depth] + padded[:, :, 0:depth])
    applied = -0.5 * lap + potential * values
    return jnp.stack(
        [
            shift_re * values[0] - shift_im * values[1] - applied[0],
            shift_re * values[1] + shift_im * values[0] - applied[1],
        ]
    )


def residual_sum(values):
    return lax.psum(bilinear(values, values), "dom")


def moment_terms(solution, residual, sources, angle_now, shift_re, shift_im):
    applied = jnp.stack(
        [
            shift_re * solution[0] - shift_im * solution[1] - sources[0] + residual[0],
            shift_re * solution[1] + shift_im * solution[0] - sources[1] + residual[1],
        ]
    )
    angles = (jnp.arange(MOMENTS).astype(jnp.float32) + 1.0) * angle_now
    coeffs = 0.25 * jnp.stack([jnp.cos(angles), jnp.sin(angles)])
    s_terms = complex_mul(coeffs[:, :, None, None, None], solution[:, None])
    h_terms = complex_mul(coeffs[:, :, None, None, None], applied[:, None])
    width = MOMENTS * solution.shape[1]
    return (s_terms.reshape(2, width, -1), h_terms.reshape(2, width, -1))


def gram_of(left, right):
    width = left.shape[1]
    joined = lax.dot_general(
        left.reshape(2 * width, -1),
        right.reshape(2 * width, -1),
        (((1,), (1,)), ((), ())),
        precision=lax.Precision.HIGHEST,
        preferred_element_type=jnp.float32,
    )
    blocks = joined.reshape(2, width, 2, width)
    return jnp.stack([blocks[0, :, 0] + blocks[1, :, 1], blocks[0, :, 1] - blocks[1, :, 0]])


def split_grid(sources, potential, iter_counts):
    complex_src = jnp.stack([sources, jnp.zeros_like(sources)])
    angle_now = (
        2.0 * math.pi * (lax.axis_index("point").astype(jnp.float32) + 0.5) / lax.axis_size("point")
    )
    shift_re = GAMMA + RADIUS * jnp.cos(angle_now)
    shift_im = RADIUS * jnp.sin(angle_now)
    limit = iter_counts[0]
    solution = jnp.zeros_like(complex_src)

    def one_turn(turn_idx, state):
        solution, residual, search, norm_now = state
        product = shifted(search, potential, shift_re, shift_im)
        curve = lax.psum(bilinear(search, product), "dom")
        step_size = complex_div(norm_now, curve)
        new_residual = residual - scaled(step_size, product)
        norm_next = residual_sum(new_residual)
        fresh = (
            solution + scaled(step_size, search),
            new_residual,
            new_residual + scaled(complex_div(norm_next, norm_now), search),
            norm_next,
        )
        keep_mask = turn_idx < limit
        return jax.tree.map(lambda newer, older: jnp.where(keep_mask, newer, older), fresh, state)

    start = (solution, complex_src, complex_src, residual_sum(complex_src))
    solution, residual, search, norm_now = lax.fori_loop(0, ITERS, one_turn, start)
    s_terms, h_terms = moment_terms(solution, residual, complex_src, angle_now, shift_re, shift_im)
    cells = sources.shape[1] * sources.shape[2] * lax.axis_size("dom")
    s_total, h_total = lax.psum((s_terms, h_terms), "point")
    gram_b, gram_a = lax.psum((gram_of(s_total, s_total), gram_of(s_total, h_total)), "dom")
    return (gram_b / cells, gram_a / cells)


Y_IN, X_IN = 2, 4
Y_OUT, X_OUT = GX // Y_IN, GX // X_IN
ROWS = Y_IN * X_IN
LANES = Y_OUT * X_OUT
SUB = 8
BASIS = ITERS + 1
CORES = 2
UNROLL = 4
H_SCALE = 2.0 / COEF_NEAR
FAR_SCALED = 0.5 * H_SCALE * COEF_FAR


def pack_kernel(depth, groups, counts, rows, out, tile):
    columns = rows.shape[0] // (SUB * groups * depth + depth)
    first_level = columns * SUB * groups * depth
    source = lax.broadcasted_iota(jnp.int32, (LANES, LANES), 0)
    target = lax.broadcasted_iota(jnp.int32, (LANES, LANES), 1)
    inner = target // (LANES // ROWS)
    outer = target % (LANES // ROWS)
    cell = (outer // X_OUT * Y_IN + inner // X_IN) * GX + outer % X_OUT * X_IN + inner % X_IN
    swap = jnp.where(source == cell, 1.0, 0.0).astype(jnp.float32)
    parts = []
    for deep in range(depth):
        for group in range(groups):
            for column in range(columns):
                start = (group * SUB * columns + column) * depth + deep
                parts.append(rows[pl.ds(start, SUB, stride=columns * depth), :])
        parts.append(rows[pl.ds(first_level + deep, columns, stride=depth), :])
    mixed = exact_dot(jnp.concatenate(parts, axis=0), swap, ((1,), (0,)))
    block = LANES // ROWS
    lane_block = lax.broadcasted_iota(jnp.int32, (SUB, LANES), 1) // block
    row = lax.broadcasted_iota(jnp.int32, (SUB, LANES), 0)
    for deep in range(depth):
        base = deep * (groups + 1) * columns * SUB - deep * (columns - 1) * SUB
        for group in range(groups):
            pieces = [
                mixed[base + (group * columns + column) * SUB :][:SUB] for column in range(columns)
            ]
            for m in range(ROWS):
                value = pieces[m]
                for column in range(columns):
                    if column != m:
                        moved = pltpu.roll(pieces[column], (column - m) * block % LANES, 1)
                        value = jnp.where(lane_block == column, moved, value)
                start = ((deep * ROWS + m) * groups + group) * SUB
                out[start : start + SUB, :] = value
        piece = mixed[base + groups * columns * SUB :][:SUB]
        value = piece
        for far in range(1, columns):
            moved = pltpu.roll(pltpu.roll(piece, far * block, 1), columns - far, 0)
            value = jnp.where(lane_block == (row + far) % columns, moved, value)
        start = depth * ROWS * SUB * groups + deep * ROWS
        out[start : start + ROWS, :] = value
    tile[...] = jnp.broadcast_to(counts[...].astype(jnp.float32), (SUB, LANES))


def packed_block(sources, potential, iter_counts):
    count, depth, cells = sources.shape
    columns = cells // LANES
    rows = sources.reshape(count, depth, columns, LANES).transpose(0, 2, 1, 3).reshape(-1, LANES)
    levels = potential.reshape(depth, columns, LANES).transpose(1, 0, 2).reshape(-1, LANES)
    vmem = pl.BlockSpec(memory_space=pltpu.VMEM)
    size = depth * ROWS * (count + 1)
    return pl.pallas_call(
        functools.partial(pack_kernel, depth, count // SUB),
        out_shape=(
            jax.ShapeDtypeStruct((size, LANES), jnp.float32),
            jax.ShapeDtypeStruct((SUB, LANES), jnp.float32),
        ),
        in_specs=[vmem, vmem],
        out_specs=(vmem, vmem),
        compiler_params=pltpu.CompilerParams(vmem_limit_bytes=4 * 2**20),
        name="pack",
    )(iter_counts.reshape(1, 1), jnp.concatenate([rows, levels], axis=0))


def lane_sum(values):
    return jnp.broadcast_to(jnp.sum(values, axis=1, keepdims=True), values.shape)


def ratio(top, bottom):
    return jnp.where(bottom > 0.0, top / jnp.where(bottom > 0.0, bottom, 1.0), 0.0)


def tree_sum(values):
    while len(values) > 1:
        values = [sum(values[i : i + 2][1:], values[i]) for i in range(0, len(values), 2)]
    return values[0]


def plane_rows(vector, plane, rows):
    return [vector[plane, rows, m * LANES : (m + 1) * LANES] for m in range(ROWS)]


def y_rolls(here):
    return [
        (pltpu.roll(value, LANES - X_OUT, 1), pltpu.roll(value, X_OUT, 1)) for value in here
    ]


def x_rolls(here, rolled, last_x, first_x):
    halos = []
    for yi in range(Y_IN):
        first = yi * X_IN
        halo = [
            pltpu.roll(jnp.where(last_x, rolled[m][0], here[m]), 1, 1)
            for m in range(first + X_IN - 2, first + X_IN)
        ]
        halo += [
            pltpu.roll(jnp.where(first_x, rolled[m][1], here[m]), LANES - 1, 1)
            for m in range(first, first + 2)
        ]
        halos.append(halo)
    return halos


def apply_plane(vector, diagonal, plane, rows, here, rolled, ahead, last_x, first_x):
    planes = vector.shape[0]
    above, below, above_2, below_2 = (
        plane_rows(vector, (plane + far) % planes, rows) for far in (1, -1, 2, -2)
    )
    near = [above[m] + below[m] for m in range(ROWS)]
    far = [above_2[m] + below_2[m] for m in range(ROWS)]
    halos = x_rolls(here, rolled, last_x, first_x)
    for m in range(ROWS):
        other = m + X_IN if m < X_IN else m - X_IN
        near[m] = near[m] + (here[other] + rolled[other][1 if m < X_IN else 0])
        far[m] = far[m] + (rolled[m][0] + rolled[m][1])
    for m in range(ROWS):
        yi, xi = m // X_IN, m % X_IN
        for x in (xi - 1, xi + 1):
            if 0 <= x < X_IN:
                near[m] = near[m] + here[yi * X_IN + x]
        for x in (xi - 2, xi + 2):
            if 0 <= x < X_IN:
                far[m] = far[m] + here[yi * X_IN + x]
    coming = ahead()
    out = []
    for yi in range(Y_IN):
        low, high = halos[yi][:2], halos[yi][2:]
        first, last = yi * X_IN, (yi + 1) * X_IN - 1
        near[first] = near[first] + low[1]
        near[last] = near[last] + high[0]
        for m, halo in zip((first, first + 1, last - 1, last), low + high):
            far[m] = far[m] + halo
        for m in range(first, last + 1):
            level = diagonal[plane, :, m * LANES : (m + 1) * LANES]
            out.append(level * here[m] - near[m] - FAR_SCALED * far[m])
    return out, coming


def cmul(first, second):
    return (
        first[0] * second[0] - first[1] * second[1],
        first[0] * second[1] + first[1] * second[0],
    )


def moment_coeffs(point, points, count):
    lane = lax.broadcasted_iota(jnp.int32, (1, LANES), 1)
    moment = lax.rem(lane, MOMENTS * count) // count
    angle = 2.0 * math.pi * (point + 0.5) / points
    parts = []
    for func in (math.cos, math.sin):
        value = jnp.full((1, LANES), 0.25 * func(angle), jnp.float32)
        for k in range(1, MOMENTS):
            value = jnp.where(moment == k, 0.25 * func((k + 1) * angle), value)
        parts.append(value)
    return parts


def weights_of(alphas, norms, limits, count):
    points = len(limits)
    shape = (count, LANES)
    half = MOMENTS * count
    lane = lax.broadcasted_iota(jnp.int32, shape, 1)
    source = lax.broadcasted_iota(jnp.int32, shape, 0)
    own = lax.rem(lane, count) == source
    left_half = lane < half
    betas = [ratio(norms[i + 1], norms[i]) for i in range(ITERS - 1)]
    sums = [[jnp.zeros(shape, jnp.float32)] * 2 for _ in range(BASIS)]
    zero = jnp.zeros(shape, jnp.float32)
    one = jnp.ones(shape, jnp.float32)
    for point in range(points):
        angle = 2.0 * math.pi * (point + 0.5) / points
        shift = (GAMMA + RADIUS * math.cos(angle), RADIUS * math.sin(angle))
        scaled_shift = (H_SCALE * shift[0], H_SCALE * shift[1])
        limit = limits[point]
        product = (one, zero)
        products = [product]
        links = []
        pivot = (scaled_shift[0] - alphas[0], zero + scaled_shift[1])
        for i in range(ITERS):
            size = 1.0 / (pivot[0] * pivot[0] + pivot[1] * pivot[1])
            inverse = (pivot[0] * size, -pivot[1] * size)
            product = cmul(product, inverse)
            products.append(product)
            if i < ITERS - 1:
                link = (betas[i] * inverse[0], betas[i] * inverse[1])
                links.append(link)
                pivot = (scaled_shift[0] - alphas[i + 1] - link[0], scaled_shift[1] - link[1])
        solved = [None] * ITERS
        for i in reversed(range(ITERS)):
            value = (H_SCALE * products[i + 1][0], H_SCALE * products[i + 1][1])
            if i < ITERS - 1:
                step = cmul(links[i], solved[i + 1])
                value = (value[0] + step[0], value[1] + step[1])
            used = limit > i
            solved[i] = (jnp.where(used, value[0], 0.0), jnp.where(used, value[1], 0.0))
        applied = []
        for i in range(BASIS):
            left = limit == i
            rest = (
                jnp.where(left, products[i][0], 0.0),
                jnp.where(left, products[i][1], 0.0),
            )
            if i < ITERS:
                turned = (
                    shift[0] * solved[i][0] - shift[1] * solved[i][1],
                    shift[0] * solved[i][1] + shift[1] * solved[i][0],
                )
                rest = (rest[0] + turned[0], rest[1] + turned[1])
            if i == 0:
                rest = (rest[0] - 1.0, rest[1])
            applied.append(rest)
        tail = applied[ITERS]
        for back, factor in ((1, alphas[ITERS - 1]), (2, betas[ITERS - 2])):
            part = applied[ITERS - back]
            applied[ITERS - back] = (part[0] - factor * tail[0], part[1] - factor * tail[1])
        moment = moment_coeffs(point, points, count)
        for i in range(BASIS):
            left = solved[i] if i < ITERS else (zero, zero)
            both = (
                jnp.where(left_half, left[0], applied[i][0]),
                jnp.where(left_half, left[1], applied[i][1]),
            )
            term = cmul(moment, both)
            sums[i] = [sums[i][0] + term[0], sums[i][1] + term[1]]
    return [[jnp.where(own, part, 0.0) for part in pair] for pair in sums]


def exact_dot(first, second, dims):
    return lax.dot_general(
        first,
        second,
        (dims, ((), ())),
        precision=lax.Precision.HIGHEST,
        preferred_element_type=jnp.float32,
    )


def krylov_kernel(parts, count, *refs):
    blocks, (vectors, applied, scalars, first_work, second_work, diagonal) = refs[:parts], refs[parts:]
    planes = diagonal.shape[0]
    depth = planes // parts
    groups = count // SUB
    lane = lax.broadcasted_iota(jnp.int32, (SUB, LANES), 1)
    last_x = lax.rem(lane, X_OUT) == X_OUT - 1
    first_x = lax.rem(lane, X_OUT) == 0
    here = lax.axis_index("dom")
    for turn in range(parts):
        slab = jnp.bitwise_xor(here, turn) * depth
        for deep in range(depth):
            for m in range(ROWS):
                start = (deep * ROWS + m) * count
                lanes = slice(m * LANES, (m + 1) * LANES)
                value = blocks[turn][start : start + count, :]
                first_work[slab + deep, :, lanes] = value
                vectors[0, slab + deep, :, lanes] = value
            start = depth * ROWS * count + deep * ROWS
            levels = H_SCALE * (blocks[turn][start : start + ROWS, :] + 3.75)
            for m in range(ROWS):
                level = jnp.broadcast_to(levels[m : m + 1, :], (SUB, LANES))
                diagonal[slab + deep, :, m * LANES : (m + 1) * LANES] = level
    second_work[...] = jnp.zeros_like(second_work)
    scalars[ITERS] = jnp.zeros((count, LANES), jnp.float32)

    all_rows = [pl.ds(group * SUB, SUB) for group in range(groups)]
    all_lanes = [slice(m * LANES, (m + 1) * LANES) for m in range(ROWS)]
    for group, rows in enumerate(all_rows):
        norm = []
        for plane in range(planes):
            values = [first_work[plane, rows, lanes] for lanes in all_lanes]
            norm.append(tree_sum([value * value for value in values]))
        scalars[ITERS + 1, rows, :] = lane_sum(tree_sum(norm))

    def half_turn(i, work, before):
        units = [(plane, group) for plane in range(planes) for group in range(groups)]
        curve = [[] for _ in range(groups)]
        here = plane_rows(work, 0, all_rows[0])
        state = (here, y_rolls(here))
        for (plane, group), coming in zip(units, units[1:] + [None]):

            def ahead(coming=coming):
                if coming is None:
                    return None
                here = plane_rows(work, coming[0], all_rows[coming[1]])
                return here, y_rolls(here)

            rows = all_rows[group]
            value = state[0]
            out, state = apply_plane(
                work, diagonal, plane, rows, *state, ahead, last_x, first_x
            )
            for m, lanes in enumerate(all_lanes):
                applied[plane, rows, lanes] = out[m]
            curve[group].append(tree_sum([value[m] * out[m] for m in range(ROWS)]))
        curves = [lane_sum(tree_sum(parts_of)) for parts_of in curve]
        alphas = []
        for group, rows in enumerate(all_rows):
            alphas.append(ratio(curves[group], scalars[ITERS + 1 + i, rows, :]))
            scalars[i, rows, :] = alphas[group]

        @pl.when(i < ITERS - 1)
        def _():
            norms = []
            for group, rows in enumerate(all_rows):
                beta = ratio(scalars[ITERS + 1 + i, rows, :], scalars[ITERS + i, rows, :])
                norm = []
                for plane in range(planes):
                    values = []
                    for lanes in all_lanes:
                        value = applied[plane, rows, lanes]
                        value = value - alphas[group] * work[plane, rows, lanes]
                        value = value - beta * before[plane, rows, lanes]
                        before[plane, rows, lanes] = value
                        vectors[i + 1, plane, rows, lanes] = value
                        values.append(value * value)
                    norm.append(tree_sum(values))
                norms.append(lane_sum(tree_sum(norm)))
            for group, rows in enumerate(all_rows):
                scalars[ITERS + 2 + i, rows, :] = norms[group]

    def turn(step, carry):
        half_turn(2 * step, first_work, second_work)
        half_turn(2 * step + 1, second_work, first_work)
        return carry

    lax.fori_loop(0, ITERS // 2, turn, 0)


def gram_kernel(points, scalars, *refs):
    tiles = refs[:points]
    archive, applied, out_b, out_a, gram, limits = refs[points:]
    planes, count, _ = applied.shape
    groups = count // SUB
    size = BASIS * count
    gram[...] = jnp.zeros_like(gram)

    def gram_turn(plane, carry):
        values = [archive[i, plane] for i in range(ITERS)] + [applied[plane]]
        values = jnp.concatenate(values, axis=0)
        high = values.astype(jnp.bfloat16)
        low = (values - high.astype(jnp.float32)).astype(jnp.bfloat16)
        gram[...] += lax.dot_general(
            jnp.concatenate([high, low], axis=0),
            high,
            (((1,), (1,)), ((), ())),
            preferred_element_type=jnp.float32,
        )
        return carry

    lax.fori_loop(0, planes, gram_turn, 0, unroll=UNROLL)
    cross = gram[size:, :]
    pairs = gram[:size, :] + cross + cross.T

    here = lax.axis_index("point")
    core = jnp.bitwise_and(lax.axis_index("dom"), CORES - 1)
    for far, tile in zip((0, 1 + core, 3, 2 - core), tiles):
        limits[jnp.bitwise_xor(here, far)] = tile[...]
    bounds = [jnp.concatenate([limits[j]] * groups, axis=0) for j in range(points)]
    alphas = [scalars[i] for i in range(ITERS)]
    norms = [scalars[ITERS + 1 + i] for i in range(ITERS)]
    weights = weights_of(alphas, norms, bounds, count)
    real = jnp.concatenate([pair[0] for pair in weights], axis=0)
    imag = jnp.concatenate([pair[1] for pair in weights], axis=0)
    right = exact_dot(pairs, jnp.concatenate([real, imag], axis=1), ((1,), (0,)))
    half = MOMENTS * count
    left = jnp.concatenate([real[:, :half], imag[:, :half]], axis=1)
    joined = exact_dot(left.T, right, ((1,), (0,)))
    scale = 1.0 / (planes * ROWS * LANES)
    width = 2 * half
    real = (joined[:half, :width] + joined[half:, width:]) * scale
    imag = (joined[:half, width:] - joined[half:, :width]) * scale
    out_b[0] = real[:, :half]
    out_b[1] = imag[:, :half]
    out_a[0] = real[:, half:]
    out_a[1] = imag[:, half:]


def swapped(values, axis, size, mask):
    return lax.ppermute(values, axis, [(index ^ mask, index) for index in range(size)])


def whole_grid(sources, potential, iter_counts, *, parts, points):
    count, depth, _ = sources.shape
    planes = parts * depth
    block, tile = packed_block(sources, potential, iter_counts)
    even = [block] + [swapped(block, "dom", parts, mask) for mask in range(CORES, parts, CORES)]
    mixed = [
        ((point ^ (1 + part % CORES)) * parts + part, point * parts + part)
        for point in range(points)
        for part in range(parts)
    ]
    tiles = [lax.ppermute(tile, ("point", "dom"), mixed), swapped(tile, "point", points, 3)]
    even[1], *tiles = lax.optimization_barrier((even[1], *tiles))
    tiles.append(swapped(tiles[0], "dom", parts, 1))
    odd = [swapped(value, "dom", parts, 1) for value in even]
    blocks = [value for pair in zip(even, odd) for value in pair]
    vmem = pl.BlockSpec(memory_space=pltpu.VMEM)
    vector = (planes, count, ROWS * LANES)
    cells = planes * ROWS * LANES
    vectors, applied, scalars = pl.pallas_call(
        functools.partial(krylov_kernel, parts, count),
        out_shape=(
            jax.ShapeDtypeStruct((ITERS,) + vector, jnp.float32),
            jax.ShapeDtypeStruct(vector, jnp.float32),
            jax.ShapeDtypeStruct((2 * ITERS + 1, count, LANES), jnp.float32),
        ),
        in_specs=[vmem] * parts,
        out_specs=(vmem,) * 3,
        scratch_shapes=[
            pltpu.VMEM(vector, jnp.float32),
            pltpu.VMEM(vector, jnp.float32),
            pltpu.VMEM((planes, SUB, ROWS * LANES), jnp.float32),
        ],
        compiler_params=pltpu.CompilerParams(vmem_limit_bytes=16 * 2**20),
        name="krylov",
    )(*blocks)
    size = BASIS * count
    width = MOMENTS * count
    out = jax.ShapeDtypeStruct((2, width, width), jnp.float32)
    return pl.pallas_call(
        functools.partial(gram_kernel, points),
        out_shape=(out, out),
        in_specs=[vmem] * (3 + points),
        out_specs=(vmem, vmem),
        scratch_shapes=[
            pltpu.VMEM((2 * size, size), jnp.float32),
            pltpu.VMEM((points, SUB, LANES), jnp.float32),
        ],
        compiler_params=pltpu.CompilerParams(vmem_limit_bytes=16 * 2**20),
        name="gram",
    )(scalars, tile, *tiles, vectors, applied)


def on_device(sources, potential, iter_counts):
    parts, points = lax.axis_size("dom"), lax.axis_size("point")
    count, depth, cells = sources.shape
    held = BASIS * count * parts * depth * cells * 4
    fits = (
        held <= 16 * 2**20
        and parts == 8
        and points == 4
        and count == 2 * SUB
        and 2 * MOMENTS * count == LANES
        and parts * depth == 16
        and cells == GX * GX == ROWS * LANES
    )
    if not fits:
        return split_grid(sources, potential, iter_counts)
    return whole_grid(sources, potential, iter_counts, parts=parts, points=points)


def solution(mesh):
    placed = (P(None, "dom", None), P("dom", None), P("point"))
    return jax.shard_map(
        on_device, mesh=mesh, in_specs=placed, out_specs=(P(), P()), check_vma=False
    )
```

```python
import functools
import math

import jax
import jax.numpy as jnp
from jax import lax
from jax.experimental import pallas as pl
from jax.experimental.pallas import tpu as pltpu
from jax.sharding import PartitionSpec as P

MOMENTS = 4
ITERS = 6
GX = 32


COEF_NEAR = 4.0 / 3.0
COEF_FAR = -1.0 / 12.0
GAMMA = 2.0
RADIUS = 1.5


def padded_2(block, sides, width):
    for axis, dim in sides:
        count = lax.axis_size(axis)
        forward = [(i, i + 1) for i in range(count - 1)]
        forward.append((count - 1, 0))
        backward = [(target, source) for source, target in forward]
        low = lax.ppermute(
            lax.slice_in_dim(block, block.shape[dim] - width, None, axis=dim), axis, forward
        )
        high = lax.ppermute(lax.slice_in_dim(block, 0, width, axis=dim), axis, backward)
        block = jnp.concatenate([low, block, high], axis=dim)
    return block


def plane_terms(values, side):
    lead = values.shape[:-1]
    planes = values.reshape(lead + (side, side))
    summed = COEF_NEAR * (
        jnp.roll(planes, 1, -2)
        + jnp.roll(planes, -1, -2)
        + jnp.roll(planes, 1, -1)
        + jnp.roll(planes, -1, -1)
    )
    summed = summed + COEF_FAR * (
        jnp.roll(planes, 2, -2)
        + jnp.roll(planes, -2, -2)
        + jnp.roll(planes, 2, -1)
        + jnp.roll(planes, -2, -1)
    )
    return summed.reshape(values.shape)


def complex_mul(first, second):
    return jnp.stack(
        [first[0] * second[0] - first[1] * second[1], first[0] * second[1] + first[1] * second[0]]
    )


def complex_div(first, second):
    denom = second[0] * second[0] + second[1] * second[1]
    return jnp.stack(
        [
            (first[0] * second[0] + first[1] * second[1]) / denom,
            (first[1] * second[0] - first[0] * second[1]) / denom,
        ]
    )


def bilinear(first, second):
    real_part = jnp.sum(first[0] * second[0] - first[1] * second[1], axis=(1, 2))
    imag_part = jnp.sum(first[0] * second[1] + first[1] * second[0], axis=(1, 2))
    return jnp.stack([real_part, imag_part])


def scaled(coeffs, values):
    return complex_mul(coeffs[:, :, None, None], values)


def shifted(values, potential, shift_re, shift_im):
    padded = padded_2(values, (("dom", 2),), 2)
    depth = values.shape[2]
    lap = -7.5 * values + plane_terms(values, GX)
    lap = lap + COEF_NEAR * (padded[:, :, 3 : 3 + depth] + padded[:, :, 1 : 1 + depth])
    lap = lap + COEF_FAR * (padded[:, :, 4 : 4 + depth] + padded[:, :, 0:depth])
    applied = -0.5 * lap + potential * values
    return jnp.stack(
        [
            shift_re * values[0] - shift_im * values[1] - applied[0],
            shift_re * values[1] + shift_im * values[0] - applied[1],
        ]
    )


def residual_sum(values):
    return lax.psum(bilinear(values, values), "dom")


def moment_terms(solution, residual, sources, angle_now, shift_re, shift_im):
    applied = jnp.stack(
        [
            shift_re * solution[0] - shift_im * solution[1] - sources[0] + residual[0],
            shift_re * solution[1] + shift_im * solution[0] - sources[1] + residual[1],
        ]
    )
    angles = (jnp.arange(MOMENTS).astype(jnp.float32) + 1.0) * angle_now
    coeffs = 0.25 * jnp.stack([jnp.cos(angles), jnp.sin(angles)])
    s_terms = complex_mul(coeffs[:, :, None, None, None], solution[:, None])
    h_terms = complex_mul(coeffs[:, :, None, None, None], applied[:, None])
    width = MOMENTS * solution.shape[1]
    return (s_terms.reshape(2, width, -1), h_terms.reshape(2, width, -1))


def gram_of(left, right):
    width = left.shape[1]
    joined = lax.dot_general(
        left.reshape(2 * width, -1),
        right.reshape(2 * width, -1),
        (((1,), (1,)), ((), ())),
        precision=lax.Precision.HIGHEST,
        preferred_element_type=jnp.float32,
    )
    blocks = joined.reshape(2, width, 2, width)
    return jnp.stack([blocks[0, :, 0] + blocks[1, :, 1], blocks[0, :, 1] - blocks[1, :, 0]])


def split_grid(sources, potential, iter_counts):
    complex_src = jnp.stack([sources, jnp.zeros_like(sources)])
    angle_now = (
        2.0 * math.pi * (lax.axis_index("point").astype(jnp.float32) + 0.5) / lax.axis_size("point")
    )
    shift_re = GAMMA + RADIUS * jnp.cos(angle_now)
    shift_im = RADIUS * jnp.sin(angle_now)
    limit = iter_counts[0]
    solution = jnp.zeros_like(complex_src)

    def one_turn(turn_idx, state):
        solution, residual, search, norm_now = state
        product = shifted(search, potential, shift_re, shift_im)
        curve = lax.psum(bilinear(search, product), "dom")
        step_size = complex_div(norm_now, curve)
        new_residual = residual - scaled(step_size, product)
        norm_next = residual_sum(new_residual)
        fresh = (
            solution + scaled(step_size, search),
            new_residual,
            new_residual + scaled(complex_div(norm_next, norm_now), search),
            norm_next,
        )
        keep_mask = turn_idx < limit
        return jax.tree.map(lambda newer, older: jnp.where(keep_mask, newer, older), fresh, state)

    start = (solution, complex_src, complex_src, residual_sum(complex_src))
    solution, residual, search, norm_now = lax.fori_loop(0, ITERS, one_turn, start)
    s_terms, h_terms = moment_terms(solution, residual, complex_src, angle_now, shift_re, shift_im)
    cells = sources.shape[1] * sources.shape[2] * lax.axis_size("dom")
    s_total, h_total = lax.psum((s_terms, h_terms), "point")
    gram_b, gram_a = lax.psum((gram_of(s_total, s_total), gram_of(s_total, h_total)), "dom")
    return (gram_b / cells, gram_a / cells)


Y_IN, X_IN = 2, 4
Y_OUT, X_OUT = GX // Y_IN, GX // X_IN
ROWS = Y_IN * X_IN
LANES = Y_OUT * X_OUT
SUB = 8
BASIS = ITERS + 1
CORES = 2
H_SCALE = 2.0 / COEF_NEAR
FAR_SCALED = 0.5 * H_SCALE * COEF_FAR


def pack_kernel(depth, groups, counts, rows, out, tile):
    columns = rows.shape[0] // (SUB * groups * depth + depth)
    first_level = columns * SUB * groups * depth
    source = lax.broadcasted_iota(jnp.int32, (LANES, LANES), 0)
    target = lax.broadcasted_iota(jnp.int32, (LANES, LANES), 1)
    inner = target // (LANES // ROWS)
    outer = target % (LANES // ROWS)
    cell = (outer // X_OUT * Y_IN + inner // X_IN) * GX + outer % X_OUT * X_IN + inner % X_IN
    swap = jnp.where(source == cell, 1.0, 0.0).astype(jnp.float32)
    parts = []
    for deep in range(depth):
        for group in range(groups):
            for column in range(columns):
                start = (group * SUB * columns + column) * depth + deep
                parts.append(rows[pl.ds(start, SUB, stride=columns * depth), :])
        parts.append(rows[pl.ds(first_level + deep, columns, stride=depth), :])
    mixed = exact_dot(jnp.concatenate(parts, axis=0), swap, ((1,), (0,)))
    block = LANES // ROWS
    lane_block = lax.broadcasted_iota(jnp.int32, (SUB, LANES), 1) // block
    row = lax.broadcasted_iota(jnp.int32, (SUB, LANES), 0)
    for deep in range(depth):
        base = deep * (groups + 1) * columns * SUB - deep * (columns - 1) * SUB
        for group in range(groups):
            pieces = [
                mixed[base + (group * columns + column) * SUB :][:SUB] for column in range(columns)
            ]
            for m in range(ROWS):
                value = pieces[m]
                for column in range(columns):
                    if column != m:
                        moved = pltpu.roll(pieces[column], (column - m) * block % LANES, 1)
                        value = jnp.where(lane_block == column, moved, value)
                start = ((deep * ROWS + m) * groups + group) * SUB
                out[start : start + SUB, :] = value
        piece = mixed[base + groups * columns * SUB :][:SUB]
        value = piece
        for far in range(1, columns):
            moved = pltpu.roll(pltpu.roll(piece, far * block, 1), columns - far, 0)
            value = jnp.where(lane_block == (row + far) % columns, moved, value)
        start = depth * ROWS * SUB * groups + deep * ROWS
        out[start : start + ROWS, :] = value
    tile[...] = jnp.broadcast_to(counts[...].astype(jnp.float32), (SUB, LANES))


def packed_block(sources, potential, iter_counts):
    count, depth, cells = sources.shape
    columns = cells // LANES
    rows = sources.reshape(count, depth, columns, LANES).transpose(0, 2, 1, 3).reshape(-1, LANES)
    levels = potential.reshape(depth, columns, LANES).transpose(1, 0, 2).reshape(-1, LANES)
    vmem = pl.BlockSpec(memory_space=pltpu.VMEM)
    size = depth * ROWS * (count + 1)
    return pl.pallas_call(
        functools.partial(pack_kernel, depth, count // SUB),
        out_shape=(
            jax.ShapeDtypeStruct((size, LANES), jnp.float32),
            jax.ShapeDtypeStruct((SUB, LANES), jnp.float32),
        ),
        in_specs=[vmem, vmem],
        out_specs=(vmem, vmem),
        compiler_params=pltpu.CompilerParams(vmem_limit_bytes=4 * 2**20),
        name="pack",
    )(iter_counts.reshape(1, 1), jnp.concatenate([rows, levels], axis=0))


def lane_sum(values):
    return jnp.broadcast_to(jnp.sum(values, axis=1, keepdims=True), values.shape)


def ratio(top, bottom):
    return jnp.where(bottom > 0.0, top / jnp.where(bottom > 0.0, bottom, 1.0), 0.0)


def tree_sum(values):
    while len(values) > 1:
        values = [sum(values[i : i + 2][1:], values[i]) for i in range(0, len(values), 2)]
    return values[0]


def plane_rows(vector, plane, rows):
    return [vector[plane, rows, m * LANES : (m + 1) * LANES] for m in range(ROWS)]


def y_parts(here, last_x, first_x):
    y_up = [pltpu.roll(value, LANES - X_OUT, 1) for value in here]
    y_down = [pltpu.roll(value, X_OUT, 1) for value in here]
    sums, edges = [], []
    for m in range(ROWS):
        near = y_down[m + X_IN] if m < X_IN else y_up[m - X_IN]
        sums.append(near + FAR_SCALED * (y_up[m] + y_down[m]))
        if m % X_IN < 2:
            edges.append(jnp.where(first_x, y_down[m], here[m]))
        else:
            edges.append(jnp.where(last_x, y_up[m], here[m]))
    return sums, edges


def apply_plane(vector, sums, edges, diagonal, plane, rows):
    planes = vector.shape[0]
    halos = []
    for m, edge in enumerate(plane_rows(edges, plane, rows)):
        halos.append(pltpu.roll(edge, LANES - 1 if m % X_IN < 2 else 1, 1))
    here, above, below, above_2, below_2 = (
        plane_rows(vector, (plane + far) % planes, rows) for far in (0, 1, -1, 2, -2)
    )
    y_sums = plane_rows(sums, plane, rows)
    out = []
    for yi in range(Y_IN):
        first = yi * X_IN
        line, halo = here[first : first + X_IN], halos[first : first + X_IN]
        wide = halo[2:] + line + halo[:2]
        for xi in range(X_IN):
            m = first + xi
            other = m + X_IN if yi == 0 else m - X_IN
            near = here[other] + (above[m] + below[m])
            far = above_2[m] + below_2[m]
            near = near + (wide[xi + 1] + wide[xi + 3])
            far = far + (wide[xi] + wide[xi + 4])
            level = diagonal[plane, :, m * LANES : (m + 1) * LANES]
            out.append((level * here[m] - y_sums[m]) - near - FAR_SCALED * far)
    return here, out


def cmul(first, second):
    return (
        first[0] * second[0] - first[1] * second[1],
        first[0] * second[1] + first[1] * second[0],
    )


def picked(index, values):
    result = jnp.float32(values[0])
    for i, value in enumerate(values[1:], 1):
        result = jnp.where(index == i, jnp.float32(value), result)
    return result


def moment_coeffs(point, angles, count):
    lane = lax.broadcasted_iota(jnp.int32, (1, LANES), 1)
    moment = lax.rem(lane, MOMENTS * count) // count
    parts = []
    for func in (math.cos, math.sin):
        value = jnp.zeros((1, LANES), jnp.float32)
        for k in range(MOMENTS):
            coeff = picked(point, [0.25 * func((k + 1) * angle) for angle in angles])
            value = jnp.where(moment == k, coeff, value)
        parts.append(value)
    return parts


def weights_of(point, points, alphas, norms, limit):
    shape = alphas[0].shape
    count = shape[0]
    lane = lax.broadcasted_iota(jnp.int32, shape, 1)
    source = lax.broadcasted_iota(jnp.int32, shape, 0)
    own = lax.rem(lane, count) == source
    left_half = lane < MOMENTS * count
    betas = [ratio(norms[i + 1], norms[i]) for i in range(ITERS - 1)]
    zero = jnp.zeros(shape, jnp.float32)
    one = jnp.ones(shape, jnp.float32)
    angles = [2.0 * math.pi * (j + 0.5) / points for j in range(points)]
    shift = (
        picked(point, [GAMMA + RADIUS * math.cos(angle) for angle in angles]),
        picked(point, [RADIUS * math.sin(angle) for angle in angles]),
    )
    scaled_shift = (H_SCALE * shift[0], H_SCALE * shift[1])
    product = (one, zero)
    products = [product]
    links = []
    pivot = (scaled_shift[0] - alphas[0], zero + scaled_shift[1])
    for i in range(ITERS):
        size = 1.0 / (pivot[0] * pivot[0] + pivot[1] * pivot[1])
        inverse = (pivot[0] * size, -pivot[1] * size)
        product = cmul(product, inverse)
        products.append(product)
        if i < ITERS - 1:
            link = (betas[i] * inverse[0], betas[i] * inverse[1])
            links.append(link)
            pivot = (scaled_shift[0] - alphas[i + 1] - link[0], scaled_shift[1] - link[1])
    solved = [None] * ITERS
    for i in reversed(range(ITERS)):
        value = (H_SCALE * products[i + 1][0], H_SCALE * products[i + 1][1])
        if i < ITERS - 1:
            step = cmul(links[i], solved[i + 1])
            value = (value[0] + step[0], value[1] + step[1])
        used = limit > i
        solved[i] = (jnp.where(used, value[0], 0.0), jnp.where(used, value[1], 0.0))
    applied = []
    for i in range(BASIS):
        left = limit == i
        rest = (jnp.where(left, products[i][0], 0.0), jnp.where(left, products[i][1], 0.0))
        if i < ITERS:
            turned = cmul(shift, solved[i])
            rest = (rest[0] + turned[0], rest[1] + turned[1])
        if i == 0:
            rest = (rest[0] - 1.0, rest[1])
        applied.append(rest)
    tail = applied[ITERS]
    for back, factor in ((1, alphas[ITERS - 1]), (2, betas[ITERS - 2])):
        part = applied[ITERS - back]
        applied[ITERS - back] = (part[0] - factor * tail[0], part[1] - factor * tail[1])
    moment = moment_coeffs(point, angles, count)
    weights = []
    for i in range(BASIS):
        left = solved[i] if i < ITERS else (zero, zero)
        both = (
            jnp.where(left_half, left[0], applied[i][0]),
            jnp.where(left_half, left[1], applied[i][1]),
        )
        weights.append([jnp.where(own, part, 0.0) for part in cmul(moment, both)])
    return weights


def exact_dot(first, second, dims):
    return lax.dot_general(
        first,
        second,
        (dims, ((), ())),
        precision=lax.Precision.HIGHEST,
        preferred_element_type=jnp.float32,
    )


def krylov_kernel(parts, count, *refs):
    blocks, (vectors, applied, scalars) = refs[:parts], refs[parts : parts + 3]
    first_work, second_work, diagonal, sums, edges = refs[parts + 3 :]
    planes = diagonal.shape[0]
    depth = planes // parts
    groups = count // SUB
    lane = lax.broadcasted_iota(jnp.int32, (SUB, LANES), 1)
    last_x = lax.rem(lane, X_OUT) == X_OUT - 1
    first_x = lax.rem(lane, X_OUT) == 0
    here = lax.axis_index("dom")
    for turn in range(parts):
        slab = jnp.bitwise_xor(here, turn) * depth
        for deep in range(depth):
            for m in range(ROWS):
                start = (deep * ROWS + m) * count
                lanes = slice(m * LANES, (m + 1) * LANES)
                value = blocks[turn][start : start + count, :]
                first_work[slab + deep, :, lanes] = value
                vectors[0, slab + deep, :, lanes] = value
            start = depth * ROWS * count + deep * ROWS
            levels = H_SCALE * (blocks[turn][start : start + ROWS, :] + 3.75)
            for m in range(ROWS):
                level = jnp.broadcast_to(levels[m : m + 1, :], (SUB, LANES))
                diagonal[slab + deep, :, m * LANES : (m + 1) * LANES] = level
    second_work[...] = jnp.zeros_like(second_work)
    scalars[ITERS] = jnp.zeros((count, LANES), jnp.float32)

    all_rows = [pl.ds(group * SUB, SUB) for group in range(groups)]
    all_lanes = [slice(m * LANES, (m + 1) * LANES) for m in range(ROWS)]
    def keep_y_parts(plane, rows, values):
        for ref, parts_of in zip((sums, edges), y_parts(values, last_x, first_x)):
            for lanes, part in zip(all_lanes, parts_of):
                ref[plane, rows, lanes] = part

    for group, rows in enumerate(all_rows):
        norm = []
        for plane in range(planes):
            values = plane_rows(first_work, plane, rows)
            keep_y_parts(plane, rows, values)
            norm.append(tree_sum([value * value for value in values]))
        scalars[ITERS + 1, rows, :] = lane_sum(tree_sum(norm))

    def half_turn(i, work, before):
        curve = [[] for _ in range(groups)]
        for plane in range(planes):
            for group, rows in enumerate(all_rows):
                value, out = apply_plane(work, sums, edges, diagonal, plane, rows)
                for m, lanes in enumerate(all_lanes):
                    applied[plane, rows, lanes] = out[m]
                curve[group].append(tree_sum([value[m] * out[m] for m in range(ROWS)]))
        curves = [lane_sum(tree_sum(parts_of)) for parts_of in curve]
        alphas = []
        for group, rows in enumerate(all_rows):
            alphas.append(ratio(curves[group], scalars[ITERS + 1 + i, rows, :]))
            scalars[i, rows, :] = alphas[group]

        @pl.when(i < ITERS - 1)
        def _():
            norms = []
            for group, rows in enumerate(all_rows):
                beta = ratio(scalars[ITERS + 1 + i, rows, :], scalars[ITERS + i, rows, :])
                norm = []
                for plane in range(planes):
                    values = []
                    for lanes in all_lanes:
                        value = applied[plane, rows, lanes]
                        value = value - alphas[group] * work[plane, rows, lanes]
                        value = value - beta * before[plane, rows, lanes]
                        before[plane, rows, lanes] = value
                        vectors[i + 1, plane, rows, lanes] = value
                        values.append(value)
                    keep_y_parts(plane, rows, values)
                    norm.append(tree_sum([value * value for value in values]))
                norms.append(lane_sum(tree_sum(norm)))
            for group, rows in enumerate(all_rows):
                scalars[ITERS + 2 + i, rows, :] = norms[group]

    def turn(step, carry):
        half_turn(2 * step, first_work, second_work)
        half_turn(2 * step + 1, second_work, first_work)
        return carry

    lax.fori_loop(0, ITERS // 2, turn, 0)


def gram_kernel(points, scalars, *refs):
    tiles = refs[:points]
    archive, applied, out_b, out_a, gram, limits, weights = refs[points:]
    planes, count, _ = applied.shape
    groups = count // SUB
    size = BASIS * count
    here = lax.axis_index("point")
    core = jnp.bitwise_and(lax.axis_index("dom"), CORES - 1)
    for far, tile in zip((0, 1 + core, 3, 2 - core), tiles):
        limits[jnp.bitwise_xor(here, far)] = tile[...]
    gram[...] = jnp.zeros_like(gram)
    weights[...] = jnp.zeros_like(weights)

    def turn(point, carry):
        limit = jnp.concatenate([limits[point]] * groups, axis=0)
        alphas = [scalars[i] for i in range(ITERS)]
        norms = [scalars[ITERS + 1 + i] for i in range(ITERS)]
        total = None
        for deep in range(planes // points):
            plane = point * (planes // points) + deep
            values = [archive[i, plane] for i in range(ITERS)] + [applied[plane]]
            values = jnp.concatenate(values, axis=0)
            high = values.astype(jnp.bfloat16)
            low = (values - high.astype(jnp.float32)).astype(jnp.bfloat16)
            product = lax.dot_general(
                jnp.concatenate([high, low], axis=0),
                high,
                (((1,), (1,)), ((), ())),
                preferred_element_type=jnp.float32,
            )
            total = product if total is None else total + product
        gram[...] += total
        for i, pair in enumerate(weights_of(point, points, alphas, norms, limit)):
            for part, value in enumerate(pair):
                weights[i * count : (i + 1) * count, part * LANES : (part + 1) * LANES] += value
        return carry

    lax.fori_loop(0, points, turn, 0)
    cross = gram[size:, :]
    pairs = gram[:size, :] + cross + cross.T
    right = exact_dot(pairs, weights[...], ((1,), (0,)))
    real, imag = weights[:, :LANES], weights[:, LANES:]
    half = MOMENTS * count
    left = jnp.concatenate([real[:, :half], imag[:, :half]], axis=1)
    joined = exact_dot(left.T, right, ((1,), (0,)))
    scale = 1.0 / (planes * ROWS * LANES)
    width = 2 * half
    real = (joined[:half, :width] + joined[half:, width:]) * scale
    imag = (joined[:half, width:] - joined[half:, :width]) * scale
    out_b[0] = real[:, :half]
    out_b[1] = imag[:, :half]
    out_a[0] = real[:, half:]
    out_a[1] = imag[:, half:]


def swapped(values, axis, size, mask):
    return lax.ppermute(values, axis, [(index ^ mask, index) for index in range(size)])


def whole_grid(sources, potential, iter_counts, *, parts, points):
    count, depth, _ = sources.shape
    planes = parts * depth
    block, tile = packed_block(sources, potential, iter_counts)
    even = [block] + [swapped(block, "dom", parts, mask) for mask in range(CORES, parts, CORES)]
    mixed = [
        ((point ^ (1 + part % CORES)) * parts + part, point * parts + part)
        for point in range(points)
        for part in range(parts)
    ]
    tiles = [lax.ppermute(tile, ("point", "dom"), mixed), swapped(tile, "point", points, 3)]
    even[1], *tiles = lax.optimization_barrier((even[1], *tiles))
    tiles.append(swapped(tiles[0], "dom", parts, 1))
    odd = [swapped(value, "dom", parts, 1) for value in even]
    blocks = [value for pair in zip(even, odd) for value in pair]
    vmem = pl.BlockSpec(memory_space=pltpu.VMEM)
    vector = (planes, count, ROWS * LANES)
    cells = planes * ROWS * LANES
    vectors, applied, scalars = pl.pallas_call(
        functools.partial(krylov_kernel, parts, count),
        out_shape=(
            jax.ShapeDtypeStruct((ITERS,) + vector, jnp.float32),
            jax.ShapeDtypeStruct(vector, jnp.float32),
            jax.ShapeDtypeStruct((2 * ITERS + 1, count, LANES), jnp.float32),
        ),
        in_specs=[vmem] * parts,
        out_specs=(vmem,) * 3,
        scratch_shapes=[
            pltpu.VMEM(vector, jnp.float32),
            pltpu.VMEM(vector, jnp.float32),
            pltpu.VMEM((planes, SUB, ROWS * LANES), jnp.float32),
            pltpu.VMEM(vector, jnp.float32),
            pltpu.VMEM(vector, jnp.float32),
        ],
        compiler_params=pltpu.CompilerParams(vmem_limit_bytes=16 * 2**20),
        name="krylov",
    )(*blocks)
    size = BASIS * count
    width = MOMENTS * count
    out = jax.ShapeDtypeStruct((2, width, width), jnp.float32)
    return pl.pallas_call(
        functools.partial(gram_kernel, points),
        out_shape=(out, out),
        in_specs=[vmem] * (3 + points),
        out_specs=(vmem, vmem),
        scratch_shapes=[
            pltpu.VMEM((2 * size, size), jnp.float32),
            pltpu.VMEM((points, SUB, LANES), jnp.float32),
            pltpu.VMEM((size, 2 * LANES), jnp.float32),
        ],
        compiler_params=pltpu.CompilerParams(vmem_limit_bytes=16 * 2**20),
        name="gram",
    )(scalars, tile, *tiles, vectors, applied)


def on_device(sources, potential, iter_counts):
    parts, points = lax.axis_size("dom"), lax.axis_size("point")
    count, depth, cells = sources.shape
    held = BASIS * count * parts * depth * cells * 4
    fits = (
        held <= 16 * 2**20
        and parts == 8
        and points == 4
        and count == 2 * SUB
        and 2 * MOMENTS * count == LANES
        and parts * depth == 16
        and cells == GX * GX == ROWS * LANES
    )
    if not fits:
        return split_grid(sources, potential, iter_counts)
    return whole_grid(sources, potential, iter_counts, parts=parts, points=points)


def solution(mesh):
    placed = (P(None, "dom", None), P("dom", None), P("point"))
    return jax.shard_map(
        on_device, mesh=mesh, in_specs=placed, out_specs=(P(), P()), check_vma=False
    )
```

```python
import functools
import math

import jax
import jax.numpy as jnp
from jax import lax
from jax.experimental import pallas as pl
from jax.experimental.pallas import tpu as pltpu
from jax.sharding import PartitionSpec as P

MOMENTS = 4
ITERS = 6
GX = 32


COEF_NEAR = 4.0 / 3.0
COEF_FAR = -1.0 / 12.0
GAMMA = 2.0
RADIUS = 1.5


def padded_2(block, sides, width):
    for axis, dim in sides:
        count = lax.axis_size(axis)
        forward = [(i, i + 1) for i in range(count - 1)]
        forward.append((count - 1, 0))
        backward = [(target, source) for source, target in forward]
        low = lax.ppermute(
            lax.slice_in_dim(block, block.shape[dim] - width, None, axis=dim), axis, forward
        )
        high = lax.ppermute(lax.slice_in_dim(block, 0, width, axis=dim), axis, backward)
        block = jnp.concatenate([low, block, high], axis=dim)
    return block


def plane_terms(values, side):
    lead = values.shape[:-1]
    planes = values.reshape(lead + (side, side))
    summed = COEF_NEAR * (
        jnp.roll(planes, 1, -2)
        + jnp.roll(planes, -1, -2)
        + jnp.roll(planes, 1, -1)
        + jnp.roll(planes, -1, -1)
    )
    summed = summed + COEF_FAR * (
        jnp.roll(planes, 2, -2)
        + jnp.roll(planes, -2, -2)
        + jnp.roll(planes, 2, -1)
        + jnp.roll(planes, -2, -1)
    )
    return summed.reshape(values.shape)


def complex_mul(first, second):
    return jnp.stack(
        [first[0] * second[0] - first[1] * second[1], first[0] * second[1] + first[1] * second[0]]
    )


def complex_div(first, second):
    denom = second[0] * second[0] + second[1] * second[1]
    return jnp.stack(
        [
            (first[0] * second[0] + first[1] * second[1]) / denom,
            (first[1] * second[0] - first[0] * second[1]) / denom,
        ]
    )


def bilinear(first, second):
    real_part = jnp.sum(first[0] * second[0] - first[1] * second[1], axis=(1, 2))
    imag_part = jnp.sum(first[0] * second[1] + first[1] * second[0], axis=(1, 2))
    return jnp.stack([real_part, imag_part])


def scaled(coeffs, values):
    return complex_mul(coeffs[:, :, None, None], values)


def shifted(values, potential, shift_re, shift_im):
    padded = padded_2(values, (("dom", 2),), 2)
    depth = values.shape[2]
    lap = -7.5 * values + plane_terms(values, GX)
    lap = lap + COEF_NEAR * (padded[:, :, 3 : 3 + depth] + padded[:, :, 1 : 1 + depth])
    lap = lap + COEF_FAR * (padded[:, :, 4 : 4 + depth] + padded[:, :, 0:depth])
    applied = -0.5 * lap + potential * values
    return jnp.stack(
        [
            shift_re * values[0] - shift_im * values[1] - applied[0],
            shift_re * values[1] + shift_im * values[0] - applied[1],
        ]
    )


def residual_sum(values):
    return lax.psum(bilinear(values, values), "dom")


def moment_terms(solution, residual, sources, angle_now, shift_re, shift_im):
    applied = jnp.stack(
        [
            shift_re * solution[0] - shift_im * solution[1] - sources[0] + residual[0],
            shift_re * solution[1] + shift_im * solution[0] - sources[1] + residual[1],
        ]
    )
    angles = (jnp.arange(MOMENTS).astype(jnp.float32) + 1.0) * angle_now
    coeffs = 0.25 * jnp.stack([jnp.cos(angles), jnp.sin(angles)])
    s_terms = complex_mul(coeffs[:, :, None, None, None], solution[:, None])
    h_terms = complex_mul(coeffs[:, :, None, None, None], applied[:, None])
    width = MOMENTS * solution.shape[1]
    return (s_terms.reshape(2, width, -1), h_terms.reshape(2, width, -1))


def gram_of(left, right):
    width = left.shape[1]
    joined = lax.dot_general(
        left.reshape(2 * width, -1),
        right.reshape(2 * width, -1),
        (((1,), (1,)), ((), ())),
        precision=lax.Precision.HIGHEST,
        preferred_element_type=jnp.float32,
    )
    blocks = joined.reshape(2, width, 2, width)
    return jnp.stack([blocks[0, :, 0] + blocks[1, :, 1], blocks[0, :, 1] - blocks[1, :, 0]])


def split_grid(sources, potential, iter_counts):
    complex_src = jnp.stack([sources, jnp.zeros_like(sources)])
    angle_now = (
        2.0 * math.pi * (lax.axis_index("point").astype(jnp.float32) + 0.5) / lax.axis_size("point")
    )
    shift_re = GAMMA + RADIUS * jnp.cos(angle_now)
    shift_im = RADIUS * jnp.sin(angle_now)
    limit = iter_counts[0]
    solution = jnp.zeros_like(complex_src)

    def one_turn(turn_idx, state):
        solution, residual, search, norm_now = state
        product = shifted(search, potential, shift_re, shift_im)
        curve = lax.psum(bilinear(search, product), "dom")
        step_size = complex_div(norm_now, curve)
        new_residual = residual - scaled(step_size, product)
        norm_next = residual_sum(new_residual)
        fresh = (
            solution + scaled(step_size, search),
            new_residual,
            new_residual + scaled(complex_div(norm_next, norm_now), search),
            norm_next,
        )
        keep_mask = turn_idx < limit
        return jax.tree.map(lambda newer, older: jnp.where(keep_mask, newer, older), fresh, state)

    start = (solution, complex_src, complex_src, residual_sum(complex_src))
    solution, residual, search, norm_now = lax.fori_loop(0, ITERS, one_turn, start)
    s_terms, h_terms = moment_terms(solution, residual, complex_src, angle_now, shift_re, shift_im)
    cells = sources.shape[1] * sources.shape[2] * lax.axis_size("dom")
    s_total, h_total = lax.psum((s_terms, h_terms), "point")
    gram_b, gram_a = lax.psum((gram_of(s_total, s_total), gram_of(s_total, h_total)), "dom")
    return (gram_b / cells, gram_a / cells)


Y_IN, X_IN = 2, 4
Y_OUT, X_OUT = GX // Y_IN, GX // X_IN
ROWS = Y_IN * X_IN
LANES = Y_OUT * X_OUT
SUB = 8
BASIS = ITERS + 1
CORES = 2
H_SCALE = 2.0 / COEF_NEAR
FAR_SCALED = 0.5 * H_SCALE * COEF_FAR


def pack_kernel(depth, groups, counts, rows, out, tile):
    columns = rows.shape[0] // (SUB * groups * depth + depth)
    first_level = columns * SUB * groups * depth
    source = lax.broadcasted_iota(jnp.int32, (LANES, LANES), 0)
    target = lax.broadcasted_iota(jnp.int32, (LANES, LANES), 1)
    inner = target // (LANES // ROWS)
    outer = target % (LANES // ROWS)
    cell = (outer // X_OUT * Y_IN + inner // X_IN) * GX + outer % X_OUT * X_IN + inner % X_IN
    swap = jnp.where(source == cell, 1.0, 0.0).astype(jnp.float32)
    parts = []
    for deep in range(depth):
        for group in range(groups):
            for column in range(columns):
                start = (group * SUB * columns + column) * depth + deep
                parts.append(rows[pl.ds(start, SUB, stride=columns * depth), :])
        parts.append(rows[pl.ds(first_level + deep, columns, stride=depth), :])
    mixed = exact_dot(jnp.concatenate(parts, axis=0), swap, ((1,), (0,)))
    block = LANES // ROWS
    lane_block = lax.broadcasted_iota(jnp.int32, (SUB, LANES), 1) // block
    row = lax.broadcasted_iota(jnp.int32, (SUB, LANES), 0)
    for deep in range(depth):
        base = deep * (groups + 1) * columns * SUB - deep * (columns - 1) * SUB
        for group in range(groups):
            pieces = [
                mixed[base + (group * columns + column) * SUB :][:SUB] for column in range(columns)
            ]
            for m in range(ROWS):
                value = pieces[m]
                for column in range(columns):
                    if column != m:
                        moved = pltpu.roll(pieces[column], (column - m) * block % LANES, 1)
                        value = jnp.where(lane_block == column, moved, value)
                start = ((deep * ROWS + m) * groups + group) * SUB
                out[start : start + SUB, :] = value
        piece = mixed[base + groups * columns * SUB :][:SUB]
        value = piece
        for far in range(1, columns):
            moved = pltpu.roll(pltpu.roll(piece, far * block, 1), columns - far, 0)
            value = jnp.where(lane_block == (row + far) % columns, moved, value)
        start = depth * ROWS * SUB * groups + deep * ROWS
        out[start : start + ROWS, :] = value
    tile[...] = jnp.broadcast_to(counts[...].astype(jnp.float32), (SUB, LANES))


def packed_block(sources, potential, iter_counts):
    count, depth, cells = sources.shape
    columns = cells // LANES
    rows = sources.reshape(count, depth, columns, LANES).transpose(0, 2, 1, 3).reshape(-1, LANES)
    levels = potential.reshape(depth, columns, LANES).transpose(1, 0, 2).reshape(-1, LANES)
    vmem = pl.BlockSpec(memory_space=pltpu.VMEM)
    size = depth * ROWS * (count + 1)
    return pl.pallas_call(
        functools.partial(pack_kernel, depth, count // SUB),
        out_shape=(
            jax.ShapeDtypeStruct((size, LANES), jnp.float32),
            jax.ShapeDtypeStruct((SUB, LANES), jnp.float32),
        ),
        in_specs=[vmem, vmem],
        out_specs=(vmem, vmem),
        compiler_params=pltpu.CompilerParams(vmem_limit_bytes=4 * 2**20),
        name="pack",
    )(iter_counts.reshape(1, 1), jnp.concatenate([rows, levels], axis=0))


def lane_sum(values):
    return jnp.broadcast_to(jnp.sum(values, axis=1, keepdims=True), values.shape)


def ratio(top, bottom):
    return jnp.where(bottom > 0.0, top / jnp.where(bottom > 0.0, bottom, 1.0), 0.0)


def tree_sum(values):
    while len(values) > 1:
        values = [sum(values[i : i + 2][1:], values[i]) for i in range(0, len(values), 2)]
    return values[0]


def plane_rows(vector, plane, rows):
    return [vector[plane, rows, m * LANES : (m + 1) * LANES] for m in range(ROWS)]


def y_parts(here, last_x, first_x):
    y_up = [pltpu.roll(value, LANES - X_OUT, 1) for value in here]
    y_down = [pltpu.roll(value, X_OUT, 1) for value in here]
    sums, edges = [], []
    for m in range(ROWS):
        near = y_down[m + X_IN] if m < X_IN else y_up[m - X_IN]
        sums.append(near + FAR_SCALED * (y_up[m] + y_down[m]))
        if m % X_IN < 2:
            edges.append(jnp.where(first_x, y_down[m], here[m]))
        else:
            edges.append(jnp.where(last_x, y_up[m], here[m]))
    return sums, edges


def apply_plane(vector, sums, edges, diagonal, plane, rows):
    planes = vector.shape[0]
    halos = []
    for m, edge in enumerate(plane_rows(edges, plane, rows)):
        halos.append(pltpu.roll(edge, LANES - 1 if m % X_IN < 2 else 1, 1))
    here, above, below, above_2, below_2 = (
        plane_rows(vector, (plane + far) % planes, rows) for far in (0, 1, -1, 2, -2)
    )
    y_sums = plane_rows(sums, plane, rows)
    out = []
    for yi in range(Y_IN):
        first = yi * X_IN
        line, halo = here[first : first + X_IN], halos[first : first + X_IN]
        wide = halo[2:] + line + halo[:2]
        for xi in range(X_IN):
            m = first + xi
            other = m + X_IN if yi == 0 else m - X_IN
            near = here[other] + (above[m] + below[m])
            far = above_2[m] + below_2[m]
            near = near + (wide[xi + 1] + wide[xi + 3])
            far = far + (wide[xi] + wide[xi + 4])
            level = diagonal[plane, :, m * LANES : (m + 1) * LANES]
            out.append((level * here[m] - y_sums[m]) - near - FAR_SCALED * far)
    return here, out


def cmul(first, second):
    return (
        first[0] * second[0] - first[1] * second[1],
        first[0] * second[1] + first[1] * second[0],
    )


def picked(index, values):
    result = jnp.float32(values[0])
    for i, value in enumerate(values[1:], 1):
        result = jnp.where(index == i, jnp.float32(value), result)
    return result


def moment_coeffs(point, angles, count):
    lane = lax.broadcasted_iota(jnp.int32, (1, LANES), 1)
    moment = lax.rem(lane, MOMENTS * count) // count
    parts = []
    for func in (math.cos, math.sin):
        value = jnp.zeros((1, LANES), jnp.float32)
        for k in range(MOMENTS):
            coeff = picked(point, [0.25 * func((k + 1) * angle) for angle in angles])
            value = jnp.where(moment == k, coeff, value)
        parts.append(value)
    return parts


def weights_of(point, points, alphas, norms, limit):
    shape = alphas[0].shape
    count = shape[0]
    lane = lax.broadcasted_iota(jnp.int32, shape, 1)
    source = lax.broadcasted_iota(jnp.int32, shape, 0)
    own = lax.rem(lane, count) == source
    left_half = lane < MOMENTS * count
    betas = [ratio(norms[i + 1], norms[i]) for i in range(ITERS - 1)]
    zero = jnp.zeros(shape, jnp.float32)
    one = jnp.ones(shape, jnp.float32)
    angles = [2.0 * math.pi * (j + 0.5) / points for j in range(points)]
    shift = (
        picked(point, [GAMMA + RADIUS * math.cos(angle) for angle in angles]),
        picked(point, [RADIUS * math.sin(angle) for angle in angles]),
    )
    scaled_shift = (H_SCALE * shift[0], H_SCALE * shift[1])
    product = (one, zero)
    products = [product]
    links = []
    pivot = (scaled_shift[0] - alphas[0], zero + scaled_shift[1])
    for i in range(ITERS):
        size = 1.0 / (pivot[0] * pivot[0] + pivot[1] * pivot[1])
        inverse = (pivot[0] * size, -pivot[1] * size)
        product = cmul(product, inverse)
        products.append(product)
        if i < ITERS - 1:
            link = (betas[i] * inverse[0], betas[i] * inverse[1])
            links.append(link)
            pivot = (scaled_shift[0] - alphas[i + 1] - link[0], scaled_shift[1] - link[1])
    solved = [None] * ITERS
    for i in reversed(range(ITERS)):
        value = (H_SCALE * products[i + 1][0], H_SCALE * products[i + 1][1])
        if i < ITERS - 1:
            step = cmul(links[i], solved[i + 1])
            value = (value[0] + step[0], value[1] + step[1])
        used = limit > i
        solved[i] = (jnp.where(used, value[0], 0.0), jnp.where(used, value[1], 0.0))
    applied = []
    for i in range(BASIS):
        left = limit == i
        rest = (jnp.where(left, products[i][0], 0.0), jnp.where(left, products[i][1], 0.0))
        if i < ITERS:
            turned = cmul(shift, solved[i])
            rest = (rest[0] + turned[0], rest[1] + turned[1])
        if i == 0:
            rest = (rest[0] - 1.0, rest[1])
        applied.append(rest)
    tail = applied[ITERS]
    for back, factor in ((1, alphas[ITERS - 1]), (2, betas[ITERS - 2])):
        part = applied[ITERS - back]
        applied[ITERS - back] = (part[0] - factor * tail[0], part[1] - factor * tail[1])
    moment = moment_coeffs(point, angles, count)
    weights = []
    for i in range(BASIS):
        left = solved[i] if i < ITERS else (zero, zero)
        both = (
            jnp.where(left_half, left[0], applied[i][0]),
            jnp.where(left_half, left[1], applied[i][1]),
        )
        weights.append([jnp.where(own, part, 0.0) for part in cmul(moment, both)])
    return weights


def exact_dot(first, second, dims):
    return lax.dot_general(
        first,
        second,
        (dims, ((), ())),
        precision=lax.Precision.HIGHEST,
        preferred_element_type=jnp.float32,
    )


def split(values):
    high = values.astype(jnp.bfloat16)
    return high, (values - high.astype(jnp.float32)).astype(jnp.bfloat16)


def krylov_kernel(parts, count, *refs):
    blocks, (highs, lows, applied, scalars) = refs[:parts], refs[parts : parts + 4]
    first_work, second_work, diagonal, sums, edges, partial = refs[parts + 4 :]
    planes = diagonal.shape[0]
    depth = planes // parts
    groups = count // SUB
    lane = lax.broadcasted_iota(jnp.int32, (SUB, LANES), 1)
    last_x = lax.rem(lane, X_OUT) == X_OUT - 1
    first_x = lax.rem(lane, X_OUT) == 0
    here = lax.axis_index("dom")
    for turn in range(parts):
        slab = jnp.bitwise_xor(here, turn) * depth
        for deep in range(depth):
            for m in range(ROWS):
                start = (deep * ROWS + m) * count
                lanes = slice(m * LANES, (m + 1) * LANES)
                value = blocks[turn][start : start + count, :]
                first_work[slab + deep, :, lanes] = value
                highs[0, slab + deep, :, lanes], lows[0, slab + deep, :, lanes] = split(value)
            start = depth * ROWS * count + deep * ROWS
            levels = H_SCALE * (blocks[turn][start : start + ROWS, :] + 3.75)
            for m in range(ROWS):
                level = jnp.broadcast_to(levels[m : m + 1, :], (SUB, LANES))
                diagonal[slab + deep, :, m * LANES : (m + 1) * LANES] = level
    second_work[...] = jnp.zeros_like(second_work)
    scalars[ITERS] = jnp.zeros((count, LANES), jnp.float32)

    all_rows = [pl.ds(group * SUB, SUB) for group in range(groups)]
    all_lanes = [slice(m * LANES, (m + 1) * LANES) for m in range(ROWS)]
    def keep_y_parts(plane, rows, values):
        for ref, parts_of in zip((sums, edges), y_parts(values, last_x, first_x)):
            for lanes, part in zip(all_lanes, parts_of):
                ref[plane, rows, lanes] = part

    for group, rows in enumerate(all_rows):
        norm = []
        for plane in range(planes):
            values = plane_rows(first_work, plane, rows)
            keep_y_parts(plane, rows, values)
            norm.append(tree_sum([value * value for value in values]))
        partial[rows, :] = tree_sum(norm)

    def update_pass(i, work, before, alphas, betas):
        norm = [[] for _ in range(groups)]
        for plane in range(planes):
            columns = []
            for group, rows in enumerate(all_rows):
                values = []
                for lanes in all_lanes:
                    value = applied[plane, rows, lanes] - betas[group] * before[plane, rows, lanes]
                    value = value - alphas[group] * work[plane, rows, lanes]
                    before[plane, rows, lanes] = value
                    values.append(value)
                keep_y_parts(plane, rows, values)
                norm[group].append(tree_sum([value * value for value in values]))
                columns.append(values)
            for lanes, *column in zip(all_lanes, *columns):
                high, low = split(jnp.concatenate(column, axis=0))
                highs[i + 1, plane, :, lanes] = high
                lows[i + 1, plane, :, lanes] = low
        for rows, terms in zip(all_rows, norm):
            partial[rows, :] = tree_sum(terms)

    def half_turn(i, work, before, may_end):
        norms = [lane_sum(partial[rows, :]) for rows in all_rows]
        betas = [
            ratio(norm, scalars[ITERS + i, rows, :]) for norm, rows in zip(norms, all_rows)
        ]
        inverses = [ratio(jnp.ones_like(norm), norm) for norm in norms]
        for norm, rows in zip(norms, all_rows):
            scalars[ITERS + 1 + i, rows, :] = norm
        curve = [[] for _ in range(groups)]
        for plane in range(planes):
            for group, rows in enumerate(all_rows):
                value, out = apply_plane(work, sums, edges, diagonal, plane, rows)
                for m, lanes in enumerate(all_lanes):
                    applied[plane, rows, lanes] = out[m]
                curve[group].append(tree_sum([value[m] * out[m] for m in range(ROWS)]))
        alphas = [lane_sum(tree_sum(curve[g])) * inverses[g] for g in range(groups)]
        for alpha, rows in zip(alphas, all_rows):
            scalars[i, rows, :] = alpha
        if may_end:
            pl.when(i < ITERS - 1)(lambda: update_pass(i, work, before, alphas, betas))
        else:
            update_pass(i, work, before, alphas, betas)

    def turn(step, carry):
        half_turn(2 * step, first_work, second_work, False)
        half_turn(2 * step + 1, second_work, first_work, True)
        return carry

    lax.fori_loop(0, ITERS // 2, turn, 0)


def gram_kernel(points, scalars, *refs):
    tiles = refs[:points]
    highs, lows, applied, out_b, out_a, gram, limits, weights = refs[points:]
    planes, count, _ = applied.shape
    groups = count // SUB
    size = BASIS * count
    here = lax.axis_index("point")
    core = jnp.bitwise_and(lax.axis_index("dom"), CORES - 1)
    for far, tile in zip((0, 1 + core, 3, 2 - core), tiles):
        limits[jnp.bitwise_xor(here, far)] = tile[...]
    gram[...] = jnp.zeros_like(gram)
    weights[...] = jnp.zeros_like(weights)

    def turn(point, carry):
        limit = jnp.concatenate([limits[point]] * groups, axis=0)
        alphas = [scalars[i] for i in range(ITERS)]
        norms = [scalars[ITERS + 1 + i] for i in range(ITERS)]
        total = None
        for deep in range(planes // points):
            plane = point * (planes // points) + deep
            last_high, last_low = split(applied[plane])
            high = jnp.concatenate([highs[i, plane] for i in range(ITERS)] + [last_high], axis=0)
            low = jnp.concatenate([lows[i, plane] for i in range(ITERS)] + [last_low], axis=0)
            product = lax.dot_general(
                jnp.concatenate([high, low], axis=0),
                high,
                (((1,), (1,)), ((), ())),
                preferred_element_type=jnp.float32,
            )
            total = product if total is None else total + product
        gram[...] += total
        for i, pair in enumerate(weights_of(point, points, alphas, norms, limit)):
            for part, value in enumerate(pair):
                weights[i * count : (i + 1) * count, part * LANES : (part + 1) * LANES] += value
        return carry

    lax.fori_loop(0, points, turn, 0)
    cross = gram[size:, :]
    pairs = gram[:size, :] + cross + cross.T
    right = exact_dot(pairs, weights[...], ((1,), (0,)))
    real, imag = weights[:, :LANES], weights[:, LANES:]
    half = MOMENTS * count
    left = jnp.concatenate([real[:, :half], imag[:, :half]], axis=1)
    joined = exact_dot(left.T, right, ((1,), (0,)))
    scale = 1.0 / (planes * ROWS * LANES)
    width = 2 * half
    real = (joined[:half, :width] + joined[half:, width:]) * scale
    imag = (joined[:half, width:] - joined[half:, :width]) * scale
    out_b[0] = real[:, :half]
    out_b[1] = imag[:, :half]
    out_a[0] = real[:, half:]
    out_a[1] = imag[:, half:]


def swapped(values, axis, size, mask):
    return lax.ppermute(values, axis, [(index ^ mask, index) for index in range(size)])


def whole_grid(sources, potential, iter_counts, *, parts, points):
    count, depth, _ = sources.shape
    planes = parts * depth
    block, tile = packed_block(sources, potential, iter_counts)
    even = [block] + [swapped(block, "dom", parts, mask) for mask in range(CORES, parts, CORES)]
    mixed = [
        ((point ^ (1 + part % CORES)) * parts + part, point * parts + part)
        for point in range(points)
        for part in range(parts)
    ]
    tiles = [lax.ppermute(tile, ("point", "dom"), mixed), swapped(tile, "point", points, 3)]
    even[1], *tiles = lax.optimization_barrier((even[1], *tiles))
    tiles.append(swapped(tiles[0], "dom", parts, 1))
    odd = [swapped(value, "dom", parts, 1) for value in even]
    blocks = [value for pair in zip(even, odd) for value in pair]
    vmem = pl.BlockSpec(memory_space=pltpu.VMEM)
    vector = (planes, count, ROWS * LANES)
    cells = planes * ROWS * LANES
    highs, lows, applied, scalars = pl.pallas_call(
        functools.partial(krylov_kernel, parts, count),
        out_shape=(
            jax.ShapeDtypeStruct((ITERS,) + vector, jnp.bfloat16),
            jax.ShapeDtypeStruct((ITERS,) + vector, jnp.bfloat16),
            jax.ShapeDtypeStruct(vector, jnp.float32),
            jax.ShapeDtypeStruct((2 * ITERS + 1, count, LANES), jnp.float32),
        ),
        in_specs=[vmem] * parts,
        out_specs=(vmem,) * 4,
        scratch_shapes=[
            pltpu.VMEM(vector, jnp.float32),
            pltpu.VMEM(vector, jnp.float32),
            pltpu.VMEM((planes, SUB, ROWS * LANES), jnp.float32),
            pltpu.VMEM(vector, jnp.float32),
            pltpu.VMEM(vector, jnp.float32),
            pltpu.VMEM((count, LANES), jnp.float32),
        ],
        compiler_params=pltpu.CompilerParams(vmem_limit_bytes=16 * 2**20),
        name="krylov",
    )(*blocks)
    size = BASIS * count
    width = MOMENTS * count
    out = jax.ShapeDtypeStruct((2, width, width), jnp.float32)
    return pl.pallas_call(
        functools.partial(gram_kernel, points),
        out_shape=(out, out),
        in_specs=[vmem] * (4 + points),
        out_specs=(vmem, vmem),
        scratch_shapes=[
            pltpu.VMEM((2 * size, size), jnp.float32),
            pltpu.VMEM((points, SUB, LANES), jnp.float32),
            pltpu.VMEM((size, 2 * LANES), jnp.float32),
        ],
        compiler_params=pltpu.CompilerParams(vmem_limit_bytes=16 * 2**20),
        name="gram",
    )(scalars, tile, *tiles, highs, lows, applied)


def on_device(sources, potential, iter_counts):
    parts, points = lax.axis_size("dom"), lax.axis_size("point")
    count, depth, cells = sources.shape
    held = BASIS * count * parts * depth * cells * 4
    fits = (
        held <= 16 * 2**20
        and parts == 8
        and points == 4
        and count == 2 * SUB
        and 2 * MOMENTS * count == LANES
        and parts * depth == 16
        and cells == GX * GX == ROWS * LANES
    )
    if not fits:
        return split_grid(sources, potential, iter_counts)
    return whole_grid(sources, potential, iter_counts, parts=parts, points=points)


def solution(mesh):
    placed = (P(None, "dom", None), P("dom", None), P("point"))
    return jax.shard_map(
        on_device, mesh=mesh, in_specs=placed, out_specs=(P(), P()), check_vma=False
    )
```

```python
import functools
import math

import jax
import jax.numpy as jnp
from jax import lax
from jax.experimental import pallas as pl
from jax.experimental.pallas import tpu as pltpu
from jax.sharding import PartitionSpec as P

MOMENTS = 4
ITERS = 6
GX = 32


COEF_NEAR = 4.0 / 3.0
COEF_FAR = -1.0 / 12.0
GAMMA = 2.0
RADIUS = 1.5


def padded_2(block, sides, width):
    for axis, dim in sides:
        count = lax.axis_size(axis)
        forward = [(i, i + 1) for i in range(count - 1)]
        forward.append((count - 1, 0))
        backward = [(target, source) for source, target in forward]
        low = lax.ppermute(
            lax.slice_in_dim(block, block.shape[dim] - width, None, axis=dim), axis, forward
        )
        high = lax.ppermute(lax.slice_in_dim(block, 0, width, axis=dim), axis, backward)
        block = jnp.concatenate([low, block, high], axis=dim)
    return block


def plane_terms(values, side):
    lead = values.shape[:-1]
    planes = values.reshape(lead + (side, side))
    summed = COEF_NEAR * (
        jnp.roll(planes, 1, -2)
        + jnp.roll(planes, -1, -2)
        + jnp.roll(planes, 1, -1)
        + jnp.roll(planes, -1, -1)
    )
    summed = summed + COEF_FAR * (
        jnp.roll(planes, 2, -2)
        + jnp.roll(planes, -2, -2)
        + jnp.roll(planes, 2, -1)
        + jnp.roll(planes, -2, -1)
    )
    return summed.reshape(values.shape)


def complex_mul(first, second):
    return jnp.stack(
        [first[0] * second[0] - first[1] * second[1], first[0] * second[1] + first[1] * second[0]]
    )


def complex_div(first, second):
    denom = second[0] * second[0] + second[1] * second[1]
    return jnp.stack(
        [
            (first[0] * second[0] + first[1] * second[1]) / denom,
            (first[1] * second[0] - first[0] * second[1]) / denom,
        ]
    )


def bilinear(first, second):
    real_part = jnp.sum(first[0] * second[0] - first[1] * second[1], axis=(1, 2))
    imag_part = jnp.sum(first[0] * second[1] + first[1] * second[0], axis=(1, 2))
    return jnp.stack([real_part, imag_part])


def scaled(coeffs, values):
    return complex_mul(coeffs[:, :, None, None], values)


def shifted(values, potential, shift_re, shift_im):
    padded = padded_2(values, (("dom", 2),), 2)
    depth = values.shape[2]
    lap = -7.5 * values + plane_terms(values, GX)
    lap = lap + COEF_NEAR * (padded[:, :, 3 : 3 + depth] + padded[:, :, 1 : 1 + depth])
    lap = lap + COEF_FAR * (padded[:, :, 4 : 4 + depth] + padded[:, :, 0:depth])
    applied = -0.5 * lap + potential * values
    return jnp.stack(
        [
            shift_re * values[0] - shift_im * values[1] - applied[0],
            shift_re * values[1] + shift_im * values[0] - applied[1],
        ]
    )


def residual_sum(values):
    return lax.psum(bilinear(values, values), "dom")


def moment_terms(solution, residual, sources, angle_now, shift_re, shift_im):
    applied = jnp.stack(
        [
            shift_re * solution[0] - shift_im * solution[1] - sources[0] + residual[0],
            shift_re * solution[1] + shift_im * solution[0] - sources[1] + residual[1],
        ]
    )
    angles = (jnp.arange(MOMENTS).astype(jnp.float32) + 1.0) * angle_now
    coeffs = 0.25 * jnp.stack([jnp.cos(angles), jnp.sin(angles)])
    s_terms = complex_mul(coeffs[:, :, None, None, None], solution[:, None])
    h_terms = complex_mul(coeffs[:, :, None, None, None], applied[:, None])
    width = MOMENTS * solution.shape[1]
    return (s_terms.reshape(2, width, -1), h_terms.reshape(2, width, -1))


def gram_of(left, right):
    width = left.shape[1]
    joined = lax.dot_general(
        left.reshape(2 * width, -1),
        right.reshape(2 * width, -1),
        (((1,), (1,)), ((), ())),
        precision=lax.Precision.HIGHEST,
        preferred_element_type=jnp.float32,
    )
    blocks = joined.reshape(2, width, 2, width)
    return jnp.stack([blocks[0, :, 0] + blocks[1, :, 1], blocks[0, :, 1] - blocks[1, :, 0]])


def split_grid(sources, potential, iter_counts):
    complex_src = jnp.stack([sources, jnp.zeros_like(sources)])
    angle_now = (
        2.0 * math.pi * (lax.axis_index("point").astype(jnp.float32) + 0.5) / lax.axis_size("point")
    )
    shift_re = GAMMA + RADIUS * jnp.cos(angle_now)
    shift_im = RADIUS * jnp.sin(angle_now)
    limit = iter_counts[0]
    solution = jnp.zeros_like(complex_src)

    def one_turn(turn_idx, state):
        solution, residual, search, norm_now = state
        product = shifted(search, potential, shift_re, shift_im)
        curve = lax.psum(bilinear(search, product), "dom")
        step_size = complex_div(norm_now, curve)
        new_residual = residual - scaled(step_size, product)
        norm_next = residual_sum(new_residual)
        fresh = (
            solution + scaled(step_size, search),
            new_residual,
            new_residual + scaled(complex_div(norm_next, norm_now), search),
            norm_next,
        )
        keep_mask = turn_idx < limit
        return jax.tree.map(lambda newer, older: jnp.where(keep_mask, newer, older), fresh, state)

    start = (solution, complex_src, complex_src, residual_sum(complex_src))
    solution, residual, search, norm_now = lax.fori_loop(0, ITERS, one_turn, start)
    s_terms, h_terms = moment_terms(solution, residual, complex_src, angle_now, shift_re, shift_im)
    cells = sources.shape[1] * sources.shape[2] * lax.axis_size("dom")
    s_total, h_total = lax.psum((s_terms, h_terms), "point")
    gram_b, gram_a = lax.psum((gram_of(s_total, s_total), gram_of(s_total, h_total)), "dom")
    return (gram_b / cells, gram_a / cells)


Y_IN, X_IN = 2, 4
Y_OUT, X_OUT = GX // Y_IN, GX // X_IN
ROWS = Y_IN * X_IN
LANES = Y_OUT * X_OUT
SUB = 8
BASIS = ITERS + 1
CORES = 2
H_SCALE = 2.0 / COEF_NEAR
FAR_SCALED = 0.5 * H_SCALE * COEF_FAR


def pack_kernel(depth, groups, counts, rows, out, tile):
    columns = rows.shape[0] // (SUB * groups * depth + depth)
    first_level = columns * SUB * groups * depth
    source = lax.broadcasted_iota(jnp.int32, (LANES, LANES), 0)
    target = lax.broadcasted_iota(jnp.int32, (LANES, LANES), 1)
    inner = target // (LANES // ROWS)
    outer = target % (LANES // ROWS)
    cell = (outer // X_OUT * Y_IN + inner // X_IN) * GX + outer % X_OUT * X_IN + inner % X_IN
    swap = jnp.where(source == cell, 1.0, 0.0).astype(jnp.float32)
    parts = []
    for deep in range(depth):
        for group in range(groups):
            for column in range(columns):
                start = (group * SUB * columns + column) * depth + deep
                parts.append(rows[pl.ds(start, SUB, stride=columns * depth), :])
        parts.append(rows[pl.ds(first_level + deep, columns, stride=depth), :])
    mixed = exact_dot(jnp.concatenate(parts, axis=0), swap, ((1,), (0,)))
    block = LANES // ROWS
    lane_block = lax.broadcasted_iota(jnp.int32, (SUB, LANES), 1) // block
    row = lax.broadcasted_iota(jnp.int32, (SUB, LANES), 0)
    for deep in range(depth):
        base = deep * (groups + 1) * columns * SUB - deep * (columns - 1) * SUB
        for group in range(groups):
            pieces = [
                mixed[base + (group * columns + column) * SUB :][:SUB] for column in range(columns)
            ]
            for m in range(ROWS):
                value = pieces[m]
                for column in range(columns):
                    if column != m:
                        moved = pltpu.roll(pieces[column], (column - m) * block % LANES, 1)
                        value = jnp.where(lane_block == column, moved, value)
                start = ((deep * ROWS + m) * groups + group) * SUB
                out[start : start + SUB, :] = value
        piece = mixed[base + groups * columns * SUB :][:SUB]
        value = piece
        for far in range(1, columns):
            moved = pltpu.roll(pltpu.roll(piece, far * block, 1), columns - far, 0)
            value = jnp.where(lane_block == (row + far) % columns, moved, value)
        start = depth * ROWS * SUB * groups + deep * ROWS
        out[start : start + ROWS, :] = value
    tile[...] = jnp.broadcast_to(counts[...].astype(jnp.float32), (SUB, LANES))


def packed_block(sources, potential, iter_counts):
    count, depth, cells = sources.shape
    columns = cells // LANES
    rows = sources.reshape(count, depth, columns, LANES).transpose(0, 2, 1, 3).reshape(-1, LANES)
    levels = potential.reshape(depth, columns, LANES).transpose(1, 0, 2).reshape(-1, LANES)
    vmem = pl.BlockSpec(memory_space=pltpu.VMEM)
    size = depth * ROWS * (count + 1)
    return pl.pallas_call(
        functools.partial(pack_kernel, depth, count // SUB),
        out_shape=(
            jax.ShapeDtypeStruct((size, LANES), jnp.float32),
            jax.ShapeDtypeStruct((SUB, LANES), jnp.float32),
        ),
        in_specs=[vmem, vmem],
        out_specs=(vmem, vmem),
        compiler_params=pltpu.CompilerParams(vmem_limit_bytes=4 * 2**20),
        name="pack",
    )(iter_counts.reshape(1, 1), jnp.concatenate([rows, levels], axis=0))


def lane_sum(values):
    return jnp.broadcast_to(jnp.sum(values, axis=1, keepdims=True), values.shape)


def ratio(top, bottom):
    return jnp.where(bottom > 0.0, top / jnp.where(bottom > 0.0, bottom, 1.0), 0.0)


def tree_sum(values):
    while len(values) > 1:
        values = [sum(values[i : i + 2][1:], values[i]) for i in range(0, len(values), 2)]
    return values[0]


def plane_rows(vector, plane, rows):
    return [vector[plane, rows, m * LANES : (m + 1) * LANES] for m in range(ROWS)]


def y_parts(here, last_x, first_x):
    y_up = [pltpu.roll(value, LANES - X_OUT, 1) for value in here]
    y_down = [pltpu.roll(value, X_OUT, 1) for value in here]
    sums, edges = [], []
    for m in range(ROWS):
        near = y_down[m + X_IN] if m < X_IN else y_up[m - X_IN]
        sums.append(near + FAR_SCALED * (y_up[m] + y_down[m]))
        if m % X_IN < 2:
            edges.append(jnp.where(first_x, y_down[m], here[m]))
        else:
            edges.append(jnp.where(last_x, y_up[m], here[m]))
    return sums, edges


def apply_plane(vector, sums, edges, diagonal, plane, rows):
    planes = vector.shape[0]
    halos = []
    for m, edge in enumerate(plane_rows(edges, plane, rows)):
        halos.append(pltpu.roll(edge, LANES - 1 if m % X_IN < 2 else 1, 1))
    here, above, below, above_2, below_2 = (
        plane_rows(vector, (plane + far) % planes, rows) for far in (0, 1, -1, 2, -2)
    )
    y_sums = plane_rows(sums, plane, rows)
    out = []
    for yi in range(Y_IN):
        first = yi * X_IN
        line, halo = here[first : first + X_IN], halos[first : first + X_IN]
        wide = halo[2:] + line + halo[:2]
        for xi in range(X_IN):
            m = first + xi
            other = m + X_IN if yi == 0 else m - X_IN
            near = here[other] + (above[m] + below[m])
            far = above_2[m] + below_2[m]
            near = near + (wide[xi + 1] + wide[xi + 3])
            far = far + (wide[xi] + wide[xi + 4])
            level = diagonal[plane, :, m * LANES : (m + 1) * LANES]
            out.append((level * here[m] - y_sums[m]) - near - FAR_SCALED * far)
    return here, out


def cmul(first, second):
    return (
        first[0] * second[0] - first[1] * second[1],
        first[0] * second[1] + first[1] * second[0],
    )


def picked(index, values):
    result = jnp.float32(values[0])
    for i, value in enumerate(values[1:], 1):
        result = jnp.where(index == i, jnp.float32(value), result)
    return result


def moment_coeffs(point, angles, count):
    lane = lax.broadcasted_iota(jnp.int32, (1, LANES), 1)
    moment = lax.rem(lane, MOMENTS * count) // count
    parts = []
    for func in (math.cos, math.sin):
        value = jnp.zeros((1, LANES), jnp.float32)
        for k in range(MOMENTS):
            coeff = picked(point, [0.25 * func((k + 1) * angle) for angle in angles])
            value = jnp.where(moment == k, coeff, value)
        parts.append(value)
    return parts


def weights_of(point, points, alphas, norms, limit):
    shape = alphas[0].shape
    count = shape[0]
    lane = lax.broadcasted_iota(jnp.int32, shape, 1)
    source = lax.broadcasted_iota(jnp.int32, shape, 0)
    own = lax.rem(lane, count) == source
    left_half = lane < MOMENTS * count
    betas = [ratio(norms[i + 1], norms[i]) for i in range(ITERS - 1)]
    zero = jnp.zeros(shape, jnp.float32)
    one = jnp.ones(shape, jnp.float32)
    angles = [2.0 * math.pi * (j + 0.5) / points for j in range(points)]
    shift = (
        picked(point, [GAMMA + RADIUS * math.cos(angle) for angle in angles]),
        picked(point, [RADIUS * math.sin(angle) for angle in angles]),
    )
    scaled_shift = (H_SCALE * shift[0], H_SCALE * shift[1])
    product = (one, zero)
    products = [product]
    links = []
    pivot = (scaled_shift[0] - alphas[0], zero + scaled_shift[1])
    for i in range(ITERS):
        size = 1.0 / (pivot[0] * pivot[0] + pivot[1] * pivot[1])
        inverse = (pivot[0] * size, -pivot[1] * size)
        product = cmul(product, inverse)
        products.append(product)
        if i < ITERS - 1:
            link = (betas[i] * inverse[0], betas[i] * inverse[1])
            links.append(link)
            pivot = (scaled_shift[0] - alphas[i + 1] - link[0], scaled_shift[1] - link[1])
    solved = [None] * ITERS
    for i in reversed(range(ITERS)):
        value = (H_SCALE * products[i + 1][0], H_SCALE * products[i + 1][1])
        if i < ITERS - 1:
            step = cmul(links[i], solved[i + 1])
            value = (value[0] + step[0], value[1] + step[1])
        used = limit > i
        solved[i] = (jnp.where(used, value[0], 0.0), jnp.where(used, value[1], 0.0))
    applied = []
    for i in range(BASIS):
        left = limit == i
        rest = (jnp.where(left, products[i][0], 0.0), jnp.where(left, products[i][1], 0.0))
        if i < ITERS:
            turned = cmul(shift, solved[i])
            rest = (rest[0] + turned[0], rest[1] + turned[1])
        if i == 0:
            rest = (rest[0] - 1.0, rest[1])
        applied.append(rest)
    tail = applied[ITERS]
    for back, factor in ((1, alphas[ITERS - 1]), (2, betas[ITERS - 2])):
        part = applied[ITERS - back]
        applied[ITERS - back] = (part[0] - factor * tail[0], part[1] - factor * tail[1])
    moment = moment_coeffs(point, angles, count)
    weights = []
    for i in range(BASIS):
        left = solved[i] if i < ITERS else (zero, zero)
        both = (
            jnp.where(left_half, left[0], applied[i][0]),
            jnp.where(left_half, left[1], applied[i][1]),
        )
        weights.append([jnp.where(own, part, 0.0) for part in cmul(moment, both)])
    return weights


def exact_dot(first, second, dims):
    return lax.dot_general(
        first,
        second,
        (dims, ((), ())),
        precision=lax.Precision.HIGHEST,
        preferred_element_type=jnp.float32,
    )


def split(values):
    high = values.astype(jnp.bfloat16)
    return high, (values - high.astype(jnp.float32)).astype(jnp.bfloat16)


def split_dot(first, second):
    high, low = split(first)
    high_2, low_2 = split(second)
    return lax.dot_general(
        jnp.concatenate([high, high, low], axis=1),
        jnp.concatenate([high_2, low_2, high_2], axis=0),
        (((1,), (0,)), ((), ())),
        preferred_element_type=jnp.float32,
    )


def krylov_kernel(parts, count, *refs):
    blocks, (highs, lows, applied, scalars) = refs[:parts], refs[parts : parts + 4]
    first_work, second_work, diagonal, sums, edges, partial = refs[parts + 4 :]
    planes = diagonal.shape[0]
    depth = planes // parts
    groups = count // SUB
    lane = lax.broadcasted_iota(jnp.int32, (SUB, LANES), 1)
    last_x = lax.rem(lane, X_OUT) == X_OUT - 1
    first_x = lax.rem(lane, X_OUT) == 0
    here = lax.axis_index("dom")
    for turn in range(parts):
        slab = jnp.bitwise_xor(here, turn) * depth
        for deep in range(depth):
            for m in range(ROWS):
                start = (deep * ROWS + m) * count
                lanes = slice(m * LANES, (m + 1) * LANES)
                value = blocks[turn][start : start + count, :]
                first_work[slab + deep, :, lanes] = value
                highs[0, slab + deep, :, lanes], lows[0, slab + deep, :, lanes] = split(value)
            start = depth * ROWS * count + deep * ROWS
            levels = H_SCALE * (blocks[turn][start : start + ROWS, :] + 3.75)
            for m in range(ROWS):
                level = jnp.broadcast_to(levels[m : m + 1, :], (SUB, LANES))
                diagonal[slab + deep, :, m * LANES : (m + 1) * LANES] = level
    second_work[...] = jnp.zeros_like(second_work)
    scalars[ITERS] = jnp.zeros((count, LANES), jnp.float32)

    all_rows = [pl.ds(group * SUB, SUB) for group in range(groups)]
    all_lanes = [slice(m * LANES, (m + 1) * LANES) for m in range(ROWS)]
    def keep_y_parts(plane, rows, values):
        for ref, parts_of in zip((sums, edges), y_parts(values, last_x, first_x)):
            for lanes, part in zip(all_lanes, parts_of):
                ref[plane, rows, lanes] = part

    for group, rows in enumerate(all_rows):
        norm = []
        for plane in range(planes):
            values = plane_rows(first_work, plane, rows)
            keep_y_parts(plane, rows, values)
            norm.append(tree_sum([value * value for value in values]))
        partial[rows, :] = tree_sum(norm)

    def update_pass(i, work, before, alphas, betas):
        norm = [[] for _ in range(groups)]
        for plane in range(planes):
            columns = []
            for group, rows in enumerate(all_rows):
                values = []
                for lanes in all_lanes:
                    value = applied[plane, rows, lanes] - betas[group] * before[plane, rows, lanes]
                    value = value - alphas[group] * work[plane, rows, lanes]
                    before[plane, rows, lanes] = value
                    values.append(value)
                keep_y_parts(plane, rows, values)
                norm[group].append(tree_sum([value * value for value in values]))
                columns.append(values)
            for lanes, *column in zip(all_lanes, *columns):
                high, low = split(jnp.concatenate(column, axis=0))
                highs[i + 1, plane, :, lanes] = high
                lows[i + 1, plane, :, lanes] = low
        for rows, terms in zip(all_rows, norm):
            partial[rows, :] = tree_sum(terms)

    def half_turn(i, work, before, may_end):
        norms = [lane_sum(partial[rows, :]) for rows in all_rows]
        betas = [
            ratio(norm, scalars[ITERS + i, rows, :]) for norm, rows in zip(norms, all_rows)
        ]
        inverses = [ratio(jnp.ones_like(norm), norm) for norm in norms]
        for norm, rows in zip(norms, all_rows):
            scalars[ITERS + 1 + i, rows, :] = norm
        curve = [[] for _ in range(groups)]
        for plane in range(planes):
            for group, rows in enumerate(all_rows):
                value, out = apply_plane(work, sums, edges, diagonal, plane, rows)
                for m, lanes in enumerate(all_lanes):
                    applied[plane, rows, lanes] = out[m]
                curve[group].append(tree_sum([value[m] * out[m] for m in range(ROWS)]))
        alphas = [lane_sum(tree_sum(curve[g])) * inverses[g] for g in range(groups)]
        for alpha, rows in zip(alphas, all_rows):
            scalars[i, rows, :] = alpha
        if may_end:
            pl.when(i < ITERS - 1)(lambda: update_pass(i, work, before, alphas, betas))
        else:
            update_pass(i, work, before, alphas, betas)

    def turn(step, carry):
        half_turn(2 * step, first_work, second_work, False)
        half_turn(2 * step + 1, second_work, first_work, True)
        return carry

    lax.fori_loop(0, ITERS // 2, turn, 0)


def gram_kernel(points, scalars, *refs):
    tiles = refs[:points]
    highs, lows, applied, out_b, out_a, gram, limits, weights = refs[points:]
    planes, count, _ = applied.shape
    groups = count // SUB
    size = gram.shape[1]
    here = lax.axis_index("point")
    core = jnp.bitwise_and(lax.axis_index("dom"), CORES - 1)
    for far, tile in zip((0, 1 + core, 3, 2 - core), tiles):
        limits[jnp.bitwise_xor(here, far)] = tile[...]
    gram[...] = jnp.zeros_like(gram)
    weights[...] = jnp.zeros_like(weights)

    def turn(point, carry):
        limit = jnp.concatenate([limits[point]] * groups, axis=0)
        alphas = [scalars[i] for i in range(ITERS)]
        norms = [scalars[ITERS + 1 + i] for i in range(ITERS)]
        total = None
        for deep in range(planes // points):
            plane = point * (planes // points) + deep
            last_high, last_low = split(applied[plane])
            pad = [jnp.zeros((size - BASIS * count, ROWS * LANES), jnp.bfloat16)]
            high = [highs[i, plane] for i in range(ITERS)] + [last_high]
            high = jnp.concatenate(high + pad, axis=0)
            low = [lows[i, plane] for i in range(ITERS)] + [last_low]
            low = jnp.concatenate(low + pad, axis=0)
            product = lax.dot_general(
                jnp.concatenate([high, low], axis=0),
                high,
                (((1,), (1,)), ((), ())),
                preferred_element_type=jnp.float32,
            )
            total = product if total is None else total + product
        gram[...] += total
        for i, pair in enumerate(weights_of(point, points, alphas, norms, limit)):
            for part, value in enumerate(pair):
                weights[i * count : (i + 1) * count, part * LANES : (part + 1) * LANES] += value
        return carry

    lax.fori_loop(0, points, turn, 0)
    cross = gram[size:, :]
    pairs = gram[:size, :] + cross + cross.T
    right = split_dot(pairs, weights[...])
    real, imag = weights[:, :LANES], weights[:, LANES:]
    half = MOMENTS * count
    left = jnp.concatenate([real[:, :half], imag[:, :half]], axis=1)
    joined = split_dot(left.T, right)
    scale = 1.0 / (planes * ROWS * LANES)
    width = 2 * half
    real = (joined[:half, :width] + joined[half:, width:]) * scale
    imag = (joined[:half, width:] - joined[half:, :width]) * scale
    out_b[0] = real[:, :half]
    out_b[1] = imag[:, :half]
    out_a[0] = real[:, half:]
    out_a[1] = imag[:, half:]


def swapped(values, axis, size, mask):
    return lax.ppermute(values, axis, [(index ^ mask, index) for index in range(size)])


def whole_grid(sources, potential, iter_counts, *, parts, points):
    count, depth, _ = sources.shape
    planes = parts * depth
    block, tile = packed_block(sources, potential, iter_counts)
    even = [block] + [swapped(block, "dom", parts, mask) for mask in range(CORES, parts, CORES)]
    mixed = [
        ((point ^ (1 + part % CORES)) * parts + part, point * parts + part)
        for point in range(points)
        for part in range(parts)
    ]
    tiles = [lax.ppermute(tile, ("point", "dom"), mixed), swapped(tile, "point", points, 3)]
    even[1], *tiles = lax.optimization_barrier((even[1], *tiles))
    tiles.append(swapped(tiles[0], "dom", parts, 1))
    odd = [swapped(value, "dom", parts, 1) for value in even]
    blocks = [value for pair in zip(even, odd) for value in pair]
    vmem = pl.BlockSpec(memory_space=pltpu.VMEM)
    vector = (planes, count, ROWS * LANES)
    cells = planes * ROWS * LANES
    highs, lows, applied, scalars = pl.pallas_call(
        functools.partial(krylov_kernel, parts, count),
        out_shape=(
            jax.ShapeDtypeStruct((ITERS,) + vector, jnp.bfloat16),
            jax.ShapeDtypeStruct((ITERS,) + vector, jnp.bfloat16),
            jax.ShapeDtypeStruct(vector, jnp.float32),
            jax.ShapeDtypeStruct((2 * ITERS + 1, count, LANES), jnp.float32),
        ),
        in_specs=[vmem] * parts,
        out_specs=(vmem,) * 4,
        scratch_shapes=[
            pltpu.VMEM(vector, jnp.float32),
            pltpu.VMEM(vector, jnp.float32),
            pltpu.VMEM((planes, SUB, ROWS * LANES), jnp.float32),
            pltpu.VMEM(vector, jnp.float32),
            pltpu.VMEM(vector, jnp.float32),
            pltpu.VMEM((count, LANES), jnp.float32),
        ],
        compiler_params=pltpu.CompilerParams(vmem_limit_bytes=16 * 2**20),
        name="krylov",
    )(*blocks)
    size = -(-BASIS * count // LANES) * LANES
    width = MOMENTS * count
    out = jax.ShapeDtypeStruct((2, width, width), jnp.float32)
    return pl.pallas_call(
        functools.partial(gram_kernel, points),
        out_shape=(out, out),
        in_specs=[vmem] * (4 + points),
        out_specs=(vmem, vmem),
        scratch_shapes=[
            pltpu.VMEM((2 * size, size), jnp.float32),
            pltpu.VMEM((points, SUB, LANES), jnp.float32),
            pltpu.VMEM((size, 2 * LANES), jnp.float32),
        ],
        compiler_params=pltpu.CompilerParams(vmem_limit_bytes=16 * 2**20),
        name="gram",
    )(scalars, tile, *tiles, highs, lows, applied)


def on_device(sources, potential, iter_counts):
    parts, points = lax.axis_size("dom"), lax.axis_size("point")
    count, depth, cells = sources.shape
    held = BASIS * count * parts * depth * cells * 4
    fits = (
        held <= 16 * 2**20
        and parts == 8
        and points == 4
        and count == 2 * SUB
        and 2 * MOMENTS * count == LANES
        and parts * depth == 16
        and cells == GX * GX == ROWS * LANES
    )
    if not fits:
        return split_grid(sources, potential, iter_counts)
    return whole_grid(sources, potential, iter_counts, parts=parts, points=points)


def solution(mesh):
    placed = (P(None, "dom", None), P("dom", None), P("point"))
    return jax.shard_map(
        on_device, mesh=mesh, in_specs=placed, out_specs=(P(), P()), check_vma=False
    )
```

```python
import functools
import math

import jax
import jax.numpy as jnp
from jax import lax
from jax.experimental import pallas as pl
from jax.experimental.pallas import tpu as pltpu
from jax.sharding import PartitionSpec as P

MOMENTS = 4
ITERS = 6
GX = 32


COEF_NEAR = 4.0 / 3.0
COEF_FAR = -1.0 / 12.0
GAMMA = 2.0
RADIUS = 1.5


def padded_2(block, sides, width):
    for axis, dim in sides:
        count = lax.axis_size(axis)
        forward = [(i, i + 1) for i in range(count - 1)]
        forward.append((count - 1, 0))
        backward = [(target, source) for source, target in forward]
        low = lax.ppermute(
            lax.slice_in_dim(block, block.shape[dim] - width, None, axis=dim), axis, forward
        )
        high = lax.ppermute(lax.slice_in_dim(block, 0, width, axis=dim), axis, backward)
        block = jnp.concatenate([low, block, high], axis=dim)
    return block


def plane_terms(values, side):
    lead = values.shape[:-1]
    planes = values.reshape(lead + (side, side))
    summed = COEF_NEAR * (
        jnp.roll(planes, 1, -2)
        + jnp.roll(planes, -1, -2)
        + jnp.roll(planes, 1, -1)
        + jnp.roll(planes, -1, -1)
    )
    summed = summed + COEF_FAR * (
        jnp.roll(planes, 2, -2)
        + jnp.roll(planes, -2, -2)
        + jnp.roll(planes, 2, -1)
        + jnp.roll(planes, -2, -1)
    )
    return summed.reshape(values.shape)


def complex_mul(first, second):
    return jnp.stack(
        [first[0] * second[0] - first[1] * second[1], first[0] * second[1] + first[1] * second[0]]
    )


def complex_div(first, second):
    denom = second[0] * second[0] + second[1] * second[1]
    return jnp.stack(
        [
            (first[0] * second[0] + first[1] * second[1]) / denom,
            (first[1] * second[0] - first[0] * second[1]) / denom,
        ]
    )


def bilinear(first, second):
    real_part = jnp.sum(first[0] * second[0] - first[1] * second[1], axis=(1, 2))
    imag_part = jnp.sum(first[0] * second[1] + first[1] * second[0], axis=(1, 2))
    return jnp.stack([real_part, imag_part])


def scaled(coeffs, values):
    return complex_mul(coeffs[:, :, None, None], values)


def shifted(values, potential, shift_re, shift_im):
    padded = padded_2(values, (("dom", 2),), 2)
    depth = values.shape[2]
    lap = -7.5 * values + plane_terms(values, GX)
    lap = lap + COEF_NEAR * (padded[:, :, 3 : 3 + depth] + padded[:, :, 1 : 1 + depth])
    lap = lap + COEF_FAR * (padded[:, :, 4 : 4 + depth] + padded[:, :, 0:depth])
    applied = -0.5 * lap + potential * values
    return jnp.stack(
        [
            shift_re * values[0] - shift_im * values[1] - applied[0],
            shift_re * values[1] + shift_im * values[0] - applied[1],
        ]
    )


def residual_sum(values):
    return lax.psum(bilinear(values, values), "dom")


def moment_terms(solution, residual, sources, angle_now, shift_re, shift_im):
    applied = jnp.stack(
        [
            shift_re * solution[0] - shift_im * solution[1] - sources[0] + residual[0],
            shift_re * solution[1] + shift_im * solution[0] - sources[1] + residual[1],
        ]
    )
    angles = (jnp.arange(MOMENTS).astype(jnp.float32) + 1.0) * angle_now
    coeffs = 0.25 * jnp.stack([jnp.cos(angles), jnp.sin(angles)])
    s_terms = complex_mul(coeffs[:, :, None, None, None], solution[:, None])
    h_terms = complex_mul(coeffs[:, :, None, None, None], applied[:, None])
    width = MOMENTS * solution.shape[1]
    return (s_terms.reshape(2, width, -1), h_terms.reshape(2, width, -1))


def gram_of(left, right):
    width = left.shape[1]
    joined = lax.dot_general(
        left.reshape(2 * width, -1),
        right.reshape(2 * width, -1),
        (((1,), (1,)), ((), ())),
        precision=lax.Precision.HIGHEST,
        preferred_element_type=jnp.float32,
    )
    blocks = joined.reshape(2, width, 2, width)
    return jnp.stack([blocks[0, :, 0] + blocks[1, :, 1], blocks[0, :, 1] - blocks[1, :, 0]])


def split_grid(sources, potential, iter_counts):
    complex_src = jnp.stack([sources, jnp.zeros_like(sources)])
    angle_now = (
        2.0 * math.pi * (lax.axis_index("point").astype(jnp.float32) + 0.5) / lax.axis_size("point")
    )
    shift_re = GAMMA + RADIUS * jnp.cos(angle_now)
    shift_im = RADIUS * jnp.sin(angle_now)
    limit = iter_counts[0]
    solution = jnp.zeros_like(complex_src)

    def one_turn(turn_idx, state):
        solution, residual, search, norm_now = state
        product = shifted(search, potential, shift_re, shift_im)
        curve = lax.psum(bilinear(search, product), "dom")
        step_size = complex_div(norm_now, curve)
        new_residual = residual - scaled(step_size, product)
        norm_next = residual_sum(new_residual)
        fresh = (
            solution + scaled(step_size, search),
            new_residual,
            new_residual + scaled(complex_div(norm_next, norm_now), search),
            norm_next,
        )
        keep_mask = turn_idx < limit
        return jax.tree.map(lambda newer, older: jnp.where(keep_mask, newer, older), fresh, state)

    start = (solution, complex_src, complex_src, residual_sum(complex_src))
    solution, residual, search, norm_now = lax.fori_loop(0, ITERS, one_turn, start)
    s_terms, h_terms = moment_terms(solution, residual, complex_src, angle_now, shift_re, shift_im)
    cells = sources.shape[1] * sources.shape[2] * lax.axis_size("dom")
    s_total, h_total = lax.psum((s_terms, h_terms), "point")
    gram_b, gram_a = lax.psum((gram_of(s_total, s_total), gram_of(s_total, h_total)), "dom")
    return (gram_b / cells, gram_a / cells)


Y_IN, X_IN = 2, 4
Y_OUT, X_OUT = GX // Y_IN, GX // X_IN
ROWS = Y_IN * X_IN
LANES = Y_OUT * X_OUT
SUB = 8
BASIS = ITERS + 1
CORES = 2
H_SCALE = 2.0 / COEF_NEAR
FAR_SCALED = 0.5 * H_SCALE * COEF_FAR


def pack_kernel(depth, groups, counts, rows, out, tile):
    columns = rows.shape[0] // (SUB * groups * depth + depth)
    first_level = columns * SUB * groups * depth
    source = lax.broadcasted_iota(jnp.int32, (LANES, LANES), 0)
    target = lax.broadcasted_iota(jnp.int32, (LANES, LANES), 1)
    inner = target // (LANES // ROWS)
    outer = target % (LANES // ROWS)
    cell = (outer // X_OUT * Y_IN + inner // X_IN) * GX + outer % X_OUT * X_IN + inner % X_IN
    swap = jnp.where(source == cell, 1.0, 0.0).astype(jnp.float32)
    parts = []
    for deep in range(depth):
        for group in range(groups):
            for column in range(columns):
                start = (group * SUB * columns + column) * depth + deep
                parts.append(rows[pl.ds(start, SUB, stride=columns * depth), :])
        parts.append(rows[pl.ds(first_level + deep, columns, stride=depth), :])
    mixed = exact_dot(jnp.concatenate(parts, axis=0), swap, ((1,), (0,)))
    block = LANES // ROWS
    lane_block = lax.broadcasted_iota(jnp.int32, (SUB, LANES), 1) // block
    row = lax.broadcasted_iota(jnp.int32, (SUB, LANES), 0)
    for deep in range(depth):
        base = deep * (groups + 1) * columns * SUB - deep * (columns - 1) * SUB
        for group in range(groups):
            pieces = [
                mixed[base + (group * columns + column) * SUB :][:SUB] for column in range(columns)
            ]
            for m in range(ROWS):
                value = pieces[m]
                for column in range(columns):
                    if column != m:
                        moved = pltpu.roll(pieces[column], (column - m) * block % LANES, 1)
                        value = jnp.where(lane_block == column, moved, value)
                start = ((deep * ROWS + m) * groups + group) * SUB
                out[start : start + SUB, :] = value
        piece = mixed[base + groups * columns * SUB :][:SUB]
        value = piece
        for far in range(1, columns):
            moved = pltpu.roll(pltpu.roll(piece, far * block, 1), columns - far, 0)
            value = jnp.where(lane_block == (row + far) % columns, moved, value)
        start = depth * ROWS * SUB * groups + deep * ROWS
        out[start : start + ROWS, :] = value
    tile[...] = jnp.broadcast_to(counts[...].astype(jnp.float32), (SUB, LANES))


def packed_block(sources, potential, iter_counts):
    count, depth, cells = sources.shape
    columns = cells // LANES
    rows = sources.reshape(count, depth, columns, LANES).transpose(0, 2, 1, 3).reshape(-1, LANES)
    levels = potential.reshape(depth, columns, LANES).transpose(1, 0, 2).reshape(-1, LANES)
    vmem = pl.BlockSpec(memory_space=pltpu.VMEM)
    size = depth * ROWS * (count + 1)
    return pl.pallas_call(
        functools.partial(pack_kernel, depth, count // SUB),
        out_shape=(
            jax.ShapeDtypeStruct((size, LANES), jnp.float32),
            jax.ShapeDtypeStruct((SUB, LANES), jnp.float32),
        ),
        in_specs=[vmem, vmem],
        out_specs=(vmem, vmem),
        compiler_params=pltpu.CompilerParams(vmem_limit_bytes=4 * 2**20),
        name="pack",
    )(iter_counts.reshape(1, 1), jnp.concatenate([rows, levels], axis=0))


def lane_sum(values):
    return jnp.broadcast_to(jnp.sum(values, axis=1, keepdims=True), values.shape)


def ratio(top, bottom):
    return jnp.where(bottom > 0.0, top / jnp.where(bottom > 0.0, bottom, 1.0), 0.0)


def tree_sum(values):
    while len(values) > 1:
        values = [sum(values[i : i + 2][1:], values[i]) for i in range(0, len(values), 2)]
    return values[0]


def plane_rows(vector, plane, rows):
    return [vector[plane, rows, m * LANES : (m + 1) * LANES] for m in range(ROWS)]


def y_parts(here, last_x, first_x):
    y_up = [pltpu.roll(value, LANES - X_OUT, 1) for value in here]
    y_down = [pltpu.roll(value, X_OUT, 1) for value in here]
    sums, edges = [], []
    for m in range(ROWS):
        near = y_down[m + X_IN] if m < X_IN else y_up[m - X_IN]
        sums.append(near + FAR_SCALED * (y_up[m] + y_down[m]))
        if m % X_IN < 2:
            edges.append(jnp.where(first_x, y_down[m], here[m]))
        else:
            edges.append(jnp.where(last_x, y_up[m], here[m]))
    return sums, edges


def apply_plane(vector, sums, edges, diagonal, plane, rows):
    planes = vector.shape[0]
    halos = []
    for m, edge in enumerate(plane_rows(edges, plane, rows)):
        halos.append(pltpu.roll(edge, LANES - 1 if m % X_IN < 2 else 1, 1))
    here, above, below, above_2, below_2 = (
        plane_rows(vector, (plane + far) % planes, rows) for far in (0, 1, -1, 2, -2)
    )
    y_sums = plane_rows(sums, plane, rows)
    out = []
    for yi in range(Y_IN):
        first = yi * X_IN
        line, halo = here[first : first + X_IN], halos[first : first + X_IN]
        wide = halo[2:] + line + halo[:2]
        for xi in range(X_IN):
            m = first + xi
            other = m + X_IN if yi == 0 else m - X_IN
            near = here[other] + (above[m] + below[m])
            far = above_2[m] + below_2[m]
            near = near + (wide[xi + 1] + wide[xi + 3])
            far = far + (wide[xi] + wide[xi + 4])
            level = diagonal[plane, :, m * LANES : (m + 1) * LANES]
            out.append((level * here[m] - y_sums[m]) - near - FAR_SCALED * far)
    return here, out


def cmul(first, second):
    return (
        first[0] * second[0] - first[1] * second[1],
        first[0] * second[1] + first[1] * second[0],
    )


def moment_coeffs(angle, shape):
    count = shape[0]
    lane = lax.broadcasted_iota(jnp.int32, shape, 1)
    moment = lax.rem(lane, MOMENTS * count) // count
    parts = []
    for func in (math.cos, math.sin):
        value = jnp.full(shape, 0.25 * func(angle), jnp.float32)
        for k in range(1, MOMENTS):
            value = jnp.where(moment == k, 0.25 * func((k + 1) * angle), value)
        parts.append(value)
    return parts


def weights_of(alphas, norms, limits):
    points = len(limits)
    count = limits[0].shape[0]
    shape = (points * count, LANES)
    lane = lax.broadcasted_iota(jnp.int32, shape, 1)
    left_half = lane < MOMENTS * count
    own = lax.rem(lane[:count], count) == lax.broadcasted_iota(jnp.int32, (count, LANES), 0)

    def stacked(values):
        return jnp.concatenate(values, axis=0)

    def constant(values):
        return stacked([jnp.full((count, LANES), value, jnp.float32) for value in values])

    limit = stacked(limits)
    betas = [stacked([ratio(norms[i + 1], norms[i])] * points) for i in range(ITERS - 1)]
    alphas = [stacked([alpha] * points) for alpha in alphas]
    zero = jnp.zeros(shape, jnp.float32)
    one = jnp.ones(shape, jnp.float32)
    angles = [2.0 * math.pi * (j + 0.5) / points for j in range(points)]
    shift = (
        constant([GAMMA + RADIUS * math.cos(angle) for angle in angles]),
        constant([RADIUS * math.sin(angle) for angle in angles]),
    )
    scaled_shift = (H_SCALE * shift[0], H_SCALE * shift[1])
    product = (one, zero)
    products = [product]
    links = []
    pivot = (scaled_shift[0] - alphas[0], scaled_shift[1])
    for i in range(ITERS):
        size = 1.0 / (pivot[0] * pivot[0] + pivot[1] * pivot[1])
        inverse = (pivot[0] * size, -pivot[1] * size)
        product = cmul(product, inverse)
        products.append(product)
        if i < ITERS - 1:
            link = (betas[i] * inverse[0], betas[i] * inverse[1])
            links.append(link)
            pivot = (scaled_shift[0] - alphas[i + 1] - link[0], scaled_shift[1] - link[1])
    solved = [None] * ITERS
    for i in reversed(range(ITERS)):
        value = (H_SCALE * products[i + 1][0], H_SCALE * products[i + 1][1])
        if i < ITERS - 1:
            step = cmul(links[i], solved[i + 1])
            value = (value[0] + step[0], value[1] + step[1])
        used = limit > i
        solved[i] = (jnp.where(used, value[0], 0.0), jnp.where(used, value[1], 0.0))
    applied = []
    for i in range(BASIS):
        left = limit == i
        rest = (jnp.where(left, products[i][0], 0.0), jnp.where(left, products[i][1], 0.0))
        if i < ITERS:
            turned = cmul(shift, solved[i])
            rest = (rest[0] + turned[0], rest[1] + turned[1])
        if i == 0:
            rest = (rest[0] - 1.0, rest[1])
        applied.append(rest)
    tail = applied[ITERS]
    for back, factor in ((1, alphas[ITERS - 1]), (2, betas[ITERS - 2])):
        part = applied[ITERS - back]
        applied[ITERS - back] = (part[0] - factor * tail[0], part[1] - factor * tail[1])
    moments = [moment_coeffs(angle, (count, LANES)) for angle in angles]
    moment = tuple(stacked([pair[part] for pair in moments]) for part in range(2))
    weights = []
    for i in range(BASIS):
        left = solved[i] if i < ITERS else (zero, zero)
        both = (
            jnp.where(left_half, left[0], applied[i][0]),
            jnp.where(left_half, left[1], applied[i][1]),
        )
        terms = cmul(moment, both)
        weights.append(
            [
                jnp.where(own, tree_sum([part[j * count :][:count] for j in range(points)]), 0.0)
                for part in terms
            ]
        )
    return weights


def exact_dot(first, second, dims):
    return lax.dot_general(
        first,
        second,
        (dims, ((), ())),
        precision=lax.Precision.HIGHEST,
        preferred_element_type=jnp.float32,
    )


def split(values):
    high = values.astype(jnp.bfloat16)
    return high, (values - high.astype(jnp.float32)).astype(jnp.bfloat16)


def krylov_kernel(parts, count, *refs):
    blocks, (highs, lows, applied, scalars) = refs[:parts], refs[parts : parts + 4]
    first_work, second_work, diagonal, sums, edges, partial = refs[parts + 4 :]
    planes = diagonal.shape[0]
    depth = planes // parts
    groups = count // SUB
    lane = lax.broadcasted_iota(jnp.int32, (SUB, LANES), 1)
    last_x = lax.rem(lane, X_OUT) == X_OUT - 1
    first_x = lax.rem(lane, X_OUT) == 0
    here = lax.axis_index("dom")
    for turn in range(parts):
        slab = jnp.bitwise_xor(here, turn) * depth
        for deep in range(depth):
            for m in range(ROWS):
                start = (deep * ROWS + m) * count
                lanes = slice(m * LANES, (m + 1) * LANES)
                value = blocks[turn][start : start + count, :]
                first_work[slab + deep, :, lanes] = value
                highs[0, slab + deep, :, lanes], lows[0, slab + deep, :, lanes] = split(value)
            start = depth * ROWS * count + deep * ROWS
            levels = H_SCALE * (blocks[turn][start : start + ROWS, :] + 3.75)
            for m in range(ROWS):
                level = jnp.broadcast_to(levels[m : m + 1, :], (SUB, LANES))
                diagonal[slab + deep, :, m * LANES : (m + 1) * LANES] = level
    second_work[...] = jnp.zeros_like(second_work)
    scalars[ITERS] = jnp.zeros((count, LANES), jnp.float32)

    all_rows = [pl.ds(group * SUB, SUB) for group in range(groups)]
    all_lanes = [slice(m * LANES, (m + 1) * LANES) for m in range(ROWS)]
    def keep_y_parts(plane, rows, values):
        for ref, parts_of in zip((sums, edges), y_parts(values, last_x, first_x)):
            for lanes, part in zip(all_lanes, parts_of):
                ref[plane, rows, lanes] = part

    for group, rows in enumerate(all_rows):
        norm = []
        for plane in range(planes):
            values = plane_rows(first_work, plane, rows)
            keep_y_parts(plane, rows, values)
            norm.append(tree_sum([value * value for value in values]))
        partial[rows, :] = tree_sum(norm)

    def update_pass(i, work, before, alphas, betas):
        norm = [[] for _ in range(groups)]
        for plane in range(planes):
            columns = []
            for group, rows in enumerate(all_rows):
                values = []
                for lanes in all_lanes:
                    value = applied[plane, rows, lanes] - betas[group] * before[plane, rows, lanes]
                    value = value - alphas[group] * work[plane, rows, lanes]
                    before[plane, rows, lanes] = value
                    values.append(value)
                keep_y_parts(plane, rows, values)
                norm[group].append(tree_sum([value * value for value in values]))
                columns.append(values)
            for lanes, *column in zip(all_lanes, *columns):
                high, low = split(jnp.concatenate(column, axis=0))
                highs[i + 1, plane, :, lanes] = high
                lows[i + 1, plane, :, lanes] = low
        for rows, terms in zip(all_rows, norm):
            partial[rows, :] = tree_sum(terms)

    def half_turn(i, work, before, may_end):
        norms = [lane_sum(partial[rows, :]) for rows in all_rows]
        betas = [
            ratio(norm, scalars[ITERS + i, rows, :]) for norm, rows in zip(norms, all_rows)
        ]
        inverses = [ratio(jnp.ones_like(norm), norm) for norm in norms]
        for norm, rows in zip(norms, all_rows):
            scalars[ITERS + 1 + i, rows, :] = norm
        curve = [[] for _ in range(groups)]
        for plane in range(planes):
            for group, rows in enumerate(all_rows):
                value, out = apply_plane(work, sums, edges, diagonal, plane, rows)
                for m, lanes in enumerate(all_lanes):
                    applied[plane, rows, lanes] = out[m]
                curve[group].append(tree_sum([value[m] * out[m] for m in range(ROWS)]))
        alphas = [lane_sum(tree_sum(curve[g])) * inverses[g] for g in range(groups)]
        for alpha, rows in zip(alphas, all_rows):
            scalars[i, rows, :] = alpha
        if may_end:
            pl.when(i < ITERS - 1)(lambda: update_pass(i, work, before, alphas, betas))
        else:
            update_pass(i, work, before, alphas, betas)

    def turn(step, carry):
        half_turn(2 * step, first_work, second_work, False)
        half_turn(2 * step + 1, second_work, first_work, True)
        return carry

    lax.fori_loop(0, ITERS // 2, turn, 0)


def gram_kernel(points, scalars, *refs):
    tiles = refs[:points]
    highs, lows, applied, out_b, out_a, limits = refs[points:]
    planes, count, _ = applied.shape
    groups = count // SUB
    size = BASIS * count
    here = lax.axis_index("point")
    core = jnp.bitwise_and(lax.axis_index("dom"), CORES - 1)
    for far, tile in zip((0, 1 + core, 3, 2 - core), tiles):
        limits[jnp.bitwise_xor(here, far)] = tile[...]

    bounds = [jnp.concatenate([limits[j]] * groups, axis=0) for j in range(points)]
    alphas = [scalars[i] for i in range(ITERS)]
    norms = [scalars[ITERS + 1 + i] for i in range(ITERS)]
    weights = weights_of(alphas, norms, bounds)
    real = jnp.concatenate([pair[0] for pair in weights], axis=0)
    imag = jnp.concatenate([pair[1] for pair in weights], axis=0)
    gram = None
    for plane in range(planes):
        last_high, last_low = split(applied[plane])
        high = jnp.concatenate([highs[i, plane] for i in range(ITERS)] + [last_high], axis=0)
        low = jnp.concatenate([lows[i, plane] for i in range(ITERS)] + [last_low], axis=0)
        product = lax.dot_general(
            jnp.concatenate([high, low], axis=0),
            high,
            (((1,), (1,)), ((), ())),
            preferred_element_type=jnp.float32,
        )
        gram = product if gram is None else gram + product
    cross = gram[size:, :]
    pairs = gram[:size, :] + cross + cross.T
    right = exact_dot(pairs, jnp.concatenate([real, imag], axis=1), ((1,), (0,)))
    half = MOMENTS * count
    left = jnp.concatenate([real[:, :half], imag[:, :half]], axis=1)
    joined = exact_dot(left.T, right, ((1,), (0,)))
    scale = 1.0 / (planes * ROWS * LANES)
    width = 2 * half
    real = (joined[:half, :width] + joined[half:, width:]) * scale
    imag = (joined[:half, width:] - joined[half:, :width]) * scale
    out_b[0] = real[:, :half]
    out_b[1] = imag[:, :half]
    out_a[0] = real[:, half:]
    out_a[1] = imag[:, half:]


def swapped(values, axis, size, mask):
    return lax.ppermute(values, axis, [(index ^ mask, index) for index in range(size)])


def whole_grid(sources, potential, iter_counts, *, parts, points):
    count, depth, _ = sources.shape
    planes = parts * depth
    block, tile = packed_block(sources, potential, iter_counts)
    even = [block] + [swapped(block, "dom", parts, mask) for mask in range(CORES, parts, CORES)]
    mixed = [
        ((point ^ (1 + part % CORES)) * parts + part, point * parts + part)
        for point in range(points)
        for part in range(parts)
    ]
    tiles = [lax.ppermute(tile, ("point", "dom"), mixed), swapped(tile, "point", points, 3)]
    even[1], *tiles = lax.optimization_barrier((even[1], *tiles))
    tiles.append(swapped(tiles[0], "dom", parts, 1))
    odd = [swapped(value, "dom", parts, 1) for value in even]
    blocks = [value for pair in zip(even, odd) for value in pair]
    vmem = pl.BlockSpec(memory_space=pltpu.VMEM)
    vector = (planes, count, ROWS * LANES)
    cells = planes * ROWS * LANES
    highs, lows, applied, scalars = pl.pallas_call(
        functools.partial(krylov_kernel, parts, count),
        out_shape=(
            jax.ShapeDtypeStruct((ITERS,) + vector, jnp.bfloat16),
            jax.ShapeDtypeStruct((ITERS,) + vector, jnp.bfloat16),
            jax.ShapeDtypeStruct(vector, jnp.float32),
            jax.ShapeDtypeStruct((2 * ITERS + 1, count, LANES), jnp.float32),
        ),
        in_specs=[vmem] * parts,
        out_specs=(vmem,) * 4,
        scratch_shapes=[
            pltpu.VMEM(vector, jnp.float32),
            pltpu.VMEM(vector, jnp.float32),
            pltpu.VMEM((planes, SUB, ROWS * LANES), jnp.float32),
            pltpu.VMEM(vector, jnp.float32),
            pltpu.VMEM(vector, jnp.float32),
            pltpu.VMEM((count, LANES), jnp.float32),
        ],
        compiler_params=pltpu.CompilerParams(vmem_limit_bytes=16 * 2**20),
        name="krylov",
    )(*blocks)
    width = MOMENTS * count
    out = jax.ShapeDtypeStruct((2, width, width), jnp.float32)
    return pl.pallas_call(
        functools.partial(gram_kernel, points),
        out_shape=(out, out),
        in_specs=[vmem] * (4 + points),
        out_specs=(vmem, vmem),
        scratch_shapes=[pltpu.VMEM((points, SUB, LANES), jnp.float32)],
        compiler_params=pltpu.CompilerParams(vmem_limit_bytes=16 * 2**20),
        name="gram",
    )(scalars, tile, *tiles, highs, lows, applied)


def on_device(sources, potential, iter_counts):
    parts, points = lax.axis_size("dom"), lax.axis_size("point")
    count, depth, cells = sources.shape
    held = BASIS * count * parts * depth * cells * 4
    fits = (
        held <= 16 * 2**20
        and parts == 8
        and points == 4
        and count == 2 * SUB
        and 2 * MOMENTS * count == LANES
        and parts * depth == 16
        and cells == GX * GX == ROWS * LANES
    )
    if not fits:
        return split_grid(sources, potential, iter_counts)
    return whole_grid(sources, potential, iter_counts, parts=parts, points=points)


def solution(mesh):
    placed = (P(None, "dom", None), P("dom", None), P("point"))
    return jax.shard_map(
        on_device, mesh=mesh, in_specs=placed, out_specs=(P(), P()), check_vma=False
    )
```

```python
import functools
import math

import jax
import jax.numpy as jnp
from jax import lax
from jax.experimental import pallas as pl
from jax.experimental.pallas import tpu as pltpu
from jax.sharding import PartitionSpec as P

MOMENTS = 4
ITERS = 6
GX = 32


COEF_NEAR = 4.0 / 3.0
COEF_FAR = -1.0 / 12.0
GAMMA = 2.0
RADIUS = 1.5


def padded_2(block, sides, width):
    for axis, dim in sides:
        count = lax.axis_size(axis)
        forward = [(i, i + 1) for i in range(count - 1)]
        forward.append((count - 1, 0))
        backward = [(target, source) for source, target in forward]
        low = lax.ppermute(
            lax.slice_in_dim(block, block.shape[dim] - width, None, axis=dim), axis, forward
        )
        high = lax.ppermute(lax.slice_in_dim(block, 0, width, axis=dim), axis, backward)
        block = jnp.concatenate([low, block, high], axis=dim)
    return block


def plane_terms(values, side):
    lead = values.shape[:-1]
    planes = values.reshape(lead + (side, side))
    summed = COEF_NEAR * (
        jnp.roll(planes, 1, -2)
        + jnp.roll(planes, -1, -2)
        + jnp.roll(planes, 1, -1)
        + jnp.roll(planes, -1, -1)
    )
    summed = summed + COEF_FAR * (
        jnp.roll(planes, 2, -2)
        + jnp.roll(planes, -2, -2)
        + jnp.roll(planes, 2, -1)
        + jnp.roll(planes, -2, -1)
    )
    return summed.reshape(values.shape)


def complex_mul(first, second):
    return jnp.stack(
        [first[0] * second[0] - first[1] * second[1], first[0] * second[1] + first[1] * second[0]]
    )


def complex_div(first, second):
    denom = second[0] * second[0] + second[1] * second[1]
    return jnp.stack(
        [
            (first[0] * second[0] + first[1] * second[1]) / denom,
            (first[1] * second[0] - first[0] * second[1]) / denom,
        ]
    )


def bilinear(first, second):
    real_part = jnp.sum(first[0] * second[0] - first[1] * second[1], axis=(1, 2))
    imag_part = jnp.sum(first[0] * second[1] + first[1] * second[0], axis=(1, 2))
    return jnp.stack([real_part, imag_part])


def scaled(coeffs, values):
    return complex_mul(coeffs[:, :, None, None], values)


def shifted(values, potential, shift_re, shift_im):
    padded = padded_2(values, (("dom", 2),), 2)
    depth = values.shape[2]
    lap = -7.5 * values + plane_terms(values, GX)
    lap = lap + COEF_NEAR * (padded[:, :, 3 : 3 + depth] + padded[:, :, 1 : 1 + depth])
    lap = lap + COEF_FAR * (padded[:, :, 4 : 4 + depth] + padded[:, :, 0:depth])
    applied = -0.5 * lap + potential * values
    return jnp.stack(
        [
            shift_re * values[0] - shift_im * values[1] - applied[0],
            shift_re * values[1] + shift_im * values[0] - applied[1],
        ]
    )


def residual_sum(values):
    return lax.psum(bilinear(values, values), "dom")


def moment_terms(solution, residual, sources, angle_now, shift_re, shift_im):
    applied = jnp.stack(
        [
            shift_re * solution[0] - shift_im * solution[1] - sources[0] + residual[0],
            shift_re * solution[1] + shift_im * solution[0] - sources[1] + residual[1],
        ]
    )
    angles = (jnp.arange(MOMENTS).astype(jnp.float32) + 1.0) * angle_now
    coeffs = 0.25 * jnp.stack([jnp.cos(angles), jnp.sin(angles)])
    s_terms = complex_mul(coeffs[:, :, None, None, None], solution[:, None])
    h_terms = complex_mul(coeffs[:, :, None, None, None], applied[:, None])
    width = MOMENTS * solution.shape[1]
    return (s_terms.reshape(2, width, -1), h_terms.reshape(2, width, -1))


def gram_of(left, right):
    width = left.shape[1]
    joined = lax.dot_general(
        left.reshape(2 * width, -1),
        right.reshape(2 * width, -1),
        (((1,), (1,)), ((), ())),
        precision=lax.Precision.HIGHEST,
        preferred_element_type=jnp.float32,
    )
    blocks = joined.reshape(2, width, 2, width)
    return jnp.stack([blocks[0, :, 0] + blocks[1, :, 1], blocks[0, :, 1] - blocks[1, :, 0]])


def split_grid(sources, potential, iter_counts):
    complex_src = jnp.stack([sources, jnp.zeros_like(sources)])
    angle_now = (
        2.0 * math.pi * (lax.axis_index("point").astype(jnp.float32) + 0.5) / lax.axis_size("point")
    )
    shift_re = GAMMA + RADIUS * jnp.cos(angle_now)
    shift_im = RADIUS * jnp.sin(angle_now)
    limit = iter_counts[0]
    solution = jnp.zeros_like(complex_src)

    def one_turn(turn_idx, state):
        solution, residual, search, norm_now = state
        product = shifted(search, potential, shift_re, shift_im)
        curve = lax.psum(bilinear(search, product), "dom")
        step_size = complex_div(norm_now, curve)
        new_residual = residual - scaled(step_size, product)
        norm_next = residual_sum(new_residual)
        fresh = (
            solution + scaled(step_size, search),
            new_residual,
            new_residual + scaled(complex_div(norm_next, norm_now), search),
            norm_next,
        )
        keep_mask = turn_idx < limit
        return jax.tree.map(lambda newer, older: jnp.where(keep_mask, newer, older), fresh, state)

    start = (solution, complex_src, complex_src, residual_sum(complex_src))
    solution, residual, search, norm_now = lax.fori_loop(0, ITERS, one_turn, start)
    s_terms, h_terms = moment_terms(solution, residual, complex_src, angle_now, shift_re, shift_im)
    cells = sources.shape[1] * sources.shape[2] * lax.axis_size("dom")
    s_total, h_total = lax.psum((s_terms, h_terms), "point")
    gram_b, gram_a = lax.psum((gram_of(s_total, s_total), gram_of(s_total, h_total)), "dom")
    return (gram_b / cells, gram_a / cells)


Y_IN, X_IN = 2, 4
Y_OUT, X_OUT = GX // Y_IN, GX // X_IN
ROWS = Y_IN * X_IN
LANES = Y_OUT * X_OUT
SUB = 8
BASIS = ITERS + 1
CORES = 2
TOGETHER = 4
H_SCALE = 2.0 / COEF_NEAR
FAR_SCALED = 0.5 * H_SCALE * COEF_FAR


def pack_kernel(depth, groups, counts, rows, out, tile):
    columns = rows.shape[0] // (SUB * groups * depth + depth)
    first_level = columns * SUB * groups * depth
    source = lax.broadcasted_iota(jnp.int32, (LANES, LANES), 0)
    target = lax.broadcasted_iota(jnp.int32, (LANES, LANES), 1)
    inner = target // (LANES // ROWS)
    outer = target % (LANES // ROWS)
    cell = (outer // X_OUT * Y_IN + inner // X_IN) * GX + outer % X_OUT * X_IN + inner % X_IN
    swap = jnp.where(source == cell, 1.0, 0.0).astype(jnp.float32)
    parts = []
    for deep in range(depth):
        for group in range(groups):
            for column in range(columns):
                start = (group * SUB * columns + column) * depth + deep
                parts.append(rows[pl.ds(start, SUB, stride=columns * depth), :])
        parts.append(rows[pl.ds(first_level + deep, columns, stride=depth), :])
    mixed = exact_dot(jnp.concatenate(parts, axis=0), swap, ((1,), (0,)))
    block = LANES // ROWS
    lane_block = lax.broadcasted_iota(jnp.int32, (SUB, LANES), 1) // block
    row = lax.broadcasted_iota(jnp.int32, (SUB, LANES), 0)
    for deep in range(depth):
        base = deep * (groups + 1) * columns * SUB - deep * (columns - 1) * SUB
        for group in range(groups):
            pieces = [
                mixed[base + (group * columns + column) * SUB :][:SUB] for column in range(columns)
            ]
            for m in range(ROWS):
                value = pieces[m]
                for column in range(columns):
                    if column != m:
                        moved = pltpu.roll(pieces[column], (column - m) * block % LANES, 1)
                        value = jnp.where(lane_block == column, moved, value)
                start = ((deep * ROWS + m) * groups + group) * SUB
                out[start : start + SUB, :] = value
        piece = mixed[base + groups * columns * SUB :][:SUB]
        value = piece
        for far in range(1, columns):
            moved = pltpu.roll(pltpu.roll(piece, far * block, 1), columns - far, 0)
            value = jnp.where(lane_block == (row + far) % columns, moved, value)
        start = depth * ROWS * SUB * groups + deep * ROWS
        out[start : start + ROWS, :] = value
    tile[...] = jnp.broadcast_to(counts[...].astype(jnp.float32), (SUB, LANES))


def packed_block(sources, potential, iter_counts):
    count, depth, cells = sources.shape
    columns = cells // LANES
    rows = sources.reshape(count, depth, columns, LANES).transpose(0, 2, 1, 3).reshape(-1, LANES)
    levels = potential.reshape(depth, columns, LANES).transpose(1, 0, 2).reshape(-1, LANES)
    vmem = pl.BlockSpec(memory_space=pltpu.VMEM)
    size = depth * ROWS * (count + 1)
    return pl.pallas_call(
        functools.partial(pack_kernel, depth, count // SUB),
        out_shape=(
            jax.ShapeDtypeStruct((size, LANES), jnp.float32),
            jax.ShapeDtypeStruct((SUB, LANES), jnp.float32),
        ),
        in_specs=[vmem, vmem],
        out_specs=(vmem, vmem),
        compiler_params=pltpu.CompilerParams(vmem_limit_bytes=4 * 2**20),
        name="pack",
    )(iter_counts.reshape(1, 1), jnp.concatenate([rows, levels], axis=0))


def lane_sum(values):
    return jnp.broadcast_to(jnp.sum(values, axis=1, keepdims=True), values.shape)


def ratio(top, bottom):
    return jnp.where(bottom > 0.0, top / jnp.where(bottom > 0.0, bottom, 1.0), 0.0)


def tree_sum(values):
    while len(values) > 1:
        values = [sum(values[i : i + 2][1:], values[i]) for i in range(0, len(values), 2)]
    return values[0]


def plane_rows(vector, plane, rows):
    return [vector[plane, rows, m * LANES : (m + 1) * LANES] for m in range(ROWS)]


def y_parts(here, last_x, first_x):
    y_up = [pltpu.roll(value, LANES - X_OUT, 1) for value in here]
    y_down = [pltpu.roll(value, X_OUT, 1) for value in here]
    sums, edges = [], []
    for m in range(ROWS):
        near = y_down[m + X_IN] if m < X_IN else y_up[m - X_IN]
        sums.append(near + FAR_SCALED * (y_up[m] + y_down[m]))
        if m % X_IN < 2:
            edges.append(jnp.where(first_x, y_down[m], here[m]))
        else:
            edges.append(jnp.where(last_x, y_up[m], here[m]))
    return sums, edges


def apply_plane(vector, sums, edges, diagonal, plane, rows):
    planes = vector.shape[0]
    halos = []
    for m, edge in enumerate(plane_rows(edges, plane, rows)):
        halos.append(pltpu.roll(edge, LANES - 1 if m % X_IN < 2 else 1, 1))
    here, above, below, above_2, below_2 = (
        plane_rows(vector, jnp.bitwise_and(plane + (far + planes), planes - 1), rows)
        for far in (0, 1, -1, 2, -2)
    )
    y_sums = plane_rows(sums, plane, rows)
    out = []
    for yi in range(Y_IN):
        first = yi * X_IN
        line, halo = here[first : first + X_IN], halos[first : first + X_IN]
        wide = halo[2:] + line + halo[:2]
        for xi in range(X_IN):
            m = first + xi
            other = m + X_IN if yi == 0 else m - X_IN
            near = here[other] + (above[m] + below[m])
            far = above_2[m] + below_2[m]
            near = near + (wide[xi + 1] + wide[xi + 3])
            far = far + (wide[xi] + wide[xi + 4])
            level = diagonal[plane, :, m * LANES : (m + 1) * LANES]
            out.append((level * here[m] - y_sums[m]) - near - FAR_SCALED * far)
    return here, out


def cmul(first, second):
    return (
        first[0] * second[0] - first[1] * second[1],
        first[0] * second[1] + first[1] * second[0],
    )


def moment_coeffs(angle, shape):
    count = shape[0]
    lane = lax.broadcasted_iota(jnp.int32, shape, 1)
    moment = lax.rem(lane, MOMENTS * count) // count
    parts = []
    for func in (math.cos, math.sin):
        value = jnp.full(shape, 0.25 * func(angle), jnp.float32)
        for k in range(1, MOMENTS):
            value = jnp.where(moment == k, 0.25 * func((k + 1) * angle), value)
        parts.append(value)
    return parts


def weights_of(alphas, norms, limits):
    points = len(limits)
    count = limits[0].shape[0]
    shape = (points * count, LANES)
    lane = lax.broadcasted_iota(jnp.int32, shape, 1)
    left_half = lane < MOMENTS * count
    own = lax.rem(lane[:count], count) == lax.broadcasted_iota(jnp.int32, (count, LANES), 0)

    def stacked(values):
        return jnp.concatenate(values, axis=0)

    def constant(values):
        return stacked([jnp.full((count, LANES), value, jnp.float32) for value in values])

    limit = stacked(limits)
    betas = [stacked([ratio(norms[i + 1], norms[i])] * points) for i in range(ITERS - 1)]
    alphas = [stacked([alpha] * points) for alpha in alphas]
    zero = jnp.zeros(shape, jnp.float32)
    one = jnp.ones(shape, jnp.float32)
    angles = [2.0 * math.pi * (j + 0.5) / points for j in range(points)]
    shift = (
        constant([GAMMA + RADIUS * math.cos(angle) for angle in angles]),
        constant([RADIUS * math.sin(angle) for angle in angles]),
    )
    scaled_shift = (H_SCALE * shift[0], H_SCALE * shift[1])
    product = (one, zero)
    products = [product]
    links = []
    pivot = (scaled_shift[0] - alphas[0], scaled_shift[1])
    for i in range(ITERS):
        size = 1.0 / (pivot[0] * pivot[0] + pivot[1] * pivot[1])
        inverse = (pivot[0] * size, -pivot[1] * size)
        product = cmul(product, inverse)
        products.append(product)
        if i < ITERS - 1:
            link = (betas[i] * inverse[0], betas[i] * inverse[1])
            links.append(link)
            pivot = (scaled_shift[0] - alphas[i + 1] - link[0], scaled_shift[1] - link[1])
    solved = [None] * ITERS
    for i in reversed(range(ITERS)):
        value = (H_SCALE * products[i + 1][0], H_SCALE * products[i + 1][1])
        if i < ITERS - 1:
            step = cmul(links[i], solved[i + 1])
            value = (value[0] + step[0], value[1] + step[1])
        used = limit > i
        solved[i] = (jnp.where(used, value[0], 0.0), jnp.where(used, value[1], 0.0))
    applied = []
    for i in range(BASIS):
        left = limit == i
        rest = (jnp.where(left, products[i][0], 0.0), jnp.where(left, products[i][1], 0.0))
        if i < ITERS:
            turned = cmul(shift, solved[i])
            rest = (rest[0] + turned[0], rest[1] + turned[1])
        if i == 0:
            rest = (rest[0] - 1.0, rest[1])
        applied.append(rest)
    tail = applied[ITERS]
    for back, factor in ((1, alphas[ITERS - 1]), (2, betas[ITERS - 2])):
        part = applied[ITERS - back]
        applied[ITERS - back] = (part[0] - factor * tail[0], part[1] - factor * tail[1])
    moments = [moment_coeffs(angle, (count, LANES)) for angle in angles]
    moment = tuple(stacked([pair[part] for pair in moments]) for part in range(2))
    weights = []
    for i in range(BASIS):
        left = solved[i] if i < ITERS else (zero, zero)
        both = (
            jnp.where(left_half, left[0], applied[i][0]),
            jnp.where(left_half, left[1], applied[i][1]),
        )
        terms = cmul(moment, both)
        weights.append(
            [
                jnp.where(own, tree_sum([part[j * count :][:count] for j in range(points)]), 0.0)
                for part in terms
            ]
        )
    return weights


def exact_dot(first, second, dims):
    return lax.dot_general(
        first,
        second,
        (dims, ((), ())),
        precision=lax.Precision.HIGHEST,
        preferred_element_type=jnp.float32,
    )


def split(values):
    high = values.astype(jnp.bfloat16)
    return high, (values - high.astype(jnp.float32)).astype(jnp.bfloat16)


def krylov_kernel(parts, count, *refs):
    blocks, (highs, lows, applied, scalars) = refs[:parts], refs[parts : parts + 4]
    first_work, second_work, diagonal, sums, edges, partial = refs[parts + 4 :]
    planes = diagonal.shape[0]
    depth = planes // parts
    groups = count // SUB
    lane = lax.broadcasted_iota(jnp.int32, (SUB, LANES), 1)
    last_x = lax.rem(lane, X_OUT) == X_OUT - 1
    first_x = lax.rem(lane, X_OUT) == 0
    here = lax.axis_index("dom")
    for turn in range(parts):
        slab = jnp.bitwise_xor(here, turn) * depth
        for deep in range(depth):
            for m in range(ROWS):
                start = (deep * ROWS + m) * count
                lanes = slice(m * LANES, (m + 1) * LANES)
                value = blocks[turn][start : start + count, :]
                first_work[slab + deep, :, lanes] = value
                highs[0, slab + deep, :, lanes], lows[0, slab + deep, :, lanes] = split(value)
            start = depth * ROWS * count + deep * ROWS
            levels = H_SCALE * (blocks[turn][start : start + ROWS, :] + 3.75)
            for m in range(ROWS):
                level = jnp.broadcast_to(levels[m : m + 1, :], (SUB, LANES))
                diagonal[slab + deep, :, m * LANES : (m + 1) * LANES] = level
    second_work[...] = jnp.zeros_like(second_work)
    scalars[ITERS] = jnp.zeros((count, LANES), jnp.float32)

    all_rows = [pl.ds(group * SUB, SUB) for group in range(groups)]
    all_lanes = [slice(m * LANES, (m + 1) * LANES) for m in range(ROWS)]
    def keep_y_parts(plane, rows, values):
        for ref, parts_of in zip((sums, edges), y_parts(values, last_x, first_x)):
            for lanes, part in zip(all_lanes, parts_of):
                ref[plane, rows, lanes] = part

    def over_planes(one_plane):
        def turn(step, sums):
            for deep in range(TOGETHER):
                terms = one_plane(step * TOGETHER + deep)
                sums = [total + term for total, term in zip(sums, terms)]
            return tuple(sums)

        blank = jnp.zeros((SUB, LANES), jnp.float32)
        return lax.fori_loop(0, planes // TOGETHER, turn, (blank,) * groups)

    def keep_norms(terms):
        for rows, term in zip(all_rows, terms):
            partial[rows, :] = term

    def first_plane(plane):
        terms = []
        for rows in all_rows:
            values = plane_rows(first_work, plane, rows)
            keep_y_parts(plane, rows, values)
            terms.append(tree_sum([value * value for value in values]))
        return terms

    keep_norms(over_planes(first_plane))

    def update_pass(i, work, before, alphas, betas):
        def one_plane(plane):
            columns, terms = [], []
            for group, rows in enumerate(all_rows):
                values = []
                for lanes in all_lanes:
                    value = applied[plane, rows, lanes] - betas[group] * before[plane, rows, lanes]
                    value = value - alphas[group] * work[plane, rows, lanes]
                    before[plane, rows, lanes] = value
                    values.append(value)
                keep_y_parts(plane, rows, values)
                terms.append(tree_sum([value * value for value in values]))
                columns.append(values)
            for lanes, *column in zip(all_lanes, *columns):
                high, low = split(jnp.concatenate(column, axis=0))
                highs[i + 1, plane, :, lanes] = high
                lows[i + 1, plane, :, lanes] = low
            return terms

        keep_norms(over_planes(one_plane))

    def half_turn(i, work, before, may_end):
        norms = [lane_sum(partial[rows, :]) for rows in all_rows]
        betas = [
            ratio(norm, scalars[ITERS + i, rows, :]) for norm, rows in zip(norms, all_rows)
        ]
        inverses = [ratio(jnp.ones_like(norm), norm) for norm in norms]
        for norm, rows in zip(norms, all_rows):
            scalars[ITERS + 1 + i, rows, :] = norm

        def one_plane(plane):
            terms = []
            for rows in all_rows:
                value, out = apply_plane(work, sums, edges, diagonal, plane, rows)
                for m, lanes in enumerate(all_lanes):
                    applied[plane, rows, lanes] = out[m]
                terms.append(tree_sum([value[m] * out[m] for m in range(ROWS)]))
            return terms

        curves = over_planes(one_plane)
        alphas = [lane_sum(curves[g]) * inverses[g] for g in range(groups)]
        for alpha, rows in zip(alphas, all_rows):
            scalars[i, rows, :] = alpha
        if may_end:
            pl.when(i < ITERS - 1)(lambda: update_pass(i, work, before, alphas, betas))
        else:
            update_pass(i, work, before, alphas, betas)

    def turn(step, carry):
        half_turn(2 * step, first_work, second_work, False)
        half_turn(2 * step + 1, second_work, first_work, True)
        return carry

    lax.fori_loop(0, ITERS // 2, turn, 0)


def gram_kernel(points, scalars, *refs):
    tiles = refs[:points]
    highs, lows, applied, out_b, out_a, limits = refs[points:]
    planes, count, _ = applied.shape
    groups = count // SUB
    size = BASIS * count
    here = lax.axis_index("point")
    core = jnp.bitwise_and(lax.axis_index("dom"), CORES - 1)
    for far, tile in zip((0, 1 + core, 3, 2 - core), tiles):
        limits[jnp.bitwise_xor(here, far)] = tile[...]

    bounds = [jnp.concatenate([limits[j]] * groups, axis=0) for j in range(points)]
    alphas = [scalars[i] for i in range(ITERS)]
    norms = [scalars[ITERS + 1 + i] for i in range(ITERS)]
    weights = weights_of(alphas, norms, bounds)
    real = jnp.concatenate([pair[0] for pair in weights], axis=0)
    imag = jnp.concatenate([pair[1] for pair in weights], axis=0)
    gram = None
    for plane in range(planes):
        last_high, last_low = split(applied[plane])
        high = jnp.concatenate([highs[i, plane] for i in range(ITERS)] + [last_high], axis=0)
        low = jnp.concatenate([lows[i, plane] for i in range(ITERS)] + [last_low], axis=0)
        product = lax.dot_general(
            jnp.concatenate([high, low], axis=0),
            high,
            (((1,), (1,)), ((), ())),
            preferred_element_type=jnp.float32,
        )
        gram = product if gram is None else gram + product
    cross = gram[size:, :]
    pairs = gram[:size, :] + cross + cross.T
    right = exact_dot(pairs, jnp.concatenate([real, imag], axis=1), ((1,), (0,)))
    half = MOMENTS * count
    left = jnp.concatenate([real[:, :half], imag[:, :half]], axis=1)
    joined = exact_dot(left.T, right, ((1,), (0,)))
    scale = 1.0 / (planes * ROWS * LANES)
    width = 2 * half
    real = (joined[:half, :width] + joined[half:, width:]) * scale
    imag = (joined[:half, width:] - joined[half:, :width]) * scale
    out_b[0] = real[:, :half]
    out_b[1] = imag[:, :half]
    out_a[0] = real[:, half:]
    out_a[1] = imag[:, half:]


def swapped(values, axis, size, mask):
    return lax.ppermute(values, axis, [(index ^ mask, index) for index in range(size)])


def whole_grid(sources, potential, iter_counts, *, parts, points):
    count, depth, _ = sources.shape
    planes = parts * depth
    block, tile = packed_block(sources, potential, iter_counts)
    even = [block] + [swapped(block, "dom", parts, mask) for mask in range(CORES, parts, CORES)]
    mixed = [
        ((point ^ (1 + part % CORES)) * parts + part, point * parts + part)
        for point in range(points)
        for part in range(parts)
    ]
    tiles = [lax.ppermute(tile, ("point", "dom"), mixed), swapped(tile, "point", points, 3)]
    even[1], *tiles = lax.optimization_barrier((even[1], *tiles))
    tiles.append(swapped(tiles[0], "dom", parts, 1))
    odd = [swapped(value, "dom", parts, 1) for value in even]
    blocks = [value for pair in zip(even, odd) for value in pair]
    vmem = pl.BlockSpec(memory_space=pltpu.VMEM)
    vector = (planes, count, ROWS * LANES)
    cells = planes * ROWS * LANES
    highs, lows, applied, scalars = pl.pallas_call(
        functools.partial(krylov_kernel, parts, count),
        out_shape=(
            jax.ShapeDtypeStruct((ITERS,) + vector, jnp.bfloat16),
            jax.ShapeDtypeStruct((ITERS,) + vector, jnp.bfloat16),
            jax.ShapeDtypeStruct(vector, jnp.float32),
            jax.ShapeDtypeStruct((2 * ITERS + 1, count, LANES), jnp.float32),
        ),
        in_specs=[vmem] * parts,
        out_specs=(vmem,) * 4,
        scratch_shapes=[
            pltpu.VMEM(vector, jnp.float32),
            pltpu.VMEM(vector, jnp.float32),
            pltpu.VMEM((planes, SUB, ROWS * LANES), jnp.float32),
            pltpu.VMEM(vector, jnp.float32),
            pltpu.VMEM(vector, jnp.float32),
            pltpu.VMEM((count, LANES), jnp.float32),
        ],
        compiler_params=pltpu.CompilerParams(vmem_limit_bytes=16 * 2**20),
        name="krylov",
    )(*blocks)
    width = MOMENTS * count
    out = jax.ShapeDtypeStruct((2, width, width), jnp.float32)
    return pl.pallas_call(
        functools.partial(gram_kernel, points),
        out_shape=(out, out),
        in_specs=[vmem] * (4 + points),
        out_specs=(vmem, vmem),
        scratch_shapes=[pltpu.VMEM((points, SUB, LANES), jnp.float32)],
        compiler_params=pltpu.CompilerParams(vmem_limit_bytes=16 * 2**20),
        name="gram",
    )(scalars, tile, *tiles, highs, lows, applied)


def on_device(sources, potential, iter_counts):
    parts, points = lax.axis_size("dom"), lax.axis_size("point")
    count, depth, cells = sources.shape
    held = BASIS * count * parts * depth * cells * 4
    fits = (
        held <= 16 * 2**20
        and parts == 8
        and points == 4
        and count == 2 * SUB
        and 2 * MOMENTS * count == LANES
        and parts * depth == 16
        and cells == GX * GX == ROWS * LANES
    )
    if not fits:
        return split_grid(sources, potential, iter_counts)
    return whole_grid(sources, potential, iter_counts, parts=parts, points=points)


def solution(mesh):
    placed = (P(None, "dom", None), P("dom", None), P("point"))
    return jax.shard_map(
        on_device, mesh=mesh, in_specs=placed, out_specs=(P(), P()), check_vma=False
    )
```

```python
import functools
import math

import jax
import jax.numpy as jnp
from jax import lax
from jax.experimental import pallas as pl
from jax.experimental.pallas import tpu as pltpu
from jax.sharding import PartitionSpec as P

MOMENTS = 4
ITERS = 6
GX = 32


COEF_NEAR = 4.0 / 3.0
COEF_FAR = -1.0 / 12.0
GAMMA = 2.0
RADIUS = 1.5


def padded_2(block, sides, width):
    for axis, dim in sides:
        count = lax.axis_size(axis)
        forward = [(i, i + 1) for i in range(count - 1)]
        forward.append((count - 1, 0))
        backward = [(target, source) for source, target in forward]
        low = lax.ppermute(
            lax.slice_in_dim(block, block.shape[dim] - width, None, axis=dim), axis, forward
        )
        high = lax.ppermute(lax.slice_in_dim(block, 0, width, axis=dim), axis, backward)
        block = jnp.concatenate([low, block, high], axis=dim)
    return block


def plane_terms(values, side):
    lead = values.shape[:-1]
    planes = values.reshape(lead + (side, side))
    summed = COEF_NEAR * (
        jnp.roll(planes, 1, -2)
        + jnp.roll(planes, -1, -2)
        + jnp.roll(planes, 1, -1)
        + jnp.roll(planes, -1, -1)
    )
    summed = summed + COEF_FAR * (
        jnp.roll(planes, 2, -2)
        + jnp.roll(planes, -2, -2)
        + jnp.roll(planes, 2, -1)
        + jnp.roll(planes, -2, -1)
    )
    return summed.reshape(values.shape)


def complex_mul(first, second):
    return jnp.stack(
        [first[0] * second[0] - first[1] * second[1], first[0] * second[1] + first[1] * second[0]]
    )


def complex_div(first, second):
    denom = second[0] * second[0] + second[1] * second[1]
    return jnp.stack(
        [
            (first[0] * second[0] + first[1] * second[1]) / denom,
            (first[1] * second[0] - first[0] * second[1]) / denom,
        ]
    )


def bilinear(first, second):
    real_part = jnp.sum(first[0] * second[0] - first[1] * second[1], axis=(1, 2))
    imag_part = jnp.sum(first[0] * second[1] + first[1] * second[0], axis=(1, 2))
    return jnp.stack([real_part, imag_part])


def scaled(coeffs, values):
    return complex_mul(coeffs[:, :, None, None], values)


def shifted(values, potential, shift_re, shift_im):
    padded = padded_2(values, (("dom", 2),), 2)
    depth = values.shape[2]
    lap = -7.5 * values + plane_terms(values, GX)
    lap = lap + COEF_NEAR * (padded[:, :, 3 : 3 + depth] + padded[:, :, 1 : 1 + depth])
    lap = lap + COEF_FAR * (padded[:, :, 4 : 4 + depth] + padded[:, :, 0:depth])
    applied = -0.5 * lap + potential * values
    return jnp.stack(
        [
            shift_re * values[0] - shift_im * values[1] - applied[0],
            shift_re * values[1] + shift_im * values[0] - applied[1],
        ]
    )


def residual_sum(values):
    return lax.psum(bilinear(values, values), "dom")


def moment_terms(solution, residual, sources, angle_now, shift_re, shift_im):
    applied = jnp.stack(
        [
            shift_re * solution[0] - shift_im * solution[1] - sources[0] + residual[0],
            shift_re * solution[1] + shift_im * solution[0] - sources[1] + residual[1],
        ]
    )
    angles = (jnp.arange(MOMENTS).astype(jnp.float32) + 1.0) * angle_now
    coeffs = 0.25 * jnp.stack([jnp.cos(angles), jnp.sin(angles)])
    s_terms = complex_mul(coeffs[:, :, None, None, None], solution[:, None])
    h_terms = complex_mul(coeffs[:, :, None, None, None], applied[:, None])
    width = MOMENTS * solution.shape[1]
    return (s_terms.reshape(2, width, -1), h_terms.reshape(2, width, -1))


def gram_of(left, right):
    width = left.shape[1]
    joined = lax.dot_general(
        left.reshape(2 * width, -1),
        right.reshape(2 * width, -1),
        (((1,), (1,)), ((), ())),
        precision=lax.Precision.HIGHEST,
        preferred_element_type=jnp.float32,
    )
    blocks = joined.reshape(2, width, 2, width)
    return jnp.stack([blocks[0, :, 0] + blocks[1, :, 1], blocks[0, :, 1] - blocks[1, :, 0]])


def split_grid(sources, potential, iter_counts):
    complex_src = jnp.stack([sources, jnp.zeros_like(sources)])
    angle_now = (
        2.0 * math.pi * (lax.axis_index("point").astype(jnp.float32) + 0.5) / lax.axis_size("point")
    )
    shift_re = GAMMA + RADIUS * jnp.cos(angle_now)
    shift_im = RADIUS * jnp.sin(angle_now)
    limit = iter_counts[0]
    solution = jnp.zeros_like(complex_src)

    def one_turn(turn_idx, state):
        solution, residual, search, norm_now = state
        product = shifted(search, potential, shift_re, shift_im)
        curve = lax.psum(bilinear(search, product), "dom")
        step_size = complex_div(norm_now, curve)
        new_residual = residual - scaled(step_size, product)
        norm_next = residual_sum(new_residual)
        fresh = (
            solution + scaled(step_size, search),
            new_residual,
            new_residual + scaled(complex_div(norm_next, norm_now), search),
            norm_next,
        )
        keep_mask = turn_idx < limit
        return jax.tree.map(lambda newer, older: jnp.where(keep_mask, newer, older), fresh, state)

    start = (solution, complex_src, complex_src, residual_sum(complex_src))
    solution, residual, search, norm_now = lax.fori_loop(0, ITERS, one_turn, start)
    s_terms, h_terms = moment_terms(solution, residual, complex_src, angle_now, shift_re, shift_im)
    cells = sources.shape[1] * sources.shape[2] * lax.axis_size("dom")
    s_total, h_total = lax.psum((s_terms, h_terms), "point")
    gram_b, gram_a = lax.psum((gram_of(s_total, s_total), gram_of(s_total, h_total)), "dom")
    return (gram_b / cells, gram_a / cells)


Y_IN, X_IN = 2, 4
Y_OUT, X_OUT = GX // Y_IN, GX // X_IN
ROWS = Y_IN * X_IN
LANES = Y_OUT * X_OUT
SUB = 8
BASIS = ITERS + 1
CORES = 2
H_SCALE = 2.0 / COEF_NEAR
FAR_SCALED = 0.5 * H_SCALE * COEF_FAR


def pack_kernel(depth, groups, counts, rows, out, tile):
    columns = rows.shape[0] // (SUB * groups * depth + depth)
    first_level = columns * SUB * groups * depth
    source = lax.broadcasted_iota(jnp.int32, (LANES, LANES), 0)
    target = lax.broadcasted_iota(jnp.int32, (LANES, LANES), 1)
    inner = target // (LANES // ROWS)
    outer = target % (LANES // ROWS)
    cell = (outer // X_OUT * Y_IN + inner // X_IN) * GX + outer % X_OUT * X_IN + inner % X_IN
    swap = jnp.where(source == cell, 1.0, 0.0).astype(jnp.float32)
    parts = []
    for deep in range(depth):
        for group in range(groups):
            for column in range(columns):
                start = (group * SUB * columns + column) * depth + deep
                parts.append(rows[pl.ds(start, SUB, stride=columns * depth), :])
        parts.append(rows[pl.ds(first_level + deep, columns, stride=depth), :])
    mixed = exact_dot(jnp.concatenate(parts, axis=0), swap, ((1,), (0,)))
    block = LANES // ROWS
    lane_block = lax.broadcasted_iota(jnp.int32, (SUB, LANES), 1) // block
    row = lax.broadcasted_iota(jnp.int32, (SUB, LANES), 0)
    for deep in range(depth):
        base = deep * (groups + 1) * columns * SUB - deep * (columns - 1) * SUB
        for group in range(groups):
            pieces = [
                mixed[base + (group * columns + column) * SUB :][:SUB] for column in range(columns)
            ]
            for m in range(ROWS):
                value = pieces[m]
                for column in range(columns):
                    if column != m:
                        moved = pltpu.roll(pieces[column], (column - m) * block % LANES, 1)
                        value = jnp.where(lane_block == column, moved, value)
                start = ((deep * ROWS + m) * groups + group) * SUB
                out[start : start + SUB, :] = value
        piece = mixed[base + groups * columns * SUB :][:SUB]
        value = piece
        for far in range(1, columns):
            moved = pltpu.roll(pltpu.roll(piece, far * block, 1), columns - far, 0)
            value = jnp.where(lane_block == (row + far) % columns, moved, value)
        start = depth * ROWS * SUB * groups + deep * ROWS
        out[start : start + ROWS, :] = value
    tile[...] = jnp.broadcast_to(counts[...].astype(jnp.float32), tile.shape)


def packed_block(sources, potential, iter_counts):
    count, depth, cells = sources.shape
    columns = cells // LANES
    rows = sources.reshape(count, depth, columns, LANES).transpose(0, 2, 1, 3).reshape(-1, LANES)
    levels = potential.reshape(depth, columns, LANES).transpose(1, 0, 2).reshape(-1, LANES)
    vmem = pl.BlockSpec(memory_space=pltpu.VMEM)
    size = depth * ROWS * (count + 1)
    return pl.pallas_call(
        functools.partial(pack_kernel, depth, count // SUB),
        out_shape=(
            jax.ShapeDtypeStruct((size, LANES), jnp.float32),
            jax.ShapeDtypeStruct((136, LANES), jnp.float32),
        ),
        in_specs=[vmem, vmem],
        out_specs=(vmem, vmem),
        compiler_params=pltpu.CompilerParams(vmem_limit_bytes=4 * 2**20),
        name="pack",
    )(iter_counts.reshape(1, 1), jnp.concatenate([rows, levels], axis=0))


def lane_sum(values):
    return jnp.broadcast_to(jnp.sum(values, axis=1, keepdims=True), values.shape)


def ratio(top, bottom):
    return jnp.where(bottom > 0.0, top / jnp.where(bottom > 0.0, bottom, 1.0), 0.0)


def tree_sum(values):
    while len(values) > 1:
        values = [sum(values[i : i + 2][1:], values[i]) for i in range(0, len(values), 2)]
    return values[0]


def plane_rows(vector, plane, rows):
    return [vector[plane, rows, m * LANES : (m + 1) * LANES] for m in range(ROWS)]


def y_parts(here, last_x, first_x):
    y_up = [pltpu.roll(value, LANES - X_OUT, 1) for value in here]
    y_down = [pltpu.roll(value, X_OUT, 1) for value in here]
    sums, edges = [], []
    for m in range(ROWS):
        near = y_down[m + X_IN] if m < X_IN else y_up[m - X_IN]
        sums.append(near + FAR_SCALED * (y_up[m] + y_down[m]))
        if m % X_IN < 2:
            edges.append(jnp.where(first_x, y_down[m], here[m]))
        else:
            edges.append(jnp.where(last_x, y_up[m], here[m]))
    return sums, edges


def apply_plane(vector, sums, edges, diagonal, plane, rows):
    planes = vector.shape[0]
    halos = []
    for m, edge in enumerate(plane_rows(edges, plane, rows)):
        halos.append(pltpu.roll(edge, LANES - 1 if m % X_IN < 2 else 1, 1))
    here, above, below, above_2, below_2 = (
        plane_rows(vector, (plane + far) % planes, rows) for far in (0, 1, -1, 2, -2)
    )
    y_sums = plane_rows(sums, plane, rows)
    out = []
    for yi in range(Y_IN):
        first = yi * X_IN
        line, halo = here[first : first + X_IN], halos[first : first + X_IN]
        wide = halo[2:] + line + halo[:2]
        for xi in range(X_IN):
            m = first + xi
            other = m + X_IN if yi == 0 else m - X_IN
            near = here[other] + (above[m] + below[m])
            far = above_2[m] + below_2[m]
            near = near + (wide[xi + 1] + wide[xi + 3])
            far = far + (wide[xi] + wide[xi + 4])
            level = diagonal[plane, :, m * LANES : (m + 1) * LANES]
            out.append((level * here[m] - y_sums[m]) - near - FAR_SCALED * far)
    return here, out


def cmul(first, second):
    return (
        first[0] * second[0] - first[1] * second[1],
        first[0] * second[1] + first[1] * second[0],
    )


def moment_coeffs(angle, shape):
    count = shape[0]
    lane = lax.broadcasted_iota(jnp.int32, shape, 1)
    moment = lax.rem(lane, MOMENTS * count) // count
    parts = []
    for func in (math.cos, math.sin):
        value = jnp.full(shape, 0.25 * func(angle), jnp.float32)
        for k in range(1, MOMENTS):
            value = jnp.where(moment == k, 0.25 * func((k + 1) * angle), value)
        parts.append(value)
    return parts


def weights_of(alphas, norms, limits):
    points = len(limits)
    count = limits[0].shape[0]
    shape = (points * count, LANES)
    lane = lax.broadcasted_iota(jnp.int32, shape, 1)
    left_half = lane < MOMENTS * count
    own = lax.rem(lane[:count], count) == lax.broadcasted_iota(jnp.int32, (count, LANES), 0)

    def stacked(values):
        return jnp.concatenate(values, axis=0)

    def constant(values):
        return stacked([jnp.full((count, LANES), value, jnp.float32) for value in values])

    limit = stacked(limits)
    betas = [stacked([ratio(norms[i + 1], norms[i])] * points) for i in range(ITERS - 1)]
    alphas = [stacked([alpha] * points) for alpha in alphas]
    zero = jnp.zeros(shape, jnp.float32)
    one = jnp.ones(shape, jnp.float32)
    angles = [2.0 * math.pi * (j + 0.5) / points for j in range(points)]
    shift = (
        constant([GAMMA + RADIUS * math.cos(angle) for angle in angles]),
        constant([RADIUS * math.sin(angle) for angle in angles]),
    )
    scaled_shift = (H_SCALE * shift[0], H_SCALE * shift[1])
    product = (one, zero)
    products = [product]
    links = []
    pivot = (scaled_shift[0] - alphas[0], scaled_shift[1])
    for i in range(ITERS):
        size = 1.0 / (pivot[0] * pivot[0] + pivot[1] * pivot[1])
        inverse = (pivot[0] * size, -pivot[1] * size)
        product = cmul(product, inverse)
        products.append(product)
        if i < ITERS - 1:
            link = (betas[i] * inverse[0], betas[i] * inverse[1])
            links.append(link)
            pivot = (scaled_shift[0] - alphas[i + 1] - link[0], scaled_shift[1] - link[1])
    solved = [None] * ITERS
    for i in reversed(range(ITERS)):
        value = (H_SCALE * products[i + 1][0], H_SCALE * products[i + 1][1])
        if i < ITERS - 1:
            step = cmul(links[i], solved[i + 1])
            value = (value[0] + step[0], value[1] + step[1])
        used = limit > i
        solved[i] = (jnp.where(used, value[0], 0.0), jnp.where(used, value[1], 0.0))
    applied = []
    for i in range(BASIS):
        left = limit == i
        rest = (jnp.where(left, products[i][0], 0.0), jnp.where(left, products[i][1], 0.0))
        if i < ITERS:
            turned = cmul(shift, solved[i])
            rest = (rest[0] + turned[0], rest[1] + turned[1])
        if i == 0:
            rest = (rest[0] - 1.0, rest[1])
        applied.append(rest)
    tail = applied[ITERS]
    for back, factor in ((1, alphas[ITERS - 1]), (2, betas[ITERS - 2])):
        part = applied[ITERS - back]
        applied[ITERS - back] = (part[0] - factor * tail[0], part[1] - factor * tail[1])
    moments = [moment_coeffs(angle, (count, LANES)) for angle in angles]
    moment = tuple(stacked([pair[part] for pair in moments]) for part in range(2))
    weights = []
    for i in range(BASIS):
        left = solved[i] if i < ITERS else (zero, zero)
        both = (
            jnp.where(left_half, left[0], applied[i][0]),
            jnp.where(left_half, left[1], applied[i][1]),
        )
        terms = cmul(moment, both)
        weights.append(
            [
                jnp.where(own, tree_sum([part[j * count :][:count] for j in range(points)]), 0.0)
                for part in terms
            ]
        )
    return weights


def exact_dot(first, second, dims):
    return lax.dot_general(
        first,
        second,
        (dims, ((), ())),
        precision=lax.Precision.HIGHEST,
        preferred_element_type=jnp.float32,
    )


def split(values):
    high = values.astype(jnp.bfloat16)
    return high, (values - high.astype(jnp.float32)).astype(jnp.bfloat16)


def krylov_kernel(parts, count, *refs):
    blocks, (highs, lows, applied, scalars) = refs[:parts], refs[parts : parts + 4]
    first_work, second_work, diagonal, sums, edges, partial = refs[parts + 4 :]
    planes = diagonal.shape[0]
    depth = planes // parts
    groups = count // SUB
    lane = lax.broadcasted_iota(jnp.int32, (SUB, LANES), 1)
    last_x = lax.rem(lane, X_OUT) == X_OUT - 1
    first_x = lax.rem(lane, X_OUT) == 0
    here = lax.axis_index("dom")
    for turn in range(parts):
        slab = jnp.bitwise_xor(here, turn) * depth
        for deep in range(depth):
            for m in range(ROWS):
                start = (deep * ROWS + m) * count
                lanes = slice(m * LANES, (m + 1) * LANES)
                value = blocks[turn][start : start + count, :]
                first_work[slab + deep, :, lanes] = value
                highs[0, slab + deep, :, lanes], lows[0, slab + deep, :, lanes] = split(value)
            start = depth * ROWS * count + deep * ROWS
            levels = H_SCALE * (blocks[turn][start : start + ROWS, :] + 3.75)
            for m in range(ROWS):
                level = jnp.broadcast_to(levels[m : m + 1, :], (SUB, LANES))
                diagonal[slab + deep, :, m * LANES : (m + 1) * LANES] = level
    second_work[...] = jnp.zeros_like(second_work)
    scalars[ITERS] = jnp.zeros((count, LANES), jnp.float32)

    all_rows = [pl.ds(group * SUB, SUB) for group in range(groups)]
    all_lanes = [slice(m * LANES, (m + 1) * LANES) for m in range(ROWS)]
    def keep_y_parts(plane, rows, values):
        for ref, parts_of in zip((sums, edges), y_parts(values, last_x, first_x)):
            for lanes, part in zip(all_lanes, parts_of):
                ref[plane, rows, lanes] = part

    for group, rows in enumerate(all_rows):
        norm = []
        for plane in range(planes):
            values = plane_rows(first_work, plane, rows)
            keep_y_parts(plane, rows, values)
            norm.append(tree_sum([value * value for value in values]))
        partial[rows, :] = tree_sum(norm)

    def update_pass(i, work, before, alphas, betas):
        norm = [[] for _ in range(groups)]
        for plane in range(planes):
            columns = []
            for group, rows in enumerate(all_rows):
                values = []
                for lanes in all_lanes:
                    value = applied[plane, rows, lanes] - betas[group] * before[plane, rows, lanes]
                    value = value - alphas[group] * work[plane, rows, lanes]
                    before[plane, rows, lanes] = value
                    values.append(value)
                keep_y_parts(plane, rows, values)
                norm[group].append(tree_sum([value * value for value in values]))
                columns.append(values)
            for lanes, *column in zip(all_lanes, *columns):
                high, low = split(jnp.concatenate(column, axis=0))
                highs[i + 1, plane, :, lanes] = high
                lows[i + 1, plane, :, lanes] = low
        for rows, terms in zip(all_rows, norm):
            partial[rows, :] = tree_sum(terms)

    def half_turn(i, work, before, may_end):
        norms = [lane_sum(partial[rows, :]) for rows in all_rows]
        betas = [
            ratio(norm, scalars[ITERS + i, rows, :]) for norm, rows in zip(norms, all_rows)
        ]
        inverses = [ratio(jnp.ones_like(norm), norm) for norm in norms]
        for norm, rows in zip(norms, all_rows):
            scalars[ITERS + 1 + i, rows, :] = norm
        curve = [[] for _ in range(groups)]
        for plane in range(planes):
            for group, rows in enumerate(all_rows):
                value, out = apply_plane(work, sums, edges, diagonal, plane, rows)
                for m, lanes in enumerate(all_lanes):
                    applied[plane, rows, lanes] = out[m]
                curve[group].append(tree_sum([value[m] * out[m] for m in range(ROWS)]))
        alphas = [lane_sum(tree_sum(curve[g])) * inverses[g] for g in range(groups)]
        for alpha, rows in zip(alphas, all_rows):
            scalars[i, rows, :] = alpha
        if may_end:
            pl.when(i < ITERS - 1)(lambda: update_pass(i, work, before, alphas, betas))
        else:
            update_pass(i, work, before, alphas, betas)

    def turn(step, carry):
        half_turn(2 * step, first_work, second_work, False)
        half_turn(2 * step + 1, second_work, first_work, True)
        return carry

    lax.fori_loop(0, ITERS // 2, turn, 0)


def gram_kernel(points, scalars, *refs):
    tiles = refs[:points]
    highs, lows, applied, out_b, out_a, limits = refs[points:]
    planes, count, _ = applied.shape
    groups = count // SUB
    size = BASIS * count
    here = lax.axis_index("point")
    core = jnp.bitwise_and(lax.axis_index("dom"), CORES - 1)
    for far, tile in zip((0, 1 + core, 3, 2 - core), tiles):
        limits[jnp.bitwise_xor(here, far)] = tile[:SUB, :]

    bounds = [jnp.concatenate([limits[j]] * groups, axis=0) for j in range(points)]
    alphas = [scalars[i] for i in range(ITERS)]
    norms = [scalars[ITERS + 1 + i] for i in range(ITERS)]
    weights = weights_of(alphas, norms, bounds)
    real = jnp.concatenate([pair[0] for pair in weights], axis=0)
    imag = jnp.concatenate([pair[1] for pair in weights], axis=0)
    gram = None
    for plane in range(planes):
        last_high, last_low = split(applied[plane])
        high = jnp.concatenate([highs[i, plane] for i in range(ITERS)] + [last_high], axis=0)
        low = jnp.concatenate([lows[i, plane] for i in range(ITERS)] + [last_low], axis=0)
        product = lax.dot_general(
            jnp.concatenate([high, low], axis=0),
            high,
            (((1,), (1,)), ((), ())),
            preferred_element_type=jnp.float32,
        )
        gram = product if gram is None else gram + product
    cross = gram[size:, :]
    pairs = gram[:size, :] + cross + cross.T
    right = exact_dot(pairs, jnp.concatenate([real, imag], axis=1), ((1,), (0,)))
    half = MOMENTS * count
    left = jnp.concatenate([real[:, :half], imag[:, :half]], axis=1)
    joined = exact_dot(left.T, right, ((1,), (0,)))
    scale = 1.0 / (planes * ROWS * LANES)
    width = 2 * half
    real = (joined[:half, :width] + joined[half:, width:]) * scale
    imag = (joined[:half, width:] - joined[half:, :width]) * scale
    out_b[0] = real[:, :half]
    out_b[1] = imag[:, :half]
    out_a[0] = real[:, half:]
    out_a[1] = imag[:, half:]


def swapped(values, axis, size, mask):
    return lax.ppermute(values, axis, [(index ^ mask, index) for index in range(size)])


def whole_grid(sources, potential, iter_counts, *, parts, points):
    count, depth, _ = sources.shape
    planes = parts * depth
    block, tile = packed_block(sources, potential, iter_counts)
    even = [block] + [swapped(block, "dom", parts, mask) for mask in range(CORES, parts, CORES)]
    mixed = [
        ((point ^ (1 + part % CORES)) * parts + part, point * parts + part)
        for point in range(points)
        for part in range(parts)
    ]
    tiles = [lax.ppermute(tile, ("point", "dom"), mixed), swapped(tile, "point", points, 3)]
    tiles = list(lax.optimization_barrier(tuple(tiles)))
    tiles.append(swapped(tiles[0], "dom", parts, 1))
    own, even[1] = lax.optimization_barrier((block, even[1]))
    odd = [swapped(value, "dom", parts, 1) for value in [own] + even[1:]]
    blocks = [value for pair in zip(even, odd) for value in pair]
    vmem = pl.BlockSpec(memory_space=pltpu.VMEM)
    vector = (planes, count, ROWS * LANES)
    cells = planes * ROWS * LANES
    highs, lows, applied, scalars = pl.pallas_call(
        functools.partial(krylov_kernel, parts, count),
        out_shape=(
            jax.ShapeDtypeStruct((ITERS,) + vector, jnp.bfloat16),
            jax.ShapeDtypeStruct((ITERS,) + vector, jnp.bfloat16),
            jax.ShapeDtypeStruct(vector, jnp.float32),
            jax.ShapeDtypeStruct((2 * ITERS + 1, count, LANES), jnp.float32),
        ),
        in_specs=[vmem] * parts,
        out_specs=(vmem,) * 4,
        scratch_shapes=[
            pltpu.VMEM(vector, jnp.float32),
            pltpu.VMEM(vector, jnp.float32),
            pltpu.VMEM((planes, SUB, ROWS * LANES), jnp.float32),
            pltpu.VMEM(vector, jnp.float32),
            pltpu.VMEM(vector, jnp.float32),
            pltpu.VMEM((count, LANES), jnp.float32),
        ],
        compiler_params=pltpu.CompilerParams(vmem_limit_bytes=16 * 2**20),
        name="krylov",
    )(*blocks)
    width = MOMENTS * count
    out = jax.ShapeDtypeStruct((2, width, width), jnp.float32)
    return pl.pallas_call(
        functools.partial(gram_kernel, points),
        out_shape=(out, out),
        in_specs=[vmem] * (4 + points),
        out_specs=(vmem, vmem),
        scratch_shapes=[pltpu.VMEM((points, SUB, LANES), jnp.float32)],
        compiler_params=pltpu.CompilerParams(vmem_limit_bytes=16 * 2**20),
        name="gram",
    )(scalars, tile, *tiles, highs, lows, applied)


def on_device(sources, potential, iter_counts):
    parts, points = lax.axis_size("dom"), lax.axis_size("point")
    count, depth, cells = sources.shape
    held = BASIS * count * parts * depth * cells * 4
    fits = (
        held <= 16 * 2**20
        and parts == 8
        and points == 4
        and count == 2 * SUB
        and 2 * MOMENTS * count == LANES
        and parts * depth == 16
        and cells == GX * GX == ROWS * LANES
    )
    if not fits:
        return split_grid(sources, potential, iter_counts)
    return whole_grid(sources, potential, iter_counts, parts=parts, points=points)


def solution(mesh):
    placed = (P(None, "dom", None), P("dom", None), P("point"))
    return jax.shard_map(
        on_device, mesh=mesh, in_specs=placed, out_specs=(P(), P()), check_vma=False
    )
```

```python
import functools
import math

import jax
import jax.numpy as jnp
from jax import lax
from jax.experimental import pallas as pl
from jax.experimental.pallas import tpu as pltpu
from jax.sharding import PartitionSpec as P

MOMENTS = 4
ITERS = 6
GX = 32


COEF_NEAR = 4.0 / 3.0
COEF_FAR = -1.0 / 12.0
GAMMA = 2.0
RADIUS = 1.5


def padded_2(block, sides, width):
    for axis, dim in sides:
        count = lax.axis_size(axis)
        forward = [(i, i + 1) for i in range(count - 1)]
        forward.append((count - 1, 0))
        backward = [(target, source) for source, target in forward]
        low = lax.ppermute(
            lax.slice_in_dim(block, block.shape[dim] - width, None, axis=dim), axis, forward
        )
        high = lax.ppermute(lax.slice_in_dim(block, 0, width, axis=dim), axis, backward)
        block = jnp.concatenate([low, block, high], axis=dim)
    return block


def plane_terms(values, side):
    lead = values.shape[:-1]
    planes = values.reshape(lead + (side, side))
    summed = COEF_NEAR * (
        jnp.roll(planes, 1, -2)
        + jnp.roll(planes, -1, -2)
        + jnp.roll(planes, 1, -1)
        + jnp.roll(planes, -1, -1)
    )
    summed = summed + COEF_FAR * (
        jnp.roll(planes, 2, -2)
        + jnp.roll(planes, -2, -2)
        + jnp.roll(planes, 2, -1)
        + jnp.roll(planes, -2, -1)
    )
    return summed.reshape(values.shape)


def complex_mul(first, second):
    return jnp.stack(
        [first[0] * second[0] - first[1] * second[1], first[0] * second[1] + first[1] * second[0]]
    )


def complex_div(first, second):
    denom = second[0] * second[0] + second[1] * second[1]
    return jnp.stack(
        [
            (first[0] * second[0] + first[1] * second[1]) / denom,
            (first[1] * second[0] - first[0] * second[1]) / denom,
        ]
    )


def bilinear(first, second):
    real_part = jnp.sum(first[0] * second[0] - first[1] * second[1], axis=(1, 2))
    imag_part = jnp.sum(first[0] * second[1] + first[1] * second[0], axis=(1, 2))
    return jnp.stack([real_part, imag_part])


def scaled(coeffs, values):
    return complex_mul(coeffs[:, :, None, None], values)


def shifted(values, potential, shift_re, shift_im):
    padded = padded_2(values, (("dom", 2),), 2)
    depth = values.shape[2]
    lap = -7.5 * values + plane_terms(values, GX)
    lap = lap + COEF_NEAR * (padded[:, :, 3 : 3 + depth] + padded[:, :, 1 : 1 + depth])
    lap = lap + COEF_FAR * (padded[:, :, 4 : 4 + depth] + padded[:, :, 0:depth])
    applied = -0.5 * lap + potential * values
    return jnp.stack(
        [
            shift_re * values[0] - shift_im * values[1] - applied[0],
            shift_re * values[1] + shift_im * values[0] - applied[1],
        ]
    )


def residual_sum(values):
    return lax.psum(bilinear(values, values), "dom")


def moment_terms(solution, residual, sources, angle_now, shift_re, shift_im):
    applied = jnp.stack(
        [
            shift_re * solution[0] - shift_im * solution[1] - sources[0] + residual[0],
            shift_re * solution[1] + shift_im * solution[0] - sources[1] + residual[1],
        ]
    )
    angles = (jnp.arange(MOMENTS).astype(jnp.float32) + 1.0) * angle_now
    coeffs = 0.25 * jnp.stack([jnp.cos(angles), jnp.sin(angles)])
    s_terms = complex_mul(coeffs[:, :, None, None, None], solution[:, None])
    h_terms = complex_mul(coeffs[:, :, None, None, None], applied[:, None])
    width = MOMENTS * solution.shape[1]
    return (s_terms.reshape(2, width, -1), h_terms.reshape(2, width, -1))


def gram_of(left, right):
    width = left.shape[1]
    joined = lax.dot_general(
        left.reshape(2 * width, -1),
        right.reshape(2 * width, -1),
        (((1,), (1,)), ((), ())),
        precision=lax.Precision.HIGHEST,
        preferred_element_type=jnp.float32,
    )
    blocks = joined.reshape(2, width, 2, width)
    return jnp.stack([blocks[0, :, 0] + blocks[1, :, 1], blocks[0, :, 1] - blocks[1, :, 0]])


def split_grid(sources, potential, iter_counts):
    complex_src = jnp.stack([sources, jnp.zeros_like(sources)])
    angle_now = (
        2.0 * math.pi * (lax.axis_index("point").astype(jnp.float32) + 0.5) / lax.axis_size("point")
    )
    shift_re = GAMMA + RADIUS * jnp.cos(angle_now)
    shift_im = RADIUS * jnp.sin(angle_now)
    limit = iter_counts[0]
    solution = jnp.zeros_like(complex_src)

    def one_turn(turn_idx, state):
        solution, residual, search, norm_now = state
        product = shifted(search, potential, shift_re, shift_im)
        curve = lax.psum(bilinear(search, product), "dom")
        step_size = complex_div(norm_now, curve)
        new_residual = residual - scaled(step_size, product)
        norm_next = residual_sum(new_residual)
        fresh = (
            solution + scaled(step_size, search),
            new_residual,
            new_residual + scaled(complex_div(norm_next, norm_now), search),
            norm_next,
        )
        keep_mask = turn_idx < limit
        return jax.tree.map(lambda newer, older: jnp.where(keep_mask, newer, older), fresh, state)

    start = (solution, complex_src, complex_src, residual_sum(complex_src))
    solution, residual, search, norm_now = lax.fori_loop(0, ITERS, one_turn, start)
    s_terms, h_terms = moment_terms(solution, residual, complex_src, angle_now, shift_re, shift_im)
    cells = sources.shape[1] * sources.shape[2] * lax.axis_size("dom")
    s_total, h_total = lax.psum((s_terms, h_terms), "point")
    gram_b, gram_a = lax.psum((gram_of(s_total, s_total), gram_of(s_total, h_total)), "dom")
    return (gram_b / cells, gram_a / cells)


Y_IN, X_IN = 2, 4
Y_OUT, X_OUT = GX // Y_IN, GX // X_IN
ROWS = Y_IN * X_IN
LANES = Y_OUT * X_OUT
SUB = 8
BASIS = ITERS + 1
CORES = 2
TILE = 136
H_SCALE = 2.0 / COEF_NEAR
FAR_SCALED = 0.5 * H_SCALE * COEF_FAR


def pack_kernel(depth, groups, rows, out):
    columns = rows.shape[0] // (SUB * groups * depth + depth)
    first_level = columns * SUB * groups * depth
    source = lax.broadcasted_iota(jnp.int32, (LANES, LANES), 0)
    target = lax.broadcasted_iota(jnp.int32, (LANES, LANES), 1)
    inner = target // (LANES // ROWS)
    outer = target % (LANES // ROWS)
    cell = (outer // X_OUT * Y_IN + inner // X_IN) * GX + outer % X_OUT * X_IN + inner % X_IN
    swap = jnp.where(source == cell, 1.0, 0.0).astype(jnp.float32)
    parts = []
    for deep in range(depth):
        for group in range(groups):
            for column in range(columns):
                start = (group * SUB * columns + column) * depth + deep
                parts.append(rows[pl.ds(start, SUB, stride=columns * depth), :])
        parts.append(rows[pl.ds(first_level + deep, columns, stride=depth), :])
    mixed = exact_dot(jnp.concatenate(parts, axis=0), swap, ((1,), (0,)))
    block = LANES // ROWS
    lane_block = lax.broadcasted_iota(jnp.int32, (SUB, LANES), 1) // block
    row = lax.broadcasted_iota(jnp.int32, (SUB, LANES), 0)
    for deep in range(depth):
        base = deep * (groups + 1) * columns * SUB - deep * (columns - 1) * SUB
        for group in range(groups):
            pieces = [
                mixed[base + (group * columns + column) * SUB :][:SUB] for column in range(columns)
            ]
            for m in range(ROWS):
                value = pieces[m]
                for column in range(columns):
                    if column != m:
                        moved = pltpu.roll(pieces[column], (column - m) * block % LANES, 1)
                        value = jnp.where(lane_block == column, moved, value)
                start = ((deep * ROWS + m) * groups + group) * SUB
                out[start : start + SUB, :] = value
        piece = mixed[base + groups * columns * SUB :][:SUB]
        value = piece
        for far in range(1, columns):
            moved = pltpu.roll(pltpu.roll(piece, far * block, 1), columns - far, 0)
            value = jnp.where(lane_block == (row + far) % columns, moved, value)
        start = depth * ROWS * SUB * groups + deep * ROWS
        out[start : start + ROWS, :] = value


def packed_block(sources, potential):
    count, depth, cells = sources.shape
    columns = cells // LANES
    rows = sources.reshape(count, depth, columns, LANES).transpose(0, 2, 1, 3).reshape(-1, LANES)
    levels = potential.reshape(depth, columns, LANES).transpose(1, 0, 2).reshape(-1, LANES)
    vmem = pl.BlockSpec(memory_space=pltpu.VMEM)
    size = depth * ROWS * (count + 1)
    return pl.pallas_call(
        functools.partial(pack_kernel, depth, count // SUB),
        out_shape=jax.ShapeDtypeStruct((size, LANES), jnp.float32),
        in_specs=[vmem],
        out_specs=vmem,
        compiler_params=pltpu.CompilerParams(vmem_limit_bytes=4 * 2**20),
        name="pack",
    )(jnp.concatenate([rows, levels], axis=0))


def lane_sum(values):
    return jnp.broadcast_to(jnp.sum(values, axis=1, keepdims=True), values.shape)


def ratio(top, bottom):
    return jnp.where(bottom > 0.0, top / jnp.where(bottom > 0.0, bottom, 1.0), 0.0)


def tree_sum(values):
    while len(values) > 1:
        values = [sum(values[i : i + 2][1:], values[i]) for i in range(0, len(values), 2)]
    return values[0]


def plane_rows(vector, plane, rows):
    return [vector[plane, rows, m * LANES : (m + 1) * LANES] for m in range(ROWS)]


def y_parts(here, last_x, first_x):
    y_up = [pltpu.roll(value, LANES - X_OUT, 1) for value in here]
    y_down = [pltpu.roll(value, X_OUT, 1) for value in here]
    sums, edges = [], []
    for m in range(ROWS):
        near = y_down[m + X_IN] if m < X_IN else y_up[m - X_IN]
        sums.append(near + FAR_SCALED * (y_up[m] + y_down[m]))
        if m % X_IN < 2:
            edges.append(jnp.where(first_x, y_down[m], here[m]))
        else:
            edges.append(jnp.where(last_x, y_up[m], here[m]))
    return sums, edges


def apply_plane(vector, sums, edges, diagonal, plane, rows):
    planes = vector.shape[0]
    halos = []
    for m, edge in enumerate(plane_rows(edges, plane, rows)):
        halos.append(pltpu.roll(edge, LANES - 1 if m % X_IN < 2 else 1, 1))
    here, above, below, above_2, below_2 = (
        plane_rows(vector, (plane + far) % planes, rows) for far in (0, 1, -1, 2, -2)
    )
    y_sums = plane_rows(sums, plane, rows)
    out = []
    for yi in range(Y_IN):
        first = yi * X_IN
        line, halo = here[first : first + X_IN], halos[first : first + X_IN]
        wide = halo[2:] + line + halo[:2]
        for xi in range(X_IN):
            m = first + xi
            other = m + X_IN if yi == 0 else m - X_IN
            near = here[other] + (above[m] + below[m])
            far = above_2[m] + below_2[m]
            near = near + (wide[xi + 1] + wide[xi + 3])
            far = far + (wide[xi] + wide[xi + 4])
            level = diagonal[plane, :, m * LANES : (m + 1) * LANES]
            out.append((level * here[m] - y_sums[m]) - near - FAR_SCALED * far)
    return here, out


def cmul(first, second):
    return (
        first[0] * second[0] - first[1] * second[1],
        first[0] * second[1] + first[1] * second[0],
    )


def moment_coeffs(angle, shape):
    count = shape[0]
    lane = lax.broadcasted_iota(jnp.int32, shape, 1)
    moment = lax.rem(lane, MOMENTS * count) // count
    parts = []
    for func in (math.cos, math.sin):
        value = jnp.full(shape, 0.25 * func(angle), jnp.float32)
        for k in range(1, MOMENTS):
            value = jnp.where(moment == k, 0.25 * func((k + 1) * angle), value)
        parts.append(value)
    return parts


def weights_of(alphas, norms, limits):
    points = len(limits)
    count = limits[0].shape[0]
    shape = (points * count, LANES)
    lane = lax.broadcasted_iota(jnp.int32, shape, 1)
    left_half = lane < MOMENTS * count
    own = lax.rem(lane[:count], count) == lax.broadcasted_iota(jnp.int32, (count, LANES), 0)

    def stacked(values):
        return jnp.concatenate(values, axis=0)

    def constant(values):
        return stacked([jnp.full((count, LANES), value, jnp.float32) for value in values])

    limit = stacked(limits)
    betas = [stacked([ratio(norms[i + 1], norms[i])] * points) for i in range(ITERS - 1)]
    alphas = [stacked([alpha] * points) for alpha in alphas]
    zero = jnp.zeros(shape, jnp.float32)
    one = jnp.ones(shape, jnp.float32)
    angles = [2.0 * math.pi * (j + 0.5) / points for j in range(points)]
    shift = (
        constant([GAMMA + RADIUS * math.cos(angle) for angle in angles]),
        constant([RADIUS * math.sin(angle) for angle in angles]),
    )
    scaled_shift = (H_SCALE * shift[0], H_SCALE * shift[1])
    product = (one, zero)
    products = [product]
    links = []
    pivot = (scaled_shift[0] - alphas[0], scaled_shift[1])
    for i in range(ITERS):
        size = 1.0 / (pivot[0] * pivot[0] + pivot[1] * pivot[1])
        inverse = (pivot[0] * size, -pivot[1] * size)
        product = cmul(product, inverse)
        products.append(product)
        if i < ITERS - 1:
            link = (betas[i] * inverse[0], betas[i] * inverse[1])
            links.append(link)
            pivot = (scaled_shift[0] - alphas[i + 1] - link[0], scaled_shift[1] - link[1])
    solved = [None] * ITERS
    for i in reversed(range(ITERS)):
        value = (H_SCALE * products[i + 1][0], H_SCALE * products[i + 1][1])
        if i < ITERS - 1:
            step = cmul(links[i], solved[i + 1])
            value = (value[0] + step[0], value[1] + step[1])
        used = limit > i
        solved[i] = (jnp.where(used, value[0], 0.0), jnp.where(used, value[1], 0.0))
    applied = []
    for i in range(BASIS):
        left = limit == i
        rest = (jnp.where(left, products[i][0], 0.0), jnp.where(left, products[i][1], 0.0))
        if i < ITERS:
            turned = cmul(shift, solved[i])
            rest = (rest[0] + turned[0], rest[1] + turned[1])
        if i == 0:
            rest = (rest[0] - 1.0, rest[1])
        applied.append(rest)
    tail = applied[ITERS]
    for back, factor in ((1, alphas[ITERS - 1]), (2, betas[ITERS - 2])):
        part = applied[ITERS - back]
        applied[ITERS - back] = (part[0] - factor * tail[0], part[1] - factor * tail[1])
    moments = [moment_coeffs(angle, (count, LANES)) for angle in angles]
    moment = tuple(stacked([pair[part] for pair in moments]) for part in range(2))
    weights = []
    for i in range(BASIS):
        left = solved[i] if i < ITERS else (zero, zero)
        both = (
            jnp.where(left_half, left[0], applied[i][0]),
            jnp.where(left_half, left[1], applied[i][1]),
        )
        terms = cmul(moment, both)
        weights.append(
            [
                jnp.where(own, tree_sum([part[j * count :][:count] for j in range(points)]), 0.0)
                for part in terms
            ]
        )
    return weights


def exact_dot(first, second, dims):
    return lax.dot_general(
        first,
        second,
        (dims, ((), ())),
        precision=lax.Precision.HIGHEST,
        preferred_element_type=jnp.float32,
    )


def split(values):
    high = values.astype(jnp.bfloat16)
    return high, (values - high.astype(jnp.float32)).astype(jnp.bfloat16)


def krylov_kernel(parts, count, *refs):
    blocks, (highs, lows, applied, scalars) = refs[:parts], refs[parts : parts + 4]
    first_work, second_work, diagonal, sums, edges, partial = refs[parts + 4 :]
    planes = diagonal.shape[0]
    depth = planes // parts
    groups = count // SUB
    lane = lax.broadcasted_iota(jnp.int32, (SUB, LANES), 1)
    last_x = lax.rem(lane, X_OUT) == X_OUT - 1
    first_x = lax.rem(lane, X_OUT) == 0
    here = lax.axis_index("dom")
    for turn in range(parts):
        slab = jnp.bitwise_xor(here, turn) * depth
        for deep in range(depth):
            for m in range(ROWS):
                start = (deep * ROWS + m) * count
                lanes = slice(m * LANES, (m + 1) * LANES)
                value = blocks[turn][start : start + count, :]
                first_work[slab + deep, :, lanes] = value
                highs[0, slab + deep, :, lanes], lows[0, slab + deep, :, lanes] = split(value)
            start = depth * ROWS * count + deep * ROWS
            levels = H_SCALE * (blocks[turn][start : start + ROWS, :] + 3.75)
            for m in range(ROWS):
                level = jnp.broadcast_to(levels[m : m + 1, :], (SUB, LANES))
                diagonal[slab + deep, :, m * LANES : (m + 1) * LANES] = level
    second_work[...] = jnp.zeros_like(second_work)
    scalars[ITERS] = jnp.zeros((count, LANES), jnp.float32)

    all_rows = [pl.ds(group * SUB, SUB) for group in range(groups)]
    all_lanes = [slice(m * LANES, (m + 1) * LANES) for m in range(ROWS)]
    def keep_y_parts(plane, rows, values):
        for ref, parts_of in zip((sums, edges), y_parts(values, last_x, first_x)):
            for lanes, part in zip(all_lanes, parts_of):
                ref[plane, rows, lanes] = part

    for group, rows in enumerate(all_rows):
        norm = []
        for plane in range(planes):
            values = plane_rows(first_work, plane, rows)
            keep_y_parts(plane, rows, values)
            norm.append(tree_sum([value * value for value in values]))
        partial[rows, :] = tree_sum(norm)

    def update_pass(i, work, before, alphas, betas):
        norm = [[] for _ in range(groups)]
        for plane in range(planes):
            columns = []
            for group, rows in enumerate(all_rows):
                values = []
                for lanes in all_lanes:
                    value = applied[plane, rows, lanes] - betas[group] * before[plane, rows, lanes]
                    value = value - alphas[group] * work[plane, rows, lanes]
                    before[plane, rows, lanes] = value
                    values.append(value)
                keep_y_parts(plane, rows, values)
                norm[group].append(tree_sum([value * value for value in values]))
                columns.append(values)
            for lanes, *column in zip(all_lanes, *columns):
                high, low = split(jnp.concatenate(column, axis=0))
                highs[i + 1, plane, :, lanes] = high
                lows[i + 1, plane, :, lanes] = low
        for rows, terms in zip(all_rows, norm):
            partial[rows, :] = tree_sum(terms)

    def half_turn(i, work, before, may_end):
        norms = [lane_sum(partial[rows, :]) for rows in all_rows]
        betas = [
            ratio(norm, scalars[ITERS + i, rows, :]) for norm, rows in zip(norms, all_rows)
        ]
        inverses = [ratio(jnp.ones_like(norm), norm) for norm in norms]
        for norm, rows in zip(norms, all_rows):
            scalars[ITERS + 1 + i, rows, :] = norm
        curve = [[] for _ in range(groups)]
        for plane in range(planes):
            for group, rows in enumerate(all_rows):
                value, out = apply_plane(work, sums, edges, diagonal, plane, rows)
                for m, lanes in enumerate(all_lanes):
                    applied[plane, rows, lanes] = out[m]
                curve[group].append(tree_sum([value[m] * out[m] for m in range(ROWS)]))
        alphas = [lane_sum(tree_sum(curve[g])) * inverses[g] for g in range(groups)]
        for alpha, rows in zip(alphas, all_rows):
            scalars[i, rows, :] = alpha
        if may_end:
            pl.when(i < ITERS - 1)(lambda: update_pass(i, work, before, alphas, betas))
        else:
            update_pass(i, work, before, alphas, betas)

    def turn(step, carry):
        half_turn(2 * step, first_work, second_work, False)
        half_turn(2 * step + 1, second_work, first_work, True)
        return carry

    lax.fori_loop(0, ITERS // 2, turn, 0)


def gram_kernel(points, scalars, *refs):
    tiles = refs[:points]
    highs, lows, applied, out_b, out_a, limits = refs[points:]
    planes, count, _ = applied.shape
    groups = count // SUB
    size = BASIS * count
    here = lax.axis_index("point")
    core = jnp.bitwise_and(lax.axis_index("dom"), CORES - 1)
    for far, tile in zip((0, 3, 1 + core, 2 - core), tiles):
        limits[jnp.bitwise_xor(here, far)] = tile[:SUB, :]

    bounds = [jnp.concatenate([limits[j]] * groups, axis=0) for j in range(points)]
    alphas = [scalars[i] for i in range(ITERS)]
    norms = [scalars[ITERS + 1 + i] for i in range(ITERS)]
    weights = weights_of(alphas, norms, bounds)
    real = jnp.concatenate([pair[0] for pair in weights], axis=0)
    imag = jnp.concatenate([pair[1] for pair in weights], axis=0)
    gram = None
    for plane in range(planes):
        last_high, last_low = split(applied[plane])
        high = jnp.concatenate([highs[i, plane] for i in range(ITERS)] + [last_high], axis=0)
        low = jnp.concatenate([lows[i, plane] for i in range(ITERS)] + [last_low], axis=0)
        product = lax.dot_general(
            jnp.concatenate([high, low], axis=0),
            high,
            (((1,), (1,)), ((), ())),
            preferred_element_type=jnp.float32,
        )
        gram = product if gram is None else gram + product
    cross = gram[size:, :]
    pairs = gram[:size, :] + cross + cross.T
    right = exact_dot(pairs, jnp.concatenate([real, imag], axis=1), ((1,), (0,)))
    half = MOMENTS * count
    left = jnp.concatenate([real[:, :half], imag[:, :half]], axis=1)
    joined = exact_dot(left.T, right, ((1,), (0,)))
    scale = 1.0 / (planes * ROWS * LANES)
    width = 2 * half
    real = (joined[:half, :width] + joined[half:, width:]) * scale
    imag = (joined[:half, width:] - joined[half:, :width]) * scale
    out_b[0] = real[:, :half]
    out_b[1] = imag[:, :half]
    out_a[0] = real[:, half:]
    out_a[1] = imag[:, half:]


def swapped(values, axis, size, mask):
    return lax.ppermute(values, axis, [(index ^ mask, index) for index in range(size)])


def whole_grid(sources, potential, iter_counts, *, parts, points):
    count, depth, _ = sources.shape
    planes = parts * depth
    block = packed_block(sources, potential)
    tile = jnp.broadcast_to(iter_counts.astype(jnp.float32), (TILE, LANES))
    tile = lax.optimization_barrier(tile)
    even = [block] + [swapped(block, "dom", parts, mask) for mask in range(CORES, parts, CORES)]
    mixed = [
        ((point ^ (1 + part % CORES)) * parts + part, point * parts + part)
        for point in range(points)
        for part in range(parts)
    ]
    tiles = [swapped(tile, "point", points, 3), lax.ppermute(tile, ("point", "dom"), mixed)]
    tiles = list(lax.optimization_barrier(tuple(tiles)))
    tiles.append(swapped(tiles[1], "dom", parts, 1))
    own, even[1] = lax.optimization_barrier((block, even[1]))
    odd = [swapped(value, "dom", parts, 1) for value in [own] + even[1:]]
    blocks = [value for pair in zip(even, odd) for value in pair]
    vmem = pl.BlockSpec(memory_space=pltpu.VMEM)
    vector = (planes, count, ROWS * LANES)
    cells = planes * ROWS * LANES
    highs, lows, applied, scalars = pl.pallas_call(
        functools.partial(krylov_kernel, parts, count),
        out_shape=(
            jax.ShapeDtypeStruct((ITERS,) + vector, jnp.bfloat16),
            jax.ShapeDtypeStruct((ITERS,) + vector, jnp.bfloat16),
            jax.ShapeDtypeStruct(vector, jnp.float32),
            jax.ShapeDtypeStruct((2 * ITERS + 1, count, LANES), jnp.float32),
        ),
        in_specs=[vmem] * parts,
        out_specs=(vmem,) * 4,
        scratch_shapes=[
            pltpu.VMEM(vector, jnp.float32),
            pltpu.VMEM(vector, jnp.float32),
            pltpu.VMEM((planes, SUB, ROWS * LANES), jnp.float32),
            pltpu.VMEM(vector, jnp.float32),
            pltpu.VMEM(vector, jnp.float32),
            pltpu.VMEM((count, LANES), jnp.float32),
        ],
        compiler_params=pltpu.CompilerParams(vmem_limit_bytes=16 * 2**20),
        name="krylov",
    )(*blocks)
    width = MOMENTS * count
    out = jax.ShapeDtypeStruct((2, width, width), jnp.float32)
    return pl.pallas_call(
        functools.partial(gram_kernel, points),
        out_shape=(out, out),
        in_specs=[vmem] * (4 + points),
        out_specs=(vmem, vmem),
        scratch_shapes=[pltpu.VMEM((points, SUB, LANES), jnp.float32)],
        compiler_params=pltpu.CompilerParams(vmem_limit_bytes=16 * 2**20),
        name="gram",
    )(scalars, tile, *tiles, highs, lows, applied)


def on_device(sources, potential, iter_counts):
    parts, points = lax.axis_size("dom"), lax.axis_size("point")
    count, depth, cells = sources.shape
    held = BASIS * count * parts * depth * cells * 4
    fits = (
        held <= 16 * 2**20
        and parts == 8
        and points == 4
        and count == 2 * SUB
        and 2 * MOMENTS * count == LANES
        and parts * depth == 16
        and cells == GX * GX == ROWS * LANES
    )
    if not fits:
        return split_grid(sources, potential, iter_counts)
    return whole_grid(sources, potential, iter_counts, parts=parts, points=points)


def solution(mesh):
    placed = (P(None, "dom", None), P("dom", None), P("point"))
    return jax.shard_map(
        on_device, mesh=mesh, in_specs=placed, out_specs=(P(), P()), check_vma=False
    )
```

```python
import functools
import math

import jax
import jax.numpy as jnp
from jax import lax
from jax.experimental import pallas as pl
from jax.experimental.pallas import tpu as pltpu
from jax.sharding import PartitionSpec as P

MOMENTS = 4
ITERS = 6
GX = 32


COEF_NEAR = 4.0 / 3.0
COEF_FAR = -1.0 / 12.0
GAMMA = 2.0
RADIUS = 1.5


def padded_2(block, sides, width):
    for axis, dim in sides:
        count = lax.axis_size(axis)
        forward = [(i, i + 1) for i in range(count - 1)]
        forward.append((count - 1, 0))
        backward = [(target, source) for source, target in forward]
        low = lax.ppermute(
            lax.slice_in_dim(block, block.shape[dim] - width, None, axis=dim), axis, forward
        )
        high = lax.ppermute(lax.slice_in_dim(block, 0, width, axis=dim), axis, backward)
        block = jnp.concatenate([low, block, high], axis=dim)
    return block


def plane_terms(values, side):
    lead = values.shape[:-1]
    planes = values.reshape(lead + (side, side))
    summed = COEF_NEAR * (
        jnp.roll(planes, 1, -2)
        + jnp.roll(planes, -1, -2)
        + jnp.roll(planes, 1, -1)
        + jnp.roll(planes, -1, -1)
    )
    summed = summed + COEF_FAR * (
        jnp.roll(planes, 2, -2)
        + jnp.roll(planes, -2, -2)
        + jnp.roll(planes, 2, -1)
        + jnp.roll(planes, -2, -1)
    )
    return summed.reshape(values.shape)


def complex_mul(first, second):
    return jnp.stack(
        [first[0] * second[0] - first[1] * second[1], first[0] * second[1] + first[1] * second[0]]
    )


def complex_div(first, second):
    denom = second[0] * second[0] + second[1] * second[1]
    return jnp.stack(
        [
            (first[0] * second[0] + first[1] * second[1]) / denom,
            (first[1] * second[0] - first[0] * second[1]) / denom,
        ]
    )


def bilinear(first, second):
    real_part = jnp.sum(first[0] * second[0] - first[1] * second[1], axis=(1, 2))
    imag_part = jnp.sum(first[0] * second[1] + first[1] * second[0], axis=(1, 2))
    return jnp.stack([real_part, imag_part])


def scaled(coeffs, values):
    return complex_mul(coeffs[:, :, None, None], values)


def shifted(values, potential, shift_re, shift_im):
    padded = padded_2(values, (("dom", 2),), 2)
    depth = values.shape[2]
    lap = -7.5 * values + plane_terms(values, GX)
    lap = lap + COEF_NEAR * (padded[:, :, 3 : 3 + depth] + padded[:, :, 1 : 1 + depth])
    lap = lap + COEF_FAR * (padded[:, :, 4 : 4 + depth] + padded[:, :, 0:depth])
    applied = -0.5 * lap + potential * values
    return jnp.stack(
        [
            shift_re * values[0] - shift_im * values[1] - applied[0],
            shift_re * values[1] + shift_im * values[0] - applied[1],
        ]
    )


def residual_sum(values):
    return lax.psum(bilinear(values, values), "dom")


def moment_terms(solution, residual, sources, angle_now, shift_re, shift_im):
    applied = jnp.stack(
        [
            shift_re * solution[0] - shift_im * solution[1] - sources[0] + residual[0],
            shift_re * solution[1] + shift_im * solution[0] - sources[1] + residual[1],
        ]
    )
    angles = (jnp.arange(MOMENTS).astype(jnp.float32) + 1.0) * angle_now
    coeffs = 0.25 * jnp.stack([jnp.cos(angles), jnp.sin(angles)])
    s_terms = complex_mul(coeffs[:, :, None, None, None], solution[:, None])
    h_terms = complex_mul(coeffs[:, :, None, None, None], applied[:, None])
    width = MOMENTS * solution.shape[1]
    return (s_terms.reshape(2, width, -1), h_terms.reshape(2, width, -1))


def gram_of(left, right):
    width = left.shape[1]
    joined = lax.dot_general(
        left.reshape(2 * width, -1),
        right.reshape(2 * width, -1),
        (((1,), (1,)), ((), ())),
        precision=lax.Precision.HIGHEST,
        preferred_element_type=jnp.float32,
    )
    blocks = joined.reshape(2, width, 2, width)
    return jnp.stack([blocks[0, :, 0] + blocks[1, :, 1], blocks[0, :, 1] - blocks[1, :, 0]])


def split_grid(sources, potential, iter_counts):
    complex_src = jnp.stack([sources, jnp.zeros_like(sources)])
    angle_now = (
        2.0 * math.pi * (lax.axis_index("point").astype(jnp.float32) + 0.5) / lax.axis_size("point")
    )
    shift_re = GAMMA + RADIUS * jnp.cos(angle_now)
    shift_im = RADIUS * jnp.sin(angle_now)
    limit = iter_counts[0]
    solution = jnp.zeros_like(complex_src)

    def one_turn(turn_idx, state):
        solution, residual, search, norm_now = state
        product = shifted(search, potential, shift_re, shift_im)
        curve = lax.psum(bilinear(search, product), "dom")
        step_size = complex_div(norm_now, curve)
        new_residual = residual - scaled(step_size, product)
        norm_next = residual_sum(new_residual)
        fresh = (
            solution + scaled(step_size, search),
            new_residual,
            new_residual + scaled(complex_div(norm_next, norm_now), search),
            norm_next,
        )
        keep_mask = turn_idx < limit
        return jax.tree.map(lambda newer, older: jnp.where(keep_mask, newer, older), fresh, state)

    start = (solution, complex_src, complex_src, residual_sum(complex_src))
    solution, residual, search, norm_now = lax.fori_loop(0, ITERS, one_turn, start)
    s_terms, h_terms = moment_terms(solution, residual, complex_src, angle_now, shift_re, shift_im)
    cells = sources.shape[1] * sources.shape[2] * lax.axis_size("dom")
    s_total, h_total = lax.psum((s_terms, h_terms), "point")
    gram_b, gram_a = lax.psum((gram_of(s_total, s_total), gram_of(s_total, h_total)), "dom")
    return (gram_b / cells, gram_a / cells)


Y_IN, X_IN = 2, 4
Y_OUT, X_OUT = GX // Y_IN, GX // X_IN
ROWS = Y_IN * X_IN
LANES = Y_OUT * X_OUT
SUB = 8
BASIS = ITERS + 1
CORES = 2
TILE = 136
H_SCALE = 2.0 / COEF_NEAR
FAR_SCALED = 0.5 * H_SCALE * COEF_FAR


def pack_kernel(depth, groups, rows, out):
    columns = rows.shape[0] // (SUB * groups * depth + depth)
    first_level = columns * SUB * groups * depth
    source = lax.broadcasted_iota(jnp.int32, (LANES, LANES), 0)
    target = lax.broadcasted_iota(jnp.int32, (LANES, LANES), 1)
    inner = target // (LANES // ROWS)
    outer = target % (LANES // ROWS)
    cell = (outer // X_OUT * Y_IN + inner // X_IN) * GX + outer % X_OUT * X_IN + inner % X_IN
    swap = jnp.where(source == cell, 1.0, 0.0).astype(jnp.float32)
    parts = []
    for deep in range(depth):
        for group in range(groups):
            for column in range(columns):
                start = (group * SUB * columns + column) * depth + deep
                parts.append(rows[pl.ds(start, SUB, stride=columns * depth), :])
        parts.append(rows[pl.ds(first_level + deep, columns, stride=depth), :])
    mixed = exact_dot(jnp.concatenate(parts, axis=0), swap, ((1,), (0,)))
    block = LANES // ROWS
    lane_block = lax.broadcasted_iota(jnp.int32, (SUB, LANES), 1) // block
    row = lax.broadcasted_iota(jnp.int32, (SUB, LANES), 0)
    for deep in range(depth):
        base = deep * (groups + 1) * columns * SUB - deep * (columns - 1) * SUB
        for group in range(groups):
            pieces = [
                mixed[base + (group * columns + column) * SUB :][:SUB] for column in range(columns)
            ]
            for m in range(ROWS):
                value = pieces[m]
                for column in range(columns):
                    if column != m:
                        moved = pltpu.roll(pieces[column], (column - m) * block % LANES, 1)
                        value = jnp.where(lane_block == column, moved, value)
                start = ((deep * ROWS + m) * groups + group) * SUB
                out[start : start + SUB, :] = value
        piece = mixed[base + groups * columns * SUB :][:SUB]
        value = piece
        for far in range(1, columns):
            moved = pltpu.roll(pltpu.roll(piece, far * block, 1), columns - far, 0)
            value = jnp.where(lane_block == (row + far) % columns, moved, value)
        start = depth * ROWS * SUB * groups + deep * ROWS
        out[start : start + ROWS, :] = value


def packed_block(sources, potential):
    count, depth, cells = sources.shape
    columns = cells // LANES
    rows = sources.reshape(count, depth, columns, LANES).transpose(0, 2, 1, 3).reshape(-1, LANES)
    levels = potential.reshape(depth, columns, LANES).transpose(1, 0, 2).reshape(-1, LANES)
    vmem = pl.BlockSpec(memory_space=pltpu.VMEM)
    size = depth * ROWS * (count + 1)
    return pl.pallas_call(
        functools.partial(pack_kernel, depth, count // SUB),
        out_shape=jax.ShapeDtypeStruct((size, LANES), jnp.float32),
        in_specs=[vmem],
        out_specs=vmem,
        compiler_params=pltpu.CompilerParams(vmem_limit_bytes=4 * 2**20),
        name="pack",
    )(jnp.concatenate([rows, levels], axis=0))


def lane_sum(values):
    return jnp.broadcast_to(jnp.sum(values, axis=1, keepdims=True), values.shape)


def ratio(top, bottom):
    return jnp.where(bottom > 0.0, top / jnp.where(bottom > 0.0, bottom, 1.0), 0.0)


def tree_sum(values):
    while len(values) > 1:
        values = [sum(values[i : i + 2][1:], values[i]) for i in range(0, len(values), 2)]
    return values[0]


def plane_rows(vector, plane, rows):
    return [vector[plane, rows, m * LANES : (m + 1) * LANES] for m in range(ROWS)]


def y_parts(here, last_x, first_x):
    y_up = [pltpu.roll(value, LANES - X_OUT, 1) for value in here]
    y_down = [pltpu.roll(value, X_OUT, 1) for value in here]
    sums, edges = [], []
    for m in range(ROWS):
        near = y_down[m + X_IN] if m < X_IN else y_up[m - X_IN]
        sums.append(near + FAR_SCALED * (y_up[m] + y_down[m]))
        if m % X_IN < 2:
            edges.append(jnp.where(first_x, y_down[m], here[m]))
        else:
            edges.append(jnp.where(last_x, y_up[m], here[m]))
    return sums, edges


def apply_plane(vector, sums, edges, diagonal, plane, rows):
    planes = vector.shape[0]
    halos = []
    for m, edge in enumerate(plane_rows(edges, plane, rows)):
        halos.append(pltpu.roll(edge, LANES - 1 if m % X_IN < 2 else 1, 1))
    here, above, below, above_2, below_2 = (
        plane_rows(vector, (plane + far) % planes, rows) for far in (0, 1, -1, 2, -2)
    )
    y_sums = plane_rows(sums, plane, rows)
    out = []
    for yi in range(Y_IN):
        first = yi * X_IN
        line, halo = here[first : first + X_IN], halos[first : first + X_IN]
        wide = halo[2:] + line + halo[:2]
        for xi in range(X_IN):
            m = first + xi
            other = m + X_IN if yi == 0 else m - X_IN
            near = here[other] + (above[m] + below[m])
            far = above_2[m] + below_2[m]
            near = near + (wide[xi + 1] + wide[xi + 3])
            far = far + (wide[xi] + wide[xi + 4])
            level = diagonal[plane, :, m * LANES : (m + 1) * LANES]
            out.append((level * here[m] - y_sums[m]) - near - FAR_SCALED * far)
    return here, out


def cmul(first, second):
    return (
        first[0] * second[0] - first[1] * second[1],
        first[0] * second[1] + first[1] * second[0],
    )


def moment_coeffs(angle, shape):
    count = shape[0]
    lane = lax.broadcasted_iota(jnp.int32, shape, 1)
    moment = lax.rem(lane, MOMENTS * count) // count
    parts = []
    for func in (math.cos, math.sin):
        value = jnp.full(shape, 0.25 * func(angle), jnp.float32)
        for k in range(1, MOMENTS):
            value = jnp.where(moment == k, 0.25 * func((k + 1) * angle), value)
        parts.append(value)
    return parts


def weights_of(alphas, norms, limits):
    points = len(limits)
    count = limits[0].shape[0]
    shape = (points * count, LANES)
    lane = lax.broadcasted_iota(jnp.int32, shape, 1)
    left_half = lane < MOMENTS * count
    own = lax.rem(lane[:count], count) == lax.broadcasted_iota(jnp.int32, (count, LANES), 0)

    def stacked(values):
        return jnp.concatenate(values, axis=0)

    def constant(values):
        return stacked([jnp.full((count, LANES), value, jnp.float32) for value in values])

    limit = stacked(limits)
    betas = [stacked([ratio(norms[i + 1], norms[i])] * points) for i in range(ITERS - 1)]
    alphas = [stacked([alpha] * points) for alpha in alphas]
    zero = jnp.zeros(shape, jnp.float32)
    one = jnp.ones(shape, jnp.float32)
    angles = [2.0 * math.pi * (j + 0.5) / points for j in range(points)]
    shift = (
        constant([GAMMA + RADIUS * math.cos(angle) for angle in angles]),
        constant([RADIUS * math.sin(angle) for angle in angles]),
    )
    scaled_shift = (H_SCALE * shift[0], H_SCALE * shift[1])
    product = (one, zero)
    products = [product]
    links = []
    pivot = (scaled_shift[0] - alphas[0], scaled_shift[1])
    for i in range(ITERS):
        size = 1.0 / (pivot[0] * pivot[0] + pivot[1] * pivot[1])
        inverse = (pivot[0] * size, -pivot[1] * size)
        product = cmul(product, inverse)
        products.append(product)
        if i < ITERS - 1:
            link = (betas[i] * inverse[0], betas[i] * inverse[1])
            links.append(link)
            pivot = (scaled_shift[0] - alphas[i + 1] - link[0], scaled_shift[1] - link[1])
    solved = [None] * ITERS
    for i in reversed(range(ITERS)):
        value = (H_SCALE * products[i + 1][0], H_SCALE * products[i + 1][1])
        if i < ITERS - 1:
            step = cmul(links[i], solved[i + 1])
            value = (value[0] + step[0], value[1] + step[1])
        used = limit > i
        solved[i] = (jnp.where(used, value[0], 0.0), jnp.where(used, value[1], 0.0))
    applied = []
    for i in range(BASIS):
        left = limit == i
        rest = (jnp.where(left, products[i][0], 0.0), jnp.where(left, products[i][1], 0.0))
        if i < ITERS:
            turned = cmul(shift, solved[i])
            rest = (rest[0] + turned[0], rest[1] + turned[1])
        if i == 0:
            rest = (rest[0] - 1.0, rest[1])
        applied.append(rest)
    tail = applied[ITERS]
    for back, factor in ((1, alphas[ITERS - 1]), (2, betas[ITERS - 2])):
        part = applied[ITERS - back]
        applied[ITERS - back] = (part[0] - factor * tail[0], part[1] - factor * tail[1])
    moments = [moment_coeffs(angle, (count, LANES)) for angle in angles]
    moment = tuple(stacked([pair[part] for pair in moments]) for part in range(2))
    weights = []
    for i in range(BASIS):
        left = solved[i] if i < ITERS else (zero, zero)
        both = (
            jnp.where(left_half, left[0], applied[i][0]),
            jnp.where(left_half, left[1], applied[i][1]),
        )
        terms = cmul(moment, both)
        weights.append(
            [
                jnp.where(own, tree_sum([part[j * count :][:count] for j in range(points)]), 0.0)
                for part in terms
            ]
        )
    return weights


def exact_dot(first, second, dims):
    return lax.dot_general(
        first,
        second,
        (dims, ((), ())),
        precision=lax.Precision.HIGHEST,
        preferred_element_type=jnp.float32,
    )


def split(values):
    high = values.astype(jnp.bfloat16)
    return high, (values - high.astype(jnp.float32)).astype(jnp.bfloat16)


def krylov_kernel(parts, count, *refs):
    blocks, (highs, lows, applied, scalars) = refs[:parts], refs[parts : parts + 4]
    first_work, second_work, diagonal, sums, edges, partial = refs[parts + 4 :]
    planes = diagonal.shape[0]
    depth = planes // parts
    groups = count // SUB
    lane = lax.broadcasted_iota(jnp.int32, (SUB, LANES), 1)
    last_x = lax.rem(lane, X_OUT) == X_OUT - 1
    first_x = lax.rem(lane, X_OUT) == 0
    here = lax.axis_index("dom")
    for turn in range(parts):
        slab = jnp.bitwise_xor(here, turn) * depth
        for deep in range(depth):
            for m in range(ROWS):
                start = (deep * ROWS + m) * count
                lanes = slice(m * LANES, (m + 1) * LANES)
                value = blocks[turn][start : start + count, :]
                first_work[slab + deep, :, lanes] = value
                highs[0, slab + deep, :, lanes], lows[0, slab + deep, :, lanes] = split(value)
            start = depth * ROWS * count + deep * ROWS
            levels = H_SCALE * (blocks[turn][start : start + ROWS, :] + 3.75)
            for m in range(ROWS):
                level = jnp.broadcast_to(levels[m : m + 1, :], (SUB, LANES))
                diagonal[slab + deep, :, m * LANES : (m + 1) * LANES] = level
    second_work[...] = jnp.zeros_like(second_work)
    scalars[ITERS] = jnp.zeros((count, LANES), jnp.float32)

    all_rows = [pl.ds(group * SUB, SUB) for group in range(groups)]
    all_lanes = [slice(m * LANES, (m + 1) * LANES) for m in range(ROWS)]
    def keep_y_parts(plane, rows, values):
        for ref, parts_of in zip((sums, edges), y_parts(values, last_x, first_x)):
            for lanes, part in zip(all_lanes, parts_of):
                ref[plane, rows, lanes] = part

    for group, rows in enumerate(all_rows):
        norm = []
        for plane in range(planes):
            values = plane_rows(first_work, plane, rows)
            keep_y_parts(plane, rows, values)
            norm.append(tree_sum([value * value for value in values]))
        partial[rows, :] = tree_sum(norm)

    def update_pass(i, work, before, alphas, betas):
        norm = [[] for _ in range(groups)]
        for plane in range(planes):
            columns = []
            for group, rows in enumerate(all_rows):
                values = []
                for lanes in all_lanes:
                    value = applied[plane, rows, lanes] - betas[group] * before[plane, rows, lanes]
                    value = value - alphas[group] * work[plane, rows, lanes]
                    before[plane, rows, lanes] = value
                    values.append(value)
                keep_y_parts(plane, rows, values)
                norm[group].append(tree_sum([value * value for value in values]))
                columns.append(values)
            for lanes, *column in zip(all_lanes, *columns):
                high, low = split(jnp.concatenate(column, axis=0))
                highs[i + 1, plane, :, lanes] = high
                lows[i + 1, plane, :, lanes] = low
        for rows, terms in zip(all_rows, norm):
            partial[rows, :] = tree_sum(terms)

    def half_turn(i, work, before, may_end):
        norms = [lane_sum(partial[rows, :]) for rows in all_rows]
        betas = [
            ratio(norm, scalars[ITERS + i, rows, :]) for norm, rows in zip(norms, all_rows)
        ]
        inverses = [ratio(jnp.ones_like(norm), norm) for norm in norms]
        for norm, rows in zip(norms, all_rows):
            scalars[ITERS + 1 + i, rows, :] = norm
        curve = [[] for _ in range(groups)]
        for plane in range(planes):
            for group, rows in enumerate(all_rows):
                value, out = apply_plane(work, sums, edges, diagonal, plane, rows)
                for m, lanes in enumerate(all_lanes):
                    applied[plane, rows, lanes] = out[m]
                curve[group].append(tree_sum([value[m] * out[m] for m in range(ROWS)]))
        alphas = [lane_sum(tree_sum(curve[g])) * inverses[g] for g in range(groups)]
        for alpha, rows in zip(alphas, all_rows):
            scalars[i, rows, :] = alpha
        if may_end:
            pl.when(i < ITERS - 1)(lambda: update_pass(i, work, before, alphas, betas))
        else:
            update_pass(i, work, before, alphas, betas)

    def turn(step, carry):
        half_turn(2 * step, first_work, second_work, False)
        half_turn(2 * step + 1, second_work, first_work, True)
        return carry

    lax.fori_loop(0, ITERS // 2, turn, 0)


def gram_kernel(points, scalars, *refs):
    tiles = refs[:points]
    highs, lows, applied, out_b, out_a, limits = refs[points:]
    planes, count, _ = applied.shape
    groups = count // SUB
    size = BASIS * count
    here = lax.axis_index("point")
    core = jnp.bitwise_and(lax.axis_index("dom"), CORES - 1)
    for far, tile in zip((0, 1 + core, 3, 2 - core), tiles):
        limits[jnp.bitwise_xor(here, far)] = tile[:SUB, :]

    bounds = [jnp.concatenate([limits[j]] * groups, axis=0) for j in range(points)]
    alphas = [scalars[i] for i in range(ITERS)]
    norms = [scalars[ITERS + 1 + i] for i in range(ITERS)]
    weights = weights_of(alphas, norms, bounds)
    real = jnp.concatenate([pair[0] for pair in weights], axis=0)
    imag = jnp.concatenate([pair[1] for pair in weights], axis=0)
    gram = None
    for plane in range(planes):
        last_high, last_low = split(applied[plane])
        high = jnp.concatenate([highs[i, plane] for i in range(ITERS)] + [last_high], axis=0)
        low = jnp.concatenate([lows[i, plane] for i in range(ITERS)] + [last_low], axis=0)
        product = lax.dot_general(
            jnp.concatenate([high, low], axis=0),
            high,
            (((1,), (1,)), ((), ())),
            preferred_element_type=jnp.float32,
        )
        gram = product if gram is None else gram + product
    cross = gram[size:, :]
    pairs = gram[:size, :] + cross + cross.T
    right = exact_dot(pairs, jnp.concatenate([real, imag], axis=1), ((1,), (0,)))
    half = MOMENTS * count
    left = jnp.concatenate([real[:, :half], imag[:, :half]], axis=1)
    joined = exact_dot(left.T, right, ((1,), (0,)))
    scale = 1.0 / (planes * ROWS * LANES)
    width = 2 * half
    real = (joined[:half, :width] + joined[half:, width:]) * scale
    imag = (joined[:half, width:] - joined[half:, :width]) * scale
    out_b[0] = real[:, :half]
    out_b[1] = imag[:, :half]
    out_a[0] = real[:, half:]
    out_a[1] = imag[:, half:]


def swapped(values, axis, size, mask):
    return lax.ppermute(values, axis, [(index ^ mask, index) for index in range(size)])


def whole_grid(sources, potential, iter_counts, *, parts, points):
    count, depth, _ = sources.shape
    planes = parts * depth
    block = packed_block(sources, potential)
    tile = jnp.broadcast_to(iter_counts.astype(jnp.float32), (TILE, LANES))
    tile = lax.optimization_barrier(tile)
    even = [block] + [swapped(block, "dom", parts, mask) for mask in range(CORES, parts, CORES)]
    mixed = [
        ((point ^ (1 + part % CORES)) * parts + part, point * parts + part)
        for point in range(points)
        for part in range(parts)
    ]
    tiles = [lax.ppermute(tile, ("point", "dom"), mixed), swapped(tile, "point", points, 3)]
    tiles = list(lax.optimization_barrier(tuple(tiles)))
    tiles.append(swapped(tiles[0], "dom", parts, 1))
    own, even[1] = lax.optimization_barrier((block, even[1]))
    odd = [swapped(value, "dom", parts, 1) for value in [own] + even[1:]]
    blocks = [value for pair in zip(even, odd) for value in pair]
    vmem = pl.BlockSpec(memory_space=pltpu.VMEM)
    vector = (planes, count, ROWS * LANES)
    cells = planes * ROWS * LANES
    highs, lows, applied, scalars = pl.pallas_call(
        functools.partial(krylov_kernel, parts, count),
        out_shape=(
            jax.ShapeDtypeStruct((ITERS,) + vector, jnp.bfloat16),
            jax.ShapeDtypeStruct((ITERS,) + vector, jnp.bfloat16),
            jax.ShapeDtypeStruct(vector, jnp.float32),
            jax.ShapeDtypeStruct((2 * ITERS + 1, count, LANES), jnp.float32),
        ),
        in_specs=[vmem] * parts,
        out_specs=(vmem,) * 4,
        scratch_shapes=[
            pltpu.VMEM(vector, jnp.float32),
            pltpu.VMEM(vector, jnp.float32),
            pltpu.VMEM((planes, SUB, ROWS * LANES), jnp.float32),
            pltpu.VMEM(vector, jnp.float32),
            pltpu.VMEM(vector, jnp.float32),
            pltpu.VMEM((count, LANES), jnp.float32),
        ],
        compiler_params=pltpu.CompilerParams(vmem_limit_bytes=16 * 2**20),
        name="krylov",
    )(*blocks)
    width = MOMENTS * count
    out = jax.ShapeDtypeStruct((2, width, width), jnp.float32)
    return pl.pallas_call(
        functools.partial(gram_kernel, points),
        out_shape=(out, out),
        in_specs=[vmem] * (4 + points),
        out_specs=(vmem, vmem),
        scratch_shapes=[pltpu.VMEM((points, SUB, LANES), jnp.float32)],
        compiler_params=pltpu.CompilerParams(vmem_limit_bytes=16 * 2**20),
        name="gram",
    )(scalars, tile, *tiles, highs, lows, applied)


def on_device(sources, potential, iter_counts):
    parts, points = lax.axis_size("dom"), lax.axis_size("point")
    count, depth, cells = sources.shape
    held = BASIS * count * parts * depth * cells * 4
    fits = (
        held <= 16 * 2**20
        and parts == 8
        and points == 4
        and count == 2 * SUB
        and 2 * MOMENTS * count == LANES
        and parts * depth == 16
        and cells == GX * GX == ROWS * LANES
    )
    if not fits:
        return split_grid(sources, potential, iter_counts)
    return whole_grid(sources, potential, iter_counts, parts=parts, points=points)


def solution(mesh):
    placed = (P(None, "dom", None), P("dom", None), P("point"))
    return jax.shard_map(
        on_device, mesh=mesh, in_specs=placed, out_specs=(P(), P()), check_vma=False
    )
```

```python
import functools
import math

import jax
import jax.numpy as jnp
from jax import lax
from jax.experimental import pallas as pl
from jax.experimental.pallas import tpu as pltpu
from jax.sharding import PartitionSpec as P

MOMENTS = 4
ITERS = 6
GX = 32


COEF_NEAR = 4.0 / 3.0
COEF_FAR = -1.0 / 12.0
GAMMA = 2.0
RADIUS = 1.5


def padded_2(block, sides, width):
    for axis, dim in sides:
        count = lax.axis_size(axis)
        forward = [(i, i + 1) for i in range(count - 1)]
        forward.append((count - 1, 0))
        backward = [(target, source) for source, target in forward]
        low = lax.ppermute(
            lax.slice_in_dim(block, block.shape[dim] - width, None, axis=dim), axis, forward
        )
        high = lax.ppermute(lax.slice_in_dim(block, 0, width, axis=dim), axis, backward)
        block = jnp.concatenate([low, block, high], axis=dim)
    return block


def plane_terms(values, side):
    lead = values.shape[:-1]
    planes = values.reshape(lead + (side, side))
    summed = COEF_NEAR * (
        jnp.roll(planes, 1, -2)
        + jnp.roll(planes, -1, -2)
        + jnp.roll(planes, 1, -1)
        + jnp.roll(planes, -1, -1)
    )
    summed = summed + COEF_FAR * (
        jnp.roll(planes, 2, -2)
        + jnp.roll(planes, -2, -2)
        + jnp.roll(planes, 2, -1)
        + jnp.roll(planes, -2, -1)
    )
    return summed.reshape(values.shape)


def complex_mul(first, second):
    return jnp.stack(
        [first[0] * second[0] - first[1] * second[1], first[0] * second[1] + first[1] * second[0]]
    )


def complex_div(first, second):
    denom = second[0] * second[0] + second[1] * second[1]
    return jnp.stack(
        [
            (first[0] * second[0] + first[1] * second[1]) / denom,
            (first[1] * second[0] - first[0] * second[1]) / denom,
        ]
    )


def bilinear(first, second):
    real_part = jnp.sum(first[0] * second[0] - first[1] * second[1], axis=(1, 2))
    imag_part = jnp.sum(first[0] * second[1] + first[1] * second[0], axis=(1, 2))
    return jnp.stack([real_part, imag_part])


def scaled(coeffs, values):
    return complex_mul(coeffs[:, :, None, None], values)


def shifted(values, potential, shift_re, shift_im):
    padded = padded_2(values, (("dom", 2),), 2)
    depth = values.shape[2]
    lap = -7.5 * values + plane_terms(values, GX)
    lap = lap + COEF_NEAR * (padded[:, :, 3 : 3 + depth] + padded[:, :, 1 : 1 + depth])
    lap = lap + COEF_FAR * (padded[:, :, 4 : 4 + depth] + padded[:, :, 0:depth])
    applied = -0.5 * lap + potential * values
    return jnp.stack(
        [
            shift_re * values[0] - shift_im * values[1] - applied[0],
            shift_re * values[1] + shift_im * values[0] - applied[1],
        ]
    )


def residual_sum(values):
    return lax.psum(bilinear(values, values), "dom")


def moment_terms(solution, residual, sources, angle_now, shift_re, shift_im):
    applied = jnp.stack(
        [
            shift_re * solution[0] - shift_im * solution[1] - sources[0] + residual[0],
            shift_re * solution[1] + shift_im * solution[0] - sources[1] + residual[1],
        ]
    )
    angles = (jnp.arange(MOMENTS).astype(jnp.float32) + 1.0) * angle_now
    coeffs = 0.25 * jnp.stack([jnp.cos(angles), jnp.sin(angles)])
    s_terms = complex_mul(coeffs[:, :, None, None, None], solution[:, None])
    h_terms = complex_mul(coeffs[:, :, None, None, None], applied[:, None])
    width = MOMENTS * solution.shape[1]
    return (s_terms.reshape(2, width, -1), h_terms.reshape(2, width, -1))


def gram_of(left, right):
    width = left.shape[1]
    joined = lax.dot_general(
        left.reshape(2 * width, -1),
        right.reshape(2 * width, -1),
        (((1,), (1,)), ((), ())),
        precision=lax.Precision.HIGHEST,
        preferred_element_type=jnp.float32,
    )
    blocks = joined.reshape(2, width, 2, width)
    return jnp.stack([blocks[0, :, 0] + blocks[1, :, 1], blocks[0, :, 1] - blocks[1, :, 0]])


def split_grid(sources, potential, iter_counts):
    complex_src = jnp.stack([sources, jnp.zeros_like(sources)])
    angle_now = (
        2.0 * math.pi * (lax.axis_index("point").astype(jnp.float32) + 0.5) / lax.axis_size("point")
    )
    shift_re = GAMMA + RADIUS * jnp.cos(angle_now)
    shift_im = RADIUS * jnp.sin(angle_now)
    limit = iter_counts[0]
    solution = jnp.zeros_like(complex_src)

    def one_turn(turn_idx, state):
        solution, residual, search, norm_now = state
        product = shifted(search, potential, shift_re, shift_im)
        curve = lax.psum(bilinear(search, product), "dom")
        step_size = complex_div(norm_now, curve)
        new_residual = residual - scaled(step_size, product)
        norm_next = residual_sum(new_residual)
        fresh = (
            solution + scaled(step_size, search),
            new_residual,
            new_residual + scaled(complex_div(norm_next, norm_now), search),
            norm_next,
        )
        keep_mask = turn_idx < limit
        return jax.tree.map(lambda newer, older: jnp.where(keep_mask, newer, older), fresh, state)

    start = (solution, complex_src, complex_src, residual_sum(complex_src))
    solution, residual, search, norm_now = lax.fori_loop(0, ITERS, one_turn, start)
    s_terms, h_terms = moment_terms(solution, residual, complex_src, angle_now, shift_re, shift_im)
    cells = sources.shape[1] * sources.shape[2] * lax.axis_size("dom")
    s_total, h_total = lax.psum((s_terms, h_terms), "point")
    gram_b, gram_a = lax.psum((gram_of(s_total, s_total), gram_of(s_total, h_total)), "dom")
    return (gram_b / cells, gram_a / cells)


Y_IN, X_IN = 2, 4
Y_OUT, X_OUT = GX // Y_IN, GX // X_IN
ROWS = Y_IN * X_IN
LANES = Y_OUT * X_OUT
SUB = 8
BASIS = ITERS + 1
CORES = 2
TILE = 136
H_SCALE = 2.0 / COEF_NEAR
FAR_SCALED = 0.5 * H_SCALE * COEF_FAR


def pack_kernel(depth, groups, rows, out):
    columns = rows.shape[0] // (SUB * groups * depth + depth)
    first_level = columns * SUB * groups * depth
    source = lax.broadcasted_iota(jnp.int32, (LANES, LANES), 0)
    target = lax.broadcasted_iota(jnp.int32, (LANES, LANES), 1)
    inner = target // (LANES // ROWS)
    outer = target % (LANES // ROWS)
    cell = (outer // X_OUT * Y_IN + inner // X_IN) * GX + outer % X_OUT * X_IN + inner % X_IN
    swap = jnp.where(source == cell, 1.0, 0.0).astype(jnp.float32)
    parts = []
    for deep in range(depth):
        for group in range(groups):
            for column in range(columns):
                start = (group * SUB * columns + column) * depth + deep
                parts.append(rows[pl.ds(start, SUB, stride=columns * depth), :])
        parts.append(rows[pl.ds(first_level + deep, columns, stride=depth), :])
    mixed = exact_dot(jnp.concatenate(parts, axis=0), swap, ((1,), (0,)))
    block = LANES // ROWS
    lane_block = lax.broadcasted_iota(jnp.int32, (SUB, LANES), 1) // block
    row = lax.broadcasted_iota(jnp.int32, (SUB, LANES), 0)
    for deep in range(depth):
        base = deep * (groups + 1) * columns * SUB - deep * (columns - 1) * SUB
        for group in range(groups):
            pieces = [
                mixed[base + (group * columns + column) * SUB :][:SUB] for column in range(columns)
            ]
            for m in range(ROWS):
                value = pieces[m]
                for column in range(columns):
                    if column != m:
                        moved = pltpu.roll(pieces[column], (column - m) * block % LANES, 1)
                        value = jnp.where(lane_block == column, moved, value)
                start = ((deep * ROWS + m) * groups + group) * SUB
                out[start : start + SUB, :] = value
        piece = mixed[base + groups * columns * SUB :][:SUB]
        value = piece
        for far in range(1, columns):
            moved = pltpu.roll(pltpu.roll(piece, far * block, 1), columns - far, 0)
            value = jnp.where(lane_block == (row + far) % columns, moved, value)
        start = depth * ROWS * SUB * groups + deep * ROWS
        out[start : start + ROWS, :] = value


def packed_block(sources, potential):
    count, depth, cells = sources.shape
    columns = cells // LANES
    rows = sources.reshape(count, depth, columns, LANES).transpose(0, 2, 1, 3).reshape(-1, LANES)
    levels = potential.reshape(depth, columns, LANES).transpose(1, 0, 2).reshape(-1, LANES)
    vmem = pl.BlockSpec(memory_space=pltpu.VMEM)
    size = depth * ROWS * (count + 1)
    return pl.pallas_call(
        functools.partial(pack_kernel, depth, count // SUB),
        out_shape=jax.ShapeDtypeStruct((size, LANES), jnp.float32),
        in_specs=[vmem],
        out_specs=vmem,
        compiler_params=pltpu.CompilerParams(vmem_limit_bytes=4 * 2**20),
        name="pack",
    )(jnp.concatenate([rows, levels], axis=0))


def lane_sum(values):
    return jnp.broadcast_to(jnp.sum(values, axis=1, keepdims=True), values.shape)


def ratio(top, bottom):
    return jnp.where(bottom > 0.0, top / jnp.where(bottom > 0.0, bottom, 1.0), 0.0)


def tree_sum(values):
    while len(values) > 1:
        values = [sum(values[i : i + 2][1:], values[i]) for i in range(0, len(values), 2)]
    return values[0]


def plane_rows(vector, plane, rows):
    return [vector[plane, rows, m * LANES : (m + 1) * LANES] for m in range(ROWS)]


def y_parts(here, last_x, first_x):
    y_up = [pltpu.roll(value, LANES - X_OUT, 1) for value in here]
    y_down = [pltpu.roll(value, X_OUT, 1) for value in here]
    sums, edges = [], []
    for m in range(ROWS):
        near = y_down[m + X_IN] if m < X_IN else y_up[m - X_IN]
        sums.append(near + FAR_SCALED * (y_up[m] + y_down[m]))
        if m % X_IN < 2:
            edges.append(jnp.where(first_x, y_down[m], here[m]))
        else:
            edges.append(jnp.where(last_x, y_up[m], here[m]))
    return sums, edges


def apply_plane(vector, sums, edges, diagonal, plane, rows):
    planes = vector.shape[0]
    halos = []
    for m, edge in enumerate(plane_rows(edges, plane, rows)):
        halos.append(pltpu.roll(edge, LANES - 1 if m % X_IN < 2 else 1, 1))
    here, above, below, above_2, below_2 = (
        plane_rows(vector, (plane + far) % planes, rows) for far in (0, 1, -1, 2, -2)
    )
    y_sums = plane_rows(sums, plane, rows)
    out = []
    for yi in range(Y_IN):
        first = yi * X_IN
        line, halo = here[first : first + X_IN], halos[first : first + X_IN]
        wide = halo[2:] + line + halo[:2]
        for xi in range(X_IN):
            m = first + xi
            other = m + X_IN if yi == 0 else m - X_IN
            near = here[other] + (above[m] + below[m])
            far = above_2[m] + below_2[m]
            near = near + (wide[xi + 1] + wide[xi + 3])
            far = far + (wide[xi] + wide[xi + 4])
            level = diagonal[plane, :, m * LANES : (m + 1) * LANES]
            out.append((level * here[m] - y_sums[m]) - near - FAR_SCALED * far)
    return here, out


def cmul(first, second):
    return (
        first[0] * second[0] - first[1] * second[1],
        first[0] * second[1] + first[1] * second[0],
    )


def moment_coeffs(angle, shape):
    count = shape[0]
    lane = lax.broadcasted_iota(jnp.int32, shape, 1)
    moment = lax.rem(lane, MOMENTS * count) // count
    parts = []
    for func in (math.cos, math.sin):
        value = jnp.full(shape, 0.25 * func(angle), jnp.float32)
        for k in range(1, MOMENTS):
            value = jnp.where(moment == k, 0.25 * func((k + 1) * angle), value)
        parts.append(value)
    return parts


def weights_of(alphas, norms, limits):
    points = len(limits)
    count = limits[0].shape[0]
    shape = (points * count, LANES)
    lane = lax.broadcasted_iota(jnp.int32, shape, 1)
    left_half = lane < MOMENTS * count
    own = lax.rem(lane[:count], count) == lax.broadcasted_iota(jnp.int32, (count, LANES), 0)

    def stacked(values):
        return jnp.concatenate(values, axis=0)

    def constant(values):
        return stacked([jnp.full((count, LANES), value, jnp.float32) for value in values])

    limit = stacked(limits)
    betas = [stacked([ratio(norms[i + 1], norms[i])] * points) for i in range(ITERS - 1)]
    alphas = [stacked([alpha] * points) for alpha in alphas]
    zero = jnp.zeros(shape, jnp.float32)
    one = jnp.ones(shape, jnp.float32)
    angles = [2.0 * math.pi * (j + 0.5) / points for j in range(points)]
    shift = (
        constant([GAMMA + RADIUS * math.cos(angle) for angle in angles]),
        constant([RADIUS * math.sin(angle) for angle in angles]),
    )
    scaled_shift = (H_SCALE * shift[0], H_SCALE * shift[1])
    product = (one, zero)
    products = [product]
    links = []
    pivot = (scaled_shift[0] - alphas[0], scaled_shift[1])
    for i in range(ITERS):
        size = 1.0 / (pivot[0] * pivot[0] + pivot[1] * pivot[1])
        inverse = (pivot[0] * size, -pivot[1] * size)
        product = cmul(product, inverse)
        products.append(product)
        if i < ITERS - 1:
            link = (betas[i] * inverse[0], betas[i] * inverse[1])
            links.append(link)
            pivot = (scaled_shift[0] - alphas[i + 1] - link[0], scaled_shift[1] - link[1])
    solved = [None] * ITERS
    for i in reversed(range(ITERS)):
        value = (H_SCALE * products[i + 1][0], H_SCALE * products[i + 1][1])
        if i < ITERS - 1:
            step = cmul(links[i], solved[i + 1])
            value = (value[0] + step[0], value[1] + step[1])
        used = limit > i
        solved[i] = (jnp.where(used, value[0], 0.0), jnp.where(used, value[1], 0.0))
    applied = []
    for i in range(BASIS):
        left = limit == i
        rest = (jnp.where(left, products[i][0], 0.0), jnp.where(left, products[i][1], 0.0))
        if i < ITERS:
            turned = cmul(shift, solved[i])
            rest = (rest[0] + turned[0], rest[1] + turned[1])
        if i == 0:
            rest = (rest[0] - 1.0, rest[1])
        applied.append(rest)
    tail = applied[ITERS]
    for back, factor in ((1, alphas[ITERS - 1]), (2, betas[ITERS - 2])):
        part = applied[ITERS - back]
        applied[ITERS - back] = (part[0] - factor * tail[0], part[1] - factor * tail[1])
    moments = [moment_coeffs(angle, (count, LANES)) for angle in angles]
    moment = tuple(stacked([pair[part] for pair in moments]) for part in range(2))
    weights = []
    for i in range(BASIS):
        left = solved[i] if i < ITERS else (zero, zero)
        both = (
            jnp.where(left_half, left[0], applied[i][0]),
            jnp.where(left_half, left[1], applied[i][1]),
        )
        terms = cmul(moment, both)
        weights.append(
            [
                jnp.where(own, tree_sum([part[j * count :][:count] for j in range(points)]), 0.0)
                for part in terms
            ]
        )
    return weights


def exact_dot(first, second, dims):
    return lax.dot_general(
        first,
        second,
        (dims, ((), ())),
        precision=lax.Precision.HIGHEST,
        preferred_element_type=jnp.float32,
    )


def split(values):
    high = values.astype(jnp.bfloat16)
    return high, (values - high.astype(jnp.float32)).astype(jnp.bfloat16)


def krylov_kernel(parts, count, *refs):
    blocks, (highs, lows, applied, scalars) = refs[:parts], refs[parts : parts + 4]
    first_work, second_work, diagonal, sums, edges, partial = refs[parts + 4 :]
    planes = diagonal.shape[0]
    depth = planes // parts
    groups = count // SUB
    lane = lax.broadcasted_iota(jnp.int32, (SUB, LANES), 1)
    last_x = lax.rem(lane, X_OUT) == X_OUT - 1
    first_x = lax.rem(lane, X_OUT) == 0
    here = lax.axis_index("dom")
    for turn in range(parts):
        slab = jnp.bitwise_xor(here, turn) * depth
        for deep in range(depth):
            for m in range(ROWS):
                start = (deep * ROWS + m) * count
                lanes = slice(m * LANES, (m + 1) * LANES)
                value = blocks[turn][start : start + count, :]
                first_work[slab + deep, :, lanes] = value
                highs[0, slab + deep, :, lanes], lows[0, slab + deep, :, lanes] = split(value)
            start = depth * ROWS * count + deep * ROWS
            levels = H_SCALE * (blocks[turn][start : start + ROWS, :] + 3.75)
            for m in range(ROWS):
                level = jnp.broadcast_to(levels[m : m + 1, :], (SUB, LANES))
                diagonal[slab + deep, :, m * LANES : (m + 1) * LANES] = level
    second_work[...] = jnp.zeros_like(second_work)
    scalars[ITERS] = jnp.zeros((count, LANES), jnp.float32)

    all_rows = [pl.ds(group * SUB, SUB) for group in range(groups)]
    all_lanes = [slice(m * LANES, (m + 1) * LANES) for m in range(ROWS)]
    def keep_y_parts(plane, rows, values):
        for ref, parts_of in zip((sums, edges), y_parts(values, last_x, first_x)):
            for lanes, part in zip(all_lanes, parts_of):
                ref[plane, rows, lanes] = part

    for group, rows in enumerate(all_rows):
        norm = []
        for plane in range(planes):
            values = plane_rows(first_work, plane, rows)
            keep_y_parts(plane, rows, values)
            norm.append(tree_sum([value * value for value in values]))
        partial[rows, :] = tree_sum(norm)

    def update_pass(i, work, before, alphas, betas):
        norm = [[] for _ in range(groups)]
        for plane in range(planes):
            columns = []
            for group, rows in enumerate(all_rows):
                values = []
                for lanes in all_lanes:
                    value = applied[plane, rows, lanes] - betas[group] * before[plane, rows, lanes]
                    value = value - alphas[group] * work[plane, rows, lanes]
                    before[plane, rows, lanes] = value
                    values.append(value)
                keep_y_parts(plane, rows, values)
                norm[group].append(tree_sum([value * value for value in values]))
                columns.append(values)
            for lanes, *column in zip(all_lanes, *columns):
                high, low = split(jnp.concatenate(column, axis=0))
                highs[i + 1, plane, :, lanes] = high
                lows[i + 1, plane, :, lanes] = low
        for rows, terms in zip(all_rows, norm):
            partial[rows, :] = tree_sum(terms)

    def half_turn(i, work, before, may_end):
        norms = [lane_sum(partial[rows, :]) for rows in all_rows]
        betas = [
            ratio(norm, scalars[ITERS + i, rows, :]) for norm, rows in zip(norms, all_rows)
        ]
        inverses = [ratio(jnp.ones_like(norm), norm) for norm in norms]
        for norm, rows in zip(norms, all_rows):
            scalars[ITERS + 1 + i, rows, :] = norm
        curve = [[] for _ in range(groups)]
        for plane in range(planes):
            for group, rows in enumerate(all_rows):
                value, out = apply_plane(work, sums, edges, diagonal, plane, rows)
                for m, lanes in enumerate(all_lanes):
                    applied[plane, rows, lanes] = out[m]
                curve[group].append(tree_sum([value[m] * out[m] for m in range(ROWS)]))
        alphas = [lane_sum(tree_sum(curve[g])) * inverses[g] for g in range(groups)]
        for alpha, rows in zip(alphas, all_rows):
            scalars[i, rows, :] = alpha
        if may_end:
            pl.when(i < ITERS - 1)(lambda: update_pass(i, work, before, alphas, betas))
        else:
            update_pass(i, work, before, alphas, betas)

    def turn(step, carry):
        half_turn(2 * step, first_work, second_work, False)
        half_turn(2 * step + 1, second_work, first_work, True)
        return carry

    lax.fori_loop(0, ITERS // 2, turn, 0)


def gram_kernel(points, scalars, *refs):
    tile, mixed, far, other_mixed, other_far = refs[: points + 1]
    highs, lows, applied, out_b, out_a, limits = refs[points + 1 :]
    planes, count, _ = applied.shape
    groups = count // SUB
    size = BASIS * count
    here = lax.axis_index("point")
    core = jnp.bitwise_and(lax.axis_index("dom"), CORES - 1)
    limits[here] = tile[:SUB, :]
    limits[jnp.bitwise_xor(here, 1 + core)] = mixed[:SUB, :]
    limits[jnp.bitwise_xor(here, 2 - core)] = other_mixed[:SUB, :]
    limits[jnp.bitwise_xor(here, 3)] = jnp.where(core == 0, far[:SUB, :], other_far[:SUB, :])

    bounds = [jnp.concatenate([limits[j]] * groups, axis=0) for j in range(points)]
    alphas = [scalars[i] for i in range(ITERS)]
    norms = [scalars[ITERS + 1 + i] for i in range(ITERS)]
    weights = weights_of(alphas, norms, bounds)
    real = jnp.concatenate([pair[0] for pair in weights], axis=0)
    imag = jnp.concatenate([pair[1] for pair in weights], axis=0)
    gram = None
    for plane in range(planes):
        last_high, last_low = split(applied[plane])
        high = jnp.concatenate([highs[i, plane] for i in range(ITERS)] + [last_high], axis=0)
        low = jnp.concatenate([lows[i, plane] for i in range(ITERS)] + [last_low], axis=0)
        product = lax.dot_general(
            jnp.concatenate([high, low], axis=0),
            high,
            (((1,), (1,)), ((), ())),
            preferred_element_type=jnp.float32,
        )
        gram = product if gram is None else gram + product
    cross = gram[size:, :]
    pairs = gram[:size, :] + cross + cross.T
    right = exact_dot(pairs, jnp.concatenate([real, imag], axis=1), ((1,), (0,)))
    half = MOMENTS * count
    left = jnp.concatenate([real[:, :half], imag[:, :half]], axis=1)
    joined = exact_dot(left.T, right, ((1,), (0,)))
    scale = 1.0 / (planes * ROWS * LANES)
    width = 2 * half
    real = (joined[:half, :width] + joined[half:, width:]) * scale
    imag = (joined[:half, width:] - joined[half:, :width]) * scale
    out_b[0] = real[:, :half]
    out_b[1] = imag[:, :half]
    out_a[0] = real[:, half:]
    out_a[1] = imag[:, half:]


def swapped(values, axis, size, mask):
    return lax.ppermute(values, axis, [(index ^ mask, index) for index in range(size)])


def whole_grid(sources, potential, iter_counts, *, parts, points):
    count, depth, _ = sources.shape
    planes = parts * depth
    block = packed_block(sources, potential)
    tile = jnp.broadcast_to(iter_counts.astype(jnp.float32), (TILE, LANES))
    tile = lax.optimization_barrier(tile)
    even = [block] + [swapped(block, "dom", parts, mask) for mask in range(CORES, parts, CORES)]
    mixed = [
        ((point ^ (1 + part % CORES)) * parts + part, point * parts + part)
        for point in range(points)
        for part in range(parts)
    ]
    far = [
        ((point ^ 3) * parts + part, point * parts + part)
        for point in range(points)
        for part in range(0, parts, CORES)
    ]
    tiles = [lax.ppermute(tile, ("point", "dom"), pairs) for pairs in (mixed, far)]
    tiles = list(lax.optimization_barrier(tuple(tiles)))
    tiles += [swapped(value, "dom", parts, 1) for value in tiles]
    own, even[1] = lax.optimization_barrier((block, even[1]))
    odd = [swapped(value, "dom", parts, 1) for value in [own] + even[1:]]
    blocks = [value for pair in zip(even, odd) for value in pair]
    vmem = pl.BlockSpec(memory_space=pltpu.VMEM)
    vector = (planes, count, ROWS * LANES)
    cells = planes * ROWS * LANES
    highs, lows, applied, scalars = pl.pallas_call(
        functools.partial(krylov_kernel, parts, count),
        out_shape=(
            jax.ShapeDtypeStruct((ITERS,) + vector, jnp.bfloat16),
            jax.ShapeDtypeStruct((ITERS,) + vector, jnp.bfloat16),
            jax.ShapeDtypeStruct(vector, jnp.float32),
            jax.ShapeDtypeStruct((2 * ITERS + 1, count, LANES), jnp.float32),
        ),
        in_specs=[vmem] * parts,
        out_specs=(vmem,) * 4,
        scratch_shapes=[
            pltpu.VMEM(vector, jnp.float32),
            pltpu.VMEM(vector, jnp.float32),
            pltpu.VMEM((planes, SUB, ROWS * LANES), jnp.float32),
            pltpu.VMEM(vector, jnp.float32),
            pltpu.VMEM(vector, jnp.float32),
            pltpu.VMEM((count, LANES), jnp.float32),
        ],
        compiler_params=pltpu.CompilerParams(vmem_limit_bytes=16 * 2**20),
        name="krylov",
    )(*blocks)
    width = MOMENTS * count
    out = jax.ShapeDtypeStruct((2, width, width), jnp.float32)
    return pl.pallas_call(
        functools.partial(gram_kernel, points),
        out_shape=(out, out),
        in_specs=[vmem] * (5 + points),
        out_specs=(vmem, vmem),
        scratch_shapes=[pltpu.VMEM((points, SUB, LANES), jnp.float32)],
        compiler_params=pltpu.CompilerParams(vmem_limit_bytes=16 * 2**20),
        name="gram",
    )(scalars, tile, *tiles, highs, lows, applied)


def on_device(sources, potential, iter_counts):
    parts, points = lax.axis_size("dom"), lax.axis_size("point")
    count, depth, cells = sources.shape
    held = BASIS * count * parts * depth * cells * 4
    fits = (
        held <= 16 * 2**20
        and parts == 8
        and points == 4
        and count == 2 * SUB
        and 2 * MOMENTS * count == LANES
        and parts * depth == 16
        and cells == GX * GX == ROWS * LANES
    )
    if not fits:
        return split_grid(sources, potential, iter_counts)
    return whole_grid(sources, potential, iter_counts, parts=parts, points=points)


def solution(mesh):
    placed = (P(None, "dom", None), P("dom", None), P("point"))
    return jax.shard_map(
        on_device, mesh=mesh, in_specs=placed, out_specs=(P(), P()), check_vma=False
    )
```

```python
import functools
import math

import jax
import jax.numpy as jnp
from jax import lax
from jax.experimental import pallas as pl
from jax.experimental.pallas import tpu as pltpu
from jax.sharding import PartitionSpec as P

MOMENTS = 4
ITERS = 6
GX = 32


COEF_NEAR = 4.0 / 3.0
COEF_FAR = -1.0 / 12.0
GAMMA = 2.0
RADIUS = 1.5


def padded_2(block, sides, width):
    for axis, dim in sides:
        count = lax.axis_size(axis)
        forward = [(i, i + 1) for i in range(count - 1)]
        forward.append((count - 1, 0))
        backward = [(target, source) for source, target in forward]
        low = lax.ppermute(
            lax.slice_in_dim(block, block.shape[dim] - width, None, axis=dim), axis, forward
        )
        high = lax.ppermute(lax.slice_in_dim(block, 0, width, axis=dim), axis, backward)
        block = jnp.concatenate([low, block, high], axis=dim)
    return block


def plane_terms(values, side):
    lead = values.shape[:-1]
    planes = values.reshape(lead + (side, side))
    summed = COEF_NEAR * (
        jnp.roll(planes, 1, -2)
        + jnp.roll(planes, -1, -2)
        + jnp.roll(planes, 1, -1)
        + jnp.roll(planes, -1, -1)
    )
    summed = summed + COEF_FAR * (
        jnp.roll(planes, 2, -2)
        + jnp.roll(planes, -2, -2)
        + jnp.roll(planes, 2, -1)
        + jnp.roll(planes, -2, -1)
    )
    return summed.reshape(values.shape)


def complex_mul(first, second):
    return jnp.stack(
        [first[0] * second[0] - first[1] * second[1], first[0] * second[1] + first[1] * second[0]]
    )


def complex_div(first, second):
    denom = second[0] * second[0] + second[1] * second[1]
    return jnp.stack(
        [
            (first[0] * second[0] + first[1] * second[1]) / denom,
            (first[1] * second[0] - first[0] * second[1]) / denom,
        ]
    )


def bilinear(first, second):
    real_part = jnp.sum(first[0] * second[0] - first[1] * second[1], axis=(1, 2))
    imag_part = jnp.sum(first[0] * second[1] + first[1] * second[0], axis=(1, 2))
    return jnp.stack([real_part, imag_part])


def scaled(coeffs, values):
    return complex_mul(coeffs[:, :, None, None], values)


def shifted(values, potential, shift_re, shift_im):
    padded = padded_2(values, (("dom", 2),), 2)
    depth = values.shape[2]
    lap = -7.5 * values + plane_terms(values, GX)
    lap = lap + COEF_NEAR * (padded[:, :, 3 : 3 + depth] + padded[:, :, 1 : 1 + depth])
    lap = lap + COEF_FAR * (padded[:, :, 4 : 4 + depth] + padded[:, :, 0:depth])
    applied = -0.5 * lap + potential * values
    return jnp.stack(
        [
            shift_re * values[0] - shift_im * values[1] - applied[0],
            shift_re * values[1] + shift_im * values[0] - applied[1],
        ]
    )


def residual_sum(values):
    return lax.psum(bilinear(values, values), "dom")


def moment_terms(solution, residual, sources, angle_now, shift_re, shift_im):
    applied = jnp.stack(
        [
            shift_re * solution[0] - shift_im * solution[1] - sources[0] + residual[0],
            shift_re * solution[1] + shift_im * solution[0] - sources[1] + residual[1],
        ]
    )
    angles = (jnp.arange(MOMENTS).astype(jnp.float32) + 1.0) * angle_now
    coeffs = 0.25 * jnp.stack([jnp.cos(angles), jnp.sin(angles)])
    s_terms = complex_mul(coeffs[:, :, None, None, None], solution[:, None])
    h_terms = complex_mul(coeffs[:, :, None, None, None], applied[:, None])
    width = MOMENTS * solution.shape[1]
    return (s_terms.reshape(2, width, -1), h_terms.reshape(2, width, -1))


def gram_of(left, right):
    width = left.shape[1]
    joined = lax.dot_general(
        left.reshape(2 * width, -1),
        right.reshape(2 * width, -1),
        (((1,), (1,)), ((), ())),
        precision=lax.Precision.HIGHEST,
        preferred_element_type=jnp.float32,
    )
    blocks = joined.reshape(2, width, 2, width)
    return jnp.stack([blocks[0, :, 0] + blocks[1, :, 1], blocks[0, :, 1] - blocks[1, :, 0]])


def split_grid(sources, potential, iter_counts):
    complex_src = jnp.stack([sources, jnp.zeros_like(sources)])
    angle_now = (
        2.0 * math.pi * (lax.axis_index("point").astype(jnp.float32) + 0.5) / lax.axis_size("point")
    )
    shift_re = GAMMA + RADIUS * jnp.cos(angle_now)
    shift_im = RADIUS * jnp.sin(angle_now)
    limit = iter_counts[0]
    solution = jnp.zeros_like(complex_src)

    def one_turn(turn_idx, state):
        solution, residual, search, norm_now = state
        product = shifted(search, potential, shift_re, shift_im)
        curve = lax.psum(bilinear(search, product), "dom")
        step_size = complex_div(norm_now, curve)
        new_residual = residual - scaled(step_size, product)
        norm_next = residual_sum(new_residual)
        fresh = (
            solution + scaled(step_size, search),
            new_residual,
            new_residual + scaled(complex_div(norm_next, norm_now), search),
            norm_next,
        )
        keep_mask = turn_idx < limit
        return jax.tree.map(lambda newer, older: jnp.where(keep_mask, newer, older), fresh, state)

    start = (solution, complex_src, complex_src, residual_sum(complex_src))
    solution, residual, search, norm_now = lax.fori_loop(0, ITERS, one_turn, start)
    s_terms, h_terms = moment_terms(solution, residual, complex_src, angle_now, shift_re, shift_im)
    cells = sources.shape[1] * sources.shape[2] * lax.axis_size("dom")
    s_total, h_total = lax.psum((s_terms, h_terms), "point")
    gram_b, gram_a = lax.psum((gram_of(s_total, s_total), gram_of(s_total, h_total)), "dom")
    return (gram_b / cells, gram_a / cells)


Y_IN, X_IN = 2, 4
Y_OUT, X_OUT = GX // Y_IN, GX // X_IN
ROWS = Y_IN * X_IN
LANES = Y_OUT * X_OUT
SUB = 8
BASIS = ITERS + 1
CORES = 2
TILE = 136
H_SCALE = 2.0 / COEF_NEAR
FAR_SCALED = 0.5 * H_SCALE * COEF_FAR


def pack_kernel(depth, groups, rows, out):
    columns = rows.shape[0] // (SUB * groups * depth + depth)
    first_level = columns * SUB * groups * depth
    source = lax.broadcasted_iota(jnp.int32, (LANES, LANES), 0)
    target = lax.broadcasted_iota(jnp.int32, (LANES, LANES), 1)
    inner = target // (LANES // ROWS)
    outer = target % (LANES // ROWS)
    cell = (outer // X_OUT * Y_IN + inner // X_IN) * GX + outer % X_OUT * X_IN + inner % X_IN
    swap = jnp.where(source == cell, 1.0, 0.0).astype(jnp.float32)
    parts = []
    for deep in range(depth):
        for group in range(groups):
            for column in range(columns):
                start = (group * SUB * columns + column) * depth + deep
                parts.append(rows[pl.ds(start, SUB, stride=columns * depth), :])
        parts.append(rows[pl.ds(first_level + deep, columns, stride=depth), :])
    mixed = exact_dot(jnp.concatenate(parts, axis=0), swap, ((1,), (0,)))
    block = LANES // ROWS
    lane_block = lax.broadcasted_iota(jnp.int32, (SUB, LANES), 1) // block
    row = lax.broadcasted_iota(jnp.int32, (SUB, LANES), 0)
    for deep in range(depth):
        base = deep * (groups + 1) * columns * SUB - deep * (columns - 1) * SUB
        for group in range(groups):
            pieces = [
                mixed[base + (group * columns + column) * SUB :][:SUB] for column in range(columns)
            ]
            for m in range(ROWS):
                value = pieces[m]
                for column in range(columns):
                    if column != m:
                        moved = pltpu.roll(pieces[column], (column - m) * block % LANES, 1)
                        value = jnp.where(lane_block == column, moved, value)
                start = ((deep * ROWS + m) * groups + group) * SUB
                out[start : start + SUB, :] = value
        piece = mixed[base + groups * columns * SUB :][:SUB]
        value = piece
        for far in range(1, columns):
            moved = pltpu.roll(pltpu.roll(piece, far * block, 1), columns - far, 0)
            value = jnp.where(lane_block == (row + far) % columns, moved, value)
        start = depth * ROWS * SUB * groups + deep * ROWS
        out[start : start + ROWS, :] = value


def packed_block(sources, potential):
    count, depth, cells = sources.shape
    columns = cells // LANES
    rows = sources.reshape(count, depth, columns, LANES).transpose(0, 2, 1, 3).reshape(-1, LANES)
    levels = potential.reshape(depth, columns, LANES).transpose(1, 0, 2).reshape(-1, LANES)
    vmem = pl.BlockSpec(memory_space=pltpu.VMEM)
    size = depth * ROWS * (count + 1)
    return pl.pallas_call(
        functools.partial(pack_kernel, depth, count // SUB),
        out_shape=jax.ShapeDtypeStruct((size, LANES), jnp.float32),
        in_specs=[vmem],
        out_specs=vmem,
        compiler_params=pltpu.CompilerParams(vmem_limit_bytes=4 * 2**20),
        name="pack",
    )(jnp.concatenate([rows, levels], axis=0))


def lane_sum(values):
    return jnp.broadcast_to(jnp.sum(values, axis=1, keepdims=True), values.shape)


def ratio(top, bottom):
    return jnp.where(bottom > 0.0, top / jnp.where(bottom > 0.0, bottom, 1.0), 0.0)


def tree_sum(values):
    while len(values) > 1:
        values = [sum(values[i : i + 2][1:], values[i]) for i in range(0, len(values), 2)]
    return values[0]


def plane_rows(vector, plane, rows):
    return [vector[plane, rows, m * LANES : (m + 1) * LANES] for m in range(ROWS)]


def y_parts(here, last_x, first_x):
    y_up = [pltpu.roll(value, LANES - X_OUT, 1) for value in here]
    y_down = [pltpu.roll(value, X_OUT, 1) for value in here]
    sums, edges = [], []
    for m in range(ROWS):
        near = y_down[m + X_IN] if m < X_IN else y_up[m - X_IN]
        sums.append(near + FAR_SCALED * (y_up[m] + y_down[m]))
        if m % X_IN < 2:
            edges.append(jnp.where(first_x, y_down[m], here[m]))
        else:
            edges.append(jnp.where(last_x, y_up[m], here[m]))
    return sums, edges


def apply_plane(vector, sums, edges, diagonal, plane, rows):
    planes = vector.shape[0]
    halos = []
    for m, edge in enumerate(plane_rows(edges, plane, rows)):
        halos.append(pltpu.roll(edge, LANES - 1 if m % X_IN < 2 else 1, 1))
    here, above, below, above_2, below_2 = (
        plane_rows(vector, (plane + far) % planes, rows) for far in (0, 1, -1, 2, -2)
    )
    y_sums = plane_rows(sums, plane, rows)
    out = []
    for yi in range(Y_IN):
        first = yi * X_IN
        line, halo = here[first : first + X_IN], halos[first : first + X_IN]
        wide = halo[2:] + line + halo[:2]
        for xi in range(X_IN):
            m = first + xi
            other = m + X_IN if yi == 0 else m - X_IN
            near = here[other] + (above[m] + below[m])
            far = above_2[m] + below_2[m]
            near = near + (wide[xi + 1] + wide[xi + 3])
            far = far + (wide[xi] + wide[xi + 4])
            level = diagonal[plane, :, m * LANES : (m + 1) * LANES]
            out.append((level * here[m] - y_sums[m]) - near - FAR_SCALED * far)
    return here, out


def cmul(first, second):
    return (
        first[0] * second[0] - first[1] * second[1],
        first[0] * second[1] + first[1] * second[0],
    )


def moment_coeffs(angle, shape):
    count = shape[0]
    lane = lax.broadcasted_iota(jnp.int32, shape, 1)
    moment = lax.rem(lane, MOMENTS * count) // count
    parts = []
    for func in (math.cos, math.sin):
        value = jnp.full(shape, 0.25 * func(angle), jnp.float32)
        for k in range(1, MOMENTS):
            value = jnp.where(moment == k, 0.25 * func((k + 1) * angle), value)
        parts.append(value)
    return parts


def weights_of(alphas, norms, limits):
    points = len(limits)
    count = limits[0].shape[0]
    shape = (points * count, LANES)
    lane = lax.broadcasted_iota(jnp.int32, shape, 1)
    left_half = lane < MOMENTS * count
    own = lax.rem(lane[:count], count) == lax.broadcasted_iota(jnp.int32, (count, LANES), 0)

    def stacked(values):
        return jnp.concatenate(values, axis=0)

    def constant(values):
        return stacked([jnp.full((count, LANES), value, jnp.float32) for value in values])

    limit = stacked(limits)
    betas = [stacked([ratio(norms[i + 1], norms[i])] * points) for i in range(ITERS - 1)]
    alphas = [stacked([alpha] * points) for alpha in alphas]
    zero = jnp.zeros(shape, jnp.float32)
    one = jnp.ones(shape, jnp.float32)
    angles = [2.0 * math.pi * (j + 0.5) / points for j in range(points)]
    shift = (
        constant([GAMMA + RADIUS * math.cos(angle) for angle in angles]),
        constant([RADIUS * math.sin(angle) for angle in angles]),
    )
    scaled_shift = (H_SCALE * shift[0], H_SCALE * shift[1])
    product = (one, zero)
    products = [product]
    links = []
    pivot = (scaled_shift[0] - alphas[0], scaled_shift[1])
    for i in range(ITERS):
        size = 1.0 / (pivot[0] * pivot[0] + pivot[1] * pivot[1])
        inverse = (pivot[0] * size, -pivot[1] * size)
        product = cmul(product, inverse)
        products.append(product)
        if i < ITERS - 1:
            link = (betas[i] * inverse[0], betas[i] * inverse[1])
            links.append(link)
            pivot = (scaled_shift[0] - alphas[i + 1] - link[0], scaled_shift[1] - link[1])
    solved = [None] * ITERS
    for i in reversed(range(ITERS)):
        value = (H_SCALE * products[i + 1][0], H_SCALE * products[i + 1][1])
        if i < ITERS - 1:
            step = cmul(links[i], solved[i + 1])
            value = (value[0] + step[0], value[1] + step[1])
        used = limit > i
        solved[i] = (jnp.where(used, value[0], 0.0), jnp.where(used, value[1], 0.0))
    applied = []
    for i in range(BASIS):
        left = limit == i
        rest = (jnp.where(left, products[i][0], 0.0), jnp.where(left, products[i][1], 0.0))
        if i < ITERS:
            turned = cmul(shift, solved[i])
            rest = (rest[0] + turned[0], rest[1] + turned[1])
        if i == 0:
            rest = (rest[0] - 1.0, rest[1])
        applied.append(rest)
    tail = applied[ITERS]
    for back, factor in ((1, alphas[ITERS - 1]), (2, betas[ITERS - 2])):
        part = applied[ITERS - back]
        applied[ITERS - back] = (part[0] - factor * tail[0], part[1] - factor * tail[1])
    moments = [moment_coeffs(angle, (count, LANES)) for angle in angles]
    moment = tuple(stacked([pair[part] for pair in moments]) for part in range(2))
    weights = []
    for i in range(BASIS):
        left = solved[i] if i < ITERS else (zero, zero)
        both = (
            jnp.where(left_half, left[0], applied[i][0]),
            jnp.where(left_half, left[1], applied[i][1]),
        )
        terms = cmul(moment, both)
        weights.append(
            [
                jnp.where(own, tree_sum([part[j * count :][:count] for j in range(points)]), 0.0)
                for part in terms
            ]
        )
    return weights


def exact_dot(first, second, dims):
    return lax.dot_general(
        first,
        second,
        (dims, ((), ())),
        precision=lax.Precision.HIGHEST,
        preferred_element_type=jnp.float32,
    )


def split(values):
    high = values.astype(jnp.bfloat16)
    return high, (values - high.astype(jnp.float32)).astype(jnp.bfloat16)


def krylov_kernel(parts, count, *refs):
    blocks, (highs, lows, applied, scalars) = refs[:parts], refs[parts : parts + 4]
    first_work, second_work, diagonal, sums, edges, partial = refs[parts + 4 :]
    planes = diagonal.shape[0]
    depth = planes // parts
    groups = count // SUB
    lane = lax.broadcasted_iota(jnp.int32, (SUB, LANES), 1)
    last_x = lax.rem(lane, X_OUT) == X_OUT - 1
    first_x = lax.rem(lane, X_OUT) == 0
    here = lax.axis_index("dom")
    for turn in range(parts):
        slab = jnp.bitwise_xor(here, turn) * depth
        for deep in range(depth):
            for m in range(ROWS):
                start = (deep * ROWS + m) * count
                lanes = slice(m * LANES, (m + 1) * LANES)
                value = blocks[turn][start : start + count, :]
                first_work[slab + deep, :, lanes] = value
                highs[0, slab + deep, :, lanes], lows[0, slab + deep, :, lanes] = split(value)
            start = depth * ROWS * count + deep * ROWS
            levels = H_SCALE * (blocks[turn][start : start + ROWS, :] + 3.75)
            for m in range(ROWS):
                level = jnp.broadcast_to(levels[m : m + 1, :], (SUB, LANES))
                diagonal[slab + deep, :, m * LANES : (m + 1) * LANES] = level
    second_work[...] = jnp.zeros_like(second_work)
    scalars[ITERS] = jnp.zeros((count, LANES), jnp.float32)

    all_rows = [pl.ds(group * SUB, SUB) for group in range(groups)]
    all_lanes = [slice(m * LANES, (m + 1) * LANES) for m in range(ROWS)]
    def keep_y_parts(plane, rows, values):
        for ref, parts_of in zip((sums, edges), y_parts(values, last_x, first_x)):
            for lanes, part in zip(all_lanes, parts_of):
                ref[plane, rows, lanes] = part

    for group, rows in enumerate(all_rows):
        norm = []
        for plane in range(planes):
            values = plane_rows(first_work, plane, rows)
            keep_y_parts(plane, rows, values)
            norm.append(tree_sum([value * value for value in values]))
        partial[rows, :] = tree_sum(norm)

    def update_pass(i, work, before, alphas, betas):
        norm = [[] for _ in range(groups)]
        for plane in range(planes):
            columns = []
            for group, rows in enumerate(all_rows):
                values = []
                for lanes in all_lanes:
                    value = applied[plane, rows, lanes] - betas[group] * before[plane, rows, lanes]
                    value = value - alphas[group] * work[plane, rows, lanes]
                    before[plane, rows, lanes] = value
                    values.append(value)
                keep_y_parts(plane, rows, values)
                norm[group].append(tree_sum([value * value for value in values]))
                columns.append(values)
            for lanes, *column in zip(all_lanes, *columns):
                high, low = split(jnp.concatenate(column, axis=0))
                highs[i + 1, plane, :, lanes] = high
                lows[i + 1, plane, :, lanes] = low
        for rows, terms in zip(all_rows, norm):
            partial[rows, :] = tree_sum(terms)

    def half_turn(i, work, before, may_end):
        norms = [lane_sum(partial[rows, :]) for rows in all_rows]
        betas = [
            ratio(norm, scalars[ITERS + i, rows, :]) for norm, rows in zip(norms, all_rows)
        ]
        inverses = [ratio(jnp.ones_like(norm), norm) for norm in norms]
        for norm, rows in zip(norms, all_rows):
            scalars[ITERS + 1 + i, rows, :] = norm
        curve = [[] for _ in range(groups)]
        for plane in range(planes):
            for group, rows in enumerate(all_rows):
                value, out = apply_plane(work, sums, edges, diagonal, plane, rows)
                for m, lanes in enumerate(all_lanes):
                    applied[plane, rows, lanes] = out[m]
                curve[group].append(tree_sum([value[m] * out[m] for m in range(ROWS)]))
        alphas = [lane_sum(tree_sum(curve[g])) * inverses[g] for g in range(groups)]
        for alpha, rows in zip(alphas, all_rows):
            scalars[i, rows, :] = alpha
        if may_end:
            pl.when(i < ITERS - 1)(lambda: update_pass(i, work, before, alphas, betas))
        else:
            update_pass(i, work, before, alphas, betas)

    def turn(step, carry):
        half_turn(2 * step, first_work, second_work, False)
        half_turn(2 * step + 1, second_work, first_work, True)
        return carry

    lax.fori_loop(0, ITERS // 2, turn, 0)


def gram_kernel(points, scalars, *refs):
    tiles = refs[:points]
    highs, lows, applied, out_b, out_a, limits = refs[points:]
    planes, count, _ = applied.shape
    groups = count // SUB
    size = BASIS * count
    here = lax.axis_index("point")
    core = jnp.bitwise_and(lax.axis_index("dom"), CORES - 1)
    for far, tile in zip((0, 1 + core, 3, 2 - core), tiles):
        limits[jnp.bitwise_xor(here, far)] = tile[:SUB, :]

    bounds = [jnp.concatenate([limits[j]] * groups, axis=0) for j in range(points)]
    alphas = [scalars[i] for i in range(ITERS)]
    norms = [scalars[ITERS + 1 + i] for i in range(ITERS)]
    gram = None
    for plane in range(planes):
        if plane == planes // 2:
            weights = weights_of(alphas, norms, bounds)
            real = jnp.concatenate([pair[0] for pair in weights], axis=0)
            imag = jnp.concatenate([pair[1] for pair in weights], axis=0)
        last_high, last_low = split(applied[plane])
        high = jnp.concatenate([highs[i, plane] for i in range(ITERS)] + [last_high], axis=0)
        low = jnp.concatenate([lows[i, plane] for i in range(ITERS)] + [last_low], axis=0)
        product = lax.dot_general(
            jnp.concatenate([high, low], axis=0),
            high,
            (((1,), (1,)), ((), ())),
            preferred_element_type=jnp.float32,
        )
        gram = product if gram is None else gram + product
    cross = gram[size:, :]
    pairs = gram[:size, :] + cross + cross.T
    right = exact_dot(pairs, jnp.concatenate([real, imag], axis=1), ((1,), (0,)))
    half = MOMENTS * count
    left = jnp.concatenate([real[:, :half], imag[:, :half]], axis=1)
    joined = exact_dot(left.T, right, ((1,), (0,)))
    scale = 1.0 / (planes * ROWS * LANES)
    width = 2 * half
    real = (joined[:half, :width] + joined[half:, width:]) * scale
    imag = (joined[:half, width:] - joined[half:, :width]) * scale
    out_b[0] = real[:, :half]
    out_b[1] = imag[:, :half]
    out_a[0] = real[:, half:]
    out_a[1] = imag[:, half:]


def swapped(values, axis, size, mask):
    return lax.ppermute(values, axis, [(index ^ mask, index) for index in range(size)])


def whole_grid(sources, potential, iter_counts, *, parts, points):
    count, depth, _ = sources.shape
    planes = parts * depth
    block = packed_block(sources, potential)
    tile = jnp.broadcast_to(iter_counts.astype(jnp.float32), (TILE, LANES))
    tile = lax.optimization_barrier(tile)
    even = [block] + [swapped(block, "dom", parts, mask) for mask in range(CORES, parts, CORES)]
    mixed = [
        ((point ^ (1 + part % CORES)) * parts + part, point * parts + part)
        for point in range(points)
        for part in range(parts)
    ]
    tiles = [lax.ppermute(tile, ("point", "dom"), mixed), swapped(tile, "point", points, 3)]
    tiles = list(lax.optimization_barrier(tuple(tiles)))
    tiles.append(swapped(tiles[0], "dom", parts, 1))
    own, even[1] = lax.optimization_barrier((block, even[1]))
    odd = [swapped(value, "dom", parts, 1) for value in [own] + even[1:]]
    blocks = [value for pair in zip(even, odd) for value in pair]
    vmem = pl.BlockSpec(memory_space=pltpu.VMEM)
    vector = (planes, count, ROWS * LANES)
    cells = planes * ROWS * LANES
    highs, lows, applied, scalars = pl.pallas_call(
        functools.partial(krylov_kernel, parts, count),
        out_shape=(
            jax.ShapeDtypeStruct((ITERS,) + vector, jnp.bfloat16),
            jax.ShapeDtypeStruct((ITERS,) + vector, jnp.bfloat16),
            jax.ShapeDtypeStruct(vector, jnp.float32),
            jax.ShapeDtypeStruct((2 * ITERS + 1, count, LANES), jnp.float32),
        ),
        in_specs=[vmem] * parts,
        out_specs=(vmem,) * 4,
        scratch_shapes=[
            pltpu.VMEM(vector, jnp.float32),
            pltpu.VMEM(vector, jnp.float32),
            pltpu.VMEM((planes, SUB, ROWS * LANES), jnp.float32),
            pltpu.VMEM(vector, jnp.float32),
            pltpu.VMEM(vector, jnp.float32),
            pltpu.VMEM((count, LANES), jnp.float32),
        ],
        compiler_params=pltpu.CompilerParams(vmem_limit_bytes=16 * 2**20),
        name="krylov",
    )(*blocks)
    width = MOMENTS * count
    out = jax.ShapeDtypeStruct((2, width, width), jnp.float32)
    return pl.pallas_call(
        functools.partial(gram_kernel, points),
        out_shape=(out, out),
        in_specs=[vmem] * (4 + points),
        out_specs=(vmem, vmem),
        scratch_shapes=[pltpu.VMEM((points, SUB, LANES), jnp.float32)],
        compiler_params=pltpu.CompilerParams(vmem_limit_bytes=16 * 2**20),
        name="gram",
    )(scalars, tile, *tiles, highs, lows, applied)


def on_device(sources, potential, iter_counts):
    parts, points = lax.axis_size("dom"), lax.axis_size("point")
    count, depth, cells = sources.shape
    held = BASIS * count * parts * depth * cells * 4
    fits = (
        held <= 16 * 2**20
        and parts == 8
        and points == 4
        and count == 2 * SUB
        and 2 * MOMENTS * count == LANES
        and parts * depth == 16
        and cells == GX * GX == ROWS * LANES
    )
    if not fits:
        return split_grid(sources, potential, iter_counts)
    return whole_grid(sources, potential, iter_counts, parts=parts, points=points)


def solution(mesh):
    placed = (P(None, "dom", None), P("dom", None), P("point"))
    return jax.shard_map(
        on_device, mesh=mesh, in_specs=placed, out_specs=(P(), P()), check_vma=False
    )
```
